128 devices in a mesh: sp: 16 (over x, y), wt: 8 (over z, core).
Axes of the slice: x: 4, y: 4, z: 4, core: 2. Of those that a mesh axis runs over, the one named last changes fastest.
Arguments:
- tokens: bfloat16 [8192, 1024], P('sp'), may hold values from -6 to 6
- norm_in: float32 [1024], replicated, may hold values from 0.5 to 1.5
- w_query: bfloat16 [1024, 1024], P(None, 'wt'), may hold values from -0.1875 to 0.1875
- w_key: bfloat16 [1024, 512], P(None, 'wt'), may hold values from -0.1875 to 0.1875
- w_value: bfloat16 [1024, 512], P(None, 'wt'), may hold values from -0.1875 to 0.1875
- query_gain: float32 [64], replicated, may hold values from 0.5 to 1.5
- key_gain: float32 [64], replicated, may hold values from 0.5 to 1.5
- w_out: bfloat16 [1024, 1024], P('wt'), may hold values from -1.5 to 1.5
- norm_mid: float32 [1024], replicated, may hold values from 0.5 to 1.5
- w_gate: bfloat16 [1024, 4608], P(None, 'wt'), may hold values from -0.1875 to 0.1875
- w_up: bfloat16 [1024, 4608], P(None, 'wt'), may hold values from -0.1875 to 0.1875
- w_down: bfloat16 [4608, 1024], P('wt'), may hold values from -0.09375 to 0.09375
- cotangent: bfloat16 [8192, 1024], P('sp'), may hold values from -6 to 6
- lengths: int32 [4], replicated, may hold values from 1 to 7936, as said below
Outputs:
- output: bfloat16 [8192, 1024], P('sp')
- grad_tokens: bfloat16 [8192, 1024], P('sp')
- grad_norm_in: float32 [1024], replicated
- grad_w_query: float32 [1024, 1024], P(None, 'wt')
- grad_w_key: float32 [1024, 512], P(None, 'wt')
- grad_w_value: float32 [1024, 512], P(None, 'wt')
- grad_query_gain: float32 [64], replicated
- grad_key_gain: float32 [64], replicated
- grad_w_out: float32 [1024, 1024], P('wt')
- grad_norm_mid: float32 [1024], replicated
- grad_w_gate: float32 [1024, 4608], P(None, 'wt')
- grad_w_up: float32 [1024, 4608], P(None, 'wt')
- grad_w_down: float32 [4608, 1024], P('wt')
The draws below stay inside these ranges and needn't reach their ends.
Inputs may be any that keep to these rules, and one draw needn't show every extreme that they name: `lengths`: every length is at least 1, they sum to 8192, and exactly one is 7936.
All inputs are finite; a program needn't handle non-finite values.
Results may differ from the reference program's by a relative error of at most 0.028.
Values may be sent and summed in bfloat16 or wider, within the bound.
A program may use at most 128 MiB of HBM per device.

```python
import jax
import jax.numpy as jnp
from jax import lax

D = 1024
HEADS = 16
KV_HEADS = 8
HD = 64
FF = 4608
TOK_DEV = 512
NSEQ = 4
TOKENS = 8192
MOST = 7936


def draw_lengths(key, part):
    key = jax.random.fold_in(key, 11)
    slot_key, cut_key = jax.random.split(key)
    rest = TOK_DEV // 2
    slot = jax.random.randint(slot_key, (), 0, NSEQ).astype(jnp.int32)
    order = jax.random.permutation(cut_key, rest - 1).astype(jnp.int32) + 1
    cuts = jnp.sort(order[:NSEQ - 2]).astype(jnp.int32)
    edges = jnp.concatenate([jnp.zeros((1,), jnp.int32), cuts, jnp.full((1,), rest, jnp.int32)])
    others = (edges[1:] - edges[:-1]).astype(jnp.int32)
    index = jnp.arange(NSEQ).astype(jnp.int32)
    before = others[jnp.clip(index, 0, NSEQ - 2)]
    after = others[jnp.clip(index - 1, 0, NSEQ - 2)]
    return jnp.where(index < slot, before, jnp.where(index == slot, MOST, after)).astype(jnp.int32)


def block_scale(rng, dims, cuts, least, top_value):
    factor_of, own = 1.0, jax.random.fold_in(rng, 6)
    for dim, parts in cuts:
        steps = jnp.exp(jax.random.uniform(jax.random.fold_in(own, dim), (parts,), jnp.float32, least / len(cuts), top_value / len(cuts)))
        factor_of = factor_of * jnp.repeat(steps, dims[dim] // parts).reshape([-1 if axis == dim else 1 for axis in range(len(dims))])
    return factor_of


def normal_values(own_key, dims, width, reach, shards=(), dtype=jnp.bfloat16):
    entries = width * jax.random.normal(own_key, dims, jnp.float32)
    if shards:
        entries = entries * block_scale(own_key, dims, shards, -0.22, 0.18)
    return jnp.clip(entries, -reach, reach).astype(dtype)


def setup_inputs(seed: int = 0) -> dict:
    streams_of = jax.random.split(jax.random.key(seed), 15)
    tokens = normal_values(streams_of[0], (TOKENS, D), 1.0, 6.0, ((0, 16),))
    norm_in = jnp.clip(1.0 + 0.1 * jax.random.normal(streams_of[1], (D,), jnp.float32), 0.5, 1.5)
    w_query = normal_values(streams_of[2], (D, HEADS * HD), D ** -0.5, 0.1875, ((1, 8),))
    w_key = normal_values(streams_of[3], (D, KV_HEADS * HD), D ** -0.5, 0.1875, ((1, 8),))
    w_value = normal_values(streams_of[4], (D, KV_HEADS * HD), D ** -0.5, 0.1875, ((1, 8),))
    query_gain = jnp.clip(1.0 + 0.1 * jax.random.normal(streams_of[5], (HD,), jnp.float32), 0.5, 1.5)
    key_gain = jnp.clip(1.0 + 0.1 * jax.random.normal(streams_of[6], (HD,), jnp.float32), 0.5, 1.5)
    w_out = normal_values(streams_of[7], (HEADS * HD, D), (D // 64) ** -0.5, 1.5, ((0, 8),))
    norm_mid = jnp.clip(1.0 + 0.1 * jax.random.normal(streams_of[8], (D,), jnp.float32), 0.5, 1.5)
    w_gate = normal_values(streams_of[9], (D, FF), D ** -0.5, 0.1875, ((1, 8),))
    w_up = normal_values(streams_of[10], (D, FF), D ** -0.5, 0.1875, ((1, 8),))
    w_down = normal_values(streams_of[11], (FF, D), FF ** -0.5, 0.09375, ((0, 8),))
    cotangent = normal_values(streams_of[12], (TOKENS, D), 1.0, 6.0, ((0, 16),))
    lengths = draw_lengths(jax.random.fold_in(streams_of[14], 71), 0)
    return dict(tokens=tokens, norm_in=norm_in, w_query=w_query, w_key=w_key, w_value=w_value, query_gain=query_gain, key_gain=key_gain, w_out=w_out, norm_mid=norm_mid, w_gate=w_gate, w_up=w_up, w_down=w_down, cotangent=cotangent, lengths=lengths)


@jax.custom_vjp
def low(v):
    return lax.optimization_barrier(v.astype(jnp.bfloat16)).astype(jnp.float32)

@jax.custom_vjp
def low_back(v):
    return v

def low_keep(v):
    return (low(v), None)

def low_pass(kept, grad):
    return (grad,)

def back_keep(v):
    return (v, None)

def back_low(kept, grad):
    return (low(grad),)
low.defvjp(low_keep, low_pass)
low_back.defvjp(back_keep, back_low)
eps = 1e-05
theta = 1000000.0
highest = lax.Precision.HIGHEST

def rms_scale(values):
    return lax.rsqrt(lax.optimization_barrier(jnp.mean(values * values, axis=-1, keepdims=True)) + eps)

def rope_tables(positions, head_dim):
    freqs = theta ** (-(jnp.arange(head_dim // 2).astype(jnp.float32) * 2.0) / head_dim)
    angles = positions.astype(jnp.float32)[:, None] * freqs[None, :]
    angles = jnp.concatenate([angles, angles], axis=-1)
    return (jnp.cos(angles), jnp.sin(angles))

def rotate(values, cosine, sine):
    half = values.shape[-1] // 2
    turned = jnp.concatenate([-values[..., half:], values[..., :half]], axis=-1)
    return values * cosine + turned * sine

def segments_of(token_ids, lengths):
    ends = jnp.cumsum(lengths).astype(jnp.int32)
    segment = lax.optimization_barrier(jnp.sum((token_ids[:, None] >= ends[None, :]).astype(jnp.int32), axis=1)).astype(jnp.int32)
    starts = (ends - lengths).astype(jnp.int32)
    which = segment[:, None] == jnp.arange(lengths.shape[0]).astype(jnp.int32)[None, :]
    start_of = lax.optimization_barrier(jnp.sum(jnp.where(which, starts[None, :], 0), axis=1)).astype(jnp.int32)
    return (segment, (token_ids - start_of).astype(jnp.int32))

def forward(tokens, norm_in, w_query, w_key, w_value, query_gain, key_gain, w_out, norm_mid, w_gate, w_up, w_down, segment, positions):
    total = tokens.shape[0]
    head_dim = query_gain.shape[0]
    heads = w_query.shape[1] // head_dim
    kv_heads = w_key.shape[1] // head_dim
    group = heads // kv_heads
    scale = head_dim ** (-0.5)
    cosine, sine = rope_tables(positions, head_dim)
    cosine = cosine[:, None, :]
    sine = sine[:, None, :]
    normed = low(tokens * rms_scale(tokens) * norm_in)
    q_proj = low_back(jnp.dot(normed, w_query, precision=highest)).reshape(total, heads, head_dim)
    k_proj = low_back(jnp.dot(normed, w_key, precision=highest)).reshape(total, kv_heads, head_dim)
    queries = low(low_back(rotate(q_proj * rms_scale(q_proj) * query_gain, cosine, sine)))
    keys = low(low_back(rotate(k_proj * rms_scale(k_proj) * key_gain, cosine, sine)))
    values = low(low_back(jnp.dot(normed, w_value, precision=highest))).reshape(total, kv_heads, head_dim)
    grouped = queries.reshape(total, kv_heads, group, head_dim)
    block = min(512, total)
    key_ids = jnp.arange(total).astype(jnp.int32)

    def attend(start):
        rows = lax.dynamic_slice_in_dim(grouped, start, block, 0)
        row_seg = lax.dynamic_slice_in_dim(segment, start, block, 0)
        row_ids = start + jnp.arange(block).astype(jnp.int32)
        scores = low_back(jnp.einsum('tgjd,sgd->gjts', rows, keys, precision=highest) * scale)
        allowed = (key_ids[None, :] <= row_ids[:, None]) & (segment[None, :] == row_seg[:, None])
        scores = jnp.where(allowed[None, None], scores, -1e+30)
        largest = lax.optimization_barrier(jnp.max(scores, axis=-1, keepdims=True))
        weights = jnp.exp(scores - largest)
        probs = weights / lax.optimization_barrier(jnp.sum(weights, axis=-1, keepdims=True))
        return jnp.einsum('gjts,sgd->tgjd', low(probs), values, precision=highest)
    starts = (jnp.arange(total // block) * block).astype(jnp.int32)
    mixed = lax.map(jax.checkpoint(attend), starts)
    mixed = low(low_back(mixed.reshape(total, heads * head_dim)))
    attn = low_back(jnp.dot(mixed, w_out, precision=highest))
    middle = tokens + attn
    normed_mid = low(middle * rms_scale(middle) * norm_mid)
    gate = low_back(jnp.dot(normed_mid, w_gate, precision=highest))
    up_proj = low_back(jnp.dot(normed_mid, w_up, precision=highest))
    act = low(jax.nn.silu(gate) * up_proj)
    return middle + jnp.dot(act, w_down, precision=highest)

def reference(tokens, norm_in, w_query, w_key, w_value, query_gain, key_gain, w_out, norm_mid, w_gate, w_up, w_down, cotangent, lengths):
    total = tokens.shape[0]
    token_ids = jnp.arange(total).astype(jnp.int32)
    segment, positions = segments_of(token_ids, lengths)
    floats = tuple((a.astype(jnp.float32) for a in (tokens, norm_in, w_query, w_key, w_value, query_gain, key_gain, w_out, norm_mid, w_gate, w_up, w_down)))

    def wrapped(*params):
        return forward(*params, segment, positions)
    result, pullback = jax.vjp(wrapped, *floats)
    grads = pullback(cotangent.astype(jnp.float32))
    return (result.astype(jnp.bfloat16), grads[0].astype(jnp.bfloat16), grads[1], grads[2], grads[3], grads[4], grads[5], grads[6], grads[7], grads[8], grads[9], grads[10], grads[11])
```

```python
import functools, math
import jax
import jax.numpy as jnp
from jax import lax
from jax.experimental import pallas as pl
from jax.experimental.pallas import tpu as pltpu
from jax.sharding import PartitionSpec as P

f32 = jnp.float32
bf16 = jnp.bfloat16
CH = 512
HALF = 256
SCALE = 0.125
C2 = SCALE * math.log2(math.e)


def starts_of(ids, len_ref):
    end = jnp.int32(0)
    start = jnp.zeros_like(ids)
    for j in range(4):
        end = end + len_ref[j]
        start = start + jnp.where(ids >= end, len_ref[j], 0)
    return start


def scalar_start(row, len_ref):
    end = jnp.int32(0)
    start = jnp.int32(0)
    for j in range(4):
        end = end + len_ref[j]
        start = start + jnp.where(row >= end, len_ref[j], 0)
    return start


def key_ranges(r0, len_ref, ch):
    low = scalar_start(r0, len_ref)
    high = scalar_start(r0 + HALF - 1, len_ref)
    first = low // ch
    last = (r0 + HALF - 1) // ch + 1
    free = jnp.clip((high + ch - 1) // ch, first, last)
    diag = jnp.clip((r0 + 1) // ch, free, last)
    return first, free, diag, last


def lanes(shape):
    return lax.broadcasted_iota(jnp.int32, shape, len(shape) - 1)


def split3(value, lane):
    hi = value.astype(bf16).astype(f32)
    rest = value - hi
    mid = rest.astype(bf16).astype(f32)
    low = rest - mid
    return jnp.where(lane == 0, hi, jnp.where(lane == 1, mid, jnp.where(lane == 2, low, 0.0)))


def tile_row(me, t, parts):
    return me * 512 if t == 0 else (parts - 1 - me) * 512 + HALF


def fwd_kernel(parts, me_ref, len_ref, q_ref, kv_ref, mix_ref, out_ref, qa_ref, qs_ref, acc_ref):
    me = me_ref[0]
    lane = lanes((HALF, 128))
    lane2 = lanes((2 * HALF, 128))
    lanek = lanes((CH, 128))
    for t in range(2):
        r0 = tile_row(me, t, parts)
        q = q_ref[t * HALF:(t + 1) * HALF, :].astype(f32)
        qs_ref[0:HALF, :] = jnp.where(lane < 64, q, 0.0).astype(bf16)
        qs_ref[HALF:, :] = jnp.where(lane < 64, pltpu.roll(q, 64, 1), 0.0).astype(bf16)
        acc_ref[...] = jnp.zeros_like(acc_ref)

        def step(c, masked):
            k0 = pl.multiple_of(c * CH, CH)
            kv = kv_ref[pl.ds(k0, CH), :]
            s = lax.dot_general(qs_ref[...], kv, (((1,), (1,)), ((), ())), preferred_element_type=f32)
            p = jnp.exp2(s * C2)
            if masked:
                rows = r0 + lax.rem(lax.broadcasted_iota(jnp.int32, (2 * HALF, 1), 0), HALF)
                keys = k0 + lax.broadcasted_iota(jnp.int32, (2 * HALF, CH), 1)
                p = jnp.where((keys <= rows) & (keys >= starts_of(rows, len_ref)), p, 0.0)
            ones = jnp.where(lanek < 64, jnp.ones_like(kv), kv)
            acc_ref[...] += jnp.dot(p.astype(bf16), ones, preferred_element_type=f32)

        first, free, diag, last = key_ranges(r0, len_ref, CH)
        pl.loop(first, free)(lambda c: step(c, True))
        pl.loop(free, diag)(lambda c: step(c, False))
        pl.loop(diag, last)(lambda c: step(c, True))

        acc = acc_ref[...]
        swapped = pltpu.roll(acc, 64, 1)
        o = swapped / acc
        m = jnp.where(lane < 64, o[:HALF], pltpu.roll(o[HALF:], 64, 1))
        mix_ref[t * HALF:(t + 1) * HALF, :] = m.astype(bf16)
        out_ref[t * HALF:(t + 1) * HALF, :] = m
        total = jnp.where(lane2 < 64, acc, swapped)
        qa_ref[t, :, 0:128] = qs_ref[...]
        qa_ref[t, :, 128:256] = split3(jnp.log(total) * (-1.0 / SCALE), lane2).astype(bf16)


def bwd_kernel(parts, me_ref, len_ref, qa_ref, out_ref, do_ref, kv_ref, dq_ref, dkv_ref, da_ref, acc_ref, dqt_ref):
    me = me_ref[0]
    lane = lanes((HALF, 128))
    ones3 = jnp.where(lanes((CH, 128)) < 3, 1.0, 0.0).astype(bf16)
    acc_ref[...] = jnp.zeros_like(acc_ref)
    for t in range(2):
        r0 = tile_row(me, t, parts)
        rows_t = slice(t * HALF, (t + 1) * HALF)
        do = do_ref[rows_t, :].astype(f32)
        prod = do * out_ref[rows_t, :]
        d0 = -jnp.sum(jnp.where(lane < 64, prod, 0.0), axis=1, keepdims=True)
        d1 = -jnp.sum(jnp.where(lane < 64, 0.0, prod), axis=1, keepdims=True)
        da_ref[0:HALF, 0:128] = jnp.where(lane < 64, 0.0, pltpu.roll(do, 64, 1)).astype(bf16)
        da_ref[HALF:, 0:128] = jnp.where(lane < 64, 0.0, do).astype(bf16)
        da_ref[0:HALF, 128:256] = split3(jnp.broadcast_to(d0, (HALF, 128)), lane).astype(bf16)
        da_ref[HALF:, 128:256] = split3(jnp.broadcast_to(d1, (HALF, 128)), lane).astype(bf16)
        dqt_ref[...] = jnp.zeros_like(dqt_ref)

        def step(c, masked):
            k0 = pl.multiple_of(c * CH, CH)
            kv = kv_ref[pl.ds(k0, CH), :]
            kva = jnp.concatenate([kv, ones3], axis=1)
            qa = qa_ref[t]
            da = da_ref[...]
            s = lax.dot_general(kva, qa, (((1,), (1,)), ((), ())), preferred_element_type=f32)
            p = jnp.exp2(s * C2)
            if masked:
                rows = r0 + lax.rem(lax.broadcasted_iota(jnp.int32, (1, 2 * HALF), 1), HALF)
                keys = k0 + lax.broadcasted_iota(jnp.int32, (CH, 2 * HALF), 0)
                p = jnp.where((keys <= rows) & (keys >= starts_of(rows, len_ref)), p, 0.0)
            dp = lax.dot_general(kva, da, (((1,), (1,)), ((), ())), preferred_element_type=f32)
            ds = (p * dp).astype(bf16)
            acc_ref[pl.ds(k0, CH), :] += jnp.dot(
                p.astype(bf16), da[:, 0:128], preferred_element_type=f32
            ) + jnp.dot(ds, qa[:, 0:128], preferred_element_type=f32)
            kt = kv.T[0:64, :]
            dqt_ref[...] += jnp.dot(kt, ds, preferred_element_type=f32)

        first, free, diag, last = key_ranges(r0, len_ref, CH)
        pl.loop(first, free)(lambda c: step(c, True))
        pl.loop(free, diag)(lambda c: step(c, False))
        pl.loop(diag, last)(lambda c: step(c, True))
        dqt = dqt_ref[...]
        both = jnp.concatenate([dqt[:, :HALF], dqt[:, HALF:]], axis=0)
        dq_ref[rows_t, :] = (both.T * SCALE).astype(bf16)
    weight = jnp.where(lanes((512, 128)) < 64, SCALE, 1.0)

    @pl.loop(0, parts)
    def _(b):
        rows = pl.ds(pl.multiple_of(b * 512, 512), 512)
        dkv_ref[rows, :] = (acc_ref[rows, :] * weight).astype(bf16)


smem = pl.BlockSpec(memory_space=pltpu.SMEM)
vmem = pl.BlockSpec(memory_space=pltpu.VMEM)


def attend(parts, me, lengths, q, kv):
    rows = 2 * HALF
    sds = jax.ShapeDtypeStruct
    return pl.pallas_call(
        functools.partial(fwd_kernel, parts),
        out_shape=(sds((rows, 128), bf16), sds((rows, 128), f32), sds((2, rows, 256), bf16)),
        in_specs=[smem, smem, vmem, vmem],
        out_specs=(vmem, vmem, vmem),
        scratch_shapes=[pltpu.VMEM((rows, 128), bf16), pltpu.VMEM((rows, 128), f32)],
        compiler_params=pltpu.CompilerParams(vmem_limit_bytes=48 << 20),
        cost_estimate=pl.CostEstimate(flops=3 << 30, bytes_accessed=4 << 20, transcendentals=5 << 20),
        name="attend",
    )(me, lengths, q, kv)


def attend_back(parts, me, lengths, qa, out, do, kv):
    rows = 2 * HALF
    sds = jax.ShapeDtypeStruct
    return pl.pallas_call(
        functools.partial(bwd_kernel, parts),
        out_shape=(sds((rows, 128), bf16), sds(kv.shape, bf16)),
        in_specs=[smem, smem, vmem, vmem, vmem, vmem],
        out_specs=(vmem, vmem),
        scratch_shapes=[pltpu.VMEM((rows, 256), bf16), pltpu.VMEM(kv.shape, f32), pltpu.VMEM((64, rows), f32)],
        compiler_params=pltpu.CompilerParams(vmem_limit_bytes=48 << 20),
        cost_estimate=pl.CostEstimate(flops=10 << 30, bytes_accessed=8 << 20, transcendentals=5 << 20),
        name="attend_back",
    )(me, lengths, qa, out, do, kv)
MESH = pl.DeviceIdType.MESH
eps = 1e-05


def rcopy(src, dst, send, recv, device):
    return pltpu.make_async_remote_copy(
        src_ref=src, dst_ref=dst, send_sem=send, recv_sem=recv, device_id=device, device_id_type=MESH
    )


def meet(devices):
    barrier = pltpu.get_barrier_semaphore()
    for device in devices:
        pl.semaphore_signal(barrier, inc=1, device_id=device, device_id_type=MESH)
    pl.semaphore_wait(barrier, len(devices))


class Place:
    def __init__(self):
        self.sp = lax.axis_index("sp")
        self.wt = lax.axis_index("wt")
        self.x, self.y = lax.div(self.sp, 4), lax.rem(self.sp, 4)
        self.z, self.c = lax.div(self.wt, 2), lax.rem(self.wt, 2)
        self.mirror = (15 - self.sp, self.wt)
        self.sibling = (self.sp, self.z * 2 + 1 - self.c)

    def along_x(self, d):
        return (lax.rem(self.x + d, 4) * 4 + self.y, self.wt)

    def along_y(self, d):
        return (self.x * 4 + lax.rem(self.y + d, 4), self.wt)

    def along_z(self, d):
        return (self.sp, lax.rem(self.z + d, 4) * 2 + self.c)

    def along_z_other(self, d):
        return (self.sp, lax.rem(self.z + d, 4) * 2 + 1 - self.c)

    def first(self, h, d):
        return self.along_x(d) if h == 0 else self.along_y(d)

    def second(self, h, d):
        return self.along_y(d) if h == 0 else self.along_x(d)

    def fsp(self, h):
        return self.x if h == 0 else self.y

    def ssp(self, h):
        return self.y if h == 0 else self.x


def spot(h, first, second):
    return (first, second) if h == 0 else (second, first)


ORDER = (2, 1, 3)


def gather_kernel(q_ref, kv_ref, qz_ref, all_ref, ms, mr, fs, fr, ss, sr):
    p = Place()
    meet([p.along_x(d) for d in ORDER] + [p.along_y(d) for d in ORDER] + [p.mirror])
    all_ref[p.x, p.y] = kv_ref[...]
    mirror = rcopy(q_ref.at[1], qz_ref.at[1], ms, mr, p.mirror)
    first, second = {}, {}
    for d in ORDER:
        for h in range(2):
            first[h, d] = rcopy(
                kv_ref.at[h], all_ref.at[p.x, p.y, h], fs.at[h, d - 1], fr.at[h, d - 1], p.first(h, d)
            )
            first[h, d].start()
    mirror.start()

    def forward(h, slot):
        a = lax.rem(p.fsp(h) + 4 - slot, 4)
        at = spot(h, a, p.ssp(h))
        for e in ORDER:
            src = kv_ref.at[h] if slot == 0 else all_ref.at[at[0], at[1], h]
            second[h, slot, e] = rcopy(
                src, all_ref.at[at[0], at[1], h], ss.at[h, slot, e - 1], sr.at[h, slot, e - 1], p.second(h, e)
            )
            second[h, slot, e].start()

    for h in range(2):
        forward(h, 0)
    qz_ref[0] = q_ref[0]
    for d in (1, 3, 2):
        for h in range(2):
            first[h, d].wait_recv()
            forward(h, d)
    mirror.wait()
    for copy in first.values():
        copy.wait_send()
    for copy in second.values():
        copy.wait()


def scatter_kernel(dkv_ref, dqz_ref, own_ref, dq_ref, r1, send, r2, ms, mr, fs, fr, ss, sr):
    p = Place()
    meet([p.along_x(d) for d in ORDER] + [p.along_y(d) for d in ORDER] + [p.mirror])
    first, second = {}, {}
    for d in ORDER:
        for h in range(2):
            to = lax.rem(p.fsp(h) + d, 4)
            src = dkv_ref.at[to, :, 0] if h == 0 else dkv_ref.at[:, to, 1]
            first[h, d] = rcopy(src, r1.at[h, d - 1], fs.at[h, d - 1], fr.at[h, d - 1], p.first(h, d))
            first[h, d].start()
    mirror = rcopy(dqz_ref.at[1], dq_ref.at[1], ms, mr, p.mirror)
    mirror.start()
    dq_ref[0] = dqz_ref[0]

    def total(h, b):
        at = spot(h, p.fsp(h), b)
        value = dkv_ref[at[0], at[1], h].astype(f32)
        for d in range(3):
            value = value + r1[h, d, b].astype(f32)
        return value

    for h in range(2):
        for d in ORDER:
            first[h, d].wait_recv()
        for e in ORDER:
            b = lax.rem(p.ssp(h) + e, 4)
            send[h, e - 1] = total(h, b).astype(bf16)
            second[h, e] = rcopy(
                send.at[h, e - 1], r2.at[h, e - 1], ss.at[h, e - 1], sr.at[h, e - 1], p.second(h, e)
            )
            second[h, e].start()
    for h in range(2):
        value = total(h, p.ssp(h))
        for e in ORDER:
            second[h, e].wait_recv()
            value = value + r2[h, e - 1].astype(f32)
        own_ref[h] = value.astype(bf16)
    mirror.wait()
    for copy in list(first.values()) + list(second.values()):
        copy.wait_send()


class WtSum:
    def __init__(self, p, part, sib, send, rz, sems):
        self.p, self.part, self.sib, self.send, self.rz = p, part, sib, send, rz
        self.cs, self.cr, self.zs, self.zr = sems
        self.second = {}

    def core(self, zz):
        return rcopy(
            self.part.at[zz * 2 + 1 - self.p.c], self.sib.at[zz], self.cs.at[zz], self.cr.at[zz], self.p.sibling
        )

    def start_core(self, zz):
        self.core(zz).start()

    def pair(self, zz):
        return self.part[zz * 2 + self.p.c].astype(f32) + self.sib[zz].astype(f32)

    def send_z(self, d):
        zz = lax.rem(self.p.z + d, 4)
        self.core(zz).wait_recv()
        self.send[d - 1] = self.pair(zz).astype(bf16)
        copy = rcopy(
            self.send.at[d - 1], self.rz.at[d - 1], self.zs.at[d - 1], self.zr.at[d - 1], self.p.along_z(d)
        )
        copy.start()
        self.second[d] = copy

    def own(self):
        self.core(self.p.z).wait_recv()
        value = self.pair(self.p.z)
        for d in (1, 3, 2):
            self.second[d].wait_recv()
            value = value + self.rz[d - 1].astype(f32)
        return value

    def finish(self):
        for zz in range(4):
            self.core(zz).wait_send()
        for copy in self.second.values():
            copy.wait_send()


class WtGather:
    def __init__(self, p, out, sems):
        self.p, self.out = p, out
        self.zs, self.zr, self.gs, self.gr = sems
        self.far, self.near = {}, {}

    def start(self):
        p = self.p
        for d in ORDER:
            self.far[d] = rcopy(
                self.out.at[p.wt], self.out.at[p.wt], self.zs.at[d - 1], self.zr.at[d - 1], p.along_z(d)
            )
            self.far[d].start()
        self.pass_on(0)

    def pass_on(self, slot):
        p = self.p
        row = lax.rem(p.z + 4 - slot, 4) * 2 + p.c
        self.near[slot] = rcopy(
            self.out.at[row], self.out.at[row], self.gs.at[slot], self.gr.at[slot], p.sibling
        )
        self.near[slot].start()

    def forward(self):
        for d in (1, 3, 2):
            self.far[d].wait_recv()
            self.pass_on(d)

    def arrived(self):
        for slot in (0, 1, 3, 2):
            self.near[slot].wait_recv()

    def finish(self):
        for copy in list(self.far.values()) + list(self.near.values()):
            copy.wait_send()


def rms_of(value):
    return lax.rsqrt(jnp.mean(value * value, axis=-1, keepdims=True) + eps)


def norm_back(values, scale, gain, grad):
    scaled = grad * gain
    inner = jnp.mean(scaled * values, axis=-1, keepdims=True)
    return scale * scaled - values * scale * scale * scale * inner


def wt_peers(p):
    return [p.sibling] + [p.along_z(d) for d in ORDER]


def middle_kernel(mix_ref, w_ref, tok_ref, gain_ref, nm_ref, mid_ref, mixo_ref, part, sib, send, rz, ms, mr, cs, cr, zs, zr, az, bz, ag, bg):
    p = Place()
    meet(wt_peers(p) + [p.mirror])
    mirror = rcopy(mix_ref.at[1], mixo_ref.at[1], ms, mr, p.mirror)
    mirror.start()
    mixo_ref[0] = mix_ref[0]
    total = WtSum(p, part, sib, send, rz, (cs, cr, zs, zr))
    for half in range(2):
        if half == 1:
            mirror.wait()
        both = jnp.dot(mixo_ref[half], w_ref[...], preferred_element_type=f32).astype(bf16)
        part[half * 4:half * 4 + 4] = both.reshape(4, 64, 1024)
        for zz in (half * 2, half * 2 + 1):
            total.start_core(zz)
    for d in ORDER:
        total.send_z(d)
    middle = tok_ref[p.wt].astype(f32) + total.own()
    mid_ref[...] = middle
    nm_ref[p.wt] = (middle * rms_of(middle) * gain_ref[...]).astype(bf16)
    spread = WtGather(p, nm_ref, (az, bz, ag, bg))
    spread.start()
    spread.forward()
    spread.arrived()
    spread.finish()
    total.finish()


def turn_kernel(dm_ref, mlp_ref, mid_ref, cot_ref, gain_ref, w_ref, out_ref, da_ref, dmid_ref, gn_ref, dz_ref, up, sib, send, rz, ms, mr, cs, cr, zs, zr, az, bz, ag, bg):
    p = Place()
    meet(wt_peers(p) + [p.mirror])
    totals = [
        WtSum(p, ref, sib.at[i], send.at[i], rz.at[i], (cs.at[i], cr.at[i], zs.at[i], zr.at[i]))
        for i, ref in enumerate((dm_ref, mlp_ref))
    ]
    for total in totals:
        for zz in range(4):
            total.start_core(zz)
    for total in totals:
        for d in ORDER:
            total.send_z(d)
    middle = mid_ref[...]
    scale = rms_of(middle)
    d_mid = totals[0].own()
    gn_ref[...] = jnp.sum(d_mid * middle * scale, axis=0, keepdims=True)
    d_middle = cot_ref[p.wt].astype(f32) + norm_back(middle, scale, gain_ref[...], d_mid)
    dmid_ref[...] = d_middle
    da_ref[p.wt] = d_middle.astype(bf16)
    spreads = [
        WtGather(p, ref, (az.at[i], bz.at[i], ag.at[i], bg.at[i])) for i, ref in enumerate((da_ref, out_ref))
    ]
    spreads[0].start()
    out_ref[p.wt] = (middle + totals[1].own()).astype(bf16)
    spreads[1].start()
    spreads[0].forward()
    spreads[0].arrived()
    mirror = rcopy(up, dz_ref.at[1], ms, mr, p.mirror)
    for half in (1, 0):
        rows = da_ref[half * 4:half * 4 + 4].reshape(256, 1024)
        d_mixed = lax.dot_general(rows, w_ref[...], (((1,), (1,)), ((), ())), preferred_element_type=f32).astype(bf16)
        if half == 1:
            up[...] = d_mixed
            mirror.start()
        else:
            dz_ref[0] = d_mixed
    spreads[1].forward()
    spreads[1].arrived()
    mirror.wait()
    for part in spreads + totals:
        part.finish()


def last_kernel(dn_ref, g_ref, tok_ref, dmid_ref, gain_ref, gn_ref, gg_ref, gt_ref, gq_ref, gkv_ref, vec_ref,
                sib, send, rz, cs, cr, zs, zr, az, bz, ag, bg,
                r1, s2, r2, gb, f1s, f1r, f2s, f2r, f3s, f3r, f4s, f4r,
                vw, vx, vy, vr, vs1, vr1, vs2, vr2, vs3, vr3):
    p = Place()
    meet(wt_peers(p) + [p.along_z_other(d) for d in ORDER] + [p.along_x(d) for d in ORDER] + [p.along_y(d) for d in ORDER])
    total = WtSum(p, dn_ref, sib, send, rz, (cs, cr, zs, zr))
    for zz in range(4):
        total.start_core(zz)
    first, second, third, fourth = {}, {}, {}, {}
    for d in ORDER:
        for h in range(2):
            to = lax.rem(p.fsp(h) + d, 4)
            src = g_ref.at[h, to] if h == 0 else g_ref.at[h, :, to]
            first[h, d] = rcopy(src, r1.at[h, d - 1], f1s.at[h, d - 1], f1r.at[h, d - 1], p.first(h, d))
            first[h, d].start()
    for d in ORDER:
        total.send_z(d)

    def part_of(h, b):
        at = spot(h, p.fsp(h), b)
        value = g_ref[h, at[0], at[1]].astype(f32)
        for d in range(3):
            value = value + r1[h, d, b].astype(f32)
        return value

    for h in range(2):
        for d in ORDER:
            first[h, d].wait_recv()
        for e in ORDER:
            s2[h, e - 1] = part_of(h, lax.rem(p.ssp(h) + e, 4)).astype(bf16)
            second[h, e] = rcopy(s2.at[h, e - 1], r2.at[h, e - 1], f2s.at[h, e - 1], f2r.at[h, e - 1], p.second(h, e))
            second[h, e].start()

    base = tok_ref[p.wt].astype(f32)
    scale = rms_of(base)
    d_normed = total.own()
    gt_ref[p.wt] = (dmid_ref[...] + norm_back(base, scale, gain_ref[...], d_normed)).astype(bf16)
    spread = WtGather(p, gt_ref, (az, bz, ag, bg))
    spread.start()
    vw[0, 0:1] = jnp.sum(d_normed * base * scale, axis=0, keepdims=True)
    vw[0, 1:2] = gn_ref[...]
    vw[0, 2:3] = gg_ref[...]
    vw[0, 3:8] = jnp.zeros((5, 1024), f32)

    def vec_round(buf, devices, sends, recvs):
        copies = []
        for i, device in enumerate(devices):
            copies.append(rcopy(buf.at[0], buf.at[i + 1], sends.at[i], recvs.at[i], device))
            copies[-1].start()
        return copies

    def vec_total(buf, copies):
        value = buf[0]
        for i, copy in enumerate(copies):
            copy.wait_recv()
            value = value + buf[i + 1]
        return value

    round1 = vec_round(vw, [p.along_z(d) for d in ORDER] + [p.along_z_other(d) for d in ORDER] + [p.sibling], vs1, vr1)

    for h in range(2):
        value = part_of(h, p.ssp(h))
        for e in ORDER:
            second[h, e].wait_recv()
            value = value + r2[h, e - 1].astype(f32)
        gb[h, p.x, p.y] = value.astype(bf16)
        for e in ORDER:
            third[h, e] = rcopy(gb.at[h, p.x, p.y], gb.at[h, p.x, p.y], f3s.at[h, e - 1], f3r.at[h, e - 1], p.second(h, e))
            third[h, e].start()

    vx[0] = vec_total(vw, round1)
    round2 = vec_round(vx, [p.along_x(d) for d in ORDER], vs2, vr2)
    for h in range(2):
        for e in ORDER:
            third[h, e].wait_recv()
        mine = gb.at[h, p.x] if h == 0 else gb.at[h, :, p.y]
        for d in ORDER:
            fourth[h, d] = rcopy(mine, mine, f4s.at[h, d - 1], f4r.at[h, d - 1], p.first(h, d))
            fourth[h, d].start()
    spread.forward()
    vy[0] = vec_total(vx, round2)
    round3 = vec_round(vy, [p.along_y(d) for d in ORDER], vs3, vr3)
    for copy in fourth.values():
        copy.wait_recv()
    gq_ref[...] = gb[0].astype(f32)
    gkv_ref[...] = gb[1].astype(f32)
    vec_ref[...] = vec_total(vy, round3)
    spread.arrived()
    spread.finish()
    total.finish()
    for group in (first, second, third, fourth):
        for copy in group.values():
            copy.wait_send()
    for copy in round1 + round2 + round3:
        copy.wait_send()


DMA = pltpu.SemaphoreType.DMA
sds = jax.ShapeDtypeStruct


def comm_call(kernel, number, out_shape, args, scratch, name):
    return pl.pallas_call(
        kernel,
        out_shape=out_shape,
        in_specs=[vmem] * len(args),
        out_specs=tuple(vmem for _ in out_shape),
        scratch_shapes=scratch,
        compiler_params=pltpu.CompilerParams(
            collective_id=number, has_side_effects=True, vmem_limit_bytes=24 << 20
        ),
        cost_estimate=pl.CostEstimate(flops=8 << 30, bytes_accessed=32 << 20, transcendentals=0),
        name=name,
    )(*args)


def gather_keys(q, kv):
    return comm_call(
        gather_kernel, 1,
        (sds((2, 256, 128), bf16), sds((4, 4, 2, 256, 128), bf16)),
        (q.reshape(2, 256, 128), kv.reshape(2, 256, 128)),
        [DMA, DMA, DMA((2, 3)), DMA((2, 3)), DMA((2, 4, 3)), DMA((2, 4, 3))],
        "gather_keys",
    )


def scatter_keys(dkv, dq):
    return comm_call(
        scatter_kernel, 2,
        (sds((2, 256, 128), bf16), sds((2, 256, 128), bf16)),
        (dkv.reshape(4, 4, 2, 256, 128), dq.reshape(2, 256, 128)),
        [pltpu.VMEM((2, 3, 4, 256, 128), bf16), pltpu.VMEM((2, 3, 256, 128), bf16), pltpu.VMEM((2, 3, 256, 128), bf16),
         DMA, DMA, DMA((2, 3)), DMA((2, 3)), DMA((2, 3)), DMA((2, 3))],
        "scatter_keys",
    )


def make_middle(mix, w_out, tokens, gain):
    rows = pltpu.VMEM
    return comm_call(
        middle_kernel, 3,
        (sds((8, 64, 1024), bf16), sds((64, 1024), f32), sds((2, 256, 128), bf16)),
        (mix.reshape(2, 256, 128), w_out, tokens.reshape(8, 64, 1024), gain.reshape(1, 1024)),
        [rows((8, 64, 1024), bf16), rows((4, 64, 1024), bf16), rows((3, 64, 1024), bf16), rows((3, 64, 1024), bf16),
         DMA, DMA, DMA((4,)), DMA((4,)), DMA((3,)), DMA((3,)), DMA((3,)), DMA((3,)), DMA((4,)), DMA((4,))],
        "make_middle",
    )


def turn_back(dm, mlp, mid, cot, gain, w_out):
    rows = pltpu.VMEM
    return comm_call(
        turn_kernel, 4,
        (sds((8, 64, 1024), bf16), sds((8, 64, 1024), bf16), sds((64, 1024), f32), sds((1, 1024), f32), sds((2, 256, 128), bf16)),
        (dm.reshape(8, 64, 1024), mlp.reshape(8, 64, 1024), mid, cot.reshape(8, 64, 1024), gain.reshape(1, 1024), w_out),
        [rows((256, 128), bf16), rows((2, 4, 64, 1024), bf16), rows((2, 3, 64, 1024), bf16), rows((2, 3, 64, 1024), bf16),
         DMA, DMA, DMA((2, 4)), DMA((2, 4)), DMA((2, 3)), DMA((2, 3)), DMA((2, 3)), DMA((2, 3)), DMA((2, 4)), DMA((2, 4))],
        "turn_back",
    )


def last_sums(dn, g, tokens, dmid, gain, gn, gg):
    rows = pltpu.VMEM
    return comm_call(
        last_kernel, 5,
        (sds((8, 64, 1024), bf16), sds((4, 4, 64, 128), f32), sds((4, 4, 64, 128), f32), sds((8, 1024), f32)),
        (dn.reshape(8, 64, 1024), g.reshape(2, 4, 4, 64, 128), tokens.reshape(8, 64, 1024), dmid, gain.reshape(1, 1024), gn, gg),
        [rows((4, 64, 1024), bf16), rows((3, 64, 1024), bf16), rows((3, 64, 1024), bf16),
         DMA((4,)), DMA((4,)), DMA((3,)), DMA((3,)), DMA((3,)), DMA((3,)), DMA((4,)), DMA((4,)),
         rows((2, 3, 4, 64, 128), bf16), rows((2, 3, 64, 128), bf16), rows((2, 3, 64, 128), bf16), rows((2, 4, 4, 64, 128), bf16),
         DMA((2, 3)), DMA((2, 3)), DMA((2, 3)), DMA((2, 3)), DMA((2, 3)), DMA((2, 3)), DMA((2, 3)), DMA((2, 3)),
         rows((8, 8, 1024), f32), rows((4, 8, 1024), f32), rows((4, 8, 1024), f32), rows((8, 1024), f32),
         DMA((7,)), DMA((7,)), DMA((3,)), DMA((3,)), DMA((3,)), DMA((3,))],
        "last_sums",
    )
def turned(value, lane):
    return jnp.where(lax.rem(lane, 64) < 32, pltpu.roll(value, 96, 1), pltpu.roll(value, 32, 1))


def head_sums(value, lane):
    s0 = jnp.sum(jnp.where(lane < 64, value, 0.0), axis=1, keepdims=True)
    s1 = jnp.sum(jnp.where(lane < 64, 0.0, value), axis=1, keepdims=True)
    return jnp.where(lane < 64, s0, s1)


def twice(gain):
    return jnp.concatenate([gain, gain], axis=1)


def proj_kernel(tok_ref, gain_ref, wq_ref, wk_ref, wv_ref, qg_ref, kg_ref, cos_ref, sin_ref, n_ref, qp_ref, kvp_ref, q_ref, kv_ref):
    lane = lanes((512, 128))
    base = tok_ref[...].astype(f32)
    normed = (base * rms_of(base) * gain_ref[...]).astype(bf16)
    n_ref[...] = normed
    wkv = jnp.concatenate([wk_ref[...], wv_ref[...]], axis=1)
    cosine, sine = cos_ref[...], sin_ref[...]
    q = jnp.dot(normed, wq_ref[...], preferred_element_type=f32)
    qp_ref[...] = q
    q = q * lax.rsqrt(head_sums(q * q, lane) * (1.0 / 64) + eps) * twice(qg_ref[...])
    q_ref[...] = (q * cosine + turned(q, lane) * sine).astype(bf16)
    kv = jnp.dot(normed, wkv, preferred_element_type=f32)
    kvp_ref[...] = kv
    k = kv * lax.rsqrt(head_sums(kv * kv, lane) * (1.0 / 64) + eps) * twice(kg_ref[...])
    k = k * cosine + turned(k, lane) * sine
    kv_ref[...] = jnp.where(lane < 64, k, kv).astype(bf16)


def proj_back_kernel(dq_ref, dkv_ref, qp_ref, kvp_ref, n_ref, wq_ref, wk_ref, wv_ref, qg_ref, kg_ref, cos_ref, sin_ref, dn_ref, g_ref, gg_ref):
    lane = lanes((512, 128))
    cosine, sine = cos_ref[...], sin_ref[...]

    def back(grad, proj, gain):
        grad = grad * cosine - turned(grad, lane) * sine
        scale = lax.rsqrt(head_sums(proj * proj, lane) * (1.0 / 64) + eps)
        scaled = grad * gain
        inner = head_sums(scaled * proj, lane) * (1.0 / 64)
        gains = jnp.sum(grad * proj * scale, axis=0, keepdims=True)
        return scale * scaled - proj * scale * scale * scale * inner, gains

    dq, gq = back(dq_ref[...].astype(f32), qp_ref[...], twice(qg_ref[...]))
    dkv_in = dkv_ref[...].astype(f32)
    dk, gk = back(dkv_in, kvp_ref[...], twice(kg_ref[...]))
    dq = dq.astype(bf16)
    dkv = jnp.where(lane < 64, dk, dkv_in).astype(bf16)
    wkv = jnp.concatenate([wk_ref[...], wv_ref[...]], axis=1)
    dn = lax.dot_general(dq, wq_ref[...], (((1,), (1,)), ((), ())), preferred_element_type=f32)
    dn = dn + lax.dot_general(dkv, wkv, (((1,), (1,)), ((), ())), preferred_element_type=f32)
    dn_ref[...] = dn.astype(bf16)
    normed = n_ref[...]
    g_ref[0] = lax.dot_general(normed, dq, (((0,), (0,)), ((), ())), preferred_element_type=f32).astype(bf16)
    g_ref[1] = lax.dot_general(normed, dkv, (((0,), (0,)), ((), ())), preferred_element_type=f32).astype(bf16)
    gg_ref[...] = jnp.concatenate([gq, gk, jnp.zeros((1, 768), f32)], axis=1)


def local_call(kernel, out_shape, args, name):
    return pl.pallas_call(
        kernel,
        out_shape=out_shape,
        in_specs=[vmem] * len(args),
        out_specs=tuple(vmem for _ in out_shape),
        compiler_params=pltpu.CompilerParams(vmem_limit_bytes=32 << 20),
        cost_estimate=pl.CostEstimate(flops=3 << 30, bytes_accessed=16 << 20, transcendentals=0),
        name=name,
    )(*args)


theta = 1000000.0


def body(tokens, norm_in, w_query, w_key, w_value, query_gain, key_gain, w_out, norm_mid, w_gate, w_up, w_down, cotangent, lengths):
    parts = lax.axis_size("sp")
    sp = lax.axis_index("sp")
    me = sp.reshape(1).astype(jnp.int32)
    ids = sp * 512 + jnp.arange(512)
    positions = ids - starts_of(ids, lengths)
    index = jnp.arange(128)
    freqs = theta ** (-((index % 32).astype(f32) * 2.0) / 64)
    angles = positions.astype(f32)[:, None] * freqs[None, :]
    cosine = jnp.cos(angles)
    sine = jnp.sin(angles) * jnp.where(index % 64 < 32, -1.0, 1.0)[None, :]
    qg, kg = query_gain.reshape(1, 64), key_gain.reshape(1, 64)
    gain_in = norm_in.reshape(1, 1024)

    normed, q_proj, kv_proj, q, kv = local_call(
        proj_kernel,
        (sds((512, 1024), bf16), sds((512, 128), f32), sds((512, 128), f32), sds((512, 128), bf16), sds((512, 128), bf16)),
        (tokens, gain_in, w_query, w_key, w_value, qg, kg, cosine, sine),
        "project",
    )
    qz, kv_all = gather_keys(q, kv)
    kv_all = kv_all.reshape(8192, 128)
    mix_z, mix_f, qa = attend(parts, me, lengths, qz.reshape(512, 128), kv_all)
    normed_mid, mid_own, mixed = make_middle(mix_z, w_out, tokens, norm_mid)
    normed_mid = normed_mid.reshape(512, 1024)
    mixed = mixed.reshape(512, 128)

    gate = jnp.dot(normed_mid, w_gate, preferred_element_type=f32)
    up_proj = jnp.dot(normed_mid, w_up, preferred_element_type=f32)
    sigmoid_gate = jax.nn.sigmoid(gate)
    act = (gate * sigmoid_gate * up_proj).astype(bf16)
    mlp_part = jnp.dot(act, w_down, preferred_element_type=f32).astype(bf16)
    d_act = jnp.einsum("td,fd->tf", cotangent, w_down, preferred_element_type=f32)
    d_gate = (d_act * up_proj * sigmoid_gate * (1.0 + gate * (1.0 - sigmoid_gate))).astype(bf16)
    d_up = (d_act * gate * sigmoid_gate).astype(bf16)
    d_mid_part = (
        jnp.einsum("tf,df->td", d_gate, w_gate, preferred_element_type=f32)
        + jnp.einsum("tf,df->td", d_up, w_up, preferred_element_type=f32)
    ).astype(bf16)
    g_down = jnp.einsum("tf,td->fd", act, cotangent, preferred_element_type=f32)
    g_gate = jnp.einsum("td,tf->df", normed_mid, d_gate, preferred_element_type=f32)
    g_up = jnp.einsum("td,tf->df", normed_mid, d_up, preferred_element_type=f32)

    output, d_attn, d_middle_own, gn, d_mix_z = turn_back(d_mid_part, mlp_part, mid_own, cotangent, norm_mid, w_out)
    g_out = jnp.einsum("tq,td->qd", mixed, d_attn.reshape(512, 1024), preferred_element_type=f32)
    g_gate, g_up, g_down, g_out = (
        lax.psum(g.astype(bf16), "sp").astype(f32) for g in (g_gate, g_up, g_down, g_out)
    )
    dq_z, dkv_all = attend_back(parts, me, lengths, qa, mix_f, d_mix_z.reshape(512, 128), kv_all)
    dkv, dq = scatter_keys(dkv_all, dq_z)
    dn_part, g_qkv, gg = local_call(
        proj_back_kernel,
        (sds((512, 1024), bf16), sds((2, 1024, 128), bf16), sds((1, 1024), f32)),
        (dq.reshape(512, 128), dkv.reshape(512, 128), q_proj, kv_proj, normed, w_query, w_key, w_value, qg, kg, cosine, sine),
        "project_back",
    )
    grad_tokens, g_query, g_kv, vec = last_sums(dn_part, g_qkv, tokens, d_middle_own, norm_in, gn, gg)
    g_query = g_query.reshape(1024, 128)
    g_kv = g_kv.reshape(1024, 128)
    return (
        output.reshape(512, 1024),
        grad_tokens.reshape(512, 1024),
        vec[0],
        g_query,
        g_kv[:, :64],
        g_kv[:, 64:],
        vec[2, :64] + vec[2, 64:128],
        vec[2, 128:192],
        g_out,
        vec[1],
        g_gate,
        g_up,
        g_down,
    )


def solution(mesh):
    placed = (
        P("sp", None), P(), P(None, "wt"), P(None, "wt"), P(None, "wt"), P(), P(), P("wt", None), P(),
        P(None, "wt"), P(None, "wt"), P("wt", None), P("sp", None), P(),
    )
    return jax.shard_map(
        body,
        mesh=mesh,
        in_specs=placed,
        out_specs=(
            P("sp", None), P("sp", None), P(), P(None, "wt"), P(None, "wt"), P(None, "wt"), P(), P(),
            P("wt", None), P(), P(None, "wt"), P(None, "wt"), P("wt", None),
        ),
        check_vma=False,
    )
```

```python
import functools, math
import jax
import jax.numpy as jnp
import numpy as np
from jax import lax
from jax.experimental import pallas as pl
from jax.experimental.pallas import tpu as pltpu
from jax.sharding import PartitionSpec as P

f32 = jnp.float32
bf16 = jnp.bfloat16
sds = jax.ShapeDtypeStruct
DMA = pltpu.SemaphoreType.DMA
CH = 512
HALF = 256
SCALE = 0.125
C2 = SCALE * math.log2(math.e)


def starts_of(ids, len_ref):
    end = jnp.int32(0)
    start = jnp.zeros_like(ids)
    for j in range(4):
        end = end + len_ref[j]
        start = start + jnp.where(ids >= end, len_ref[j], 0)
    return start


def scalar_start(row, len_ref):
    end = jnp.int32(0)
    start = jnp.int32(0)
    for j in range(4):
        end = end + len_ref[j]
        start = start + jnp.where(row >= end, len_ref[j], 0)
    return start


def lanes(shape):
    return lax.broadcasted_iota(jnp.int32, shape, len(shape) - 1)


def split3(value, lane):
    hi = value.astype(bf16).astype(f32)
    rest = value - hi
    mid = rest.astype(bf16).astype(f32)
    low = rest - mid
    return jnp.where(lane == 0, hi, jnp.where(lane == 1, mid, jnp.where(lane == 2, low, 0.0)))


def tile_row(me, t, parts):
    return me * 512 if t == 0 else (parts - 1 - me) * 512 + HALF


FAR = 8192.0


def segment_bounds(len_ref, lane):
    begin = jnp.zeros_like(lane)
    end = jnp.zeros_like(lane)
    at = jnp.int32(0)
    for j in range(4):
        begin = jnp.where(lane == 3 + j, at, begin)
        at = at + len_ref[j]
        end = jnp.where(lane == 3 + j, at, end)
    return begin, end


def inside(ids, len_ref, shape):
    lane = lanes(shape)
    begin, end = segment_bounds(len_ref, lane)
    return (ids >= begin) & (ids < end), lane


def key_columns(k0, len_ref, rows):
    ids = k0 + lax.broadcasted_iota(jnp.int32, (rows, 128), 0)
    within, lane = inside(ids, len_ref, (rows, 128))
    return jnp.where(lane < 3, 1.0, jnp.where(within, 1.0, 0.0)).astype(bf16)


def query_columns(r0, len_ref, rows):
    ids = r0 + lax.broadcasted_iota(jnp.int32, (rows, 128), 0)
    within, lane = inside(ids, len_ref, (rows, 128))
    return jnp.where((lane < 3) | (lane > 6) | within, 0.0, -FAR)


def fwd_kernel(parts, len_ref, q_ref, kv_ref, ext_ref, mix_ref, out_ref, qa_ref, acc_ref):
    me = lax.axis_index("sp")
    lane = lanes((HALF, 128))
    lane2 = lanes((2 * HALF, 128))
    lanek = lanes((CH, 128))
    for t in range(2):
        r0 = tile_row(me, t, parts)
        q = q_ref[t * HALF:(t + 1) * HALF, :].astype(f32)
        qa_ref[t, 0:HALF, 0:128] = jnp.where(lane < 64, q, 0.0).astype(bf16)
        qa_ref[t, HALF:, 0:128] = jnp.where(lane < 64, pltpu.roll(q, 64, 1), 0.0).astype(bf16)
        columns = query_columns(r0, len_ref, HALF)
        columns = jnp.concatenate([columns, columns], axis=0)
        qa_ref[t, :, 128:256] = columns.astype(bf16)
        acc_ref[...] = jnp.zeros_like(acc_ref)

        def step(c, masked):
            k0 = pl.multiple_of(c * CH, CH)
            kv = kv_ref[pl.ds(k0, CH), :]
            kva = jnp.concatenate([kv, ext_ref[pl.ds(k0, CH), :]], axis=1)
            s = lax.dot_general(qa_ref[t], kva, (((1,), (1,)), ((), ())), preferred_element_type=f32)
            p = jnp.exp2(s * C2)
            if masked:
                rows = r0 + lax.rem(lax.broadcasted_iota(jnp.int32, (2 * HALF, 1), 0), HALF)
                keys = k0 + lax.broadcasted_iota(jnp.int32, (2 * HALF, CH), 1)
                p = jnp.where(keys <= rows, p, 0.0)
            ones = jnp.where(lanek < 64, jnp.ones_like(kv), kv)
            acc_ref[...] += jnp.dot(p.astype(bf16), ones, preferred_element_type=f32)

        block = me if t == 0 else parts - 1 - me
        pl.loop(0, block)(lambda c: step(c, False))
        step(block, True)

        acc = acc_ref[...]
        swapped = pltpu.roll(acc, 64, 1)
        o = swapped / acc
        m = jnp.where(lane < 64, o[:HALF], pltpu.roll(o[HALF:], 64, 1))
        mix_ref[t * HALF:(t + 1) * HALF, :] = m.astype(bf16)
        out_ref[t * HALF:(t + 1) * HALF, :] = m
        total = jnp.where(lane2 < 64, acc, swapped)
        qa_ref[t, :, 128:256] = (split3(jnp.log(total) * (-1.0 / SCALE), lane2) + columns).astype(bf16)


def bwd_kernel(parts, qa_ref, out_ref, do_ref, kv_ref, ext_ref, red_ref, dq_ref, dkv_ref, grads_ref, da_ref, acc_ref, dqt_ref, *sems):
    me = lax.axis_index("sp")
    p = Place()
    meet([p.along_x(d) for d in ORDER] + [p.along_y(d) for d in ORDER])
    spread = SpGather(p, grads_ref, 144, sems)
    for i in range(2):
        for h in range(2):
            spread.put(i, h, red_ref[i, h])
            spread.first(i, h)
    lane = lanes((HALF, 128))
    acc_ref[...] = jnp.zeros_like(acc_ref)
    for t in range(2):
        r0 = tile_row(me, t, parts)
        rows_t = slice(t * HALF, (t + 1) * HALF)
        do = do_ref[rows_t, :].astype(f32)
        prod = do * out_ref[rows_t, :]
        d0 = -jnp.sum(jnp.where(lane < 64, prod, 0.0), axis=1, keepdims=True)
        d1 = -jnp.sum(jnp.where(lane < 64, 0.0, prod), axis=1, keepdims=True)
        da_ref[0:HALF, 0:128] = jnp.where(lane < 64, 0.0, pltpu.roll(do, 64, 1)).astype(bf16)
        da_ref[HALF:, 0:128] = jnp.where(lane < 64, 0.0, do).astype(bf16)
        da_ref[0:HALF, 128:256] = split3(jnp.broadcast_to(d0, (HALF, 128)), lane).astype(bf16)
        da_ref[HALF:, 128:256] = split3(jnp.broadcast_to(d1, (HALF, 128)), lane).astype(bf16)
        dqt_ref[...] = jnp.zeros_like(dqt_ref)

        def step(c, masked):
            k0 = pl.multiple_of(c * CH, CH)
            kv = kv_ref[pl.ds(k0, CH), :]
            kva = jnp.concatenate([kv, ext_ref[pl.ds(k0, CH), :]], axis=1)
            qa = qa_ref[t]
            da = da_ref[...]
            s = lax.dot_general(kva, qa, (((1,), (1,)), ((), ())), preferred_element_type=f32)
            p = jnp.exp2(s * C2)
            if masked:
                rows = r0 + lax.rem(lax.broadcasted_iota(jnp.int32, (1, 2 * HALF), 1), HALF)
                keys = k0 + lax.broadcasted_iota(jnp.int32, (CH, 2 * HALF), 0)
                p = jnp.where(keys <= rows, p, 0.0)
            dp = lax.dot_general(kva, da, (((1,), (1,)), ((), ())), preferred_element_type=f32)
            ds = (p * dp).astype(bf16)
            acc_ref[pl.ds(k0, CH), :] += jnp.dot(
                p.astype(bf16), da[:, 0:128], preferred_element_type=f32
            ) + jnp.dot(ds, qa[:, 0:128], preferred_element_type=f32)
            kt = kv.T[0:64, :]
            dqt_ref[...] += jnp.dot(kt, ds, preferred_element_type=f32)

        block = me if t == 0 else parts - 1 - me
        pl.loop(0, block)(lambda c: step(c, False))
        step(block, True)
        dqt = dqt_ref[...]
        if t == 0:
            for i in range(2):
                for h in range(2):
                    spread.second(i, h)
        both = jnp.concatenate([dqt[:, :HALF], dqt[:, HALF:]], axis=0)
        dq_ref[rows_t, :] = (both.T * SCALE).astype(bf16)
    weight = jnp.where(lanes((512, 128)) < 64, SCALE, 1.0)

    @pl.loop(0, parts)
    def _(b):
        rows = pl.ds(pl.multiple_of(b * 512, 512), 512)
        dkv_ref[rows, :] = (acc_ref[rows, :] * weight).astype(bf16)

    spread.finish()


smem = pl.BlockSpec(memory_space=pltpu.SMEM)
vmem = pl.BlockSpec(memory_space=pltpu.VMEM)


def attend(parts, lengths, q, kv, ext):
    rows = 2 * HALF
    return pl.pallas_call(
        functools.partial(fwd_kernel, parts),
        out_shape=(sds((rows, 128), bf16), sds((rows, 128), f32), sds((2, rows, 256), bf16)),
        in_specs=[smem, vmem, vmem, vmem],
        out_specs=(vmem, vmem, vmem),
        scratch_shapes=[pltpu.VMEM((rows, 128), f32)],
        compiler_params=pltpu.CompilerParams(vmem_limit_bytes=12 << 20),
        cost_estimate=pl.CostEstimate(flops=3 << 30, bytes_accessed=4 << 20, transcendentals=5 << 20),
        name="attend",
    )(lengths, q, kv, ext)


def attend_back(parts, qa, out, do, kv, ext, red):
    rows = 2 * HALF
    return pl.pallas_call(
        functools.partial(bwd_kernel, parts),
        out_shape=(sds((rows, 128), bf16), sds(kv.shape, bf16), sds((2, 4, 144, 1024), bf16)),
        in_specs=[vmem] * 6,
        out_specs=(vmem, vmem, vmem),
        scratch_shapes=[pltpu.VMEM((rows, 256), bf16), pltpu.VMEM(kv.shape, f32), pltpu.VMEM((64, rows), f32)]
        + SpGather.sems(2),
        compiler_params=pltpu.CompilerParams(collective_id=6, has_side_effects=True, vmem_limit_bytes=20 << 20),
        cost_estimate=pl.CostEstimate(flops=10 << 30, bytes_accessed=8 << 20, transcendentals=5 << 20),
        name="attend_back",
    )(qa, out, do, kv, ext, red)


MESH = pl.DeviceIdType.MESH
eps = 1e-05


def rcopy(src, dst, send, recv, device):
    return pltpu.make_async_remote_copy(
        src_ref=src, dst_ref=dst, send_sem=send, recv_sem=recv, device_id=device, device_id_type=MESH
    )


def meet(devices):
    barrier = pltpu.get_barrier_semaphore()
    for device in devices:
        pl.semaphore_signal(barrier, inc=1, device_id=device, device_id_type=MESH)
    pl.semaphore_wait(barrier, len(devices))


class Place:
    def __init__(self):
        self.sp = lax.axis_index("sp")
        self.wt = lax.axis_index("wt")
        self.x, self.y = lax.div(self.sp, 4), lax.rem(self.sp, 4)
        self.z, self.c = lax.div(self.wt, 2), lax.rem(self.wt, 2)
        self.mirror = (15 - self.sp, self.wt)
        self.sibling = (self.sp, self.z * 2 + 1 - self.c)

    def along_x(self, d):
        return (lax.rem(self.x + d, 4) * 4 + self.y, self.wt)

    def along_y(self, d):
        return (self.x * 4 + lax.rem(self.y + d, 4), self.wt)

    def along_z(self, d):
        return (self.sp, lax.rem(self.z + d, 4) * 2 + self.c)

    def along_z_other(self, d):
        return (self.sp, lax.rem(self.z + d, 4) * 2 + 1 - self.c)

    def first(self, h, d):
        return self.along_x(d) if h == 0 else self.along_y(d)

    def second(self, h, d):
        return self.along_y(d) if h == 0 else self.along_x(d)

    def fsp(self, h):
        return self.x if h == 0 else self.y

    def ssp(self, h):
        return self.y if h == 0 else self.x


def spot(h, first, second):
    return (first, second) if h == 0 else (second, first)


ORDER = (2, 1, 3)


def gather_kernel(len_ref, q_ref, kv_ref, qz_ref, all_ref, ext_ref, ms, mr, fs, fr, ss, sr):
    p = Place()
    meet([p.along_x(d) for d in ORDER] + [p.along_y(d) for d in ORDER] + [p.mirror])
    all_ref[p.x, p.y] = kv_ref[...]
    mirror = rcopy(q_ref.at[1], qz_ref.at[1], ms, mr, p.mirror)
    first, second = {}, {}
    for d in ORDER:
        for h in range(2):
            first[h, d] = rcopy(
                kv_ref.at[h], all_ref.at[p.x, p.y, h], fs.at[h, d - 1], fr.at[h, d - 1], p.first(h, d)
            )
            first[h, d].start()
    mirror.start()

    def forward(h, slot):
        a = lax.rem(p.fsp(h) + 4 - slot, 4)
        at = spot(h, a, p.ssp(h))
        for e in ORDER:
            src = kv_ref.at[h] if slot == 0 else all_ref.at[at[0], at[1], h]
            second[h, slot, e] = rcopy(
                src, all_ref.at[at[0], at[1], h], ss.at[h, slot, e - 1], sr.at[h, slot, e - 1], p.second(h, e)
            )
            second[h, slot, e].start()

    for h in range(2):
        forward(h, 0)
    qz_ref[0] = q_ref[0]
    @pl.loop(0, 8)
    def _(b):
        rows = pl.ds(pl.multiple_of(b * 1024, 1024), 1024)
        ext_ref[rows, :] = key_columns(b * 1024, len_ref, 1024)

    for d in (1, 3, 2):
        for h in range(2):
            first[h, d].wait_recv()
            forward(h, d)
    mirror.wait()
    for copy in first.values():
        copy.wait_send()
    for copy in second.values():
        copy.wait()


def scatter_kernel(dkv_ref, dqz_ref, own_ref, dq_ref, r1, send, r2, ms, mr, fs, fr, ss, sr):
    p = Place()
    meet([p.along_x(d) for d in ORDER] + [p.along_y(d) for d in ORDER] + [p.mirror])
    first, second = {}, {}
    for d in ORDER:
        for h in range(2):
            to = lax.rem(p.fsp(h) + d, 4)
            src = dkv_ref.at[to, :, 0] if h == 0 else dkv_ref.at[:, to, 1]
            first[h, d] = rcopy(src, r1.at[h, d - 1], fs.at[h, d - 1], fr.at[h, d - 1], p.first(h, d))
            first[h, d].start()
    mirror = rcopy(dqz_ref.at[1], dq_ref.at[1], ms, mr, p.mirror)
    mirror.start()
    dq_ref[0] = dqz_ref[0]

    def total(h, b):
        at = spot(h, p.fsp(h), b)
        value = dkv_ref[at[0], at[1], h].astype(f32)
        for d in range(3):
            value = value + r1[h, d, b].astype(f32)
        return value

    for h in range(2):
        for d in ORDER:
            first[h, d].wait_recv()
        for e in ORDER:
            b = lax.rem(p.ssp(h) + e, 4)
            send[h, e - 1] = total(h, b).astype(bf16)
            second[h, e] = rcopy(
                send.at[h, e - 1], r2.at[h, e - 1], ss.at[h, e - 1], sr.at[h, e - 1], p.second(h, e)
            )
            second[h, e].start()
    for h in range(2):
        value = total(h, p.ssp(h))
        for e in ORDER:
            second[h, e].wait_recv()
            value = value + r2[h, e - 1].astype(f32)
        own_ref[h] = value.astype(bf16)
    mirror.wait()
    for copy in list(first.values()) + list(second.values()):
        copy.wait_send()


class SpScatter:
    def __init__(self, p, srcs, rows, refs):
        self.p, self.srcs, self.rows = p, srcs, rows
        self.ra, self.rb, self.send, self.r2, self.fs, self.fr, self.ss, self.sr = refs
        self.one, self.two = {}, {}

    @staticmethod
    def scratch(n, rows):
        return [
            pltpu.VMEM((n, 3, rows, 512), bf16), pltpu.VMEM((n, 3, 4, rows, 128), bf16),
            pltpu.VMEM((n, 2, 3, rows, 128), bf16), pltpu.VMEM((n, 2, 3, rows, 128), bf16),
            DMA((n, 2, 3)), DMA((n, 2, 3)), DMA((n, 2, 3)), DMA((n, 2, 3)),
        ]

    def first(self, i):
        p = self.p
        for d in ORDER:
            to = lax.rem(p.x + d, 4)
            self.one[i, 0, d] = rcopy(
                self.srcs[i].at[to, :, pl.ds(0, 512)], self.ra.at[i, d - 1],
                self.fs.at[i, 0, d - 1], self.fr.at[i, 0, d - 1], p.along_x(d),
            )
            self.one[i, 0, d].start()
            to = lax.rem(p.y + d, 4)
            self.one[i, 1, d] = rcopy(
                self.srcs[i].at[:, :, pl.ds(columns_at(1, to), 128)], self.rb.at[i, d - 1],
                self.fs.at[i, 1, d - 1], self.fr.at[i, 1, d - 1], p.along_y(d),
            )
            self.one[i, 1, d].start()

    def part(self, i, h, b):
        p = self.p
        if h == 0:
            value = self.srcs[i][p.x, :, pl.ds(columns_at(0, b), 128)].astype(f32)
            for d in range(3):
                value = value + self.ra[i, d, :, pl.ds(columns_at(0, b), 128)].astype(f32)
            return value
        value = self.srcs[i][b, :, pl.ds(columns_at(1, p.y), 128)].astype(f32)
        for d in range(3):
            value = value + self.rb[i, d, b].astype(f32)
        return value

    def second(self, i):
        p = self.p
        for h in range(2):
            for d in ORDER:
                self.one[i, h, d].wait_recv()
            for e in ORDER:
                self.send[i, h, e - 1] = self.part(i, h, lax.rem(p.ssp(h) + e, 4)).astype(bf16)
                self.two[i, h, e] = rcopy(
                    self.send.at[i, h, e - 1], self.r2.at[i, h, e - 1],
                    self.ss.at[i, h, e - 1], self.sr.at[i, h, e - 1], p.second(h, e),
                )
                self.two[i, h, e].start()

    def own(self, i, h):
        value = self.part(i, h, self.p.ssp(h))
        for e in ORDER:
            self.two[i, h, e].wait_recv()
            value = value + self.r2[i, h, e - 1].astype(f32)
        return value

    def finish(self):
        for copy in list(self.one.values()) + list(self.two.values()):
            copy.wait_send()


def columns_at(h, b):
    return pl.multiple_of(h * 512 + b * 128, 128)


class SpGather:
    def __init__(self, p, out, rows, sems):
        self.p, self.out, self.rows = p, out, rows
        self.fs, self.fr, self.ss, self.sr = sems
        self.one, self.two = {}, {}

    @staticmethod
    def sems(n):
        return [DMA((n, 2, 3)) for _ in range(4)]

    def spot(self, h):
        p = self.p
        return p.x, pl.ds(columns_at(h, p.y), 128)

    def put(self, i, h, value):
        x, columns = self.spot(h)
        self.out[i, x, :, columns] = value

    def first(self, i, h):
        x, columns = self.spot(h)
        block = self.out.at[i, x, :, columns]
        for e in ORDER:
            self.one[i, h, e] = rcopy(
                block, block, self.fs.at[i, h, e - 1], self.fr.at[i, h, e - 1], self.p.second(h, e)
            )
            self.one[i, h, e].start()

    def second(self, i, h):
        x, columns = self.spot(h)
        for e in ORDER:
            self.one[i, h, e].wait_recv()
        block = self.out.at[i, x, :, pl.ds(0, 512)] if h == 0 else self.out.at[i, :, :, columns]
        for d in ORDER:
            self.two[i, h, d] = rcopy(
                block, block, self.ss.at[i, h, d - 1], self.sr.at[i, h, d - 1], self.p.first(h, d)
            )
            self.two[i, h, d].start()

    def arrived(self, i):
        for h in range(2):
            for d in ORDER:
                self.two[i, h, d].wait_recv()

    def finish(self):
        for copy in self.one.values():
            copy.wait_send()
        for copy in self.two.values():
            copy.wait()


class WtSum:
    def __init__(self, p, part, sib, send, rz, sems):
        self.p, self.part, self.sib, self.send, self.rz = p, part, sib, send, rz
        self.cs, self.cr, self.zs, self.zr = sems
        self.second = {}

    def core(self, zz):
        return rcopy(
            self.part.at[zz * 2 + 1 - self.p.c], self.sib.at[zz], self.cs.at[zz], self.cr.at[zz], self.p.sibling
        )

    def start_core(self, zz):
        self.core(zz).start()

    def pair(self, zz):
        return self.part[zz * 2 + self.p.c].astype(f32) + self.sib[zz].astype(f32)

    def send_z(self, d):
        zz = lax.rem(self.p.z + d, 4)
        self.core(zz).wait_recv()
        self.send[d - 1] = self.pair(zz).astype(bf16)
        copy = rcopy(
            self.send.at[d - 1], self.rz.at[d - 1], self.zs.at[d - 1], self.zr.at[d - 1], self.p.along_z(d)
        )
        copy.start()
        self.second[d] = copy

    def own(self):
        self.core(self.p.z).wait_recv()
        value = self.pair(self.p.z)
        for d in (1, 3, 2):
            self.second[d].wait_recv()
            value = value + self.rz[d - 1].astype(f32)
        return value

    def finish(self):
        for zz in range(4):
            self.core(zz).wait_send()
        for copy in self.second.values():
            copy.wait_send()


class WtGather:
    def __init__(self, p, out, sems):
        self.p, self.out = p, out
        self.zs, self.zr, self.gs, self.gr = sems
        self.far, self.near = {}, {}

    def start(self):
        p = self.p
        for d in ORDER:
            self.far[d] = rcopy(
                self.out.at[p.wt], self.out.at[p.wt], self.zs.at[d - 1], self.zr.at[d - 1], p.along_z(d)
            )
            self.far[d].start()
        self.pass_on(0)

    def pass_on(self, slot):
        p = self.p
        row = lax.rem(p.z + 4 - slot, 4) * 2 + p.c
        self.near[slot] = rcopy(
            self.out.at[row], self.out.at[row], self.gs.at[slot], self.gr.at[slot], p.sibling
        )
        self.near[slot].start()

    def forward(self):
        for d in (1, 3, 2):
            self.far[d].wait_recv()
            self.pass_on(d)

    def arrived(self):
        for slot in (0, 1, 3, 2):
            self.near[slot].wait_recv()

    def finish(self):
        for copy in list(self.far.values()) + list(self.near.values()):
            copy.wait_send()


def rms_of(value):
    return lax.rsqrt(jnp.mean(value * value, axis=-1, keepdims=True) + eps)


def norm_back(values, scale, gain, grad):
    scaled = grad * gain
    inner = jnp.mean(scaled * values, axis=-1, keepdims=True)
    return scale * scaled - values * scale * scale * scale * inner


def wt_peers(p):
    return [p.sibling] + [p.along_z(d) for d in ORDER]


def middle_kernel(mix_ref, w_ref, tok_ref, gain_ref, nm_ref, mid_ref, mixo_ref, part, sib, send, rz, ms, mr, cs, cr, zs, zr, az, bz, ag, bg):
    p = Place()
    meet(wt_peers(p) + [p.mirror])
    mirror = rcopy(mix_ref.at[1], mixo_ref.at[1], ms, mr, p.mirror)
    mirror.start()
    mixo_ref[0] = mix_ref[0]
    total = WtSum(p, part, sib, send, rz, (cs, cr, zs, zr))
    for half in range(2):
        if half == 1:
            mirror.wait()
        both = jnp.dot(mixo_ref[half], w_ref[...], preferred_element_type=f32).astype(bf16)
        part[half * 4:half * 4 + 4] = both.reshape(4, 64, 1024)
        for zz in (half * 2, half * 2 + 1):
            total.start_core(zz)
    for d in ORDER:
        total.send_z(d)
    middle = tok_ref[p.wt].astype(f32) + total.own()
    mid_ref[...] = middle
    nm_ref[p.wt] = (middle * rms_of(middle) * gain_ref[...]).astype(bf16)
    spread = WtGather(p, nm_ref, (az, bz, ag, bg))
    spread.start()
    spread.forward()
    spread.arrived()
    spread.finish()
    total.finish()


def turn_kernel(dm_ref, mlp_ref, mid_ref, cot_ref, gain_ref, w_ref, g0_ref, g1_ref, g2_ref,
                out_ref, da_ref, dmid_ref, gn_ref, dz_ref, red_ref,
                up, sib, send, rz, ms, mr, cs, cr, zs, zr, az, bz, ag, bg, *grad_refs):
    p = Place()
    meet(wt_peers(p) + [p.mirror] + [p.along_x(d) for d in ORDER] + [p.along_y(d) for d in ORDER])
    totals = [
        WtSum(p, ref, sib.at[i], send.at[i], rz.at[i], (cs.at[i], cr.at[i], zs.at[i], zr.at[i]))
        for i, ref in enumerate((dm_ref, mlp_ref))
    ]
    grads = SpScatter(p, (g0_ref, g1_ref, g2_ref), 144, grad_refs)
    for zz in range(4):
        totals[0].start_core(zz)
    for i in range(3):
        grads.first(i)
    for zz in range(4):
        totals[1].start_core(zz)
    for total in totals:
        for d in ORDER:
            total.send_z(d)
    middle = mid_ref[...]
    scale = rms_of(middle)
    d_mid = totals[0].own()
    gn_ref[...] = jnp.sum(d_mid * middle * scale, axis=0, keepdims=True)
    d_middle = cot_ref[p.wt].astype(f32) + norm_back(middle, scale, gain_ref[...], d_mid)
    dmid_ref[...] = d_middle
    da_ref[p.wt] = d_middle.astype(bf16)
    spreads = [
        WtGather(p, ref, (az.at[i], bz.at[i], ag.at[i], bg.at[i])) for i, ref in enumerate((da_ref, out_ref))
    ]
    spreads[0].start()
    grads.second(0)
    out_ref[p.wt] = (middle + totals[1].own()).astype(bf16)
    spreads[1].start()
    grads.second(1)
    spreads[0].forward()
    spreads[0].arrived()
    mirror = rcopy(up, dz_ref.at[1], ms, mr, p.mirror)
    for half in (1, 0):
        rows = da_ref[half * 4:half * 4 + 4].reshape(256, 1024)
        d_mixed = lax.dot_general(rows, w_ref[...], (((1,), (1,)), ((), ())), preferred_element_type=f32).astype(bf16)
        if half == 1:
            up[...] = d_mixed
            mirror.start()
        else:
            dz_ref[0] = d_mixed
    grads.second(2)
    spreads[1].forward()
    for i in range(3):
        for h in range(2):
            red_ref[i, h] = grads.own(i, h).astype(bf16)
    spreads[1].arrived()
    mirror.wait()
    for part in spreads + totals + [grads]:
        part.finish()


def last_kernel(dn_ref, gq_ref, go_ref, red_ref, tok_ref, dmid_ref, gain_ref, gn_ref, gg_ref,
                gt_ref, sums_ref, gd_ref, vec_ref,
                sib, send, rz, cs, cr, zs, zr, az, bz, ag, bg,
                vw, vx, vy, vs1, vr1, vs2, vr2, vs3, vr3, *more):
    p = Place()
    meet(wt_peers(p) + [p.along_z_other(d) for d in ORDER] + [p.along_x(d) for d in ORDER] + [p.along_y(d) for d in ORDER])
    total = WtSum(p, dn_ref, sib, send, rz, (cs, cr, zs, zr))
    for zz in range(4):
        total.start_core(zz)
    grads = SpScatter(p, (gq_ref.at[0], gq_ref.at[1], go_ref), 32, more[:8])
    back = SpGather(p, sums_ref, 32, more[8:12])
    down = SpGather(p, gd_ref, 144, more[12:16])
    for h in range(2):
        down.put(0, h, red_ref[h])
        down.first(0, h)
    for i in range(3):
        grads.first(i)
    for d in ORDER:
        total.send_z(d)

    vw[0] = jnp.zeros((8, 1024), f32)
    gains = jnp.zeros((1, 1024), f32)
    for w in range(8):
        base = tok_ref[w].astype(f32)
        gains = gains + jnp.sum(dn_ref[w].astype(f32) * base * rms_of(base), axis=0, keepdims=True)
    vw[0, 0:1] = gains
    vw[0, 1:2] = gn_ref[...]
    vw[0, 2:3] = gg_ref[...]

    def vec_round(buf, devices, sends, recvs):
        copies = []
        for i, device in enumerate(devices):
            copies.append(rcopy(buf.at[0], buf.at[i + 1], sends.at[i], recvs.at[i], device))
            copies[-1].start()
        return copies

    def vec_total(buf, copies):
        value = buf[0]
        for i, copy in enumerate(copies):
            copy.wait_recv()
            value = value + buf[i + 1]
        return value

    round1 = vec_round(vw, [p.along_z(d) for d in ORDER] + [p.along_z_other(d) for d in ORDER] + [p.sibling], vs1, vr1)
    for i in range(3):
        grads.second(i)
    base = tok_ref[p.wt].astype(f32)
    d_normed = total.own()
    gt_ref[p.wt] = (dmid_ref[...] + norm_back(base, rms_of(base), gain_ref[...], d_normed)).astype(bf16)
    spread = WtGather(p, gt_ref, (az, bz, ag, bg))
    spread.start()
    for i in range(3):
        for h in range(2):
            back.put(i, h, grads.own(i, h).astype(bf16))
            back.first(i, h)
    vx[0] = vec_total(vw, round1)
    round2 = vec_round(vx, [p.along_x(d) for d in ORDER], vs2, vr2)
    for h in range(2):
        down.second(0, h)
    for i in range(3):
        for h in range(2):
            back.second(i, h)
    vy[0] = vec_total(vx, round2)
    round3 = vec_round(vy, [p.along_y(d) for d in ORDER], vs3, vr3)
    spread.forward()
    vec_ref[...] = vec_total(vy, round3)
    spread.arrived()
    spread.finish()
    total.finish()
    grads.finish()
    back.finish()
    down.finish()
    for copy in round1 + round2 + round3:
        copy.wait_send()


def comm_call(kernel, number, out_shape, args, scratch, name, limit=10, first=None):
    return pl.pallas_call(
        kernel,
        out_shape=out_shape,
        in_specs=[first or vmem] + [vmem] * (len(args) - 1),
        out_specs=tuple(vmem for _ in out_shape),
        scratch_shapes=scratch,
        compiler_params=pltpu.CompilerParams(
            collective_id=number, has_side_effects=True, vmem_limit_bytes=limit << 20
        ),
        cost_estimate=pl.CostEstimate(flops=8 << 30, bytes_accessed=32 << 20, transcendentals=0),
        name=name,
    )(*args)


def gather_keys(lengths, q, kv):
    return comm_call(
        gather_kernel, 1,
        (sds((2, 256, 128), bf16), sds((4, 4, 2, 256, 128), bf16), sds((8192, 128), bf16)),
        (lengths, q.reshape(2, 256, 128), kv.reshape(2, 256, 128)),
        [DMA, DMA, DMA((2, 3)), DMA((2, 3)), DMA((2, 4, 3)), DMA((2, 4, 3))],
        "gather_keys", 4, smem,
    )


def scatter_keys(dkv, dq):
    return comm_call(
        scatter_kernel, 2,
        (sds((2, 256, 128), bf16), sds((2, 256, 128), bf16)),
        (dkv.reshape(4, 4, 2, 256, 128), dq.reshape(2, 256, 128)),
        [pltpu.VMEM((2, 3, 4, 256, 128), bf16), pltpu.VMEM((2, 3, 256, 128), bf16), pltpu.VMEM((2, 3, 256, 128), bf16),
         DMA, DMA, DMA((2, 3)), DMA((2, 3)), DMA((2, 3)), DMA((2, 3))],
        "scatter_keys",
    )


def make_middle(mix, w_out, tokens, gain):
    rows = pltpu.VMEM
    return comm_call(
        middle_kernel, 3,
        (sds((8, 64, 1024), bf16), sds((64, 1024), f32), sds((2, 256, 128), bf16)),
        (mix.reshape(2, 256, 128), w_out, tokens.reshape(8, 64, 1024), gain.reshape(1, 1024)),
        [rows((8, 64, 1024), bf16), rows((4, 64, 1024), bf16), rows((3, 64, 1024), bf16), rows((3, 64, 1024), bf16),
         DMA, DMA, DMA((4,)), DMA((4,)), DMA((3,)), DMA((3,)), DMA((3,)), DMA((3,)), DMA((4,)), DMA((4,))],
        "make_middle",
    )


def turn_back(dm, mlp, mid, cot, gain, w_out, grads):
    rows = pltpu.VMEM
    return comm_call(
        turn_kernel, 4,
        (sds((8, 64, 1024), bf16), sds((8, 64, 1024), bf16), sds((64, 1024), f32), sds((1, 1024), f32),
         sds((2, 256, 128), bf16), sds((3, 2, 144, 128), bf16)),
        (dm.reshape(8, 64, 1024), mlp.reshape(8, 64, 1024), mid, cot.reshape(8, 64, 1024), gain.reshape(1, 1024), w_out)
        + tuple(g.reshape(4, 144, 1024) for g in grads),
        [rows((256, 128), bf16), rows((2, 4, 64, 1024), bf16), rows((2, 3, 64, 1024), bf16), rows((2, 3, 64, 1024), bf16),
         DMA, DMA, DMA((2, 4)), DMA((2, 4)), DMA((2, 3)), DMA((2, 3)), DMA((2, 3)), DMA((2, 3)), DMA((2, 4)), DMA((2, 4))]
        + SpScatter.scratch(3, 144),
        "turn_back", 16,
    )


def last_sums(dn, gq, go, red, tokens, dmid, gain, gn, gg):
    rows = pltpu.VMEM
    return comm_call(
        last_kernel, 5,
        (sds((8, 64, 1024), bf16), sds((3, 4, 32, 1024), bf16), sds((1, 4, 144, 1024), bf16), sds((8, 1024), f32)),
        (dn.reshape(8, 64, 1024), gq.reshape(2, 4, 32, 1024), go.reshape(4, 32, 1024), red, tokens.reshape(8, 64, 1024),
         dmid, gain.reshape(1, 1024), gn, gg),
        [rows((4, 64, 1024), bf16), rows((3, 64, 1024), bf16), rows((3, 64, 1024), bf16),
         DMA((4,)), DMA((4,)), DMA((3,)), DMA((3,)), DMA((3,)), DMA((3,)), DMA((4,)), DMA((4,)),
         rows((8, 8, 1024), f32), rows((4, 8, 1024), f32), rows((4, 8, 1024), f32),
         DMA((7,)), DMA((7,)), DMA((3,)), DMA((3,)), DMA((3,)), DMA((3,))]
        + SpScatter.scratch(3, 32) + SpGather.sems(3) + SpGather.sems(1),
        "last_sums", 10,
    )


def turned(value, lane):
    return jnp.where(lax.rem(lane, 64) < 32, pltpu.roll(value, 96, 1), pltpu.roll(value, 32, 1))


def head_sums(value, lane):
    s0 = jnp.sum(jnp.where(lane < 64, value, 0.0), axis=1, keepdims=True)
    s1 = jnp.sum(jnp.where(lane < 64, 0.0, value), axis=1, keepdims=True)
    return jnp.where(lane < 64, s0, s1)


def twice(gain):
    return jnp.concatenate([gain, gain], axis=1)


def nt(a, b):
    return lax.dot_general(a, b, (((1,), (1,)), ((), ())), preferred_element_type=f32)


def tn(a, b):
    return lax.dot_general(a, b, (((0,), (0,)), ((), ())), preferred_element_type=f32)


def proj_kernel(len_ref, tok_ref, gain_ref, wq_ref, wk_ref, wv_ref, qg_ref, kg_ref, freq_ref,
                n_ref, qp_ref, kvp_ref, q_ref, kv_ref, cos_ref, sin_ref):
    lane = lanes((512, 128))
    ids = lax.axis_index("sp") * 512 + lax.broadcasted_iota(jnp.int32, (1, 512), 1)
    positions = (ids - starts_of(ids, len_ref)).astype(f32)
    angles = positions * freq_ref[:, 0:1]
    cosine, sine = jnp.cos(angles), jnp.sin(angles)
    cosine = jnp.concatenate([cosine] * 4, axis=0).T
    sine = jnp.concatenate([-sine, sine, -sine, sine], axis=0).T
    cos_ref[...] = cosine
    sin_ref[...] = sine
    base = tok_ref[...].astype(f32)
    normed = (base * rms_of(base) * gain_ref[...]).astype(bf16)
    n_ref[...] = normed
    wkv = jnp.concatenate([wk_ref[...], wv_ref[...]], axis=0)
    q = jnp.dot(normed, wq_ref[...], preferred_element_type=f32)
    qp_ref[...] = q
    q = q * lax.rsqrt(head_sums(q * q, lane) * (1.0 / 64) + eps) * twice(qg_ref[...])
    q_ref[...] = (q * cosine + turned(q, lane) * sine).astype(bf16)
    kv = nt(normed, wkv)
    kvp_ref[...] = kv
    k = kv * lax.rsqrt(head_sums(kv * kv, lane) * (1.0 / 64) + eps) * twice(kg_ref[...])
    k = k * cosine + turned(k, lane) * sine
    kv_ref[...] = jnp.where(lane < 64, k, kv).astype(bf16)


def proj_back_kernel(dq_ref, dkv_ref, qp_ref, kvp_ref, n_ref, wq_ref, wk_ref, wv_ref, qg_ref, kg_ref, cos_ref, sin_ref, dn_ref, g_ref, gg_ref):
    lane = lanes((512, 128))
    cosine, sine = cos_ref[...], sin_ref[...]

    def back(grad, proj, gain):
        grad = grad * cosine - turned(grad, lane) * sine
        scale = lax.rsqrt(head_sums(proj * proj, lane) * (1.0 / 64) + eps)
        scaled = grad * gain
        inner = head_sums(scaled * proj, lane) * (1.0 / 64)
        gains = jnp.sum(grad * proj * scale, axis=0, keepdims=True)
        return scale * scaled - proj * scale * scale * scale * inner, gains

    dq, gq = back(dq_ref[...].astype(f32), qp_ref[...], twice(qg_ref[...]))
    dkv_in = dkv_ref[...].astype(f32)
    dk, gk = back(dkv_in, kvp_ref[...], twice(kg_ref[...]))
    dq = dq.astype(bf16)
    dkv = jnp.where(lane < 64, dk, dkv_in).astype(bf16)
    wkv = jnp.concatenate([wk_ref[...], wv_ref[...]], axis=0)
    dn_ref[...] = (nt(dq, wq_ref[...]) + jnp.dot(dkv, wkv, preferred_element_type=f32)).astype(bf16)
    normed = n_ref[...]
    g_ref[0] = tn(dq, normed).astype(bf16)
    g_ref[1] = tn(dkv, normed).astype(bf16)
    gg_ref[...] = jnp.concatenate([gq, gk, jnp.zeros((1, 768), f32)], axis=1)


def local_call(kernel, out_shape, args, name, first=None):
    return pl.pallas_call(
        kernel,
        out_shape=out_shape,
        in_specs=[first or vmem] + [vmem] * (len(args) - 1),
        out_specs=tuple(vmem for _ in out_shape),
        compiler_params=pltpu.CompilerParams(vmem_limit_bytes=16 << 20),
        cost_estimate=pl.CostEstimate(flops=3 << 30, bytes_accessed=16 << 20, transcendentals=0),
        name=name,
    )(*args)


theta = 1000000.0


def body(tokens, norm_in, w_query, w_key, w_value, query_gain, key_gain, w_out, norm_mid, w_gate, w_up, w_down, cotangent, lengths):
    parts = lax.axis_size("sp")
    freqs = theta ** (-(np.arange(32).astype(np.float64) * 2.0) / 64)
    freqs = jnp.asarray(np.broadcast_to(freqs.astype(np.float32)[:, None], (32, 128)))
    qg, kg = query_gain.reshape(1, 64), key_gain.reshape(1, 64)
    wk, wv = w_key.T, w_value.T
    wide = sds((512, 128), f32)

    normed, q_proj, kv_proj, q, kv, cosine, sine = local_call(
        proj_kernel,
        (sds((512, 1024), bf16), wide, wide, sds((512, 128), bf16), sds((512, 128), bf16), wide, wide),
        (lengths, tokens, norm_in.reshape(1, 1024), w_query, wk, wv, qg, kg, freqs),
        "project", smem,
    )
    qz, kv_all, ext = gather_keys(lengths, q, kv)
    kv_all = kv_all.reshape(8192, 128)
    mix_z, mix_f, qa = attend(parts, lengths, qz.reshape(512, 128), kv_all, ext)
    normed_mid, mid_own, mixed = make_middle(mix_z, w_out, tokens, norm_mid)
    normed_mid = normed_mid.reshape(512, 1024)
    mixed = mixed.reshape(512, 128)

    gate = jnp.dot(normed_mid, w_gate, preferred_element_type=f32)
    up_proj = jnp.dot(normed_mid, w_up, preferred_element_type=f32)
    sigmoid_gate = jax.nn.sigmoid(gate)
    act = (gate * sigmoid_gate * up_proj).astype(bf16)
    mlp_part = jnp.dot(act, w_down, preferred_element_type=f32).astype(bf16)
    d_act = jnp.einsum("td,fd->tf", cotangent, w_down, preferred_element_type=f32)
    d_gate = (d_act * up_proj * sigmoid_gate * (1.0 + gate * (1.0 - sigmoid_gate))).astype(bf16)
    d_up = (d_act * gate * sigmoid_gate).astype(bf16)
    d_mid_part = (
        jnp.einsum("tf,df->td", d_gate, w_gate, preferred_element_type=f32)
        + jnp.einsum("tf,df->td", d_up, w_up, preferred_element_type=f32)
    ).astype(bf16)
    grads = (
        jnp.einsum("tf,td->fd", d_gate, normed_mid, preferred_element_type=f32).astype(bf16),
        jnp.einsum("tf,td->fd", d_up, normed_mid, preferred_element_type=f32).astype(bf16),
        jnp.einsum("tf,td->fd", act, cotangent, preferred_element_type=f32).astype(bf16),
    )
    output, d_attn, d_middle_own, gn, d_mix_z, red = turn_back(
        d_mid_part, mlp_part, mid_own, cotangent, norm_mid, w_out, grads
    )
    g_out = jnp.einsum("tq,td->qd", mixed, d_attn.reshape(512, 1024), preferred_element_type=f32).astype(bf16)
    dq_z, dkv_all, g_ff = attend_back(parts, qa, mix_f, d_mix_z.reshape(512, 128), kv_all, ext, red[:2])
    dkv, dq = scatter_keys(dkv_all, dq_z)
    dn_part, g_qkv, gg = local_call(
        proj_back_kernel,
        (sds((512, 1024), bf16), sds((2, 128, 1024), bf16), sds((1, 1024), f32)),
        (dq.reshape(512, 128), dkv.reshape(512, 128), q_proj, kv_proj, normed, w_query, wk, wv, qg, kg, cosine, sine),
        "project_back",
    )
    grad_tokens, sums, g_down, vec = last_sums(
        dn_part, g_qkv, g_out, red[2], tokens, d_middle_own, norm_in, gn, gg
    )
    sums = sums.reshape(3, 128, 1024).astype(f32)
    g_ff = g_ff.reshape(2, 576, 1024).astype(f32)
    return (
        output.reshape(512, 1024),
        grad_tokens.reshape(512, 1024),
        vec[0],
        sums[0].T,
        sums[1, :64].T,
        sums[1, 64:].T,
        vec[2, :64] + vec[2, 64:128],
        vec[2, 128:192],
        sums[2],
        vec[1],
        g_ff[0].T,
        g_ff[1].T,
        g_down.reshape(576, 1024).astype(f32),
    )


def solution(mesh):
    placed = (
        P("sp", None), P(), P(None, "wt"), P(None, "wt"), P(None, "wt"), P(), P(), P("wt", None), P(),
        P(None, "wt"), P(None, "wt"), P("wt", None), P("sp", None), P(),
    )
    return jax.shard_map(
        body,
        mesh=mesh,
        in_specs=placed,
        out_specs=(
            P("sp", None), P("sp", None), P(), P(None, "wt"), P(None, "wt"), P(None, "wt"), P(), P(),
            P("wt", None), P(), P(None, "wt"), P(None, "wt"), P("wt", None),
        ),
        check_vma=False,
    )
```

```python
import functools, math
import jax
import jax.numpy as jnp
import numpy as np
from jax import lax
from jax.experimental import pallas as pl
from jax.experimental.pallas import tpu as pltpu
from jax.sharding import PartitionSpec as P

f32 = jnp.float32
bf16 = jnp.bfloat16
sds = jax.ShapeDtypeStruct
DMA = pltpu.SemaphoreType.DMA
CH = 512
HALF = 256
SCALE = 0.125
EARLY = 4
C2 = SCALE * math.log2(math.e)


def starts_of(ids, len_ref):
    end = jnp.int32(0)
    start = jnp.zeros_like(ids)
    for j in range(4):
        end = end + len_ref[j]
        start = start + jnp.where(ids >= end, len_ref[j], 0)
    return start


def scalar_start(row, len_ref):
    end = jnp.int32(0)
    start = jnp.int32(0)
    for j in range(4):
        end = end + len_ref[j]
        start = start + jnp.where(row >= end, len_ref[j], 0)
    return start


def lanes(shape):
    return lax.broadcasted_iota(jnp.int32, shape, len(shape) - 1)


def split3(value, lane):
    hi = value.astype(bf16).astype(f32)
    rest = value - hi
    mid = rest.astype(bf16).astype(f32)
    low = rest - mid
    return jnp.where(lane == 0, hi, jnp.where(lane == 1, mid, jnp.where(lane == 2, low, 0.0)))


def tile_row(me, t, parts):
    return me * 512 if t == 0 else (parts - 1 - me) * 512 + HALF


FAR = 8192.0


def segment_bounds(len_ref, lane):
    begin = jnp.zeros_like(lane)
    end = jnp.zeros_like(lane)
    at = jnp.int32(0)
    for j in range(4):
        begin = jnp.where(lane == 3 + j, at, begin)
        at = at + len_ref[j]
        end = jnp.where(lane == 3 + j, at, end)
    return begin, end


def inside(ids, len_ref, shape):
    lane = lanes(shape)
    begin, end = segment_bounds(len_ref, lane)
    return (ids >= begin) & (ids < end), lane


def key_columns(k0, len_ref, rows):
    ids = k0 + lax.broadcasted_iota(jnp.int32, (rows, 128), 0)
    within, lane = inside(ids, len_ref, (rows, 128))
    return jnp.where(lane < 3, 1.0, jnp.where(within, 1.0, 0.0)).astype(bf16)


def query_columns(r0, len_ref, rows):
    ids = r0 + lax.broadcasted_iota(jnp.int32, (rows, 128), 0)
    within, lane = inside(ids, len_ref, (rows, 128))
    return jnp.where((lane < 3) | (lane > 6) | within, 0.0, -FAR)


def fwd_kernel(parts, len_ref, q_ref, kv_ref, ext_ref, mix_ref, out_ref, qa_ref, acc_ref):
    me = lax.axis_index("sp")
    lane = lanes((HALF, 128))
    lane2 = lanes((2 * HALF, 128))
    lanek = lanes((CH, 128))
    for t in range(2):
        r0 = tile_row(me, t, parts)
        q = q_ref[t * HALF:(t + 1) * HALF, :].astype(f32)
        qa_ref[t, 0:HALF, 0:128] = jnp.where(lane < 64, q, 0.0).astype(bf16)
        qa_ref[t, HALF:, 0:128] = jnp.where(lane < 64, pltpu.roll(q, 64, 1), 0.0).astype(bf16)
        columns = query_columns(r0, len_ref, HALF)
        columns = jnp.concatenate([columns, columns], axis=0)
        qa_ref[t, :, 128:256] = columns.astype(bf16)
        acc_ref[...] = jnp.zeros_like(acc_ref)

        def step(c, masked):
            k0 = pl.multiple_of(c * CH, CH)
            kv = kv_ref[pl.ds(k0, CH), :]
            kva = jnp.concatenate([kv, ext_ref[pl.ds(k0, CH), :]], axis=1)
            s = lax.dot_general(qa_ref[t], kva, (((1,), (1,)), ((), ())), preferred_element_type=f32)
            p = jnp.exp2(s * C2)
            if masked:
                rows = r0 + lax.rem(lax.broadcasted_iota(jnp.int32, (2 * HALF, 1), 0), HALF)
                keys = k0 + lax.broadcasted_iota(jnp.int32, (2 * HALF, CH), 1)
                p = jnp.where(keys <= rows, p, 0.0)
            ones = jnp.where(lanek < 64, jnp.ones_like(kv), kv)
            acc_ref[...] += jnp.dot(p.astype(bf16), ones, preferred_element_type=f32)

        block = me if t == 0 else parts - 1 - me
        pl.loop(0, block)(lambda c: step(c, False))
        step(block, True)

        acc = acc_ref[...]
        swapped = pltpu.roll(acc, 64, 1)
        o = swapped / acc
        m = jnp.where(lane < 64, o[:HALF], pltpu.roll(o[HALF:], 64, 1))
        mix_ref[t * HALF:(t + 1) * HALF, :] = m.astype(bf16)
        out_ref[t * HALF:(t + 1) * HALF, :] = m
        total = jnp.where(lane2 < 64, acc, swapped)
        qa_ref[t, :, 128:256] = (split3(jnp.log(total) * (-1.0 / SCALE), lane2) + columns).astype(bf16)


def bwd_kernel(parts, qa_ref, out_ref, do_ref, kv_ref, ext_ref, red_ref, dq_ref, dkv_ref, grads_ref, da_ref, acc_ref, dqt_ref, *sems):
    me = lax.axis_index("sp")
    p = Place()
    meet([p.along_x(d) for d in ORDER] + [p.along_y(d) for d in ORDER])
    spread = SpGather(p, grads_ref, 144, sems)
    for i in range(3):
        for h in range(2):
            spread.put(i, h, red_ref[i, h])
            spread.first(i, h)
    lane = lanes((HALF, 128))
    acc_ref[...] = jnp.zeros_like(acc_ref)
    upper_long = (me < parts // 2).astype(jnp.int32)
    for turn in range(2):
        t = upper_long if turn == 0 else 1 - upper_long
        block = me + t * (parts - 1 - 2 * me)
        r0 = block * 512 + t * HALF
        rows_t = pl.ds(pl.multiple_of(t * HALF, HALF), HALF)
        do = do_ref[rows_t, :].astype(f32)
        prod = do * out_ref[rows_t, :]
        d0 = -jnp.sum(jnp.where(lane < 64, prod, 0.0), axis=1, keepdims=True)
        d1 = -jnp.sum(jnp.where(lane < 64, 0.0, prod), axis=1, keepdims=True)
        da_ref[0:HALF, 0:128] = jnp.where(lane < 64, 0.0, pltpu.roll(do, 64, 1)).astype(bf16)
        da_ref[HALF:, 0:128] = jnp.where(lane < 64, 0.0, do).astype(bf16)
        da_ref[0:HALF, 128:256] = split3(jnp.broadcast_to(d0, (HALF, 128)), lane).astype(bf16)
        da_ref[HALF:, 128:256] = split3(jnp.broadcast_to(d1, (HALF, 128)), lane).astype(bf16)
        dqt_ref[...] = jnp.zeros_like(dqt_ref)

        def step(c, masked, t=t, r0=r0):
            k0 = pl.multiple_of(c * CH, CH)
            kv = kv_ref[pl.ds(k0, CH), :]
            kva = jnp.concatenate([kv, ext_ref[pl.ds(k0, CH), :]], axis=1)
            qa = qa_ref[t]
            da = da_ref[...]
            s = lax.dot_general(kva, qa, (((1,), (1,)), ((), ())), preferred_element_type=f32)
            p = jnp.exp2(s * C2)
            if masked:
                rows = r0 + lax.rem(lax.broadcasted_iota(jnp.int32, (1, 2 * HALF), 1), HALF)
                keys = k0 + lax.broadcasted_iota(jnp.int32, (CH, 2 * HALF), 0)
                p = jnp.where(keys <= rows, p, 0.0)
            dp = lax.dot_general(kva, da, (((1,), (1,)), ((), ())), preferred_element_type=f32)
            ds = (p * dp).astype(bf16)
            acc_ref[pl.ds(k0, CH), :] += jnp.dot(
                p.astype(bf16), da[:, 0:128], preferred_element_type=f32
            ) + jnp.dot(ds, qa[:, 0:128], preferred_element_type=f32)
            kt = kv.T[0:64, :]
            dqt_ref[...] += jnp.dot(kt, ds, preferred_element_type=f32)

        if turn == 0:
            pl.loop(0, EARLY)(lambda c: step(c, False))
            for i in range(3):
                for h in range(2):
                    spread.second(i, h)
            pl.loop(EARLY, block)(lambda c: step(c, False))
        else:
            pl.loop(0, block)(lambda c: step(c, False))
        step(block, True)
        dqt = dqt_ref[...]
        both = jnp.concatenate([dqt[:, :HALF], dqt[:, HALF:]], axis=0)
        dq_ref[rows_t, :] = (both.T * SCALE).astype(bf16)
    weight = jnp.where(lanes((512, 128)) < 64, SCALE, 1.0)

    @pl.loop(0, parts)
    def _(b):
        rows = pl.ds(pl.multiple_of(b * 512, 512), 512)
        dkv_ref[rows, :] = (acc_ref[rows, :] * weight).astype(bf16)

    spread.finish()


smem = pl.BlockSpec(memory_space=pltpu.SMEM)
vmem = pl.BlockSpec(memory_space=pltpu.VMEM)


def attend(parts, lengths, q, kv, ext):
    rows = 2 * HALF
    return pl.pallas_call(
        functools.partial(fwd_kernel, parts),
        out_shape=(sds((rows, 128), bf16), sds((rows, 128), f32), sds((2, rows, 256), bf16)),
        in_specs=[smem, vmem, vmem, vmem],
        out_specs=(vmem, vmem, vmem),
        scratch_shapes=[pltpu.VMEM((rows, 128), f32)],
        compiler_params=pltpu.CompilerParams(vmem_limit_bytes=12 << 20),
        cost_estimate=pl.CostEstimate(flops=3 << 30, bytes_accessed=4 << 20, transcendentals=5 << 20),
        name="attend",
    )(lengths, q, kv, ext)


def attend_back(parts, qa, out, do, kv, ext, red):
    rows = 2 * HALF
    return pl.pallas_call(
        functools.partial(bwd_kernel, parts),
        out_shape=(sds((rows, 128), bf16), sds(kv.shape, bf16), sds((3, 4, 144, 1024), bf16)),
        in_specs=[vmem] * 6,
        out_specs=(vmem, vmem, vmem),
        scratch_shapes=[pltpu.VMEM((rows, 256), bf16), pltpu.VMEM(kv.shape, f32), pltpu.VMEM((64, rows), f32)]
        + SpGather.sems(3),
        compiler_params=pltpu.CompilerParams(collective_id=6, has_side_effects=True, vmem_limit_bytes=20 << 20),
        cost_estimate=pl.CostEstimate(flops=10 << 30, bytes_accessed=8 << 20, transcendentals=5 << 20),
        name="attend_back",
    )(qa, out, do, kv, ext, red)


MESH = pl.DeviceIdType.MESH
eps = 1e-05


def rcopy(src, dst, send, recv, device):
    return pltpu.make_async_remote_copy(
        src_ref=src, dst_ref=dst, send_sem=send, recv_sem=recv, device_id=device, device_id_type=MESH
    )


def meet(devices):
    barrier = pltpu.get_barrier_semaphore()
    for device in devices:
        pl.semaphore_signal(barrier, inc=1, device_id=device, device_id_type=MESH)
    pl.semaphore_wait(barrier, len(devices))


class Place:
    def __init__(self):
        self.sp = lax.axis_index("sp")
        self.wt = lax.axis_index("wt")
        self.x, self.y = lax.div(self.sp, 4), lax.rem(self.sp, 4)
        self.z, self.c = lax.div(self.wt, 2), lax.rem(self.wt, 2)
        self.mirror = (15 - self.sp, self.wt)
        self.sibling = (self.sp, self.z * 2 + 1 - self.c)

    def along_x(self, d):
        return (lax.rem(self.x + d, 4) * 4 + self.y, self.wt)

    def along_y(self, d):
        return (self.x * 4 + lax.rem(self.y + d, 4), self.wt)

    def along_z(self, d):
        return (self.sp, lax.rem(self.z + d, 4) * 2 + self.c)

    def along_z_other(self, d):
        return (self.sp, lax.rem(self.z + d, 4) * 2 + 1 - self.c)

    def first(self, h, d):
        return self.along_x(d) if h == 0 else self.along_y(d)

    def second(self, h, d):
        return self.along_y(d) if h == 0 else self.along_x(d)

    def fsp(self, h):
        return self.x if h == 0 else self.y

    def ssp(self, h):
        return self.y if h == 0 else self.x


def spot(h, first, second):
    return (first, second) if h == 0 else (second, first)


ORDER = (2, 1, 3)


def gather_kernel(len_ref, q_ref, kv_ref, qz_ref, all_ref, ext_ref, ms, mr, fs, fr, ss, sr):
    p = Place()
    meet([p.along_x(d) for d in ORDER] + [p.along_y(d) for d in ORDER] + [p.mirror])
    all_ref[p.x, p.y] = kv_ref[...]
    mirror = rcopy(q_ref.at[1], qz_ref.at[1], ms, mr, p.mirror)
    first, second = {}, {}
    for d in ORDER:
        for h in range(2):
            first[h, d] = rcopy(
                kv_ref.at[h], all_ref.at[p.x, p.y, h], fs.at[h, d - 1], fr.at[h, d - 1], p.first(h, d)
            )
            first[h, d].start()
    mirror.start()

    def forward(h, slot):
        a = lax.rem(p.fsp(h) + 4 - slot, 4)
        at = spot(h, a, p.ssp(h))
        for e in ORDER:
            src = kv_ref.at[h] if slot == 0 else all_ref.at[at[0], at[1], h]
            second[h, slot, e] = rcopy(
                src, all_ref.at[at[0], at[1], h], ss.at[h, slot, e - 1], sr.at[h, slot, e - 1], p.second(h, e)
            )
            second[h, slot, e].start()

    for h in range(2):
        forward(h, 0)
    qz_ref[0] = q_ref[0]
    @pl.loop(0, 8)
    def _(b):
        rows = pl.ds(pl.multiple_of(b * 1024, 1024), 1024)
        ext_ref[rows, :] = key_columns(b * 1024, len_ref, 1024)

    for d in (1, 3, 2):
        for h in range(2):
            first[h, d].wait_recv()
            forward(h, d)
    mirror.wait()
    for copy in first.values():
        copy.wait_send()
    for copy in second.values():
        copy.wait()


class SpScatter:
    def __init__(self, p, srcs, rows, refs):
        self.p, self.srcs, self.rows = p, srcs, rows
        self.ra, self.rb, self.send, self.r2, self.fs, self.fr, self.ss, self.sr = refs
        self.one, self.two = {}, {}

    @staticmethod
    def scratch(n, rows):
        return [
            pltpu.VMEM((n, 3, rows, 512), bf16), pltpu.VMEM((n, 3, 4, rows, 128), bf16),
            pltpu.VMEM((n, 2, 3, rows, 128), bf16), pltpu.VMEM((n, 2, 3, rows, 128), bf16),
            DMA((n, 2, 3)), DMA((n, 2, 3)), DMA((n, 2, 3)), DMA((n, 2, 3)),
        ]

    def first(self, i):
        p = self.p
        for d in ORDER:
            to = lax.rem(p.x + d, 4)
            self.one[i, 0, d] = rcopy(
                self.srcs[i].at[to, :, pl.ds(0, 512)], self.ra.at[i, d - 1],
                self.fs.at[i, 0, d - 1], self.fr.at[i, 0, d - 1], p.along_x(d),
            )
            self.one[i, 0, d].start()
            to = lax.rem(p.y + d, 4)
            self.one[i, 1, d] = rcopy(
                self.srcs[i].at[:, :, pl.ds(columns_at(1, to), 128)], self.rb.at[i, d - 1],
                self.fs.at[i, 1, d - 1], self.fr.at[i, 1, d - 1], p.along_y(d),
            )
            self.one[i, 1, d].start()

    def part(self, i, h, b):
        p = self.p
        if h == 0:
            value = self.srcs[i][p.x, :, pl.ds(columns_at(0, b), 128)].astype(f32)
            for d in range(3):
                value = value + self.ra[i, d, :, pl.ds(columns_at(0, b), 128)].astype(f32)
            return value
        value = self.srcs[i][b, :, pl.ds(columns_at(1, p.y), 128)].astype(f32)
        for d in range(3):
            value = value + self.rb[i, d, b].astype(f32)
        return value

    def second(self, i):
        p = self.p
        for h in range(2):
            for d in ORDER:
                self.one[i, h, d].wait_recv()
            for e in ORDER:
                self.send[i, h, e - 1] = self.part(i, h, lax.rem(p.ssp(h) + e, 4)).astype(bf16)
                self.two[i, h, e] = rcopy(
                    self.send.at[i, h, e - 1], self.r2.at[i, h, e - 1],
                    self.ss.at[i, h, e - 1], self.sr.at[i, h, e - 1], p.second(h, e),
                )
                self.two[i, h, e].start()

    def own(self, i, h):
        value = self.part(i, h, self.p.ssp(h))
        for e in ORDER:
            self.two[i, h, e].wait_recv()
            value = value + self.r2[i, h, e - 1].astype(f32)
        return value

    def finish(self):
        for copy in list(self.one.values()) + list(self.two.values()):
            copy.wait_send()


def columns_at(h, b):
    return pl.multiple_of(h * 512 + b * 128, 128)


class SpGather:
    def __init__(self, p, out, rows, sems):
        self.p, self.out, self.rows = p, out, rows
        self.fs, self.fr, self.ss, self.sr = sems
        self.one, self.two = {}, {}

    @staticmethod
    def sems(n):
        return [DMA((n, 2, 3)) for _ in range(4)]

    def spot(self, h):
        p = self.p
        return p.x, pl.ds(columns_at(h, p.y), 128)

    def put(self, i, h, value):
        x, columns = self.spot(h)
        self.out[i, x, :, columns] = value

    def first(self, i, h):
        x, columns = self.spot(h)
        block = self.out.at[i, x, :, columns]
        for e in ORDER:
            self.one[i, h, e] = rcopy(
                block, block, self.fs.at[i, h, e - 1], self.fr.at[i, h, e - 1], self.p.second(h, e)
            )
            self.one[i, h, e].start()

    def second(self, i, h):
        x, columns = self.spot(h)
        for e in ORDER:
            self.one[i, h, e].wait_recv()
        block = self.out.at[i, x, :, pl.ds(0, 512)] if h == 0 else self.out.at[i, :, :, columns]
        for d in ORDER:
            self.two[i, h, d] = rcopy(
                block, block, self.ss.at[i, h, d - 1], self.sr.at[i, h, d - 1], self.p.first(h, d)
            )
            self.two[i, h, d].start()

    def arrived(self, i):
        for h in range(2):
            for d in ORDER:
                self.two[i, h, d].wait_recv()

    def finish(self):
        for copy in self.one.values():
            copy.wait_send()
        for copy in self.two.values():
            copy.wait()


class WtSum:
    def __init__(self, p, part, sib, send, rz, sems):
        self.p, self.part, self.sib, self.send, self.rz = p, part, sib, send, rz
        self.cs, self.cr, self.zs, self.zr = sems
        self.second = {}

    def core(self, zz):
        return rcopy(
            self.part.at[zz * 2 + 1 - self.p.c], self.sib.at[zz], self.cs.at[zz], self.cr.at[zz], self.p.sibling
        )

    def start_core(self, zz):
        self.core(zz).start()

    def pair(self, zz):
        return self.part[zz * 2 + self.p.c].astype(f32) + self.sib[zz].astype(f32)

    def send_z(self, d):
        zz = lax.rem(self.p.z + d, 4)
        self.core(zz).wait_recv()
        self.send[d - 1] = self.pair(zz).astype(bf16)
        copy = rcopy(
            self.send.at[d - 1], self.rz.at[d - 1], self.zs.at[d - 1], self.zr.at[d - 1], self.p.along_z(d)
        )
        copy.start()
        self.second[d] = copy

    def own(self):
        self.core(self.p.z).wait_recv()
        value = self.pair(self.p.z)
        for d in (1, 3, 2):
            self.second[d].wait_recv()
            value = value + self.rz[d - 1].astype(f32)
        return value

    def finish(self):
        for zz in range(4):
            self.core(zz).wait_send()
        for copy in self.second.values():
            copy.wait_send()


class WtGather:
    def __init__(self, p, out, sems):
        self.p, self.out = p, out
        self.zs, self.zr, self.gs, self.gr = sems
        self.far, self.near = {}, {}

    def start(self):
        p = self.p
        for d in ORDER:
            self.far[d] = rcopy(
                self.out.at[p.wt], self.out.at[p.wt], self.zs.at[d - 1], self.zr.at[d - 1], p.along_z(d)
            )
            self.far[d].start()
        self.pass_on(0)

    def pass_on(self, slot):
        p = self.p
        row = lax.rem(p.z + 4 - slot, 4) * 2 + p.c
        self.near[slot] = rcopy(
            self.out.at[row], self.out.at[row], self.gs.at[slot], self.gr.at[slot], p.sibling
        )
        self.near[slot].start()

    def forward(self):
        for d in (1, 3, 2):
            self.far[d].wait_recv()
            self.pass_on(d)

    def arrived(self):
        for slot in (0, 1, 3, 2):
            self.near[slot].wait_recv()

    def finish(self):
        for copy in list(self.far.values()) + list(self.near.values()):
            copy.wait_send()


def rms_of(value):
    return lax.rsqrt(jnp.mean(value * value, axis=-1, keepdims=True) + eps)


def norm_back(values, scale, gain, grad):
    scaled = grad * gain
    inner = jnp.mean(scaled * values, axis=-1, keepdims=True)
    return scale * scaled - values * scale * scale * scale * inner


def wt_peers(p):
    return [p.sibling] + [p.along_z(d) for d in ORDER]


def scatter_kernel(dkv_ref, dqz_ref, mlp_ref, mid_ref, own_ref, dq_ref, out_ref, r1, send, r2, ms, mr, fs, fr, ss, sr,
                   sib, sendz, rz, cs, cr, zs, zr, az, bz, ag, bg):
    p = Place()
    meet(wt_peers(p) + [p.along_x(d) for d in ORDER] + [p.along_y(d) for d in ORDER] + [p.mirror])
    first, second = {}, {}
    for d in ORDER:
        for h in range(2):
            to = lax.rem(p.fsp(h) + d, 4)
            src = dkv_ref.at[to, :, 0] if h == 0 else dkv_ref.at[:, to, 1]
            first[h, d] = rcopy(src, r1.at[h, d - 1], fs.at[h, d - 1], fr.at[h, d - 1], p.first(h, d))
            first[h, d].start()
    down = WtSum(p, mlp_ref, sib, sendz, rz, (cs, cr, zs, zr))
    for zz in range(4):
        down.start_core(zz)
    mirror = rcopy(dqz_ref.at[1], dq_ref.at[1], ms, mr, p.mirror)
    mirror.start()
    dq_ref[0] = dqz_ref[0]
    for d in ORDER:
        down.send_z(d)

    def total(h, b):
        at = spot(h, p.fsp(h), b)
        value = dkv_ref[at[0], at[1], h].astype(f32)
        for d in range(3):
            value = value + r1[h, d, b].astype(f32)
        return value

    out_ref[p.wt] = (mid_ref[...] + down.own()).astype(bf16)
    spread = WtGather(p, out_ref, (az, bz, ag, bg))
    spread.start()
    for h in range(2):
        for d in ORDER:
            first[h, d].wait_recv()
        for e in ORDER:
            b = lax.rem(p.ssp(h) + e, 4)
            send[h, e - 1] = total(h, b).astype(bf16)
            second[h, e] = rcopy(
                send.at[h, e - 1], r2.at[h, e - 1], ss.at[h, e - 1], sr.at[h, e - 1], p.second(h, e)
            )
            second[h, e].start()
    spread.forward()
    for h in range(2):
        value = total(h, p.ssp(h))
        for e in ORDER:
            second[h, e].wait_recv()
            value = value + r2[h, e - 1].astype(f32)
        own_ref[h] = value.astype(bf16)
    mirror.wait()
    spread.arrived()
    spread.finish()
    down.finish()
    for copy in list(first.values()) + list(second.values()):
        copy.wait_send()


def middle_kernel(mix_ref, w_ref, tok_ref, gain_ref, nm_ref, mid_ref, mixo_ref, part, sib, send, rz, ms, mr, cs, cr, zs, zr, az, bz, ag, bg):
    p = Place()
    meet(wt_peers(p) + [p.mirror])
    mirror = rcopy(mix_ref.at[1], mixo_ref.at[1], ms, mr, p.mirror)
    mirror.start()
    mixo_ref[0] = mix_ref[0]
    total = WtSum(p, part, sib, send, rz, (cs, cr, zs, zr))
    for half in range(2):
        if half == 1:
            mirror.wait()
        both = jnp.dot(mixo_ref[half], w_ref[...], preferred_element_type=f32).astype(bf16)
        part[half * 4:half * 4 + 4] = both.reshape(4, 64, 1024)
        for zz in (half * 2, half * 2 + 1):
            total.start_core(zz)
    for d in ORDER:
        total.send_z(d)
    middle = tok_ref[p.wt].astype(f32) + total.own()
    mid_ref[...] = middle
    nm_ref[p.wt] = (middle * rms_of(middle) * gain_ref[...]).astype(bf16)
    spread = WtGather(p, nm_ref, (az, bz, ag, bg))
    spread.start()
    spread.forward()
    spread.arrived()
    spread.finish()
    total.finish()


def turn_kernel(dm_ref, mid_ref, cot_ref, gain_ref, w_ref, g0_ref, g1_ref, g2_ref,
                da_ref, dmid_ref, gn_ref, dz_ref, red_ref,
                up, sib, send, rz, ms, mr, cs, cr, zs, zr, az, bz, ag, bg, *grad_refs):
    p = Place()
    meet(wt_peers(p) + [p.mirror] + [p.along_x(d) for d in ORDER] + [p.along_y(d) for d in ORDER])
    total = WtSum(p, dm_ref, sib, send, rz, (cs, cr, zs, zr))
    grads = SpScatter(p, (g0_ref, g1_ref, g2_ref), 144, grad_refs)
    for zz in range(4):
        total.start_core(zz)
    for i in range(3):
        grads.first(i)
    for d in ORDER:
        total.send_z(d)
    middle = mid_ref[...]
    scale = rms_of(middle)
    d_mid = total.own()
    gn_ref[...] = jnp.sum(d_mid * middle * scale, axis=0, keepdims=True)
    d_middle = cot_ref[p.wt].astype(f32) + norm_back(middle, scale, gain_ref[...], d_mid)
    dmid_ref[...] = d_middle
    da_ref[p.wt] = d_middle.astype(bf16)
    spread = WtGather(p, da_ref, (az, bz, ag, bg))
    spread.start()
    grads.second(0)
    spread.forward()
    spread.arrived()
    mirror = rcopy(up, dz_ref.at[1], ms, mr, p.mirror)
    for half in (1, 0):
        rows = da_ref[half * 4:half * 4 + 4].reshape(256, 1024)
        d_mixed = lax.dot_general(rows, w_ref[...], (((1,), (1,)), ((), ())), preferred_element_type=f32).astype(bf16)
        if half == 1:
            up[...] = d_mixed
            mirror.start()
        else:
            dz_ref[0] = d_mixed
    grads.second(1)
    grads.second(2)
    for i in range(3):
        for h in range(2):
            red_ref[i, h] = grads.own(i, h).astype(bf16)
    mirror.wait()
    for part in (spread, total, grads):
        part.finish()


def last_kernel(dn_ref, gq_ref, go_ref, tok_ref, dmid_ref, gain_ref, gn_ref, gg_ref,
                gt_ref, sums_ref, vec_ref,
                sib, send, rz, cs, cr, zs, zr, az, bz, ag, bg,
                vw, vx, vy, vs1, vr1, vs2, vr2, vs3, vr3, *more):
    p = Place()
    meet(wt_peers(p) + [p.along_z_other(d) for d in ORDER] + [p.along_x(d) for d in ORDER] + [p.along_y(d) for d in ORDER])
    total = WtSum(p, dn_ref, sib, send, rz, (cs, cr, zs, zr))
    for zz in range(4):
        total.start_core(zz)
    grads = SpScatter(p, (gq_ref.at[0], gq_ref.at[1], go_ref), 32, more[:8])
    back = SpGather(p, sums_ref, 32, more[8:12])
    for i in range(3):
        grads.first(i)
    for d in ORDER:
        total.send_z(d)

    vw[0] = jnp.zeros((8, 1024), f32)
    gains = jnp.zeros((1, 1024), f32)
    for w in range(8):
        base = tok_ref[w].astype(f32)
        gains = gains + jnp.sum(dn_ref[w].astype(f32) * base * rms_of(base), axis=0, keepdims=True)
    vw[0, 0:1] = gains
    vw[0, 1:2] = gn_ref[...]
    vw[0, 2:3] = gg_ref[...]

    def vec_round(buf, devices, sends, recvs):
        copies = []
        for i, device in enumerate(devices):
            copies.append(rcopy(buf.at[0], buf.at[i + 1], sends.at[i], recvs.at[i], device))
            copies[-1].start()
        return copies

    def vec_total(buf, copies):
        value = buf[0]
        for i, copy in enumerate(copies):
            copy.wait_recv()
            value = value + buf[i + 1]
        return value

    round1 = vec_round(vw, [p.along_z(d) for d in ORDER] + [p.along_z_other(d) for d in ORDER] + [p.sibling], vs1, vr1)
    for i in range(3):
        grads.second(i)
    base = tok_ref[p.wt].astype(f32)
    d_normed = total.own()
    gt_ref[p.wt] = (dmid_ref[...] + norm_back(base, rms_of(base), gain_ref[...], d_normed)).astype(bf16)
    spread = WtGather(p, gt_ref, (az, bz, ag, bg))
    spread.start()
    for i in range(3):
        for h in range(2):
            back.put(i, h, grads.own(i, h).astype(bf16))
            back.first(i, h)
    vx[0] = vec_total(vw, round1)
    round2 = vec_round(vx, [p.along_x(d) for d in ORDER], vs2, vr2)
    for i in range(3):
        for h in range(2):
            back.second(i, h)
    vy[0] = vec_total(vx, round2)
    round3 = vec_round(vy, [p.along_y(d) for d in ORDER], vs3, vr3)
    spread.forward()
    vec_ref[...] = vec_total(vy, round3)
    spread.arrived()
    spread.finish()
    total.finish()
    grads.finish()
    back.finish()
    for copy in round1 + round2 + round3:
        copy.wait_send()


WT_SEMS = [DMA((4,)), DMA((4,)), DMA((3,)), DMA((3,)), DMA((3,)), DMA((3,)), DMA((4,)), DMA((4,))]


def comm_call(kernel, number, out_shape, args, scratch, name, limit=10, first=None):
    return pl.pallas_call(
        kernel,
        out_shape=out_shape,
        in_specs=[first or vmem] + [vmem] * (len(args) - 1),
        out_specs=tuple(vmem for _ in out_shape),
        scratch_shapes=scratch,
        compiler_params=pltpu.CompilerParams(
            collective_id=number, has_side_effects=True, vmem_limit_bytes=limit << 20
        ),
        cost_estimate=pl.CostEstimate(flops=8 << 30, bytes_accessed=32 << 20, transcendentals=0),
        name=name,
    )(*args)


def gather_keys(lengths, q, kv):
    return comm_call(
        gather_kernel, 1,
        (sds((2, 256, 128), bf16), sds((4, 4, 2, 256, 128), bf16), sds((8192, 128), bf16)),
        (lengths, q.reshape(2, 256, 128), kv.reshape(2, 256, 128)),
        [DMA, DMA, DMA((2, 3)), DMA((2, 3)), DMA((2, 4, 3)), DMA((2, 4, 3))],
        "gather_keys", 4, smem,
    )


def scatter_keys(dkv, dq, mlp, mid):
    return comm_call(
        scatter_kernel, 2,
        (sds((2, 256, 128), bf16), sds((2, 256, 128), bf16), sds((8, 64, 1024), bf16)),
        (dkv.reshape(4, 4, 2, 256, 128), dq.reshape(2, 256, 128), mlp.reshape(8, 64, 1024), mid),
        [pltpu.VMEM((2, 3, 4, 256, 128), bf16), pltpu.VMEM((2, 3, 256, 128), bf16), pltpu.VMEM((2, 3, 256, 128), bf16),
         DMA, DMA, DMA((2, 3)), DMA((2, 3)), DMA((2, 3)), DMA((2, 3)),
         pltpu.VMEM((4, 64, 1024), bf16), pltpu.VMEM((3, 64, 1024), bf16), pltpu.VMEM((3, 64, 1024), bf16)] + WT_SEMS,
        "scatter_keys",
    )


def make_middle(mix, w_out, tokens, gain):
    rows = pltpu.VMEM
    return comm_call(
        middle_kernel, 3,
        (sds((8, 64, 1024), bf16), sds((64, 1024), f32), sds((2, 256, 128), bf16)),
        (mix.reshape(2, 256, 128), w_out, tokens.reshape(8, 64, 1024), gain.reshape(1, 1024)),
        [rows((8, 64, 1024), bf16), rows((4, 64, 1024), bf16), rows((3, 64, 1024), bf16), rows((3, 64, 1024), bf16),
         DMA, DMA, DMA((4,)), DMA((4,)), DMA((3,)), DMA((3,)), DMA((3,)), DMA((3,)), DMA((4,)), DMA((4,))],
        "make_middle",
    )


def turn_back(dm, mid, cot, gain, w_out, grads):
    rows = pltpu.VMEM
    return comm_call(
        turn_kernel, 4,
        (sds((8, 64, 1024), bf16), sds((64, 1024), f32), sds((1, 1024), f32),
         sds((2, 256, 128), bf16), sds((3, 2, 144, 128), bf16)),
        (dm.reshape(8, 64, 1024), mid, cot.reshape(8, 64, 1024), gain.reshape(1, 1024), w_out)
        + tuple(g.reshape(4, 144, 1024) for g in grads),
        [rows((256, 128), bf16), rows((4, 64, 1024), bf16), rows((3, 64, 1024), bf16), rows((3, 64, 1024), bf16),
         DMA, DMA] + WT_SEMS
        + SpScatter.scratch(3, 144),
        "turn_back", 16,
    )


def last_sums(dn, gq, go, tokens, dmid, gain, gn, gg):
    rows = pltpu.VMEM
    return comm_call(
        last_kernel, 5,
        (sds((8, 64, 1024), bf16), sds((3, 4, 32, 1024), bf16), sds((8, 1024), f32)),
        (dn.reshape(8, 64, 1024), gq.reshape(2, 4, 32, 1024), go.reshape(4, 32, 1024), tokens.reshape(8, 64, 1024),
         dmid, gain.reshape(1, 1024), gn, gg),
        [rows((4, 64, 1024), bf16), rows((3, 64, 1024), bf16), rows((3, 64, 1024), bf16),
         DMA((4,)), DMA((4,)), DMA((3,)), DMA((3,)), DMA((3,)), DMA((3,)), DMA((4,)), DMA((4,)),
         rows((8, 8, 1024), f32), rows((4, 8, 1024), f32), rows((4, 8, 1024), f32),
         DMA((7,)), DMA((7,)), DMA((3,)), DMA((3,)), DMA((3,)), DMA((3,))]
        + SpScatter.scratch(3, 32) + SpGather.sems(3),
        "last_sums", 10,
    )


def turned(value, lane):
    return jnp.where(lax.rem(lane, 64) < 32, pltpu.roll(value, 96, 1), pltpu.roll(value, 32, 1))


def head_sums(value, lane):
    s0 = jnp.sum(jnp.where(lane < 64, value, 0.0), axis=1, keepdims=True)
    s1 = jnp.sum(jnp.where(lane < 64, 0.0, value), axis=1, keepdims=True)
    return jnp.where(lane < 64, s0, s1)


def twice(gain):
    return jnp.concatenate([gain, gain], axis=1)


def nt(a, b):
    return lax.dot_general(a, b, (((1,), (1,)), ((), ())), preferred_element_type=f32)


def tn(a, b):
    return lax.dot_general(a, b, (((0,), (0,)), ((), ())), preferred_element_type=f32)


def proj_kernel(len_ref, tok_ref, gain_ref, wq_ref, wk_ref, wv_ref, qg_ref, kg_ref, freq_ref,
                n_ref, qp_ref, kvp_ref, q_ref, kv_ref, cos_ref, sin_ref):
    lane = lanes((512, 128))
    ids = lax.axis_index("sp") * 512 + lax.broadcasted_iota(jnp.int32, (1, 512), 1)
    positions = (ids - starts_of(ids, len_ref)).astype(f32)
    angles = positions * freq_ref[:, 0:1]
    cosine, sine = jnp.cos(angles), jnp.sin(angles)
    cosine = jnp.concatenate([cosine] * 4, axis=0).T
    sine = jnp.concatenate([-sine, sine, -sine, sine], axis=0).T
    cos_ref[...] = cosine
    sin_ref[...] = sine
    base = tok_ref[...].astype(f32)
    normed = (base * rms_of(base) * gain_ref[...]).astype(bf16)
    n_ref[...] = normed
    wkv = jnp.concatenate([wk_ref[...], wv_ref[...]], axis=0)
    q = jnp.dot(normed, wq_ref[...], preferred_element_type=f32)
    qp_ref[...] = q
    q = q * lax.rsqrt(head_sums(q * q, lane) * (1.0 / 64) + eps) * twice(qg_ref[...])
    q_ref[...] = (q * cosine + turned(q, lane) * sine).astype(bf16)
    kv = nt(normed, wkv)
    kvp_ref[...] = kv
    k = kv * lax.rsqrt(head_sums(kv * kv, lane) * (1.0 / 64) + eps) * twice(kg_ref[...])
    k = k * cosine + turned(k, lane) * sine
    kv_ref[...] = jnp.where(lane < 64, k, kv).astype(bf16)


def proj_back_kernel(dq_ref, dkv_ref, qp_ref, kvp_ref, n_ref, wq_ref, wk_ref, wv_ref, qg_ref, kg_ref, cos_ref, sin_ref, dn_ref, g_ref, gg_ref):
    lane = lanes((512, 128))
    cosine, sine = cos_ref[...], sin_ref[...]

    def back(grad, proj, gain):
        grad = grad * cosine - turned(grad, lane) * sine
        scale = lax.rsqrt(head_sums(proj * proj, lane) * (1.0 / 64) + eps)
        scaled = grad * gain
        inner = head_sums(scaled * proj, lane) * (1.0 / 64)
        gains = jnp.sum(grad * proj * scale, axis=0, keepdims=True)
        return scale * scaled - proj * scale * scale * scale * inner, gains

    dq, gq = back(dq_ref[...].astype(f32), qp_ref[...], twice(qg_ref[...]))
    dkv_in = dkv_ref[...].astype(f32)
    dk, gk = back(dkv_in, kvp_ref[...], twice(kg_ref[...]))
    dq = dq.astype(bf16)
    dkv = jnp.where(lane < 64, dk, dkv_in).astype(bf16)
    wkv = jnp.concatenate([wk_ref[...], wv_ref[...]], axis=0)
    dn_ref[...] = (nt(dq, wq_ref[...]) + jnp.dot(dkv, wkv, preferred_element_type=f32)).astype(bf16)
    normed = n_ref[...]
    g_ref[0] = tn(dq, normed).astype(bf16)
    g_ref[1] = tn(dkv, normed).astype(bf16)
    gg_ref[...] = jnp.concatenate([gq, gk, jnp.zeros((1, 768), f32)], axis=1)


def local_call(kernel, out_shape, args, name, first=None):
    return pl.pallas_call(
        kernel,
        out_shape=out_shape,
        in_specs=[first or vmem] + [vmem] * (len(args) - 1),
        out_specs=tuple(vmem for _ in out_shape),
        compiler_params=pltpu.CompilerParams(vmem_limit_bytes=16 << 20),
        cost_estimate=pl.CostEstimate(flops=3 << 30, bytes_accessed=16 << 20, transcendentals=0),
        name=name,
    )(*args)


def finish_kernel(sums_ref, ff_ref, out_in, gt_in, vec_ref, out_ref, gt_ref, gq_ref, gk_ref, gv_ref, go_ref, gg_ref, gu_ref, gd_ref,
                  ni_ref, nm_ref, qg_ref, kg_ref, wide, tall, big, sems):
    copies = []

    def write(src, dst):
        copies.append(pltpu.make_async_copy(src, dst, sems.at[len(copies)]))
        copies[-1].start()

    write(out_in, out_ref)
    write(gt_in, gt_ref)
    for i, ref in enumerate((gg_ref, gu_ref, gd_ref)):
        for part in range(2):
            rows = pl.ds(part * 288, 288)
            big[i, rows, :] = ff_ref[i, rows, :].astype(f32)
            write(big.at[i, rows], ref.at[rows])
    wide[...] = sums_ref[1:3].astype(f32)
    write(wide.at[0, 0:64], gk_ref)
    write(wide.at[0, 64:128], gv_ref)
    write(wide.at[1], go_ref)
    tall[...] = sums_ref[0].astype(f32).T
    write(tall, gq_ref)
    ni_ref[...] = vec_ref[0:1, :]
    nm_ref[...] = vec_ref[1:2, :]
    qg_ref[...] = vec_ref[2:3, 0:64] + vec_ref[2:3, 64:128]
    kg_ref[...] = vec_ref[2:3, 128:192]
    for copy in copies:
        copy.wait()


def finish(sums, ff, output, grad_tokens, vec):
    hbm = pl.BlockSpec(memory_space=pl.ANY)
    rows = sds((576, 1024), f32)
    return pl.pallas_call(
        finish_kernel,
        out_shape=(sds((512, 1024), bf16), sds((512, 1024), bf16), sds((1024, 128), f32), sds((64, 1024), f32), sds((64, 1024), f32),
                   sds((128, 1024), f32), rows, rows, rows,
                   sds((1, 1024), f32), sds((1, 1024), f32), sds((1, 64), f32), sds((1, 64), f32)),
        in_specs=[vmem] * 5,
        out_specs=tuple([hbm] * 9 + [vmem] * 4),
        scratch_shapes=[pltpu.VMEM((2, 128, 1024), f32), pltpu.VMEM((1024, 128), f32), pltpu.VMEM((3, 576, 1024), f32), DMA((12,))],
        compiler_params=pltpu.CompilerParams(vmem_limit_bytes=14 << 20),
        name="finish",
    )(sums, ff, output, grad_tokens, vec)


theta = 1000000.0


def body(tokens, norm_in, w_query, w_key, w_value, query_gain, key_gain, w_out, norm_mid, w_gate, w_up, w_down, cotangent, lengths):
    parts = lax.axis_size("sp")
    freqs = theta ** (-(np.arange(32).astype(np.float64) * 2.0) / 64)
    freqs = jnp.asarray(np.broadcast_to(freqs.astype(np.float32)[:, None], (32, 128)))
    qg, kg = query_gain.reshape(1, 64), key_gain.reshape(1, 64)
    wk, wv = w_key.T, w_value.T
    wide = sds((512, 128), f32)

    normed, q_proj, kv_proj, q, kv, cosine, sine = local_call(
        proj_kernel,
        (sds((512, 1024), bf16), wide, wide, sds((512, 128), bf16), sds((512, 128), bf16), wide, wide),
        (lengths, tokens, norm_in.reshape(1, 1024), w_query, wk, wv, qg, kg, freqs),
        "project", smem,
    )
    qz, kv_all, ext = gather_keys(lengths, q, kv)
    kv_all = kv_all.reshape(8192, 128)
    mix_z, mix_f, qa = attend(parts, lengths, qz.reshape(512, 128), kv_all, ext)
    normed_mid, mid_own, mixed = make_middle(mix_z, w_out, tokens, norm_mid)
    normed_mid = normed_mid.reshape(512, 1024)
    mixed = mixed.reshape(512, 128)

    gate = jnp.dot(normed_mid, w_gate, preferred_element_type=f32)
    up_proj = jnp.dot(normed_mid, w_up, preferred_element_type=f32)
    sigmoid_gate = jax.nn.sigmoid(gate)
    act = (gate * sigmoid_gate * up_proj).astype(bf16)
    mlp_part = jnp.dot(act, w_down, preferred_element_type=f32).astype(bf16)
    d_act = jnp.einsum("td,fd->tf", cotangent, w_down, preferred_element_type=f32)
    d_gate = (d_act * up_proj * sigmoid_gate * (1.0 + gate * (1.0 - sigmoid_gate))).astype(bf16)
    d_up = (d_act * gate * sigmoid_gate).astype(bf16)
    d_mid_part = (
        jnp.einsum("tf,df->td", d_gate, w_gate, preferred_element_type=f32)
        + jnp.einsum("tf,df->td", d_up, w_up, preferred_element_type=f32)
    ).astype(bf16)
    grads = (
        jnp.einsum("tf,td->fd", d_gate, normed_mid, preferred_element_type=f32).astype(bf16),
        jnp.einsum("tf,td->fd", d_up, normed_mid, preferred_element_type=f32).astype(bf16),
        jnp.einsum("tf,td->fd", act, cotangent, preferred_element_type=f32).astype(bf16),
    )
    d_attn, d_middle_own, gn, d_mix_z, red = turn_back(
        d_mid_part, mid_own, cotangent, norm_mid, w_out, grads
    )
    g_out = jnp.einsum("tq,td->qd", mixed, d_attn.reshape(512, 1024), preferred_element_type=f32).astype(bf16)
    dq_z, dkv_all, g_ff = attend_back(parts, qa, mix_f, d_mix_z.reshape(512, 128), kv_all, ext, red)
    dkv, dq, output = scatter_keys(dkv_all, dq_z, mlp_part, mid_own)
    dn_part, g_qkv, gg = local_call(
        proj_back_kernel,
        (sds((512, 1024), bf16), sds((2, 128, 1024), bf16), sds((1, 1024), f32)),
        (dq.reshape(512, 128), dkv.reshape(512, 128), q_proj, kv_proj, normed, w_query, wk, wv, qg, kg, cosine, sine),
        "project_back",
    )
    grad_tokens, sums, vec = last_sums(dn_part, g_qkv, g_out, tokens, d_middle_own, norm_in, gn, gg)
    (output, grad_tokens, g_query, g_key, g_value, g_out, g_gate, g_up, g_down, g_norm_in, g_norm_mid, g_qg, g_kg) = finish(
        sums.reshape(3, 128, 1024), g_ff.reshape(3, 576, 1024), output.reshape(512, 1024), grad_tokens.reshape(512, 1024), vec
    )
    return (
        output, grad_tokens, g_norm_in.reshape(1024), g_query, g_key.T, g_value.T, g_qg.reshape(64), g_kg.reshape(64),
        g_out, g_norm_mid.reshape(1024), g_gate.T, g_up.T, g_down,
    )


def solution(mesh):
    placed = (
        P("sp", None), P(), P(None, "wt"), P(None, "wt"), P(None, "wt"), P(), P(), P("wt", None), P(),
        P(None, "wt"), P(None, "wt"), P("wt", None), P("sp", None), P(),
    )
    return jax.shard_map(
        body,
        mesh=mesh,
        in_specs=placed,
        out_specs=(
            P("sp", None), P("sp", None), P(), P(None, "wt"), P(None, "wt"), P(None, "wt"), P(), P(),
            P("wt", None), P(), P(None, "wt"), P(None, "wt"), P("wt", None),
        ),
        check_vma=False,
    )
```

```python
import functools, math
import jax
import jax.numpy as jnp
import numpy as np
from jax import lax
from jax.experimental import pallas as pl
from jax.experimental.pallas import tpu as pltpu
from jax.sharding import PartitionSpec as P

f32 = jnp.float32
bf16 = jnp.bfloat16
sds = jax.ShapeDtypeStruct
DMA = pltpu.SemaphoreType.DMA
CH = 512
HALF = 256
SCALE = 0.125
C2 = SCALE * math.log2(math.e)


def starts_of(ids, len_ref):
    end = jnp.int32(0)
    start = jnp.zeros_like(ids)
    for j in range(4):
        end = end + len_ref[j]
        start = start + jnp.where(ids >= end, len_ref[j], 0)
    return start


def scalar_start(row, len_ref):
    end = jnp.int32(0)
    start = jnp.int32(0)
    for j in range(4):
        end = end + len_ref[j]
        start = start + jnp.where(row >= end, len_ref[j], 0)
    return start


def lanes(shape):
    return lax.broadcasted_iota(jnp.int32, shape, len(shape) - 1)


def split3(value, lane):
    hi = value.astype(bf16).astype(f32)
    rest = value - hi
    mid = rest.astype(bf16).astype(f32)
    low = rest - mid
    return jnp.where(lane == 0, hi, jnp.where(lane == 1, mid, jnp.where(lane == 2, low, 0.0)))


def tile_row(me, t, parts):
    return me * 512 if t == 0 else (parts - 1 - me) * 512 + HALF


FAR = 8192.0


def segment_bounds(len_ref, lane):
    begin = jnp.zeros_like(lane)
    end = jnp.zeros_like(lane)
    at = jnp.int32(0)
    for j in range(4):
        begin = jnp.where(lane == 3 + j, at, begin)
        at = at + len_ref[j]
        end = jnp.where(lane == 3 + j, at, end)
    return begin, end


def inside(ids, len_ref, shape):
    lane = lanes(shape)
    begin, end = segment_bounds(len_ref, lane)
    return (ids >= begin) & (ids < end), lane


def key_columns(k0, len_ref, rows):
    ids = k0 + lax.broadcasted_iota(jnp.int32, (rows, 128), 0)
    within, lane = inside(ids, len_ref, (rows, 128))
    return jnp.where(lane < 3, 1.0, jnp.where(within, 1.0, 0.0)).astype(bf16)


def query_columns(r0, len_ref, rows):
    ids = r0 + lax.broadcasted_iota(jnp.int32, (rows, 128), 0)
    within, lane = inside(ids, len_ref, (rows, 128))
    return jnp.where((lane < 3) | (lane > 6) | within, 0.0, -FAR)


def fwd_kernel(parts, len_ref, q_ref, kv_ref, ext_ref, mix_ref, out_ref, qa_ref, acc_ref):
    me = lax.axis_index("sp")
    lane = lanes((HALF, 128))
    lane2 = lanes((2 * HALF, 128))
    lanek = lanes((CH, 128))
    for t in range(2):
        r0 = tile_row(me, t, parts)
        q = q_ref[t * HALF:(t + 1) * HALF, :].astype(f32)
        qa_ref[t, 0:HALF, 0:128] = jnp.where(lane < 64, q, 0.0).astype(bf16)
        qa_ref[t, HALF:, 0:128] = jnp.where(lane < 64, pltpu.roll(q, 64, 1), 0.0).astype(bf16)
        columns = query_columns(r0, len_ref, HALF)
        columns = jnp.concatenate([columns, columns], axis=0)
        qa_ref[t, :, 128:256] = columns.astype(bf16)
        acc_ref[...] = jnp.zeros_like(acc_ref)

        def step(c, masked):
            k0 = pl.multiple_of(c * CH, CH)
            kv = kv_ref[pl.ds(k0, CH), :]
            kva = jnp.concatenate([kv, ext_ref[pl.ds(k0, CH), :]], axis=1)
            s = lax.dot_general(qa_ref[t], kva, (((1,), (1,)), ((), ())), preferred_element_type=f32)
            p = jnp.exp2(s * C2)
            if masked:
                rows = r0 + lax.rem(lax.broadcasted_iota(jnp.int32, (2 * HALF, 1), 0), HALF)
                keys = k0 + lax.broadcasted_iota(jnp.int32, (2 * HALF, CH), 1)
                p = jnp.where(keys <= rows, p, 0.0)
            ones = jnp.where(lanek < 64, jnp.ones_like(kv), kv)
            acc_ref[...] += jnp.dot(p.astype(bf16), ones, preferred_element_type=f32)

        block = me if t == 0 else parts - 1 - me
        pl.loop(0, block)(lambda c: step(c, False))
        step(block, True)

        acc = acc_ref[...]
        swapped = pltpu.roll(acc, 64, 1)
        o = swapped / acc
        m = jnp.where(lane < 64, o[:HALF], pltpu.roll(o[HALF:], 64, 1))
        mix_ref[t * HALF:(t + 1) * HALF, :] = m.astype(bf16)
        out_ref[t * HALF:(t + 1) * HALF, :] = m
        total = jnp.where(lane2 < 64, acc, swapped)
        qa_ref[t, :, 128:256] = (split3(jnp.log(total) * (-1.0 / SCALE), lane2) + columns).astype(bf16)


smem = pl.BlockSpec(memory_space=pltpu.SMEM)
vmem = pl.BlockSpec(memory_space=pltpu.VMEM)


def attend(parts, lengths, q, kv, ext):
    rows = 2 * HALF
    return pl.pallas_call(
        functools.partial(fwd_kernel, parts),
        out_shape=(sds((rows, 128), bf16), sds((rows, 128), f32), sds((2, rows, 256), bf16)),
        in_specs=[smem, vmem, vmem, vmem],
        out_specs=(vmem, vmem, vmem),
        scratch_shapes=[pltpu.VMEM((rows, 128), f32)],
        compiler_params=pltpu.CompilerParams(vmem_limit_bytes=12 << 20),
        cost_estimate=pl.CostEstimate(flops=3 << 30, bytes_accessed=4 << 20, transcendentals=5 << 20),
        name="attend",
    )(lengths, q, kv, ext)


MESH = pl.DeviceIdType.MESH
eps = 1e-05


def rcopy(src, dst, send, recv, device):
    return pltpu.make_async_remote_copy(
        src_ref=src, dst_ref=dst, send_sem=send, recv_sem=recv, device_id=device, device_id_type=MESH
    )


def meet(devices):
    barrier = pltpu.get_barrier_semaphore()
    for device in devices:
        pl.semaphore_signal(barrier, inc=1, device_id=device, device_id_type=MESH)
    pl.semaphore_wait(barrier, len(devices))


class Place:
    def __init__(self):
        self.sp = lax.axis_index("sp")
        self.wt = lax.axis_index("wt")
        self.x, self.y = lax.div(self.sp, 4), lax.rem(self.sp, 4)
        self.z, self.c = lax.div(self.wt, 2), lax.rem(self.wt, 2)
        self.mirror = (15 - self.sp, self.wt)
        self.sibling = (self.sp, self.z * 2 + 1 - self.c)

    def along_x(self, d):
        return (lax.rem(self.x + d, 4) * 4 + self.y, self.wt)

    def along_y(self, d):
        return (self.x * 4 + lax.rem(self.y + d, 4), self.wt)

    def along_z(self, d):
        return (self.sp, lax.rem(self.z + d, 4) * 2 + self.c)

    def along_z_other(self, d):
        return (self.sp, lax.rem(self.z + d, 4) * 2 + 1 - self.c)

    def first(self, h, d):
        return self.along_x(d) if h == 0 else self.along_y(d)

    def second(self, h, d):
        return self.along_y(d) if h == 0 else self.along_x(d)

    def fsp(self, h):
        return self.x if h == 0 else self.y

    def ssp(self, h):
        return self.y if h == 0 else self.x


def spot(h, first, second):
    return (first, second) if h == 0 else (second, first)


ORDER = (2, 1, 3)


def gather_kernel(len_ref, q_ref, kv_ref, qz_ref, all_ref, ext_ref, ms, mr, fs, fr, ss, sr):
    p = Place()
    meet([p.along_x(d) for d in ORDER] + [p.along_y(d) for d in ORDER] + [p.mirror])
    all_ref[p.x, p.y] = kv_ref[...]
    mirror = rcopy(q_ref.at[1], qz_ref.at[1], ms, mr, p.mirror)
    first, second = {}, {}
    for d in ORDER:
        for h in range(2):
            first[h, d] = rcopy(
                kv_ref.at[h], all_ref.at[p.x, p.y, h], fs.at[h, d - 1], fr.at[h, d - 1], p.first(h, d)
            )
            first[h, d].start()
    mirror.start()

    def forward(h, slot):
        a = lax.rem(p.fsp(h) + 4 - slot, 4)
        at = spot(h, a, p.ssp(h))
        for e in ORDER:
            src = kv_ref.at[h] if slot == 0 else all_ref.at[at[0], at[1], h]
            second[h, slot, e] = rcopy(
                src, all_ref.at[at[0], at[1], h], ss.at[h, slot, e - 1], sr.at[h, slot, e - 1], p.second(h, e)
            )
            second[h, slot, e].start()

    for h in range(2):
        forward(h, 0)
    qz_ref[0] = q_ref[0]
    @pl.loop(0, 8)
    def _(b):
        rows = pl.ds(pl.multiple_of(b * 1024, 1024), 1024)
        ext_ref[rows, :] = key_columns(b * 1024, len_ref, 1024)

    for d in (1, 3, 2):
        for h in range(2):
            first[h, d].wait_recv()
            forward(h, d)
    mirror.wait()
    for copy in first.values():
        copy.wait_send()
    for copy in second.values():
        copy.wait()


class SpScatter:
    def __init__(self, p, srcs, rows, refs):
        self.p, self.srcs, self.rows = p, srcs, rows
        self.ra, self.rb, self.send, self.r2, self.fs, self.fr, self.ss, self.sr = refs
        self.one, self.two = {}, {}

    @staticmethod
    def scratch(n, rows):
        return [
            pltpu.VMEM((n, 3, rows, 512), bf16), pltpu.VMEM((n, 3, 4, rows, 128), bf16),
            pltpu.VMEM((n, 2, 3, rows, 128), bf16), pltpu.VMEM((n, 2, 3, rows, 128), bf16),
            DMA((n, 2, 3)), DMA((n, 2, 3)), DMA((n, 2, 3)), DMA((n, 2, 3)),
        ]

    def first(self, i):
        p = self.p
        for d in ORDER:
            to = lax.rem(p.x + d, 4)
            self.one[i, 0, d] = rcopy(
                self.srcs[i].at[to, :, pl.ds(0, 512)], self.ra.at[i, d - 1],
                self.fs.at[i, 0, d - 1], self.fr.at[i, 0, d - 1], p.along_x(d),
            )
            self.one[i, 0, d].start()
            to = lax.rem(p.y + d, 4)
            self.one[i, 1, d] = rcopy(
                self.srcs[i].at[:, :, pl.ds(columns_at(1, to), 128)], self.rb.at[i, d - 1],
                self.fs.at[i, 1, d - 1], self.fr.at[i, 1, d - 1], p.along_y(d),
            )
            self.one[i, 1, d].start()

    def part(self, i, h, b):
        p = self.p
        if h == 0:
            value = self.srcs[i][p.x, :, pl.ds(columns_at(0, b), 128)].astype(f32)
            for d in range(3):
                value = value + self.ra[i, d, :, pl.ds(columns_at(0, b), 128)].astype(f32)
            return value
        value = self.srcs[i][b, :, pl.ds(columns_at(1, p.y), 128)].astype(f32)
        for d in range(3):
            value = value + self.rb[i, d, b].astype(f32)
        return value

    def second(self, i):
        p = self.p
        for h in range(2):
            for d in ORDER:
                self.one[i, h, d].wait_recv()
            for e in ORDER:
                self.send[i, h, e - 1] = self.part(i, h, lax.rem(p.ssp(h) + e, 4)).astype(bf16)
                self.two[i, h, e] = rcopy(
                    self.send.at[i, h, e - 1], self.r2.at[i, h, e - 1],
                    self.ss.at[i, h, e - 1], self.sr.at[i, h, e - 1], p.second(h, e),
                )
                self.two[i, h, e].start()

    def own(self, i, h):
        value = self.part(i, h, self.p.ssp(h))
        for e in ORDER:
            self.two[i, h, e].wait_recv()
            value = value + self.r2[i, h, e - 1].astype(f32)
        return value

    def finish(self):
        for copy in list(self.one.values()) + list(self.two.values()):
            copy.wait_send()


def columns_at(h, b):
    return pl.multiple_of(h * 512 + b * 128, 128)


class SpGather:
    def __init__(self, p, out, rows, sems):
        self.p, self.out, self.rows = p, out, rows
        self.fs, self.fr, self.ss, self.sr = sems
        self.one, self.two = {}, {}

    @staticmethod
    def sems(n):
        return [DMA((n, 2, 3)) for _ in range(4)]

    def spot(self, h):
        p = self.p
        return p.x, pl.ds(columns_at(h, p.y), 128)

    def put(self, i, h, value):
        x, columns = self.spot(h)
        self.out[i, x, :, columns] = value

    def first(self, i, h):
        x, columns = self.spot(h)
        block = self.out.at[i, x, :, columns]
        for e in ORDER:
            self.one[i, h, e] = rcopy(
                block, block, self.fs.at[i, h, e - 1], self.fr.at[i, h, e - 1], self.p.second(h, e)
            )
            self.one[i, h, e].start()

    def second(self, i, h):
        x, columns = self.spot(h)
        for e in ORDER:
            self.one[i, h, e].wait_recv()
        block = self.out.at[i, x, :, pl.ds(0, 512)] if h == 0 else self.out.at[i, :, :, columns]
        for d in ORDER:
            self.two[i, h, d] = rcopy(
                block, block, self.ss.at[i, h, d - 1], self.sr.at[i, h, d - 1], self.p.first(h, d)
            )
            self.two[i, h, d].start()

    def arrived(self, i):
        for h in range(2):
            for d in ORDER:
                self.two[i, h, d].wait_recv()

    def finish(self):
        for copy in self.one.values():
            copy.wait_send()
        for copy in self.two.values():
            copy.wait()


class WtSum:
    def __init__(self, p, part, sib, send, rz, sems):
        self.p, self.part, self.sib, self.send, self.rz = p, part, sib, send, rz
        self.cs, self.cr, self.zs, self.zr = sems
        self.second = {}

    def core(self, zz):
        return rcopy(
            self.part.at[zz * 2 + 1 - self.p.c], self.sib.at[zz], self.cs.at[zz], self.cr.at[zz], self.p.sibling
        )

    def start_core(self, zz):
        self.core(zz).start()

    def pair(self, zz):
        return self.part[zz * 2 + self.p.c].astype(f32) + self.sib[zz].astype(f32)

    def send_z(self, d):
        zz = lax.rem(self.p.z + d, 4)
        self.core(zz).wait_recv()
        self.send[d - 1] = self.pair(zz).astype(bf16)
        copy = rcopy(
            self.send.at[d - 1], self.rz.at[d - 1], self.zs.at[d - 1], self.zr.at[d - 1], self.p.along_z(d)
        )
        copy.start()
        self.second[d] = copy

    def own(self):
        self.core(self.p.z).wait_recv()
        value = self.pair(self.p.z)
        for d in (1, 3, 2):
            self.second[d].wait_recv()
            value = value + self.rz[d - 1].astype(f32)
        return value

    def finish(self):
        for zz in range(4):
            self.core(zz).wait_send()
        for copy in self.second.values():
            copy.wait_send()


class WtGather:
    def __init__(self, p, out, sems):
        self.p, self.out = p, out
        self.zs, self.zr, self.gs, self.gr = sems
        self.far, self.near = {}, {}

    def start(self):
        p = self.p
        for d in ORDER:
            self.far[d] = rcopy(
                self.out.at[p.wt], self.out.at[p.wt], self.zs.at[d - 1], self.zr.at[d - 1], p.along_z(d)
            )
            self.far[d].start()
        self.pass_on(0)

    def pass_on(self, slot):
        p = self.p
        row = lax.rem(p.z + 4 - slot, 4) * 2 + p.c
        self.near[slot] = rcopy(
            self.out.at[row], self.out.at[row], self.gs.at[slot], self.gr.at[slot], p.sibling
        )
        self.near[slot].start()

    def forward(self):
        for d in (1, 3, 2):
            self.far[d].wait_recv()
            self.pass_on(d)

    def arrived(self):
        for slot in (0, 1, 3, 2):
            self.near[slot].wait_recv()

    def finish(self):
        for copy in list(self.far.values()) + list(self.near.values()):
            copy.wait_send()


def rms_of(value):
    return lax.rsqrt(jnp.mean(value * value, axis=-1, keepdims=True) + eps)


def norm_back(values, scale, gain, grad):
    scaled = grad * gain
    inner = jnp.mean(scaled * values, axis=-1, keepdims=True)
    return scale * scaled - values * scale * scale * scale * inner


def wt_peers(p):
    return [p.sibling] + [p.along_z(d) for d in ORDER]


def middle_kernel(mix_ref, w_ref, tok_ref, gain_ref, nm_ref, mid_ref, mixo_ref, part, sib, send, rz, ms, mr, cs, cr, zs, zr, az, bz, ag, bg):
    p = Place()
    meet(wt_peers(p) + [p.mirror])
    mirror = rcopy(mix_ref.at[1], mixo_ref.at[1], ms, mr, p.mirror)
    mirror.start()
    mixo_ref[0] = mix_ref[0]
    total = WtSum(p, part, sib, send, rz, (cs, cr, zs, zr))
    for half in range(2):
        if half == 1:
            mirror.wait()
        both = jnp.dot(mixo_ref[half], w_ref[...], preferred_element_type=f32).astype(bf16)
        part[half * 4:half * 4 + 4] = both.reshape(4, 64, 1024)
        for zz in (half * 2, half * 2 + 1):
            total.start_core(zz)
    for d in ORDER:
        total.send_z(d)
    middle = tok_ref[p.wt].astype(f32) + total.own()
    mid_ref[...] = middle
    nm_ref[p.wt] = (middle * rms_of(middle) * gain_ref[...]).astype(bf16)
    spread = WtGather(p, nm_ref, (az, bz, ag, bg))
    spread.start()
    spread.forward()
    spread.arrived()
    spread.finish()
    total.finish()


WT_SEMS = [DMA((4,)), DMA((4,)), DMA((3,)), DMA((3,)), DMA((3,)), DMA((3,)), DMA((4,)), DMA((4,))]


def comm_call(kernel, number, out_shape, args, scratch, name, limit=10, first=None):
    return pl.pallas_call(
        kernel,
        out_shape=out_shape,
        in_specs=[first or vmem] + [vmem] * (len(args) - 1),
        out_specs=tuple(vmem for _ in out_shape),
        scratch_shapes=scratch,
        compiler_params=pltpu.CompilerParams(
            collective_id=number, has_side_effects=True, vmem_limit_bytes=limit << 20
        ),
        cost_estimate=pl.CostEstimate(flops=8 << 30, bytes_accessed=32 << 20, transcendentals=0),
        name=name,
    )(*args)


def gather_keys(lengths, q, kv):
    return comm_call(
        gather_kernel, 1,
        (sds((2, 256, 128), bf16), sds((4, 4, 2, 256, 128), bf16), sds((8192, 128), bf16)),
        (lengths, q.reshape(2, 256, 128), kv.reshape(2, 256, 128)),
        [DMA, DMA, DMA((2, 3)), DMA((2, 3)), DMA((2, 4, 3)), DMA((2, 4, 3))],
        "gather_keys", 4, smem,
    )


def make_middle(mix, w_out, tokens, gain):
    rows = pltpu.VMEM
    return comm_call(
        middle_kernel, 3,
        (sds((8, 64, 1024), bf16), sds((64, 1024), f32), sds((2, 256, 128), bf16)),
        (mix.reshape(2, 256, 128), w_out, tokens.reshape(8, 64, 1024), gain.reshape(1, 1024)),
        [rows((8, 64, 1024), bf16), rows((4, 64, 1024), bf16), rows((3, 64, 1024), bf16), rows((3, 64, 1024), bf16),
         DMA, DMA, DMA((4,)), DMA((4,)), DMA((3,)), DMA((3,)), DMA((3,)), DMA((3,)), DMA((4,)), DMA((4,))],
        "make_middle",
    )


def turned(value, lane):
    return jnp.where(lax.rem(lane, 64) < 32, pltpu.roll(value, 96, 1), pltpu.roll(value, 32, 1))


def head_sums(value, lane):
    s0 = jnp.sum(jnp.where(lane < 64, value, 0.0), axis=1, keepdims=True)
    s1 = jnp.sum(jnp.where(lane < 64, 0.0, value), axis=1, keepdims=True)
    return jnp.where(lane < 64, s0, s1)


def twice(gain):
    return jnp.concatenate([gain, gain], axis=1)


def nt(a, b):
    return lax.dot_general(a, b, (((1,), (1,)), ((), ())), preferred_element_type=f32)


def tn(a, b):
    return lax.dot_general(a, b, (((0,), (0,)), ((), ())), preferred_element_type=f32)


def proj_kernel(len_ref, tok_ref, gain_ref, wq_ref, wk_ref, wv_ref, qg_ref, kg_ref, freq_ref,
                n_ref, qp_ref, kvp_ref, q_ref, kv_ref, cos_ref, sin_ref):
    lane = lanes((512, 128))
    ids = lax.axis_index("sp") * 512 + lax.broadcasted_iota(jnp.int32, (1, 512), 1)
    positions = (ids - starts_of(ids, len_ref)).astype(f32)
    angles = positions * freq_ref[:, 0:1]
    cosine, sine = jnp.cos(angles), jnp.sin(angles)
    cosine = jnp.concatenate([cosine] * 4, axis=0).T
    sine = jnp.concatenate([-sine, sine, -sine, sine], axis=0).T
    cos_ref[...] = cosine
    sin_ref[...] = sine
    base = tok_ref[...].astype(f32)
    normed = (base * rms_of(base) * gain_ref[...]).astype(bf16)
    n_ref[...] = normed
    wkv = jnp.concatenate([wk_ref[...], wv_ref[...]], axis=0)
    q = jnp.dot(normed, wq_ref[...], preferred_element_type=f32)
    qp_ref[...] = q
    q = q * lax.rsqrt(head_sums(q * q, lane) * (1.0 / 64) + eps) * twice(qg_ref[...])
    q_ref[...] = (q * cosine + turned(q, lane) * sine).astype(bf16)
    kv = nt(normed, wkv)
    kvp_ref[...] = kv
    k = kv * lax.rsqrt(head_sums(kv * kv, lane) * (1.0 / 64) + eps) * twice(kg_ref[...])
    k = k * cosine + turned(k, lane) * sine
    kv_ref[...] = jnp.where(lane < 64, k, kv).astype(bf16)


def local_call(kernel, out_shape, args, name, first=None):
    return pl.pallas_call(
        kernel,
        out_shape=out_shape,
        in_specs=[first or vmem] + [vmem] * (len(args) - 1),
        out_specs=tuple(vmem for _ in out_shape),
        compiler_params=pltpu.CompilerParams(vmem_limit_bytes=16 << 20),
        cost_estimate=pl.CostEstimate(flops=3 << 30, bytes_accessed=16 << 20, transcendentals=0),
        name=name,
    )(*args)


class Flow:
    def __init__(self):
        self.copies = []

    def send(self, *args):
        copy = rcopy(*args)
        copy.start()
        self.copies.append(copy)
        return copy

    def finish(self):
        for copy in self.copies:
            copy.wait_send()


def backward_kernel(
    parts,
    dm_ref, mlp_ref, mid_ref, cot_ref, gain_ref, w_ref, g0_ref, g1_ref, g2_ref,
    qa_ref, mixf_ref, kv_ref, ext_ref, mixed_ref,
    qp_ref, kvp_ref, n_ref, wq_ref, wk_ref, wv_ref, qg_ref, kg_ref, cos_ref, sin_ref, tok_ref, gain_in_ref,
    out_ref, gt_ref, sums_ref, ff_ref, vec_ref,
    *scratch,
):
    scratch = list(scratch)

    def take(n):
        got = scratch[:n]
        del scratch[:n]
        return got

    p = Place()
    me = p.sp
    meet(
        wt_peers(p) + [p.along_z_other(d) for d in ORDER] + [p.mirror]
        + [p.along_x(d) for d in ORDER] + [p.along_y(d) for d in ORDER]
    )
    flow = Flow()

    def wt_sum(ref):
        sib, send, rz = take(3)
        return WtSum(p, ref, sib, send, rz, take(4))

    da, da_up, dz = take(3)
    mirror_sems = take(4)
    d_mid_sum = wt_sum(dm_ref)
    da_gather = WtGather(p, da, take(4))
    mlp_sum = wt_sum(mlp_ref)
    out_gather = WtGather(p, out_ref, take(4))
    ff = SpScatter(p, (g0_ref, g1_ref, g2_ref), 144, take(8))
    ff_back = SpGather(p, ff_ref, 144, take(4))
    dab, acc, dqt, dqz, dq, dkv, dkv_own = take(7)
    r1, send1, r2, fs, fr, ss, sr = take(7)
    dn, gqkv, gout = take(3)
    dn_sum = wt_sum(dn)
    gt_gather = WtGather(p, gt_ref, take(4))
    sums = SpScatter(p, (gout, gqkv.at[0], gqkv.at[1]), 32, take(8))
    sums_back = SpGather(p, sums_ref, 32, take(4))
    vw, vx, vy, vs1, vr1, vs2, vr2, vs3, vr3 = take(9)
    assert not scratch

    for zz in range(4):
        d_mid_sum.start_core(zz)
    ff.first(0)
    ff.first(1)
    for d in ORDER:
        d_mid_sum.send_z(d)
    for zz in range(4):
        mlp_sum.start_core(zz)
    middle = mid_ref[...]
    scale = rms_of(middle)
    d_mid = d_mid_sum.own()
    d_middle = cot_ref[p.wt].astype(f32) + norm_back(middle, scale, gain_ref[...], d_mid)
    da[p.wt] = d_middle.astype(bf16)
    da_gather.start()
    vw[0] = jnp.zeros((8, 1024), f32)
    vw[0, 1:2] = jnp.sum(d_mid * middle * scale, axis=0, keepdims=True)
    ff.second(0)
    da_gather.forward()
    da_gather.arrived()
    for half in (1, 0):
        rows = da[half * 4:half * 4 + 4].reshape(256, 1024)
        d_mixed = nt(rows, w_ref[...]).astype(bf16)
        if half == 1:
            da_up[...] = d_mixed
            mirror = flow.send(da_up, dz.at[1], mirror_sems[0], mirror_sems[1], p.mirror)
        else:
            dz[0] = d_mixed
    ff.first(2)
    for d in ORDER:
        mlp_sum.send_z(d)
    gout[...] = tn(mixed_ref[...], da[...].reshape(512, 1024)).astype(bf16).reshape(4, 32, 1024)
    ff.second(1)
    mirror.wait_recv()

    lane = lanes((HALF, 128))
    acc[...] = jnp.zeros_like(acc)
    upper_long = (me < parts // 2).astype(jnp.int32)
    for turn in range(2):
        t = upper_long if turn == 0 else 1 - upper_long
        block = me + t * (parts - 1 - 2 * me)
        r0 = block * 512 + t * HALF
        rows_t = pl.ds(pl.multiple_of(t * HALF, HALF), HALF)
        do = dz[t].astype(f32)
        prod = do * mixf_ref[rows_t, :]
        d0 = -jnp.sum(jnp.where(lane < 64, prod, 0.0), axis=1, keepdims=True)
        d1 = -jnp.sum(jnp.where(lane < 64, 0.0, prod), axis=1, keepdims=True)
        dab[0:HALF, 0:128] = jnp.where(lane < 64, 0.0, pltpu.roll(do, 64, 1)).astype(bf16)
        dab[HALF:, 0:128] = jnp.where(lane < 64, 0.0, do).astype(bf16)
        dab[0:HALF, 128:256] = split3(jnp.broadcast_to(d0, (HALF, 128)), lane).astype(bf16)
        dab[HALF:, 128:256] = split3(jnp.broadcast_to(d1, (HALF, 128)), lane).astype(bf16)
        dqt[...] = jnp.zeros_like(dqt)

        def step(c, masked, t=t, r0=r0):
            k0 = pl.multiple_of(c * CH, CH)
            kv = kv_ref[pl.ds(k0, CH), :]
            kva = jnp.concatenate([kv, ext_ref[pl.ds(k0, CH), :]], axis=1)
            qa = qa_ref[t]
            d_out = dab[...]
            s = nt(kva, qa)
            pr = jnp.exp2(s * C2)
            if masked:
                rows = r0 + lax.rem(lax.broadcasted_iota(jnp.int32, (1, 2 * HALF), 1), HALF)
                keys = k0 + lax.broadcasted_iota(jnp.int32, (CH, 2 * HALF), 0)
                pr = jnp.where(keys <= rows, pr, 0.0)
            ds = (pr * nt(kva, d_out)).astype(bf16)
            acc[pl.ds(k0, CH), :] += jnp.dot(
                pr.astype(bf16), d_out[:, 0:128], preferred_element_type=f32
            ) + jnp.dot(ds, qa[:, 0:128], preferred_element_type=f32)
            kt = kv.T[0:64, :]
            dqt[...] += jnp.dot(kt, ds, preferred_element_type=f32)

        def plain(c):
            step(c, False)

        if turn == 0:
            pl.loop(0, 4)(plain)
            for i in range(2):
                for h in range(2):
                    ff_back.put(i, h, ff.own(i, h).astype(bf16))
                    ff_back.first(i, h)
            ff.second(2)
            out_ref[p.wt] = (middle + mlp_sum.own()).astype(bf16)
            out_gather.start()
            pl.loop(4, 8)(plain)
            for h in range(2):
                ff_back.put(2, h, ff.own(2, h).astype(bf16))
                ff_back.first(2, h)
            for h in range(2):
                ff_back.second(0, h)
            out_gather.forward()
            pl.loop(8, block)(plain)
        else:
            pl.loop(0, block)(plain)
        step(block, True)
        both = jnp.concatenate([dqt[:, :HALF], dqt[:, HALF:]], axis=0)
        dqz[t] = (both.T * SCALE).astype(bf16)
    weight = jnp.where(lanes((512, 128)) < 64, SCALE, 1.0)

    @pl.loop(0, parts)
    def _(b):
        rows = pl.ds(pl.multiple_of(b * 512, 512), 512)
        dkv[lax.div(b, 4), lax.rem(b, 4)] = (acc[rows, :] * weight).astype(bf16).reshape(2, 256, 128)

    mirror = flow.send(dqz.at[1], dq.at[1], mirror_sems[2], mirror_sems[3], p.mirror)
    dq[0] = dqz[0]
    first, second = {}, {}
    for d in ORDER:
        for h in range(2):
            to = lax.rem(p.fsp(h) + d, 4)
            src = dkv.at[to, :, 0] if h == 0 else dkv.at[:, to, 1]
            first[h, d] = flow.send(src, r1.at[h, d - 1], fs.at[h, d - 1], fr.at[h, d - 1], p.first(h, d))

    def total(h, b):
        at = spot(h, p.fsp(h), b)
        value = dkv[at[0], at[1], h].astype(f32)
        for d in range(3):
            value = value + r1[h, d, b].astype(f32)
        return value

    for h in range(2):
        for d in ORDER:
            first[h, d].wait_recv()
        for e in ORDER:
            send1[h, e - 1] = total(h, lax.rem(p.ssp(h) + e, 4)).astype(bf16)
            second[h, e] = flow.send(
                send1.at[h, e - 1], r2.at[h, e - 1], ss.at[h, e - 1], sr.at[h, e - 1], p.second(h, e)
            )
    for h in range(2):
        ff_back.second(1, h)
    for h in range(2):
        value = total(h, p.ssp(h))
        for e in ORDER:
            second[h, e].wait_recv()
            value = value + r2[h, e - 1].astype(f32)
        dkv_own[h] = value.astype(bf16)
    mirror.wait_recv()

    wide = lanes((512, 128))
    cosine, sine = cos_ref[...], sin_ref[...]

    def back(grad, proj, gain):
        grad = grad * cosine - turned(grad, wide) * sine
        scale = lax.rsqrt(head_sums(proj * proj, wide) * (1.0 / 64) + eps)
        scaled = grad * gain
        inner = head_sums(scaled * proj, wide) * (1.0 / 64)
        gains = jnp.sum(grad * proj * scale, axis=0, keepdims=True)
        return scale * scaled - proj * scale * scale * scale * inner, gains

    d_q, gq = back(dq[...].reshape(512, 128).astype(f32), qp_ref[...], twice(qg_ref[...]))
    dkv_in = dkv_own[...].reshape(512, 128).astype(f32)
    d_k, gk = back(dkv_in, kvp_ref[...], twice(kg_ref[...]))
    d_q = d_q.astype(bf16)
    d_kv = jnp.where(wide < 64, d_k, dkv_in).astype(bf16)
    wkv = jnp.concatenate([wk_ref[...], wv_ref[...]], axis=0)
    dn[...] = (nt(d_q, wq_ref[...]) + jnp.dot(d_kv, wkv, preferred_element_type=f32)).astype(bf16).reshape(8, 64, 1024)
    for zz in range(4):
        dn_sum.start_core(zz)
    normed = n_ref[...]
    gqkv[0] = tn(d_q, normed).astype(bf16).reshape(4, 32, 1024)
    gqkv[1] = tn(d_kv, normed).astype(bf16).reshape(4, 32, 1024)
    for i in range(3):
        sums.first(i)
    for d in ORDER:
        dn_sum.send_z(d)

    gains = jnp.zeros((1, 1024), f32)
    for w in range(8):
        base = tok_ref[w].astype(f32)
        gains = gains + jnp.sum(dn[w].astype(f32) * base * rms_of(base), axis=0, keepdims=True)
    vw[0, 0:1] = gains
    vw[0, 2:3] = jnp.concatenate([gq, gk, jnp.zeros((1, 768), f32)], axis=1)

    def vec_round(buf, devices, sends, recvs):
        return [
            flow.send(buf.at[0], buf.at[i + 1], sends.at[i], recvs.at[i], device) for i, device in enumerate(devices)
        ]

    def vec_total(buf, copies):
        value = buf[0]
        for i, copy in enumerate(copies):
            copy.wait_recv()
            value = value + buf[i + 1]
        return value

    round1 = vec_round(vw, [p.along_z(d) for d in ORDER] + [p.along_z_other(d) for d in ORDER] + [p.sibling], vs1, vr1)
    for h in range(2):
        ff_back.second(2, h)
    for i in range(3):
        sums.second(i)
    base = tok_ref[p.wt].astype(f32)
    d_normed = dn_sum.own()
    gt_ref[p.wt] = (d_middle + norm_back(base, rms_of(base), gain_in_ref[...], d_normed)).astype(bf16)
    gt_gather.start()
    for i in range(3):
        for h in range(2):
            sums_back.put(i, h, sums.own(i, h).astype(bf16))
            sums_back.first(i, h)
    vx[0] = vec_total(vw, round1)
    round2 = vec_round(vx, [p.along_x(d) for d in ORDER], vs2, vr2)
    for i in range(3):
        for h in range(2):
            sums_back.second(i, h)
    vy[0] = vec_total(vx, round2)
    round3 = vec_round(vy, [p.along_y(d) for d in ORDER], vs3, vr3)
    gt_gather.forward()
    vec_ref[...] = vec_total(vy, round3)
    out_gather.arrived()
    gt_gather.arrived()
    for part in (d_mid_sum, da_gather, mlp_sum, out_gather, ff, ff_back, dn_sum, gt_gather, sums, sums_back, flow):
        part.finish()


def backward(parts, *args):
    rows = pltpu.VMEM
    wt_rows = [rows((4, 64, 1024), bf16), rows((3, 64, 1024), bf16), rows((3, 64, 1024), bf16)]
    wt_sum = wt_rows + WT_SEMS[:4]
    wt_gather = WT_SEMS[4:]
    half = rows((2, 256, 128), bf16)
    return comm_call(
        functools.partial(backward_kernel, parts), 4,
        (sds((8, 64, 1024), bf16), sds((8, 64, 1024), bf16), sds((3, 4, 32, 1024), bf16), sds((3, 4, 144, 1024), bf16),
         sds((8, 1024), f32)),
        args,
        [rows((8, 64, 1024), bf16), rows((256, 128), bf16), half] + [DMA] * 4
        + wt_sum + wt_gather + wt_sum + wt_gather
        + SpScatter.scratch(3, 144) + SpGather.sems(3)
        + [rows((512, 256), bf16), rows((8192, 128), f32), rows((64, 512), f32), half, half,
           rows((4, 4, 2, 256, 128), bf16), half]
        + [rows((2, 3, 4, 256, 128), bf16), rows((2, 3, 256, 128), bf16), rows((2, 3, 256, 128), bf16)]
        + [DMA((2, 3))] * 4
        + [rows((8, 64, 1024), bf16), rows((2, 4, 32, 1024), bf16), rows((4, 32, 1024), bf16)]
        + wt_sum + wt_gather
        + SpScatter.scratch(3, 32) + SpGather.sems(3)
        + [rows((8, 8, 1024), f32), rows((4, 8, 1024), f32), rows((4, 8, 1024), f32),
           DMA((7,)), DMA((7,)), DMA((3,)), DMA((3,)), DMA((3,)), DMA((3,))],
        "backward", 36,
    )


def finish_kernel(sums_ref, ff_ref, out_in, gt_in, vec_ref, out_ref, gt_ref, gq_ref, gk_ref, gv_ref, go_ref, gg_ref, gu_ref, gd_ref,
                  ni_ref, nm_ref, qg_ref, kg_ref, wide, tall, big, sems):
    copies = []

    def write(src, dst):
        copies.append(pltpu.make_async_copy(src, dst, sems.at[len(copies)]))
        copies[-1].start()

    write(out_in, out_ref)
    write(gt_in, gt_ref)
    for i, ref in enumerate((gg_ref, gu_ref, gd_ref)):
        for part in range(2):
            rows = pl.ds(part * 288, 288)
            big[i, rows, :] = ff_ref[i, rows, :].astype(f32)
            write(big.at[i, rows], ref.at[rows])
    wide[0] = sums_ref[0].astype(f32)
    wide[1] = sums_ref[2].astype(f32)
    write(wide.at[1, 0:64], gk_ref)
    write(wide.at[1, 64:128], gv_ref)
    write(wide.at[0], go_ref)
    tall[...] = sums_ref[1].astype(f32).T
    write(tall, gq_ref)
    ni_ref[...] = vec_ref[0:1, :]
    nm_ref[...] = vec_ref[1:2, :]
    qg_ref[...] = vec_ref[2:3, 0:64] + vec_ref[2:3, 64:128]
    kg_ref[...] = vec_ref[2:3, 128:192]
    for copy in copies:
        copy.wait()


def finish(sums, ff, output, grad_tokens, vec):
    hbm = pl.BlockSpec(memory_space=pl.ANY)
    rows = sds((576, 1024), f32)
    return pl.pallas_call(
        finish_kernel,
        out_shape=(sds((512, 1024), bf16), sds((512, 1024), bf16), sds((1024, 128), f32), sds((64, 1024), f32), sds((64, 1024), f32),
                   sds((128, 1024), f32), rows, rows, rows,
                   sds((1, 1024), f32), sds((1, 1024), f32), sds((1, 64), f32), sds((1, 64), f32)),
        in_specs=[vmem] * 5,
        out_specs=tuple([hbm] * 9 + [vmem] * 4),
        scratch_shapes=[pltpu.VMEM((2, 128, 1024), f32), pltpu.VMEM((1024, 128), f32), pltpu.VMEM((3, 576, 1024), f32), DMA((12,))],
        compiler_params=pltpu.CompilerParams(vmem_limit_bytes=14 << 20),
        name="finish",
    )(sums, ff, output, grad_tokens, vec)


theta = 1000000.0


def body(tokens, norm_in, w_query, w_key, w_value, query_gain, key_gain, w_out, norm_mid, w_gate, w_up, w_down, cotangent, lengths):
    parts = lax.axis_size("sp")
    freqs = theta ** (-(np.arange(32).astype(np.float64) * 2.0) / 64)
    freqs = jnp.asarray(np.broadcast_to(freqs.astype(np.float32)[:, None], (32, 128)))
    qg, kg = query_gain.reshape(1, 64), key_gain.reshape(1, 64)
    wk, wv = w_key.T, w_value.T
    wide = sds((512, 128), f32)

    normed, q_proj, kv_proj, q, kv, cosine, sine = local_call(
        proj_kernel,
        (sds((512, 1024), bf16), wide, wide, sds((512, 128), bf16), sds((512, 128), bf16), wide, wide),
        (lengths, tokens, norm_in.reshape(1, 1024), w_query, wk, wv, qg, kg, freqs),
        "project", smem,
    )
    qz, kv_all, ext = gather_keys(lengths, q, kv)
    kv_all = kv_all.reshape(8192, 128)
    mix_z, mix_f, qa = attend(parts, lengths, qz.reshape(512, 128), kv_all, ext)
    normed_mid, mid_own, mixed = make_middle(mix_z, w_out, tokens, norm_mid)
    normed_mid = normed_mid.reshape(512, 1024)
    mixed = mixed.reshape(512, 128)

    gate = jnp.dot(normed_mid, w_gate, preferred_element_type=f32)
    up_proj = jnp.dot(normed_mid, w_up, preferred_element_type=f32)
    sigmoid_gate = jax.nn.sigmoid(gate)
    act = (gate * sigmoid_gate * up_proj).astype(bf16)
    mlp_part = jnp.dot(act, w_down, preferred_element_type=f32).astype(bf16)
    d_act = jnp.einsum("td,fd->tf", cotangent, w_down, preferred_element_type=f32)
    d_gate = (d_act * up_proj * sigmoid_gate * (1.0 + gate * (1.0 - sigmoid_gate))).astype(bf16)
    d_up = (d_act * gate * sigmoid_gate).astype(bf16)
    d_mid_part = (
        jnp.einsum("tf,df->td", d_gate, w_gate, preferred_element_type=f32)
        + jnp.einsum("tf,df->td", d_up, w_up, preferred_element_type=f32)
    ).astype(bf16)
    grads = (
        jnp.einsum("tf,td->fd", d_gate, normed_mid, preferred_element_type=f32).astype(bf16),
        jnp.einsum("tf,td->fd", d_up, normed_mid, preferred_element_type=f32).astype(bf16),
        jnp.einsum("tf,td->fd", act, cotangent, preferred_element_type=f32).astype(bf16),
    )
    output, grad_tokens, sums, g_ff, vec = backward(
        parts,
        d_mid_part.reshape(8, 64, 1024), mlp_part.reshape(8, 64, 1024), mid_own, cotangent.reshape(8, 64, 1024),
        norm_mid.reshape(1, 1024), w_out, *(g.reshape(4, 144, 1024) for g in grads),
        qa, mix_f, kv_all, ext, mixed,
        q_proj, kv_proj, normed, w_query, wk, wv, qg, kg, cosine, sine, tokens.reshape(8, 64, 1024), norm_in.reshape(1, 1024),
    )
    (output, grad_tokens, g_query, g_key, g_value, g_out, g_gate, g_up, g_down, g_norm_in, g_norm_mid, g_qg, g_kg) = finish(
        sums.reshape(3, 128, 1024), g_ff.reshape(3, 576, 1024), output.reshape(512, 1024), grad_tokens.reshape(512, 1024), vec
    )
    return (
        output, grad_tokens, g_norm_in.reshape(1024), g_query, g_key.T, g_value.T, g_qg.reshape(64), g_kg.reshape(64),
        g_out, g_norm_mid.reshape(1024), g_gate.T, g_up.T, g_down,
    )


def solution(mesh):
    placed = (
        P("sp", None), P(), P(None, "wt"), P(None, "wt"), P(None, "wt"), P(), P(), P("wt", None), P(),
        P(None, "wt"), P(None, "wt"), P("wt", None), P("sp", None), P(),
    )
    return jax.shard_map(
        body,
        mesh=mesh,
        in_specs=placed,
        out_specs=(
            P("sp", None), P("sp", None), P(), P(None, "wt"), P(None, "wt"), P(None, "wt"), P(), P(),
            P("wt", None), P(), P(None, "wt"), P(None, "wt"), P("wt", None),
        ),
        check_vma=False,
    )
```

```python
import functools, math
import jax
import jax.numpy as jnp
import numpy as np
from jax import lax
from jax.experimental import pallas as pl
from jax.experimental.pallas import tpu as pltpu
from jax.sharding import PartitionSpec as P

f32 = jnp.float32
bf16 = jnp.bfloat16
sds = jax.ShapeDtypeStruct
DMA = pltpu.SemaphoreType.DMA
CH = 512
HALF = 256
SCALE = 0.125
C2 = SCALE * math.log2(math.e)


def starts_of(ids, len_ref):
    end = jnp.int32(0)
    start = jnp.zeros_like(ids)
    for j in range(4):
        end = end + len_ref[j]
        start = start + jnp.where(ids >= end, len_ref[j], 0)
    return start


def scalar_start(row, len_ref):
    end = jnp.int32(0)
    start = jnp.int32(0)
    for j in range(4):
        end = end + len_ref[j]
        start = start + jnp.where(row >= end, len_ref[j], 0)
    return start


def lanes(shape):
    return lax.broadcasted_iota(jnp.int32, shape, len(shape) - 1)


def split3(value, lane):
    hi = value.astype(bf16).astype(f32)
    rest = value - hi
    mid = rest.astype(bf16).astype(f32)
    low = rest - mid
    return jnp.where(lane == 0, hi, jnp.where(lane == 1, mid, jnp.where(lane == 2, low, 0.0)))


def tile_row(me, t, parts):
    return me * 512 if t == 0 else (parts - 1 - me) * 512 + HALF


FAR = 8192.0


def segment_bounds(len_ref, lane):
    begin = jnp.zeros_like(lane)
    end = jnp.zeros_like(lane)
    at = jnp.int32(0)
    for j in range(4):
        begin = jnp.where(lane == 3 + j, at, begin)
        at = at + len_ref[j]
        end = jnp.where(lane == 3 + j, at, end)
    return begin, end


def inside(ids, len_ref, shape):
    lane = lanes(shape)
    begin, end = segment_bounds(len_ref, lane)
    return (ids >= begin) & (ids < end), lane


def key_columns(k0, len_ref, rows):
    ids = k0 + lax.broadcasted_iota(jnp.int32, (rows, 128), 0)
    within, lane = inside(ids, len_ref, (rows, 128))
    return jnp.where(lane < 3, 1.0, jnp.where(within, 1.0, 0.0)).astype(bf16)


def query_columns(r0, len_ref, rows):
    ids = r0 + lax.broadcasted_iota(jnp.int32, (rows, 128), 0)
    within, lane = inside(ids, len_ref, (rows, 128))
    return jnp.where((lane < 3) | (lane > 6) | within, 0.0, -FAR)


smem = pl.BlockSpec(memory_space=pltpu.SMEM)
vmem = pl.BlockSpec(memory_space=pltpu.VMEM)


MESH = pl.DeviceIdType.MESH
eps = 1e-05


def rcopy(src, dst, send, recv, device):
    return pltpu.make_async_remote_copy(
        src_ref=src, dst_ref=dst, send_sem=send, recv_sem=recv, device_id=device, device_id_type=MESH
    )


def meet(devices):
    barrier = pltpu.get_barrier_semaphore()
    for device in devices:
        pl.semaphore_signal(barrier, inc=1, device_id=device, device_id_type=MESH)
    pl.semaphore_wait(barrier, len(devices))


class Place:
    def __init__(self):
        self.sp = lax.axis_index("sp")
        self.wt = lax.axis_index("wt")
        self.x, self.y = lax.div(self.sp, 4), lax.rem(self.sp, 4)
        self.z, self.c = lax.div(self.wt, 2), lax.rem(self.wt, 2)
        self.mirror = (15 - self.sp, self.wt)
        self.sibling = (self.sp, self.z * 2 + 1 - self.c)

    def along_x(self, d):
        return (lax.rem(self.x + d, 4) * 4 + self.y, self.wt)

    def along_y(self, d):
        return (self.x * 4 + lax.rem(self.y + d, 4), self.wt)

    def along_z(self, d):
        return (self.sp, lax.rem(self.z + d, 4) * 2 + self.c)

    def along_z_other(self, d):
        return (self.sp, lax.rem(self.z + d, 4) * 2 + 1 - self.c)

    def first(self, h, d):
        return self.along_x(d) if h == 0 else self.along_y(d)

    def second(self, h, d):
        return self.along_y(d) if h == 0 else self.along_x(d)

    def fsp(self, h):
        return self.x if h == 0 else self.y

    def ssp(self, h):
        return self.y if h == 0 else self.x


def spot(h, first, second):
    return (first, second) if h == 0 else (second, first)


ORDER = (2, 1, 3)


class SpScatter:
    def __init__(self, p, srcs, rows, refs):
        self.p, self.srcs, self.rows = p, srcs, rows
        self.ra, self.rb, self.send, self.r2, self.fs, self.fr, self.ss, self.sr = refs
        self.one, self.two = {}, {}

    @staticmethod
    def scratch(n, rows):
        return [
            pltpu.VMEM((n, 3, rows, 512), bf16), pltpu.VMEM((n, 3, 4, rows, 128), bf16),
            pltpu.VMEM((n, 2, 3, rows, 128), bf16), pltpu.VMEM((n, 2, 3, rows, 128), bf16),
            DMA((n, 2, 3)), DMA((n, 2, 3)), DMA((n, 2, 3)), DMA((n, 2, 3)),
        ]

    def first(self, i):
        p = self.p
        for d in ORDER:
            to = lax.rem(p.x + d, 4)
            self.one[i, 0, d] = rcopy(
                self.srcs[i].at[to, :, pl.ds(0, 512)], self.ra.at[i, d - 1],
                self.fs.at[i, 0, d - 1], self.fr.at[i, 0, d - 1], p.along_x(d),
            )
            self.one[i, 0, d].start()
            to = lax.rem(p.y + d, 4)
            self.one[i, 1, d] = rcopy(
                self.srcs[i].at[:, :, pl.ds(columns_at(1, to), 128)], self.rb.at[i, d - 1],
                self.fs.at[i, 1, d - 1], self.fr.at[i, 1, d - 1], p.along_y(d),
            )
            self.one[i, 1, d].start()

    def part(self, i, h, b):
        p = self.p
        if h == 0:
            value = self.srcs[i][p.x, :, pl.ds(columns_at(0, b), 128)].astype(f32)
            for d in range(3):
                value = value + self.ra[i, d, :, pl.ds(columns_at(0, b), 128)].astype(f32)
            return value
        value = self.srcs[i][b, :, pl.ds(columns_at(1, p.y), 128)].astype(f32)
        for d in range(3):
            value = value + self.rb[i, d, b].astype(f32)
        return value

    def second(self, i):
        p = self.p
        for h in range(2):
            for d in ORDER:
                self.one[i, h, d].wait_recv()
            for e in ORDER:
                self.send[i, h, e - 1] = self.part(i, h, lax.rem(p.ssp(h) + e, 4)).astype(bf16)
                self.two[i, h, e] = rcopy(
                    self.send.at[i, h, e - 1], self.r2.at[i, h, e - 1],
                    self.ss.at[i, h, e - 1], self.sr.at[i, h, e - 1], p.second(h, e),
                )
                self.two[i, h, e].start()

    def own(self, i, h):
        value = self.part(i, h, self.p.ssp(h))
        for e in ORDER:
            self.two[i, h, e].wait_recv()
            value = value + self.r2[i, h, e - 1].astype(f32)
        return value

    def finish(self):
        for copy in list(self.one.values()) + list(self.two.values()):
            copy.wait_send()


def columns_at(h, b):
    return pl.multiple_of(h * 512 + b * 128, 128)


class SpGather:
    def __init__(self, p, out, rows, sems):
        self.p, self.out, self.rows = p, out, rows
        self.fs, self.fr, self.ss, self.sr = sems
        self.one, self.two = {}, {}

    @staticmethod
    def sems(n):
        return [DMA((n, 2, 3)) for _ in range(4)]

    def spot(self, h):
        p = self.p
        return p.x, pl.ds(columns_at(h, p.y), 128)

    def put(self, i, h, value):
        x, columns = self.spot(h)
        self.out[i, x, :, columns] = value

    def first(self, i, h):
        x, columns = self.spot(h)
        block = self.out.at[i, x, :, columns]
        for e in ORDER:
            self.one[i, h, e] = rcopy(
                block, block, self.fs.at[i, h, e - 1], self.fr.at[i, h, e - 1], self.p.second(h, e)
            )
            self.one[i, h, e].start()

    def second(self, i, h):
        x, columns = self.spot(h)
        for e in ORDER:
            self.one[i, h, e].wait_recv()
        block = self.out.at[i, x, :, pl.ds(0, 512)] if h == 0 else self.out.at[i, :, :, columns]
        for d in ORDER:
            self.two[i, h, d] = rcopy(
                block, block, self.ss.at[i, h, d - 1], self.sr.at[i, h, d - 1], self.p.first(h, d)
            )
            self.two[i, h, d].start()

    def arrived(self, i):
        for h in range(2):
            for d in ORDER:
                self.two[i, h, d].wait_recv()

    def finish(self):
        for copy in self.one.values():
            copy.wait_send()
        for copy in self.two.values():
            copy.wait()


SPLIT = 2


def sub(s):
    return pl.ds(s * (64 // SPLIT), 64 // SPLIT)


class WtSum:
    def __init__(self, p, part, sib, send, rz, sems):
        self.p, self.part, self.sib, self.send, self.rz = p, part, sib, send, rz
        self.cs, self.cr, self.zs, self.zr = sems
        self.second = {}

    def core(self, zz, s):
        return rcopy(
            self.part.at[zz * 2 + 1 - self.p.c, sub(s)], self.sib.at[zz, sub(s)],
            self.cs.at[zz, s], self.cr.at[zz, s], self.p.sibling,
        )

    def start_core(self, zz):
        for s in range(SPLIT):
            self.core(zz, s).start()

    def pair(self, zz, s):
        return self.part[zz * 2 + self.p.c, sub(s)].astype(f32) + self.sib[zz, sub(s)].astype(f32)

    def send_z(self):
        for s in range(SPLIT):
            for d in ORDER:
                zz = lax.rem(self.p.z + d, 4)
                self.core(zz, s).wait_recv()
                self.send[d - 1, sub(s)] = self.pair(zz, s).astype(bf16)
                copy = rcopy(
                    self.send.at[d - 1, sub(s)], self.rz.at[d - 1, sub(s)],
                    self.zs.at[d - 1, s], self.zr.at[d - 1, s], self.p.along_z(d),
                )
                copy.start()
                self.second[d, s] = copy

    def own(self, s):
        self.core(self.p.z, s).wait_recv()
        value = self.pair(self.p.z, s)
        for d in (1, 3, 2):
            self.second[d, s].wait_recv()
            value = value + self.rz[d - 1, sub(s)].astype(f32)
        return value

    def finish(self):
        for zz in range(4):
            for s in range(SPLIT):
                self.core(zz, s).wait_send()
        for copy in self.second.values():
            copy.wait_send()


class WtGather:
    def __init__(self, p, out, sems):
        self.p, self.out = p, out
        self.zs, self.zr, self.gs, self.gr = sems
        self.far, self.near = {}, {}

    def start(self, s):
        p = self.p
        block = self.out.at[p.wt, sub(s)]
        for d in ORDER:
            self.far[d, s] = rcopy(block, block, self.zs.at[d - 1, s], self.zr.at[d - 1, s], p.along_z(d))
            self.far[d, s].start()
        self.pass_on(0, s)

    def pass_on(self, slot, s):
        p = self.p
        block = self.out.at[lax.rem(p.z + 4 - slot, 4) * 2 + p.c, sub(s)]
        self.near[slot, s] = rcopy(block, block, self.gs.at[slot, s], self.gr.at[slot, s], p.sibling)
        self.near[slot, s].start()

    def forward(self):
        for s in range(SPLIT):
            for d in (1, 3, 2):
                self.far[d, s].wait_recv()
                self.pass_on(d, s)

    def arrived(self):
        for copy in self.near.values():
            copy.wait_recv()

    def finish(self):
        for copy in list(self.far.values()) + list(self.near.values()):
            copy.wait_send()


def rms_of(value):
    return lax.rsqrt(jnp.mean(value * value, axis=-1, keepdims=True) + eps)


def norm_back(values, scale, gain, grad):
    scaled = grad * gain
    inner = jnp.mean(scaled * values, axis=-1, keepdims=True)
    return scale * scaled - values * scale * scale * scale * inner


def wt_peers(p):
    return [p.sibling] + [p.along_z(d) for d in ORDER]


class Flow:
    def __init__(self):
        self.copies = []

    def send(self, *args):
        copy = rcopy(*args)
        copy.start()
        self.copies.append(copy)
        return copy

    def finish(self):
        for copy in self.copies:
            copy.wait_send()


def forward_kernel(
    parts,
    len_ref, q_ref, kv_ref, tok_ref, cot_ref, w_ref, gain_ref,
    all_ref, ext_ref, qa_ref, mixf_ref, mix_ref, nm_ref, mid_ref, cotz_ref,
    qz, base, acc, part, sib, send, rz, ms, mr, cs, cr, zs, zr, az, bz, ag, bg, fs, fr, ss, sr,
):
    p = Place()
    me = p.sp
    meet(wt_peers(p) + [p.along_x(d) for d in ORDER] + [p.along_y(d) for d in ORDER] + [p.mirror])
    flow = Flow()
    first = {}
    for d in ORDER:
        for h in range(2):
            first[h, d] = flow.send(
                kv_ref.at[h], all_ref.at[p.x, p.y, h], fs.at[h, d - 1], fr.at[h, d - 1], p.first(h, d)
            )
    q_mirror = flow.send(q_ref.at[1], qz.at[1], ms.at[0], mr.at[0], p.mirror)

    def pass_on(h, slot):
        a = lax.rem(p.fsp(h) + 4 - slot, 4)
        at = spot(h, a, p.ssp(h))
        for e in ORDER:
            src = kv_ref.at[h] if slot == 0 else all_ref.at[at[0], at[1], h]
            flow.send(src, all_ref.at[at[0], at[1], h], ss.at[h, slot, e - 1], sr.at[h, slot, e - 1], p.second(h, e))

    for h in range(2):
        pass_on(h, 0)
    token_mirror = rcopy(tok_ref.at[p.wt], base, ms.at[1], mr.at[1], p.mirror)

    @pl.when(p.wt >= 4)
    def _():
        token_mirror.start()

    @pl.when(p.wt < 4)
    def _():
        base[...] = tok_ref[p.wt]

    all_ref[p.x, p.y] = kv_ref[...]
    qz[0] = q_ref[0]
    cotz_ref[0:4] = cot_ref[0:4]

    @pl.loop(0, 8)
    def _(b):
        rows = pl.ds(pl.multiple_of(b * 1024, 1024), 1024)
        ext_ref[rows, :] = key_columns(b * 1024, len_ref, 1024)

    lane = lanes((HALF, 128))
    lane2 = lanes((2 * HALF, 128))
    lanek = lanes((CH, 128))
    acc[...] = jnp.zeros_like(acc)
    blocks = (me, parts - 1 - me)
    begins = (me * 512, (parts - 1 - me) * 512 + HALF)

    def prepare(t):
        q = qz[t].astype(f32)
        qa_ref[t, 0:HALF, 0:128] = jnp.where(lane < 64, q, 0.0).astype(bf16)
        qa_ref[t, HALF:, 0:128] = jnp.where(lane < 64, pltpu.roll(q, 64, 1), 0.0).astype(bf16)
        columns = query_columns(begins[t], len_ref, HALF).astype(bf16)
        qa_ref[t, 0:HALF, 128:256] = columns
        qa_ref[t, HALF:, 128:256] = columns

    def step(t, x, y, masked):
        k0 = pl.multiple_of((x * 4 + y) * CH, CH)
        kv = all_ref[x, y].reshape(CH, 128)
        kva = jnp.concatenate([kv, ext_ref[pl.ds(k0, CH), :]], axis=1)
        pr = jnp.exp2(nt(qa_ref[t], kva) * C2)
        if masked:
            rows = begins[t] + lax.rem(lax.broadcasted_iota(jnp.int32, (2 * HALF, 1), 0), HALF)
            keys = k0 + lax.broadcasted_iota(jnp.int32, (2 * HALF, CH), 1)
            pr = jnp.where(keys <= rows, pr, 0.0)
        ones = jnp.where(lanek < 64, jnp.ones_like(kv), kv)
        acc[t] += jnp.dot(pr.astype(bf16), ones, preferred_element_type=f32)

    def both(x, y):
        block = x * 4 + y

        @pl.when(block < blocks[0])
        def _():
            step(0, x, y, False)

        @pl.when(block < blocks[1])
        def _():
            step(1, x, y, False)

        @pl.when(block == blocks[1])
        def _():
            step(1, x, y, True)

    prepare(0)
    step(0, p.x, p.y, True)
    for d in (1, 3, 2):
        for h in range(2):
            first[h, d].wait_recv()
            pass_on(h, d)
    q_mirror.wait_recv()
    prepare(1)

    @pl.when(me < blocks[1])
    def _():
        step(1, p.x, p.y, False)

    def wait_for(x, y, h, slot, e):
        block = all_ref.at[x, y, h]
        rcopy(block, block, ss.at[h, slot, e - 1], sr.at[h, slot, e - 1], p.second(h, 1)).wait_recv()

    @pl.loop(1, 4)
    def _(d):
        x = lax.rem(p.x + 4 - d, 4)
        wait_for(x, p.y, 1, 0, d)
        both(x, p.y)

    @pl.loop(1, 4)
    def _(d):
        y = lax.rem(p.y + 4 - d, 4)
        wait_for(p.x, y, 0, 0, d)
        both(p.x, y)

    @pl.loop(0, 9)
    def _(k):
        dx, dy = 1 + lax.div(k, 3), 1 + lax.rem(k, 3)
        x, y = lax.rem(p.x + 4 - dx, 4), lax.rem(p.y + 4 - dy, 4)
        wait_for(x, y, 0, dx, dy)
        wait_for(x, y, 1, dy, dx)
        both(x, y)

    total = WtSum(p, part, sib, send, rz, (cs, cr, zs, zr))
    cot_mirror = flow.send(cot_ref.at[pl.ds(4, 4)], cotz_ref.at[pl.ds(4, 4)], ms.at[2], mr.at[2], p.mirror)
    for t in range(2):
        value = acc[t]
        swapped = pltpu.roll(value, 64, 1)
        o = swapped / value
        mix = jnp.where(lane < 64, o[:HALF], pltpu.roll(o[HALF:], 64, 1))
        mixf_ref[t] = mix
        mix = mix.astype(bf16)
        mix_ref[t] = mix
        part[t * 4:t * 4 + 4] = jnp.dot(mix, w_ref[...], preferred_element_type=f32).astype(bf16).reshape(4, 64, 1024)
        for zz in (t * 2, t * 2 + 1):
            total.start_core(zz)
    total.send_z()
    for t in range(2):
        value = acc[t]
        weights = jnp.where(lane2 < 64, value, pltpu.roll(value, 64, 1))
        columns = qa_ref[t, :, 128:256].astype(f32)
        qa_ref[t, :, 128:256] = (split3(jnp.log(weights) * (-1.0 / SCALE), lane2) + columns).astype(bf16)

    @pl.when(p.wt >= 4)
    def _():
        token_mirror.wait()

    spread = WtGather(p, nm_ref, (az, bz, ag, bg))
    for s in range(SPLIT):
        middle = base[sub(s)].astype(f32) + total.own(s)
        mid_ref[sub(s)] = middle
        nm_ref[p.wt, sub(s)] = (middle * rms_of(middle) * gain_ref[...]).astype(bf16)
        spread.start(s)
    spread.forward()
    cot_mirror.wait_recv()
    spread.arrived()
    for part in (spread, total, flow):
        part.finish()


WT_SEMS = [DMA((n, SPLIT)) for n in (4, 4, 3, 3, 3, 3, 4, 4)]


def comm_call(kernel, number, out_shape, args, scratch, name, limit=10, first=None):
    return pl.pallas_call(
        kernel,
        out_shape=out_shape,
        in_specs=[first or vmem] + [vmem] * (len(args) - 1),
        out_specs=tuple(vmem for _ in out_shape),
        scratch_shapes=scratch,
        compiler_params=pltpu.CompilerParams(
            collective_id=number, has_side_effects=True, vmem_limit_bytes=limit << 20
        ),
        cost_estimate=pl.CostEstimate(flops=8 << 30, bytes_accessed=32 << 20, transcendentals=0),
        name=name,
    )(*args)


def forward(parts, lengths, q, kv, tokens, cotangent, w_out, gain):
    rows = pltpu.VMEM
    half = sds((2, 256, 128), bf16)
    full = sds((8, 64, 1024), bf16)
    return comm_call(
        functools.partial(forward_kernel, parts), 1,
        (sds((4, 4, 2, 256, 128), bf16), sds((8192, 128), bf16), sds((2, 512, 256), bf16), sds((2, 256, 128), f32),
         half, full, sds((64, 1024), f32), full),
        (lengths, q.reshape(2, 256, 128), kv.reshape(2, 256, 128), tokens.reshape(8, 64, 1024),
         cotangent.reshape(8, 64, 1024), w_out, gain.reshape(1, 1024)),
        [rows((2, 256, 128), bf16), rows((64, 1024), bf16), rows((2, 512, 128), f32), rows((8, 64, 1024), bf16),
         rows((4, 64, 1024), bf16), rows((3, 64, 1024), bf16), rows((3, 64, 1024), bf16), DMA((3,)), DMA((3,))]
        + WT_SEMS + [DMA((2, 3)), DMA((2, 3)), DMA((2, 4, 3)), DMA((2, 4, 3))],
        "forward", 16, smem,
    )


def turned(value, lane):
    return jnp.where(lax.rem(lane, 64) < 32, pltpu.roll(value, 96, 1), pltpu.roll(value, 32, 1))


def head_sums(value, lane):
    s0 = jnp.sum(jnp.where(lane < 64, value, 0.0), axis=1, keepdims=True)
    s1 = jnp.sum(jnp.where(lane < 64, 0.0, value), axis=1, keepdims=True)
    return jnp.where(lane < 64, s0, s1)


def twice(gain):
    return jnp.concatenate([gain, gain], axis=1)


def nt(a, b):
    return lax.dot_general(a, b, (((1,), (1,)), ((), ())), preferred_element_type=f32)


def tn(a, b):
    return lax.dot_general(a, b, (((0,), (0,)), ((), ())), preferred_element_type=f32)


def proj_kernel(len_ref, tok_ref, gain_ref, wq_ref, wk_ref, wv_ref, qg_ref, kg_ref, freq_ref,
                n_ref, qp_ref, kvp_ref, q_ref, kv_ref, cos_ref, sin_ref):
    lane = lanes((512, 128))
    ids = lax.axis_index("sp") * 512 + lax.broadcasted_iota(jnp.int32, (1, 512), 1)
    positions = (ids - starts_of(ids, len_ref)).astype(f32)
    angles = positions * freq_ref[:, 0:1]
    cosine, sine = jnp.cos(angles), jnp.sin(angles)
    cosine = jnp.concatenate([cosine] * 4, axis=0).T
    sine = jnp.concatenate([-sine, sine, -sine, sine], axis=0).T
    cos_ref[...] = cosine
    sin_ref[...] = sine
    base = tok_ref[...].astype(f32)
    normed = (base * rms_of(base) * gain_ref[...]).astype(bf16)
    n_ref[...] = normed
    wkv = jnp.concatenate([wk_ref[...], wv_ref[...]], axis=0)
    q = jnp.dot(normed, wq_ref[...], preferred_element_type=f32)
    qp_ref[...] = q
    q = q * lax.rsqrt(head_sums(q * q, lane) * (1.0 / 64) + eps) * twice(qg_ref[...])
    q_ref[...] = (q * cosine + turned(q, lane) * sine).astype(bf16)
    kv = nt(normed, wkv)
    kvp_ref[...] = kv
    k = kv * lax.rsqrt(head_sums(kv * kv, lane) * (1.0 / 64) + eps) * twice(kg_ref[...])
    k = k * cosine + turned(k, lane) * sine
    kv_ref[...] = jnp.where(lane < 64, k, kv).astype(bf16)


def local_call(kernel, out_shape, args, name, first=None):
    return pl.pallas_call(
        kernel,
        out_shape=out_shape,
        in_specs=[first or vmem] + [vmem] * (len(args) - 1),
        out_specs=tuple(vmem for _ in out_shape),
        compiler_params=pltpu.CompilerParams(vmem_limit_bytes=16 << 20),
        cost_estimate=pl.CostEstimate(flops=3 << 30, bytes_accessed=16 << 20, transcendentals=0),
        name=name,
    )(*args)


def backward_kernel(
    parts,
    dm_ref, mlp_ref, mid_ref, cot_ref, gain_ref, w_ref, g0_ref, g1_ref, g2_ref,
    qa_ref, mixf_ref, kv_ref, ext_ref, mixed_ref,
    qp_ref, kvp_ref, n_ref, wq_ref, wk_ref, wv_ref, qg_ref, kg_ref, cos_ref, sin_ref, tok_ref, gain_in_ref,
    out_ref, gt_ref, sums_ref, ff_ref, vec_ref,
    *scratch,
):
    scratch = list(scratch)

    def take(n):
        got = scratch[:n]
        del scratch[:n]
        return got

    p = Place()
    me = p.sp
    meet(
        wt_peers(p) + [p.along_z_other(d) for d in ORDER] + [p.mirror]
        + [p.along_x(d) for d in ORDER] + [p.along_y(d) for d in ORDER]
    )
    flow = Flow()

    def wt_sum(ref):
        sib, send, rz = take(3)
        return WtSum(p, ref, sib, send, rz, take(4))

    da, dz, dmid, dmid_o, out_own = take(5)
    mirror_sems = take(6)
    d_mid_sum = wt_sum(dm_ref)
    da_gather = WtGather(p, da, take(4))
    mlp_sum = wt_sum(mlp_ref)
    out_gather = WtGather(p, out_ref, take(4))
    ff = SpScatter(p, (g0_ref, g1_ref, g2_ref), 144, take(8))
    ff_back = SpGather(p, ff_ref, 144, take(4))
    dab, acc, dqt, dqz, dq, dkv, dkv_own = take(7)
    r1, send1, r2, fs, fr, ss, sr = take(7)
    dn, gqkv, gout = take(3)
    dn_sum = wt_sum(dn)
    gt_gather = WtGather(p, gt_ref, take(4))
    sums = SpScatter(p, (gout, gqkv.at[0], gqkv.at[1]), 32, take(8))
    sums_back = SpGather(p, sums_ref, 32, take(4))
    vw, vx, vy, vs1, vr1, vs2, vr2, vs3, vr3 = take(9)
    assert not scratch

    for zz in range(4):
        d_mid_sum.start_core(zz)
    ff.first(0)
    ff.first(1)
    d_mid_sum.send_z()
    for zz in range(4):
        mlp_sum.start_core(zz)
    vw[0] = jnp.zeros((8, 1024), f32)
    for s in range(SPLIT):
        middle = mid_ref[sub(s)]
        scale = rms_of(middle)
        d_mid = d_mid_sum.own(s)
        d_middle = cot_ref[p.wt, sub(s)].astype(f32) + norm_back(middle, scale, gain_ref[...], d_mid)
        da[p.wt, sub(s)] = d_middle.astype(bf16)
        da_gather.start(s)
        dmid[sub(s)] = d_middle
        vw[0, 1:2] += jnp.sum(d_mid * middle * scale, axis=0, keepdims=True)
    dmid_mirror = rcopy(dmid, dmid_o, mirror_sems[2], mirror_sems[3], p.mirror)

    @pl.when(p.wt >= 4)
    def _():
        dmid_mirror.start()

    mlp_sum.send_z()
    ff.second(0)
    da_gather.forward()
    acc[...] = jnp.zeros_like(acc)
    da_gather.arrived()
    dz[...] = nt(da[...].reshape(512, 1024), w_ref[...]).astype(bf16).reshape(2, 256, 128)
    ff.first(2)
    ff.second(1)

    lane = lanes((HALF, 128))
    upper_long = (me < parts // 2).astype(jnp.int32)
    for turn in range(2):
        t = upper_long if turn == 0 else 1 - upper_long
        block = me + t * (parts - 1 - 2 * me)
        r0 = block * 512 + t * HALF
        do = dz[t].astype(f32)
        prod = do * mixf_ref[t]
        d0 = -jnp.sum(jnp.where(lane < 64, prod, 0.0), axis=1, keepdims=True)
        d1 = -jnp.sum(jnp.where(lane < 64, 0.0, prod), axis=1, keepdims=True)
        dab[0:HALF, 0:128] = jnp.where(lane < 64, 0.0, pltpu.roll(do, 64, 1)).astype(bf16)
        dab[HALF:, 0:128] = jnp.where(lane < 64, 0.0, do).astype(bf16)
        dab[0:HALF, 128:256] = split3(jnp.broadcast_to(d0, (HALF, 128)), lane).astype(bf16)
        dab[HALF:, 128:256] = split3(jnp.broadcast_to(d1, (HALF, 128)), lane).astype(bf16)
        dqt[...] = jnp.zeros_like(dqt)

        def step(c, masked, t=t, r0=r0):
            k0 = pl.multiple_of(c * CH, CH)
            kv = kv_ref[pl.ds(k0, CH), :]
            kva = jnp.concatenate([kv, ext_ref[pl.ds(k0, CH), :]], axis=1)
            qa = qa_ref[t]
            d_out = dab[...]
            s = nt(kva, qa)
            pr = jnp.exp2(s * C2)
            if masked:
                rows = r0 + lax.rem(lax.broadcasted_iota(jnp.int32, (1, 2 * HALF), 1), HALF)
                keys = k0 + lax.broadcasted_iota(jnp.int32, (CH, 2 * HALF), 0)
                pr = jnp.where(keys <= rows, pr, 0.0)
            ds = (pr * nt(kva, d_out)).astype(bf16)
            acc[pl.ds(k0, CH), :] += jnp.dot(
                pr.astype(bf16), d_out[:, 0:128], preferred_element_type=f32
            ) + jnp.dot(ds, qa[:, 0:128], preferred_element_type=f32)
            kt = kv.T[0:64, :]
            dqt[...] += jnp.dot(kt, ds, preferred_element_type=f32)

        def plain(c):
            step(c, False)

        if turn == 0:
            pl.loop(0, 4)(plain)
            for i in range(2):
                for h in range(2):
                    ff_back.put(i, h, ff.own(i, h).astype(bf16))
                    ff_back.first(i, h)
            ff.second(2)
            for s in range(SPLIT):
                out_own[sub(s)] = (mid_ref[sub(s)] + mlp_sum.own(s)).astype(bf16)
            out_mirror = rcopy(out_own, out_ref.at[p.wt], mirror_sems[4], mirror_sems[5], p.mirror)

            @pl.when(p.wt >= 4)
            def _():
                out_mirror.start()

            @pl.when(p.wt < 4)
            def _():
                out_ref[p.wt] = out_own[...]

            gout[...] = tn(mixed_ref[...].reshape(512, 128), da[...].reshape(512, 1024)).astype(bf16).reshape(4, 32, 1024)
            pl.loop(4, 8)(plain)
            for h in range(2):
                ff_back.put(2, h, ff.own(2, h).astype(bf16))
                ff_back.first(2, h)
            for h in range(2):
                ff_back.second(0, h)

            @pl.when(p.wt >= 4)
            def _():
                out_mirror.wait()

            for s in range(SPLIT):
                out_gather.start(s)
            pl.loop(8, block)(plain)
        else:
            pl.loop(0, block)(plain)
        step(block, True)
        both = jnp.concatenate([dqt[:, :HALF], dqt[:, HALF:]], axis=0)
        dqz[t] = (both.T * SCALE).astype(bf16)
    weight = jnp.where(lanes((512, 128)) < 64, SCALE, 1.0)

    @pl.loop(0, parts)
    def _(b):
        rows = pl.ds(pl.multiple_of(b * 512, 512), 512)
        dkv[lax.div(b, 4), lax.rem(b, 4)] = (acc[rows, :] * weight).astype(bf16).reshape(2, 256, 128)

    mirror = flow.send(dqz.at[1], dq.at[1], mirror_sems[0], mirror_sems[1], p.mirror)
    dq[0] = dqz[0]
    first, second = {}, {}
    for d in ORDER:
        for h in range(2):
            to = lax.rem(p.fsp(h) + d, 4)
            src = dkv.at[to, :, 0] if h == 0 else dkv.at[:, to, 1]
            first[h, d] = flow.send(src, r1.at[h, d - 1], fs.at[h, d - 1], fr.at[h, d - 1], p.first(h, d))

    def total(h, b):
        at = spot(h, p.fsp(h), b)
        value = dkv[at[0], at[1], h].astype(f32)
        for d in range(3):
            value = value + r1[h, d, b].astype(f32)
        return value

    for h in range(2):
        for d in ORDER:
            first[h, d].wait_recv()
        for e in ORDER:
            send1[h, e - 1] = total(h, lax.rem(p.ssp(h) + e, 4)).astype(bf16)
            second[h, e] = flow.send(
                send1.at[h, e - 1], r2.at[h, e - 1], ss.at[h, e - 1], sr.at[h, e - 1], p.second(h, e)
            )
    out_gather.forward()
    for h in range(2):
        ff_back.second(1, h)
    for h in range(2):
        value = total(h, p.ssp(h))
        for e in ORDER:
            second[h, e].wait_recv()
            value = value + r2[h, e - 1].astype(f32)
        dkv_own[h] = value.astype(bf16)
    mirror.wait_recv()

    wide = lanes((512, 128))
    cosine, sine = cos_ref[...], sin_ref[...]

    def back(grad, proj, gain):
        grad = grad * cosine - turned(grad, wide) * sine
        scale = lax.rsqrt(head_sums(proj * proj, wide) * (1.0 / 64) + eps)
        scaled = grad * gain
        inner = head_sums(scaled * proj, wide) * (1.0 / 64)
        gains = jnp.sum(grad * proj * scale, axis=0, keepdims=True)
        return scale * scaled - proj * scale * scale * scale * inner, gains

    d_q, gq = back(dq[...].reshape(512, 128).astype(f32), qp_ref[...], twice(qg_ref[...]))
    dkv_in = dkv_own[...].reshape(512, 128).astype(f32)
    d_k, gk = back(dkv_in, kvp_ref[...], twice(kg_ref[...]))
    d_q = d_q.astype(bf16)
    d_kv = jnp.where(wide < 64, d_k, dkv_in).astype(bf16)
    wkv = jnp.concatenate([wk_ref[...], wv_ref[...]], axis=0)
    dn[...] = (nt(d_q, wq_ref[...]) + jnp.dot(d_kv, wkv, preferred_element_type=f32)).astype(bf16).reshape(8, 64, 1024)
    for zz in range(4):
        dn_sum.start_core(zz)
    normed = n_ref[...]
    gqkv[0] = tn(d_q, normed).astype(bf16).reshape(4, 32, 1024)
    gqkv[1] = tn(d_kv, normed).astype(bf16).reshape(4, 32, 1024)
    for i in range(3):
        sums.first(i)
    dn_sum.send_z()

    gains = jnp.zeros((1, 1024), f32)
    for w in range(8):
        base = tok_ref[w].astype(f32)
        gains = gains + jnp.sum(dn[w].astype(f32) * base * rms_of(base), axis=0, keepdims=True)
    vw[0, 0:1] = gains
    vw[0, 2:3] = jnp.concatenate([gq, gk, jnp.zeros((1, 768), f32)], axis=1)

    def vec_round(buf, devices, sends, recvs):
        return [
            flow.send(buf.at[0], buf.at[i + 1], sends.at[i], recvs.at[i], device) for i, device in enumerate(devices)
        ]

    def vec_total(buf, copies):
        value = buf[0]
        for i, copy in enumerate(copies):
            copy.wait_recv()
            value = value + buf[i + 1]
        return value

    round1 = vec_round(vw, [p.along_z(d) for d in ORDER] + [p.along_z_other(d) for d in ORDER] + [p.sibling], vs1, vr1)
    for h in range(2):
        ff_back.second(2, h)
    for i in range(3):
        sums.second(i)

    @pl.when(p.wt >= 4)
    def _():
        dmid_mirror.wait()

    @pl.when(p.wt < 4)
    def _():
        dmid_o[...] = dmid[...]

    for s in range(SPLIT):
        base = tok_ref[p.wt, sub(s)].astype(f32)
        d_normed = dn_sum.own(s)
        gt_ref[p.wt, sub(s)] = (
            dmid_o[sub(s)] + norm_back(base, rms_of(base), gain_in_ref[...], d_normed)
        ).astype(bf16)
        gt_gather.start(s)
    for i in range(3):
        for h in range(2):
            sums_back.put(i, h, sums.own(i, h).astype(bf16))
            sums_back.first(i, h)
    vx[0] = vec_total(vw, round1)
    round2 = vec_round(vx, [p.along_x(d) for d in ORDER], vs2, vr2)
    for i in range(3):
        for h in range(2):
            sums_back.second(i, h)
    vy[0] = vec_total(vx, round2)
    round3 = vec_round(vy, [p.along_y(d) for d in ORDER], vs3, vr3)
    gt_gather.forward()
    vec_ref[...] = vec_total(vy, round3)
    out_gather.arrived()
    gt_gather.arrived()
    for part in (d_mid_sum, da_gather, mlp_sum, out_gather, ff, ff_back, dn_sum, gt_gather, sums, sums_back, flow):
        part.finish()


def backward(parts, *args):
    rows = pltpu.VMEM
    wt_rows = [rows((4, 64, 1024), bf16), rows((3, 64, 1024), bf16), rows((3, 64, 1024), bf16)]
    wt_sum = wt_rows + WT_SEMS[:4]
    wt_gather = WT_SEMS[4:]
    half = rows((2, 256, 128), bf16)
    return comm_call(
        functools.partial(backward_kernel, parts), 4,
        (sds((8, 64, 1024), bf16), sds((8, 64, 1024), bf16), sds((3, 4, 32, 1024), bf16), sds((3, 4, 144, 1024), bf16),
         sds((8, 1024), f32)),
        args,
        [rows((8, 64, 1024), bf16), half, rows((64, 1024), f32), rows((64, 1024), f32), rows((64, 1024), bf16)] + [DMA] * 6
        + wt_sum + wt_gather + wt_sum + wt_gather
        + SpScatter.scratch(3, 144) + SpGather.sems(3)
        + [rows((512, 256), bf16), rows((8192, 128), f32), rows((64, 512), f32), half, half,
           rows((4, 4, 2, 256, 128), bf16), half]
        + [rows((2, 3, 4, 256, 128), bf16), rows((2, 3, 256, 128), bf16), rows((2, 3, 256, 128), bf16)]
        + [DMA((2, 3))] * 4
        + [rows((8, 64, 1024), bf16), rows((2, 4, 32, 1024), bf16), rows((4, 32, 1024), bf16)]
        + wt_sum + wt_gather
        + SpScatter.scratch(3, 32) + SpGather.sems(3)
        + [rows((8, 8, 1024), f32), rows((4, 8, 1024), f32), rows((4, 8, 1024), f32),
           DMA((7,)), DMA((7,)), DMA((3,)), DMA((3,)), DMA((3,)), DMA((3,))],
        "backward", 36,
    )


def finish_kernel(sums_ref, ff_ref, out_in, gt_in, vec_ref, out_ref, gt_ref, gq_ref, gk_ref, gv_ref, go_ref, gg_ref, gu_ref, gd_ref,
                  ni_ref, nm_ref, qg_ref, kg_ref, wide, tall, big, ff, sems, load_sems):
    copies = []

    def write(src, dst):
        copies.append(pltpu.make_async_copy(src, dst, sems.at[len(copies)]))
        copies[-1].start()

    write(out_in, out_ref)
    write(gt_in, gt_ref)
    loads = [pltpu.make_async_copy(ff_ref.at[i], ff.at[i], load_sems.at[i]) for i in range(3)]
    for load in loads:
        load.start()
    for i, ref in enumerate((gg_ref, gu_ref, gd_ref)):
        loads[i].wait()
        for part in range(2):
            rows = pl.ds(part * 288, 288)
            big[i, rows, :] = ff[i, rows, :].astype(f32)
            write(big.at[i, rows], ref.at[rows])
    wide[0] = sums_ref[0].astype(f32)
    wide[1] = sums_ref[2].astype(f32)
    write(wide.at[1, 0:64], gk_ref)
    write(wide.at[1, 64:128], gv_ref)
    write(wide.at[0], go_ref)
    tall[...] = sums_ref[1].astype(f32).T
    write(tall, gq_ref)
    ni_ref[...] = vec_ref[0:1, :]
    nm_ref[...] = vec_ref[1:2, :]
    qg_ref[...] = vec_ref[2:3, 0:64] + vec_ref[2:3, 64:128]
    kg_ref[...] = vec_ref[2:3, 128:192]
    for copy in copies:
        copy.wait()


def finish(sums, ff, output, grad_tokens, vec):
    hbm = pl.BlockSpec(memory_space=pl.ANY)
    rows = sds((576, 1024), f32)
    return pl.pallas_call(
        finish_kernel,
        out_shape=(sds((512, 1024), bf16), sds((512, 1024), bf16), sds((1024, 128), f32), sds((64, 1024), f32), sds((64, 1024), f32),
                   sds((128, 1024), f32), rows, rows, rows,
                   sds((1, 1024), f32), sds((1, 1024), f32), sds((1, 64), f32), sds((1, 64), f32)),
        in_specs=[vmem, hbm, vmem, vmem, vmem],
        out_specs=tuple([hbm] * 9 + [vmem] * 4),
        scratch_shapes=[pltpu.VMEM((2, 128, 1024), f32), pltpu.VMEM((1024, 128), f32), pltpu.VMEM((3, 576, 1024), f32), pltpu.VMEM((3, 576, 1024), bf16), DMA((12,)), DMA((3,))],
        compiler_params=pltpu.CompilerParams(vmem_limit_bytes=18 << 20),
        name="finish",
    )(sums, ff, output, grad_tokens, vec)


theta = 1000000.0


def body(tokens, norm_in, w_query, w_key, w_value, query_gain, key_gain, w_out, norm_mid, w_gate, w_up, w_down, cotangent, lengths):
    parts = lax.axis_size("sp")
    freqs = theta ** (-(np.arange(32).astype(np.float64) * 2.0) / 64)
    freqs = jnp.asarray(np.broadcast_to(freqs.astype(np.float32)[:, None], (32, 128)))
    qg, kg = query_gain.reshape(1, 64), key_gain.reshape(1, 64)
    wk, wv = w_key.T, w_value.T
    wide = sds((512, 128), f32)

    normed, q_proj, kv_proj, q, kv, cosine, sine = local_call(
        proj_kernel,
        (sds((512, 1024), bf16), wide, wide, sds((512, 128), bf16), sds((512, 128), bf16), wide, wide),
        (lengths, tokens, norm_in.reshape(1, 1024), w_query, wk, wv, qg, kg, freqs),
        "project", smem,
    )
    kv_all, ext, qa, mix_f, mixed, normed_mid, mid_own, cot = forward(
        parts, lengths, q, kv, tokens, cotangent, w_out, norm_mid
    )
    kv_all = kv_all.reshape(8192, 128)
    normed_mid = normed_mid.reshape(512, 1024)
    cotangent = cot.reshape(512, 1024)

    gate = jnp.dot(normed_mid, w_gate, preferred_element_type=f32)
    up_proj = jnp.dot(normed_mid, w_up, preferred_element_type=f32)
    sigmoid_gate = jax.nn.sigmoid(gate)
    act = (gate * sigmoid_gate * up_proj).astype(bf16)
    mlp_part = jnp.dot(act, w_down, preferred_element_type=f32).astype(bf16)
    d_act = jnp.einsum("td,fd->tf", cotangent, w_down, preferred_element_type=f32)
    d_gate = (d_act * up_proj * sigmoid_gate * (1.0 + gate * (1.0 - sigmoid_gate))).astype(bf16)
    d_up = (d_act * gate * sigmoid_gate).astype(bf16)
    d_mid_part = (
        jnp.einsum("tf,df->td", d_gate, w_gate, preferred_element_type=f32)
        + jnp.einsum("tf,df->td", d_up, w_up, preferred_element_type=f32)
    ).astype(bf16)
    grads = (
        jnp.einsum("tf,td->fd", d_gate, normed_mid, preferred_element_type=f32).astype(bf16),
        jnp.einsum("tf,td->fd", d_up, normed_mid, preferred_element_type=f32).astype(bf16),
        jnp.einsum("tf,td->fd", act, cotangent, preferred_element_type=f32).astype(bf16),
    )
    output, grad_tokens, sums, g_ff, vec = backward(
        parts,
        d_mid_part.reshape(8, 64, 1024), mlp_part.reshape(8, 64, 1024), mid_own, cot,
        norm_mid.reshape(1, 1024), w_out, *(g.reshape(4, 144, 1024) for g in grads),
        qa, mix_f, kv_all, ext, mixed,
        q_proj, kv_proj, normed, w_query, wk, wv, qg, kg, cosine, sine, tokens.reshape(8, 64, 1024), norm_in.reshape(1, 1024),
    )
    (output, grad_tokens, g_query, g_key, g_value, g_out, g_gate, g_up, g_down, g_norm_in, g_norm_mid, g_qg, g_kg) = finish(
        sums.reshape(3, 128, 1024), g_ff.reshape(3, 576, 1024), output.reshape(512, 1024), grad_tokens.reshape(512, 1024), vec
    )
    return (
        output, grad_tokens, g_norm_in.reshape(1024), g_query, g_key.T, g_value.T, g_qg.reshape(64), g_kg.reshape(64),
        g_out, g_norm_mid.reshape(1024), g_gate.T, g_up.T, g_down,
    )


def solution(mesh):
    placed = (
        P("sp", None), P(), P(None, "wt"), P(None, "wt"), P(None, "wt"), P(), P(), P("wt", None), P(),
        P(None, "wt"), P(None, "wt"), P("wt", None), P("sp", None), P(),
    )
    return jax.shard_map(
        body,
        mesh=mesh,
        in_specs=placed,
        out_specs=(
            P("sp", None), P("sp", None), P(), P(None, "wt"), P(None, "wt"), P(None, "wt"), P(), P(),
            P("wt", None), P(), P(None, "wt"), P(None, "wt"), P("wt", None),
        ),
        check_vma=False,
    )
```

```python
import functools, math
import jax
import jax.numpy as jnp
import numpy as np
from jax import lax
from jax.experimental import pallas as pl
from jax.experimental.pallas import tpu as pltpu
from jax.sharding import PartitionSpec as P

f32 = jnp.float32
bf16 = jnp.bfloat16
sds = jax.ShapeDtypeStruct
DMA = pltpu.SemaphoreType.DMA
CH = 512
HALF = 256
SCALE = 0.125
C2 = SCALE * math.log2(math.e)


def starts_of(ids, len_ref):
    end = jnp.int32(0)
    start = jnp.zeros_like(ids)
    for j in range(4):
        end = end + len_ref[j]
        start = start + jnp.where(ids >= end, len_ref[j], 0)
    return start


def scalar_start(row, len_ref):
    end = jnp.int32(0)
    start = jnp.int32(0)
    for j in range(4):
        end = end + len_ref[j]
        start = start + jnp.where(row >= end, len_ref[j], 0)
    return start


def lanes(shape):
    return lax.broadcasted_iota(jnp.int32, shape, len(shape) - 1)


def split3(value, lane):
    hi = value.astype(bf16).astype(f32)
    rest = value - hi
    mid = rest.astype(bf16).astype(f32)
    low = rest - mid
    return jnp.where(lane == 0, hi, jnp.where(lane == 1, mid, jnp.where(lane == 2, low, 0.0)))


def tile_row(me, t, parts):
    return me * 512 if t == 0 else (parts - 1 - me) * 512 + HALF


FAR = 8192.0


def segment_bounds(len_ref, lane):
    begin = jnp.zeros_like(lane)
    end = jnp.zeros_like(lane)
    at = jnp.int32(0)
    for j in range(4):
        begin = jnp.where(lane == 3 + j, at, begin)
        at = at + len_ref[j]
        end = jnp.where(lane == 3 + j, at, end)
    return begin, end


def inside(ids, len_ref, shape):
    lane = lanes(shape)
    begin, end = segment_bounds(len_ref, lane)
    return (ids >= begin) & (ids < end), lane


def key_columns(k0, len_ref, rows):
    ids = k0 + lax.broadcasted_iota(jnp.int32, (rows, 128), 0)
    within, lane = inside(ids, len_ref, (rows, 128))
    return jnp.where(lane < 3, 1.0, jnp.where(within, 1.0, 0.0)).astype(bf16)


def query_columns(r0, len_ref, rows):
    ids = r0 + lax.broadcasted_iota(jnp.int32, (rows, 128), 0)
    within, lane = inside(ids, len_ref, (rows, 128))
    return jnp.where((lane < 3) | (lane > 6) | within, 0.0, -FAR)


smem = pl.BlockSpec(memory_space=pltpu.SMEM)
vmem = pl.BlockSpec(memory_space=pltpu.VMEM)


MESH = pl.DeviceIdType.MESH
eps = 1e-05


def rcopy(src, dst, send, recv, device):
    return pltpu.make_async_remote_copy(
        src_ref=src, dst_ref=dst, send_sem=send, recv_sem=recv, device_id=device, device_id_type=MESH
    )


def meet(devices):
    barrier = pltpu.get_barrier_semaphore()
    for device in devices:
        pl.semaphore_signal(barrier, inc=1, device_id=device, device_id_type=MESH)
    pl.semaphore_wait(barrier, len(devices))


class Place:
    def __init__(self):
        self.sp = lax.axis_index("sp")
        self.wt = lax.axis_index("wt")
        self.x, self.y = lax.div(self.sp, 4), lax.rem(self.sp, 4)
        self.z, self.c = lax.div(self.wt, 2), lax.rem(self.wt, 2)
        self.mirror = (15 - self.sp, self.wt)
        self.sibling = (self.sp, self.z * 2 + 1 - self.c)

    def along_x(self, d):
        return (lax.rem(self.x + d, 4) * 4 + self.y, self.wt)

    def along_y(self, d):
        return (self.x * 4 + lax.rem(self.y + d, 4), self.wt)

    def along_z(self, d):
        return (self.sp, lax.rem(self.z + d, 4) * 2 + self.c)

    def along_z_other(self, d):
        return (self.sp, lax.rem(self.z + d, 4) * 2 + 1 - self.c)

    def first(self, h, d):
        return self.along_x(d) if h == 0 else self.along_y(d)

    def second(self, h, d):
        return self.along_y(d) if h == 0 else self.along_x(d)

    def fsp(self, h):
        return self.x if h == 0 else self.y

    def ssp(self, h):
        return self.y if h == 0 else self.x


def spot(h, first, second):
    return (first, second) if h == 0 else (second, first)


ORDER = (2, 1, 3)


class SpScatter:
    def __init__(self, p, srcs, rows, refs):
        self.p, self.srcs, self.rows = p, srcs, rows
        self.ra, self.rb, self.send, self.r2, self.fs, self.fr, self.ss, self.sr = refs
        self.one, self.two = {}, {}

    @staticmethod
    def scratch(n, rows):
        return [
            pltpu.VMEM((n, 3, rows, 512), bf16), pltpu.VMEM((n, 3, 4, rows, 128), bf16),
            pltpu.VMEM((n, 2, 3, rows, 128), bf16), pltpu.VMEM((n, 2, 3, rows, 128), bf16),
            DMA((n, 2, 3)), DMA((n, 2, 3)), DMA((n, 2, 3)), DMA((n, 2, 3)),
        ]

    def first(self, i):
        p = self.p
        for d in ORDER:
            to = lax.rem(p.x + d, 4)
            self.one[i, 0, d] = rcopy(
                self.srcs[i].at[to, :, pl.ds(0, 512)], self.ra.at[i, d - 1],
                self.fs.at[i, 0, d - 1], self.fr.at[i, 0, d - 1], p.along_x(d),
            )
            self.one[i, 0, d].start()
            to = lax.rem(p.y + d, 4)
            self.one[i, 1, d] = rcopy(
                self.srcs[i].at[:, :, pl.ds(columns_at(1, to), 128)], self.rb.at[i, d - 1],
                self.fs.at[i, 1, d - 1], self.fr.at[i, 1, d - 1], p.along_y(d),
            )
            self.one[i, 1, d].start()

    def part(self, i, h, b):
        p = self.p
        if h == 0:
            value = self.srcs[i][p.x, :, pl.ds(columns_at(0, b), 128)].astype(f32)
            for d in range(3):
                value = value + self.ra[i, d, :, pl.ds(columns_at(0, b), 128)].astype(f32)
            return value
        value = self.srcs[i][b, :, pl.ds(columns_at(1, p.y), 128)].astype(f32)
        for d in range(3):
            value = value + self.rb[i, d, b].astype(f32)
        return value

    def second(self, i):
        p = self.p
        for h in range(2):
            for d in ORDER:
                self.one[i, h, d].wait_recv()
            for e in ORDER:
                self.send[i, h, e - 1] = self.part(i, h, lax.rem(p.ssp(h) + e, 4)).astype(bf16)
                self.two[i, h, e] = rcopy(
                    self.send.at[i, h, e - 1], self.r2.at[i, h, e - 1],
                    self.ss.at[i, h, e - 1], self.sr.at[i, h, e - 1], p.second(h, e),
                )
                self.two[i, h, e].start()

    def own(self, i, h):
        value = self.part(i, h, self.p.ssp(h))
        for e in ORDER:
            self.two[i, h, e].wait_recv()
            value = value + self.r2[i, h, e - 1].astype(f32)
        return value

    def finish(self):
        for copy in list(self.one.values()) + list(self.two.values()):
            copy.wait_send()


def columns_at(h, b):
    return pl.multiple_of(h * 512 + b * 128, 128)


class SpGather:
    def __init__(self, p, out, rows, sems):
        self.p, self.out, self.rows = p, out, rows
        self.fs, self.fr, self.ss, self.sr = sems
        self.one, self.two = {}, {}

    @staticmethod
    def sems(n):
        return [DMA((n, 2, 3)) for _ in range(4)]

    def spot(self, h):
        p = self.p
        return p.x, pl.ds(columns_at(h, p.y), 128)

    def put(self, i, h, value):
        x, columns = self.spot(h)
        self.out[i, x, :, columns] = value

    def first(self, i, h):
        x, columns = self.spot(h)
        block = self.out.at[i, x, :, columns]
        for e in ORDER:
            self.one[i, h, e] = rcopy(
                block, block, self.fs.at[i, h, e - 1], self.fr.at[i, h, e - 1], self.p.second(h, e)
            )
            self.one[i, h, e].start()

    def second(self, i, h):
        x, columns = self.spot(h)
        for e in ORDER:
            self.one[i, h, e].wait_recv()
        block = self.out.at[i, x, :, pl.ds(0, 512)] if h == 0 else self.out.at[i, :, :, columns]
        for d in ORDER:
            self.two[i, h, d] = rcopy(
                block, block, self.ss.at[i, h, d - 1], self.sr.at[i, h, d - 1], self.p.first(h, d)
            )
            self.two[i, h, d].start()

    def arrived(self, i):
        for h in range(2):
            for d in ORDER:
                self.two[i, h, d].wait_recv()

    def finish(self):
        for copy in self.one.values():
            copy.wait_send()
        for copy in self.two.values():
            copy.wait()


SPLIT = 2


def sub(s):
    return pl.ds(s * (64 // SPLIT), 64 // SPLIT)


class WtSum:
    def __init__(self, p, part, sib, send, rz, sems):
        self.p, self.part, self.sib, self.send, self.rz = p, part, sib, send, rz
        self.cs, self.cr, self.zs, self.zr = sems
        self.second = {}

    def core(self, zz, s):
        return rcopy(
            self.part.at[zz * 2 + 1 - self.p.c, sub(s)], self.sib.at[zz, sub(s)],
            self.cs.at[zz, s], self.cr.at[zz, s], self.p.sibling,
        )

    def start_core(self, zz):
        for s in range(SPLIT):
            self.core(zz, s).start()

    def pair(self, zz, s):
        return self.part[zz * 2 + self.p.c, sub(s)].astype(f32) + self.sib[zz, sub(s)].astype(f32)

    def send_z(self):
        for s in range(SPLIT):
            for d in ORDER:
                zz = lax.rem(self.p.z + d, 4)
                self.core(zz, s).wait_recv()
                self.send[d - 1, sub(s)] = self.pair(zz, s).astype(bf16)
                copy = rcopy(
                    self.send.at[d - 1, sub(s)], self.rz.at[d - 1, sub(s)],
                    self.zs.at[d - 1, s], self.zr.at[d - 1, s], self.p.along_z(d),
                )
                copy.start()
                self.second[d, s] = copy

    def own(self, s):
        self.core(self.p.z, s).wait_recv()
        value = self.pair(self.p.z, s)
        for d in (1, 3, 2):
            self.second[d, s].wait_recv()
            value = value + self.rz[d - 1, sub(s)].astype(f32)
        return value

    def finish(self):
        for zz in range(4):
            for s in range(SPLIT):
                self.core(zz, s).wait_send()
        for copy in self.second.values():
            copy.wait_send()


class WtGather:
    def __init__(self, p, out, sems):
        self.p, self.out = p, out
        self.zs, self.zr, self.gs, self.gr = sems
        self.far, self.near = {}, {}

    def start(self, s):
        p = self.p
        block = self.out.at[p.wt, sub(s)]
        for d in ORDER:
            self.far[d, s] = rcopy(block, block, self.zs.at[d - 1, s], self.zr.at[d - 1, s], p.along_z(d))
            self.far[d, s].start()
        self.pass_on(0, s)

    def pass_on(self, slot, s):
        p = self.p
        block = self.out.at[lax.rem(p.z + 4 - slot, 4) * 2 + p.c, sub(s)]
        self.near[slot, s] = rcopy(block, block, self.gs.at[slot, s], self.gr.at[slot, s], p.sibling)
        self.near[slot, s].start()

    def forward(self):
        for s in range(SPLIT):
            for d in (1, 3, 2):
                self.far[d, s].wait_recv()
                self.pass_on(d, s)

    def arrived(self):
        for copy in self.near.values():
            copy.wait_recv()

    def finish(self):
        for copy in list(self.far.values()) + list(self.near.values()):
            copy.wait_send()


def rms_of(value):
    return lax.rsqrt(jnp.mean(value * value, axis=-1, keepdims=True) + eps)


def norm_back(values, scale, gain, grad):
    scaled = grad * gain
    inner = jnp.mean(scaled * values, axis=-1, keepdims=True)
    return scale * scaled - values * scale * scale * scale * inner


def wt_peers(p):
    return [p.sibling] + [p.along_z(d) for d in ORDER]


class Flow:
    def __init__(self):
        self.copies = []

    def send(self, *args):
        copy = rcopy(*args)
        copy.start()
        self.copies.append(copy)
        return copy

    def finish(self):
        for copy in self.copies:
            copy.wait_send()


def forward_kernel(
    parts,
    len_ref, q_ref, kv_ref, tok_ref, cot_ref, w_ref, pack_ref,
    all_ref, ext_ref, qa_ref, mixf_ref, mix_ref, nm_ref, mid_ref, cotz_ref,
    qz, base, acc, part, sib, send, rz, ms, mr, cs, cr, zs, zr, az, bz, ag, bg, fs, fr, ss, sr,
):
    p = Place()
    me = p.sp
    meet(wt_peers(p) + [p.along_x(d) for d in ORDER] + [p.along_y(d) for d in ORDER] + [p.mirror])
    flow = Flow()
    first = {}
    for d in ORDER:
        for h in range(2):
            first[h, d] = flow.send(
                kv_ref.at[h], all_ref.at[p.x, p.y, h], fs.at[h, d - 1], fr.at[h, d - 1], p.first(h, d)
            )
    q_mirror = flow.send(q_ref.at[1], qz.at[1], ms.at[0], mr.at[0], p.mirror)

    def pass_on(h, slot):
        a = lax.rem(p.fsp(h) + 4 - slot, 4)
        at = spot(h, a, p.ssp(h))
        for e in ORDER:
            src = kv_ref.at[h] if slot == 0 else all_ref.at[at[0], at[1], h]
            flow.send(src, all_ref.at[at[0], at[1], h], ss.at[h, slot, e - 1], sr.at[h, slot, e - 1], p.second(h, e))

    for h in range(2):
        pass_on(h, 0)
    token_mirror = rcopy(tok_ref.at[p.wt], base, ms.at[1], mr.at[1], p.mirror)

    @pl.when(p.wt >= 4)
    def _():
        token_mirror.start()

    @pl.when(p.wt < 4)
    def _():
        base[...] = tok_ref[p.wt]

    all_ref[p.x, p.y] = kv_ref[...]
    qz[0] = q_ref[0]
    cotz_ref[0:4] = cot_ref[0:4]

    @pl.loop(0, 8)
    def _(b):
        rows = pl.ds(pl.multiple_of(b * 1024, 1024), 1024)
        ext_ref[rows, :] = key_columns(b * 1024, len_ref, 1024)

    lane = lanes((HALF, 128))
    lane2 = lanes((2 * HALF, 128))
    lanek = lanes((CH, 128))
    acc[...] = jnp.zeros_like(acc)
    blocks = (me, parts - 1 - me)
    begins = (me * 512, (parts - 1 - me) * 512 + HALF)

    def prepare(t):
        q = qz[t].astype(f32)
        qa_ref[t, 0:HALF, 0:128] = jnp.where(lane < 64, q, 0.0).astype(bf16)
        qa_ref[t, HALF:, 0:128] = jnp.where(lane < 64, pltpu.roll(q, 64, 1), 0.0).astype(bf16)
        columns = query_columns(begins[t], len_ref, HALF).astype(bf16)
        qa_ref[t, 0:HALF, 128:256] = columns
        qa_ref[t, HALF:, 128:256] = columns

    def step(t, x, y, masked):
        k0 = pl.multiple_of((x * 4 + y) * CH, CH)
        kv = all_ref[x, y].reshape(CH, 128)
        kva = jnp.concatenate([kv, ext_ref[pl.ds(k0, CH), :]], axis=1)
        pr = jnp.exp2(nt(qa_ref[t], kva) * C2)
        if masked:
            rows = begins[t] + lax.rem(lax.broadcasted_iota(jnp.int32, (2 * HALF, 1), 0), HALF)
            keys = k0 + lax.broadcasted_iota(jnp.int32, (2 * HALF, CH), 1)
            pr = jnp.where(keys <= rows, pr, 0.0)
        ones = jnp.where(lanek < 64, jnp.ones_like(kv), kv)
        acc[t] += jnp.dot(pr.astype(bf16), ones, preferred_element_type=f32)

    def both(x, y):
        block = x * 4 + y

        @pl.when(block < blocks[0])
        def _():
            step(0, x, y, False)

        @pl.when(block < blocks[1])
        def _():
            step(1, x, y, False)

        @pl.when(block == blocks[1])
        def _():
            step(1, x, y, True)

    prepare(0)
    step(0, p.x, p.y, True)
    for d in (1, 3, 2):
        for h in range(2):
            first[h, d].wait_recv()
            pass_on(h, d)
    q_mirror.wait_recv()
    prepare(1)

    @pl.when(me < blocks[1])
    def _():
        step(1, p.x, p.y, False)

    def wait_for(x, y, h, slot, e):
        block = all_ref.at[x, y, h]
        rcopy(block, block, ss.at[h, slot, e - 1], sr.at[h, slot, e - 1], p.second(h, 1)).wait_recv()

    @pl.loop(1, 4)
    def _(d):
        x = lax.rem(p.x + 4 - d, 4)
        wait_for(x, p.y, 1, 0, d)
        both(x, p.y)

    @pl.loop(1, 4)
    def _(d):
        y = lax.rem(p.y + 4 - d, 4)
        wait_for(p.x, y, 0, 0, d)
        both(p.x, y)

    @pl.loop(0, 9)
    def _(k):
        dx, dy = 1 + lax.div(k, 3), 1 + lax.rem(k, 3)
        x, y = lax.rem(p.x + 4 - dx, 4), lax.rem(p.y + 4 - dy, 4)
        wait_for(x, y, 0, dx, dy)
        wait_for(x, y, 1, dy, dx)
        both(x, y)

    total = WtSum(p, part, sib, send, rz, (cs, cr, zs, zr))
    cot_mirror = flow.send(cot_ref.at[pl.ds(4, 4)], cotz_ref.at[pl.ds(4, 4)], ms.at[2], mr.at[2], p.mirror)
    for t in range(2):
        value = acc[t]
        swapped = pltpu.roll(value, 64, 1)
        o = swapped / value
        mix = jnp.where(lane < 64, o[:HALF], pltpu.roll(o[HALF:], 64, 1))
        mixf_ref[t] = mix
        mix = mix.astype(bf16)
        mix_ref[t] = mix
        part[t * 4:t * 4 + 4] = jnp.dot(mix, w_ref[...], preferred_element_type=f32).astype(bf16).reshape(4, 64, 1024)
        for zz in (t * 2, t * 2 + 1):
            total.start_core(zz)
    total.send_z()
    for t in range(2):
        value = acc[t]
        weights = jnp.where(lane2 < 64, value, pltpu.roll(value, 64, 1))
        columns = qa_ref[t, :, 128:256].astype(f32)
        qa_ref[t, :, 128:256] = (split3(jnp.log(weights) * (-1.0 / SCALE), lane2) + columns).astype(bf16)

    @pl.when(p.wt >= 4)
    def _():
        token_mirror.wait()

    spread = WtGather(p, nm_ref, (az, bz, ag, bg))
    for s in range(SPLIT):
        middle = base[sub(s)].astype(f32) + total.own(s)
        mid_ref[sub(s)] = middle
        nm_ref[p.wt, sub(s)] = (middle * rms_of(middle) * pack_ref[1:2]).astype(bf16)
        spread.start(s)
    spread.forward()
    cot_mirror.wait_recv()
    spread.arrived()
    for part in (spread, total, flow):
        part.finish()


WT_SEMS = [DMA((n, SPLIT)) for n in (4, 4, 3, 3, 3, 3, 4, 4)]


def comm_call(kernel, number, out_shape, args, scratch, name, limit=10, first=None):
    return pl.pallas_call(
        kernel,
        out_shape=out_shape,
        in_specs=[first or vmem] + [vmem] * (len(args) - 1),
        out_specs=tuple(vmem for _ in out_shape),
        scratch_shapes=scratch,
        compiler_params=pltpu.CompilerParams(
            collective_id=number, has_side_effects=True, vmem_limit_bytes=limit << 20
        ),
        cost_estimate=pl.CostEstimate(flops=8 << 30, bytes_accessed=32 << 20, transcendentals=0),
        name=name,
    )(*args)


def forward(parts, lengths, q, kv, tokens, cotangent, w_out, pack):
    rows = pltpu.VMEM
    half = sds((2, 256, 128), bf16)
    full = sds((8, 64, 1024), bf16)
    return comm_call(
        functools.partial(forward_kernel, parts), 1,
        (sds((4, 4, 2, 256, 128), bf16), sds((8192, 128), bf16), sds((2, 512, 256), bf16), sds((2, 256, 128), f32),
         half, full, sds((64, 1024), f32), full),
        (lengths, q.reshape(2, 256, 128), kv.reshape(2, 256, 128), tokens.reshape(8, 64, 1024),
         cotangent.reshape(8, 64, 1024), w_out, pack),
        [rows((2, 256, 128), bf16), rows((64, 1024), bf16), rows((2, 512, 128), f32), rows((8, 64, 1024), bf16),
         rows((4, 64, 1024), bf16), rows((3, 64, 1024), bf16), rows((3, 64, 1024), bf16), DMA((3,)), DMA((3,))]
        + WT_SEMS + [DMA((2, 3)), DMA((2, 3)), DMA((2, 4, 3)), DMA((2, 4, 3))],
        "forward", 16, smem,
    )


def turned(value, lane):
    return jnp.where(lax.rem(lane, 64) < 32, pltpu.roll(value, 96, 1), pltpu.roll(value, 32, 1))


def head_sums(value, lane):
    s0 = jnp.sum(jnp.where(lane < 64, value, 0.0), axis=1, keepdims=True)
    s1 = jnp.sum(jnp.where(lane < 64, 0.0, value), axis=1, keepdims=True)
    return jnp.where(lane < 64, s0, s1)


def nt(a, b):
    return lax.dot_general(a, b, (((1,), (1,)), ((), ())), preferred_element_type=f32)


def tn(a, b):
    return lax.dot_general(a, b, (((0,), (0,)), ((), ())), preferred_element_type=f32)


FREQS = [float(np.float32(1000000.0 ** (-2.0 * i / 64))) for i in range(32)]


def proj_kernel(len_ref, tok_ref, pack_ref, wq_ref, wkv_ref, n_ref, qp_ref, kvp_ref, q_ref, kv_ref, cos_ref, sin_ref):
    lane = lanes((512, 128))
    ids = lax.axis_index("sp") * 512 + lax.broadcasted_iota(jnp.int32, (1, 512), 1)
    positions = (ids - starts_of(ids, len_ref)).astype(f32)
    row = lax.broadcasted_iota(jnp.int32, (32, 512), 0)
    freqs = jnp.zeros((32, 512), f32)
    for i, freq in enumerate(FREQS):
        freqs = jnp.where(row == i, freq, freqs)
    angles = positions * freqs
    cosine, sine = jnp.cos(angles), jnp.sin(angles)
    cosine = jnp.concatenate([cosine] * 4, axis=0).T
    sine = jnp.concatenate([-sine, sine, -sine, sine], axis=0).T
    cos_ref[...] = cosine
    sin_ref[...] = sine
    base = tok_ref[...].astype(f32)
    normed = (base * rms_of(base) * pack_ref[0:1]).astype(bf16)
    n_ref[...] = normed
    q = jnp.dot(normed, wq_ref[...], preferred_element_type=f32)
    qp_ref[...] = q
    q = q * lax.rsqrt(head_sums(q * q, lane) * (1.0 / 64) + eps) * pack_ref[2:3, 0:128]
    q_ref[...] = (q * cosine + turned(q, lane) * sine).astype(bf16)
    kv = nt(normed, wkv_ref[...])
    kvp_ref[...] = kv
    k = kv * lax.rsqrt(head_sums(kv * kv, lane) * (1.0 / 64) + eps) * pack_ref[2:3, 128:256]
    k = k * cosine + turned(k, lane) * sine
    kv_ref[...] = jnp.where(lane < 64, k, kv).astype(bf16)


def project(*args):
    wide = sds((512, 128), f32)
    out_shape = (sds((512, 1024), bf16), wide, wide, sds((512, 128), bf16), sds((512, 128), bf16), wide, wide)
    return pl.pallas_call(
        proj_kernel,
        out_shape=out_shape,
        in_specs=[smem] + [vmem] * 4,
        out_specs=tuple(vmem for _ in out_shape),
        compiler_params=pltpu.CompilerParams(vmem_limit_bytes=12 << 20),
        name="project",
    )(*args)


def backward_kernel(
    parts,
    dm_ref, mlp_ref, mid_ref, cot_ref, pack_ref, w_ref, g0_ref, g1_ref, g2_ref,
    qa_ref, mixf_ref, kv_ref, ext_ref, mixed_ref,
    qp_ref, kvp_ref, n_ref, wq_ref, wkv_ref, cos_ref, sin_ref, tok_ref,
    out_ref, gt_ref, sums_ref, ff_ref, vec_ref,
    *scratch,
):
    scratch = list(scratch)

    def take(n):
        got = scratch[:n]
        del scratch[:n]
        return got

    p = Place()
    me = p.sp
    meet(
        wt_peers(p) + [p.along_z_other(d) for d in ORDER] + [p.mirror]
        + [p.along_x(d) for d in ORDER] + [p.along_y(d) for d in ORDER]
    )
    flow = Flow()

    def wt_sum(ref):
        sib, send, rz = take(3)
        return WtSum(p, ref, sib, send, rz, take(4))

    da, dz, dmid, dmid_o, out_own = take(5)
    mirror_sems = take(6)
    d_mid_sum = wt_sum(dm_ref)
    da_gather = WtGather(p, da, take(4))
    mlp_sum = wt_sum(mlp_ref)
    out_gather = WtGather(p, out_ref, take(4))
    ff = SpScatter(p, (g0_ref, g1_ref, g2_ref), 144, take(8))
    ff_back = SpGather(p, ff_ref, 144, take(4))
    dab, acc, dqt, dqz, dq, dkv, dkv_own = take(7)
    r1, send1, r2, fs, fr, ss, sr = take(7)
    dn, gqkv, gout = take(3)
    dn_sum = wt_sum(dn)
    gt_gather = WtGather(p, gt_ref, take(4))
    sums = SpScatter(p, (gout, gqkv.at[0], gqkv.at[1]), 32, take(8))
    sums_back = SpGather(p, sums_ref, 32, take(4))
    vw, vx, vy, vs1, vr1, vs2, vr2, vs3, vr3 = take(9)
    assert not scratch

    for zz in range(4):
        d_mid_sum.start_core(zz)
    for i in range(3):
        ff.first(i)
    d_mid_sum.send_z()
    vw[0] = jnp.zeros((8, 1024), f32)
    acc[...] = jnp.zeros_like(acc)
    dqt[...] = jnp.zeros_like(dqt)
    for s in range(SPLIT):
        middle = mid_ref[sub(s)]
        scale = rms_of(middle)
        d_mid = d_mid_sum.own(s)
        d_middle = cot_ref[p.wt, sub(s)].astype(f32) + norm_back(middle, scale, pack_ref[1:2], d_mid)
        da[p.wt, sub(s)] = d_middle.astype(bf16)
        da_gather.start(s)
        dmid[sub(s)] = d_middle
        vw[0, 1:2] += jnp.sum(d_mid * middle * scale, axis=0, keepdims=True)
    dmid_mirror = rcopy(dmid, dmid_o, mirror_sems[2], mirror_sems[3], p.mirror)

    @pl.when(p.wt >= 4)
    def _():
        dmid_mirror.start()

    da_gather.forward()
    da_gather.arrived()
    for zz in range(4):
        mlp_sum.start_core(zz)
    dz[...] = nt(da[...].reshape(512, 1024), w_ref[...]).astype(bf16).reshape(2, 256, 128)
    mlp_sum.send_z()

    lane = lanes((HALF, 128))
    for t in range(2):
        do = dz[t].astype(f32)
        prod = do * mixf_ref[t]
        d0 = -jnp.sum(jnp.where(lane < 64, prod, 0.0), axis=1, keepdims=True)
        d1 = -jnp.sum(jnp.where(lane < 64, 0.0, prod), axis=1, keepdims=True)
        dab[t, 0:HALF, 0:128] = jnp.where(lane < 64, 0.0, pltpu.roll(do, 64, 1)).astype(bf16)
        dab[t, HALF:, 0:128] = jnp.where(lane < 64, 0.0, do).astype(bf16)
        dab[t, 0:HALF, 128:256] = split3(jnp.broadcast_to(d0, (HALF, 128)), lane).astype(bf16)
        dab[t, HALF:, 128:256] = split3(jnp.broadcast_to(d1, (HALF, 128)), lane).astype(bf16)
    upper_long = (me < parts // 2).astype(jnp.int32)
    blocks = [me + t * (parts - 1 - 2 * me) for t in (upper_long, 1 - upper_long)]

    def step(k, masked):
        short = (k > blocks[0]).astype(jnp.int32)
        t = upper_long + short * (1 - 2 * upper_long)
        c = k - short * (blocks[0] + 1)
        k0 = pl.multiple_of(c * CH, CH)
        kv = kv_ref[pl.ds(k0, CH), :]
        kva = jnp.concatenate([kv, ext_ref[pl.ds(k0, CH), :]], axis=1)
        qa = qa_ref[t]
        d_out = dab[t]
        pr = jnp.exp2(nt(kva, qa) * C2)
        if masked:
            r0 = c * 512 + t * HALF
            rows = r0 + lax.rem(lax.broadcasted_iota(jnp.int32, (1, 2 * HALF), 1), HALF)
            keys = k0 + lax.broadcasted_iota(jnp.int32, (CH, 2 * HALF), 0)
            pr = jnp.where(keys <= rows, pr, 0.0)
        ds = (pr * nt(kva, d_out)).astype(bf16)
        acc[pl.ds(k0, CH), :] += jnp.dot(
            pr.astype(bf16), d_out[:, 0:128], preferred_element_type=f32
        ) + jnp.dot(ds, qa[:, 0:128], preferred_element_type=f32)
        kt = kv.T[0:64, :]
        dqt[t] += jnp.dot(kt, ds, preferred_element_type=f32)

    def plain(k):
        step(k, False)

    def either(k):
        pl.when(k == blocks[0])(lambda: step(k, True))
        pl.when(k != blocks[0])(lambda: step(k, False))

    ff.second(0)
    ff.second(1)
    pl.loop(0, 3)(plain)
    ff.second(2)
    pl.loop(3, 6)(plain)
    for i in range(3):
        for h in range(2):
            ff_back.put(i, h, ff.own(i, h).astype(bf16))
            ff_back.first(i, h)
    pl.loop(6, 8)(plain)
    for s in range(SPLIT):
        out_own[sub(s)] = (mid_ref[sub(s)] + mlp_sum.own(s)).astype(bf16)
    out_mirror = rcopy(out_own, out_ref.at[p.wt], mirror_sems[4], mirror_sems[5], p.mirror)

    @pl.when(p.wt >= 4)
    def _():
        out_mirror.start()

    @pl.when(p.wt < 4)
    def _():
        out_ref[p.wt] = out_own[...]

    gout[...] = tn(mixed_ref[...].reshape(512, 128), da[...].reshape(512, 1024)).astype(bf16).reshape(4, 32, 1024)
    sums.first(0)
    pl.loop(8, 12)(either)
    for h in range(2):
        ff_back.second(0, h)
    sums.second(0)

    @pl.when(p.wt >= 4)
    def _():
        out_mirror.wait()

    for s in range(SPLIT):
        out_gather.start(s)
    pl.loop(12, 16)(either)
    step(16, True)
    for t in range(2):
        both = jnp.concatenate([dqt[t, :, :HALF], dqt[t, :, HALF:]], axis=0)
        dqz[t] = (both.T * SCALE).astype(bf16)
    weight = jnp.where(lanes((512, 128)) < 64, SCALE, 1.0)

    @pl.loop(0, parts)
    def _(b):
        rows = pl.ds(pl.multiple_of(b * 512, 512), 512)
        dkv[lax.div(b, 4), lax.rem(b, 4)] = (acc[rows, :] * weight).astype(bf16).reshape(2, 256, 128)

    mirror = flow.send(dqz.at[1], dq.at[1], mirror_sems[0], mirror_sems[1], p.mirror)
    dq[0] = dqz[0]
    first, second = {}, {}
    for e in (2, 1, 3, 0):
        for d in ORDER:
            for h in range(2):
                at = spot(h, lax.rem(p.fsp(h) + d, 4), lax.rem(p.ssp(h) + e, 4))
                first[h, d, e] = flow.send(
                    dkv.at[at[0], at[1], h], r1.at[h, d - 1, e], fs.at[h, d - 1, e], fr.at[h, d - 1, e], p.first(h, d)
                )

    def total(h, e):
        at = spot(h, p.fsp(h), lax.rem(p.ssp(h) + e, 4))
        value = dkv[at[0], at[1], h].astype(f32)
        for d in ORDER:
            first[h, d, e].wait_recv()
            value = value + r1[h, d - 1, e].astype(f32)
        return value

    out_gather.forward()
    for e in ORDER:
        for h in range(2):
            send1[h, e - 1] = total(h, e).astype(bf16)
            second[h, e] = flow.send(
                send1.at[h, e - 1], r2.at[h, e - 1], ss.at[h, e - 1], sr.at[h, e - 1], p.second(h, e)
            )
    own = [total(h, 0) for h in range(2)]
    for h in range(2):
        ff_back.second(1, h)
        sums_back.put(0, h, sums.own(0, h).astype(bf16))
        sums_back.first(0, h)
    for h in range(2):
        value = own[h]
        for e in ORDER:
            second[h, e].wait_recv()
            value = value + r2[h, e - 1].astype(f32)
        dkv_own[h] = value.astype(bf16)
    mirror.wait_recv()

    wide = lanes((512, 128))
    cosine, sine = cos_ref[...], sin_ref[...]

    def back(grad, proj, gain):
        grad = grad * cosine - turned(grad, wide) * sine
        scale = lax.rsqrt(head_sums(proj * proj, wide) * (1.0 / 64) + eps)
        scaled = grad * gain
        inner = head_sums(scaled * proj, wide) * (1.0 / 64)
        gains = jnp.sum(grad * proj * scale, axis=0, keepdims=True)
        return scale * scaled - proj * scale * scale * scale * inner, gains

    d_q, gq = back(dq[...].reshape(512, 128).astype(f32), qp_ref[...], pack_ref[2:3, 0:128])
    dkv_in = dkv_own[...].reshape(512, 128).astype(f32)
    d_k, gk = back(dkv_in, kvp_ref[...], pack_ref[2:3, 128:256])
    d_q = d_q.astype(bf16)
    d_kv = jnp.where(wide < 64, d_k, dkv_in).astype(bf16)
    dn[...] = (nt(d_q, wq_ref[...]) + jnp.dot(d_kv, wkv_ref[...], preferred_element_type=f32)).astype(bf16).reshape(8, 64, 1024)
    for zz in range(4):
        dn_sum.start_core(zz)
    normed = n_ref[...]
    gqkv[0] = tn(d_q, normed).astype(bf16).reshape(4, 32, 1024)
    gqkv[1] = tn(d_kv, normed).astype(bf16).reshape(4, 32, 1024)
    for i in (1, 2):
        sums.first(i)
    dn_sum.send_z()

    gains = jnp.zeros((1, 1024), f32)
    for w in range(8):
        base = tok_ref[w].astype(f32)
        gains = gains + jnp.sum(dn[w].astype(f32) * base * rms_of(base), axis=0, keepdims=True)
    vw[0, 0:1] = gains
    vw[0, 2:3] = jnp.concatenate([gq, gk, jnp.zeros((1, 768), f32)], axis=1)

    def vec_round(buf, devices, sends, recvs):
        return [
            flow.send(buf.at[0], buf.at[i + 1], sends.at[i], recvs.at[i], device) for i, device in enumerate(devices)
        ]

    def vec_total(buf, copies):
        value = buf[0]
        for i, copy in enumerate(copies):
            copy.wait_recv()
            value = value + buf[i + 1]
        return value

    round1 = vec_round(vw, [p.along_z(d) for d in ORDER] + [p.along_z_other(d) for d in ORDER] + [p.sibling], vs1, vr1)
    for i in (1, 2):
        sums.second(i)
    for h in range(2):
        sums_back.second(0, h)
        ff_back.second(2, h)

    @pl.when(p.wt >= 4)
    def _():
        dmid_mirror.wait()

    @pl.when(p.wt < 4)
    def _():
        dmid_o[...] = dmid[...]

    for s in range(SPLIT):
        base = tok_ref[p.wt, sub(s)].astype(f32)
        d_normed = dn_sum.own(s)
        gt_ref[p.wt, sub(s)] = (
            dmid_o[sub(s)] + norm_back(base, rms_of(base), pack_ref[0:1], d_normed)
        ).astype(bf16)
        gt_gather.start(s)
    for i in (1, 2):
        for h in range(2):
            sums_back.put(i, h, sums.own(i, h).astype(bf16))
            sums_back.first(i, h)
    vx[0] = vec_total(vw, round1)
    round2 = vec_round(vx, [p.along_x(d) for d in ORDER], vs2, vr2)
    for i in (1, 2):
        for h in range(2):
            sums_back.second(i, h)
    vy[0] = vec_total(vx, round2)
    round3 = vec_round(vy, [p.along_y(d) for d in ORDER], vs3, vr3)
    gt_gather.forward()
    vec_ref[...] = vec_total(vy, round3)
    out_gather.arrived()
    gt_gather.arrived()
    for part in (d_mid_sum, da_gather, mlp_sum, out_gather, ff, ff_back, dn_sum, gt_gather, sums, sums_back, flow):
        part.finish()


def backward(parts, *args):
    rows = pltpu.VMEM
    wt_rows = [rows((4, 64, 1024), bf16), rows((3, 64, 1024), bf16), rows((3, 64, 1024), bf16)]
    wt_sum = wt_rows + WT_SEMS[:4]
    wt_gather = WT_SEMS[4:]
    half = rows((2, 256, 128), bf16)
    return comm_call(
        functools.partial(backward_kernel, parts), 4,
        (sds((8, 64, 1024), bf16), sds((8, 64, 1024), bf16), sds((3, 4, 32, 1024), bf16), sds((3, 4, 144, 1024), bf16),
         sds((8, 1024), f32)),
        args,
        [rows((8, 64, 1024), bf16), half, rows((64, 1024), f32), rows((64, 1024), f32), rows((64, 1024), bf16)] + [DMA] * 6
        + wt_sum + wt_gather + wt_sum + wt_gather
        + SpScatter.scratch(3, 144) + SpGather.sems(3)
        + [rows((2, 512, 256), bf16), rows((8192, 128), f32), rows((2, 64, 512), f32), half, half,
           rows((4, 4, 2, 256, 128), bf16), half]
        + [rows((2, 3, 4, 256, 128), bf16), rows((2, 3, 256, 128), bf16), rows((2, 3, 256, 128), bf16)]
        + [DMA((2, 3, 4)), DMA((2, 3, 4)), DMA((2, 3)), DMA((2, 3))]
        + [rows((8, 64, 1024), bf16), rows((2, 4, 32, 1024), bf16), rows((4, 32, 1024), bf16)]
        + wt_sum + wt_gather
        + SpScatter.scratch(3, 32) + SpGather.sems(3)
        + [rows((8, 8, 1024), f32), rows((4, 8, 1024), f32), rows((4, 8, 1024), f32),
           DMA((7,)), DMA((7,)), DMA((3,)), DMA((3,)), DMA((3,)), DMA((3,))],
        "backward", 30,
    )


def finish_kernel(sums_ref, ff_ref, out_in, gt_in, vec_ref, out_ref, gt_ref, gq_ref, gk_ref, gv_ref, go_ref, gg_ref, gu_ref, gd_ref,
                  ni_ref, nm_ref, qg_ref, kg_ref, wide, tall, big, ff, sems, load_sems):
    copies = []

    def write(src, dst):
        copies.append(pltpu.make_async_copy(src, dst, sems.at[len(copies)]))
        copies[-1].start()

    write(out_in, out_ref)
    write(gt_in, gt_ref)
    loads = [pltpu.make_async_copy(ff_ref.at[i], ff.at[i], load_sems.at[i]) for i in range(3)]
    for load in loads:
        load.start()
    for i, ref in enumerate((gg_ref, gu_ref, gd_ref)):
        loads[i].wait()
        for part in range(2):
            rows = pl.ds(part * 288, 288)
            big[i, rows, :] = ff[i, rows, :].astype(f32)
            write(big.at[i, rows], ref.at[rows])
    wide[0] = sums_ref[0].astype(f32)
    wide[1] = sums_ref[2].astype(f32)
    write(wide.at[1, 0:64], gk_ref)
    write(wide.at[1, 64:128], gv_ref)
    write(wide.at[0], go_ref)
    tall[...] = sums_ref[1].astype(f32).T
    write(tall, gq_ref)
    ni_ref[...] = vec_ref[0:1, :]
    nm_ref[...] = vec_ref[1:2, :]
    qg_ref[...] = vec_ref[2:3, 0:64] + vec_ref[2:3, 64:128]
    kg_ref[...] = vec_ref[2:3, 128:192]
    for copy in copies:
        copy.wait()


def finish(sums, ff, output, grad_tokens, vec):
    hbm = pl.BlockSpec(memory_space=pl.ANY)
    rows = sds((576, 1024), f32)
    return pl.pallas_call(
        finish_kernel,
        out_shape=(sds((512, 1024), bf16), sds((512, 1024), bf16), sds((1024, 128), f32), sds((64, 1024), f32), sds((64, 1024), f32),
                   sds((128, 1024), f32), rows, rows, rows,
                   sds((1, 1024), f32), sds((1, 1024), f32), sds((1, 64), f32), sds((1, 64), f32)),
        in_specs=[vmem, hbm, vmem, vmem, vmem],
        out_specs=tuple([hbm] * 9 + [vmem] * 4),
        scratch_shapes=[pltpu.VMEM((2, 128, 1024), f32), pltpu.VMEM((1024, 128), f32), pltpu.VMEM((3, 576, 1024), f32), pltpu.VMEM((3, 576, 1024), bf16), DMA((12,)), DMA((3,))],
        compiler_params=pltpu.CompilerParams(vmem_limit_bytes=18 << 20),
        name="finish",
    )(sums, ff, output, grad_tokens, vec)


def body(tokens, norm_in, w_query, w_key, w_value, query_gain, key_gain, w_out, norm_mid, w_gate, w_up, w_down, cotangent, lengths):
    parts = lax.axis_size("sp")
    gains = jnp.concatenate([query_gain, query_gain, key_gain, key_gain, jnp.zeros((768,), f32)])
    pack = jnp.concatenate([norm_in[None], norm_mid[None], gains[None], jnp.zeros((5, 1024), f32)], axis=0)
    wkv = jnp.concatenate([w_key.T, w_value.T], axis=0)

    normed, q_proj, kv_proj, q, kv, cosine, sine = project(lengths, tokens, pack, w_query, wkv)
    kv_all, ext, qa, mix_f, mixed, normed_mid, mid_own, cot = forward(
        parts, lengths, q, kv, tokens, cotangent, w_out, pack
    )
    kv_all = kv_all.reshape(8192, 128)
    normed_mid = normed_mid.reshape(512, 1024)
    cotangent = cot.reshape(512, 1024)

    gate = jnp.dot(normed_mid, w_gate, preferred_element_type=f32)
    up_proj = jnp.dot(normed_mid, w_up, preferred_element_type=f32)
    sigmoid_gate = jax.nn.sigmoid(gate)
    act = (gate * sigmoid_gate * up_proj).astype(bf16)
    mlp_part = jnp.dot(act, w_down, preferred_element_type=f32).astype(bf16)
    d_act = jnp.einsum("td,fd->tf", cotangent, w_down, preferred_element_type=f32)
    d_gate = (d_act * up_proj * sigmoid_gate * (1.0 + gate * (1.0 - sigmoid_gate))).astype(bf16)
    d_up = (d_act * gate * sigmoid_gate).astype(bf16)
    d_mid_part = (
        jnp.einsum("tf,df->td", d_gate, w_gate, preferred_element_type=f32)
        + jnp.einsum("tf,df->td", d_up, w_up, preferred_element_type=f32)
    ).astype(bf16)
    grads = (
        jnp.einsum("tf,td->fd", d_gate, normed_mid, preferred_element_type=f32).astype(bf16),
        jnp.einsum("tf,td->fd", d_up, normed_mid, preferred_element_type=f32).astype(bf16),
        jnp.einsum("tf,td->fd", act, cotangent, preferred_element_type=f32).astype(bf16),
    )
    output, grad_tokens, sums, g_ff, vec = backward(
        parts,
        d_mid_part.reshape(8, 64, 1024), mlp_part.reshape(8, 64, 1024), mid_own, cot,
        pack, w_out, *(g.reshape(4, 144, 1024) for g in grads),
        qa, mix_f, kv_all, ext, mixed,
        q_proj, kv_proj, normed, w_query, wkv, cosine, sine, tokens.reshape(8, 64, 1024),
    )
    (output, grad_tokens, g_query, g_key, g_value, g_out, g_gate, g_up, g_down, g_norm_in, g_norm_mid, g_qg, g_kg) = finish(
        sums.reshape(3, 128, 1024), g_ff.reshape(3, 576, 1024), output.reshape(512, 1024), grad_tokens.reshape(512, 1024), vec
    )
    return (
        output, grad_tokens, g_norm_in.reshape(1024), g_query, g_key.T, g_value.T, g_qg.reshape(64), g_kg.reshape(64),
        g_out, g_norm_mid.reshape(1024), g_gate.T, g_up.T, g_down,
    )


def solution(mesh):
    placed = (
        P("sp", None), P(), P(None, "wt"), P(None, "wt"), P(None, "wt"), P(), P(), P("wt", None), P(),
        P(None, "wt"), P(None, "wt"), P("wt", None), P("sp", None), P(),
    )
    return jax.shard_map(
        body,
        mesh=mesh,
        in_specs=placed,
        out_specs=(
            P("sp", None), P("sp", None), P(), P(None, "wt"), P(None, "wt"), P(None, "wt"), P(), P(),
            P("wt", None), P(), P(None, "wt"), P(None, "wt"), P("wt", None),
        ),
        check_vma=False,
    )
```

```python
import functools, math
import jax
import jax.numpy as jnp
import numpy as np
from jax import lax
from jax.experimental import pallas as pl
from jax.experimental.pallas import tpu as pltpu
from jax.sharding import PartitionSpec as P

f32 = jnp.float32
bf16 = jnp.bfloat16
sds = jax.ShapeDtypeStruct
DMA = pltpu.SemaphoreType.DMA
CH = 512
HALF = 256
SCALE = 0.125
C2 = SCALE * math.log2(math.e)


def starts_of(ids, len_ref):
    end = jnp.int32(0)
    start = jnp.zeros_like(ids)
    for j in range(4):
        end = end + len_ref[j]
        start = start + jnp.where(ids >= end, len_ref[j], 0)
    return start


def scalar_start(row, len_ref):
    end = jnp.int32(0)
    start = jnp.int32(0)
    for j in range(4):
        end = end + len_ref[j]
        start = start + jnp.where(row >= end, len_ref[j], 0)
    return start


def lanes(shape):
    return lax.broadcasted_iota(jnp.int32, shape, len(shape) - 1)


def split3(value, lane):
    hi = value.astype(bf16).astype(f32)
    rest = value - hi
    mid = rest.astype(bf16).astype(f32)
    low = rest - mid
    return jnp.where(lane == 0, hi, jnp.where(lane == 1, mid, jnp.where(lane == 2, low, 0.0)))


def tile_row(me, t, parts):
    return me * 512 if t == 0 else (parts - 1 - me) * 512 + HALF


FAR = 8192.0


def segment_bounds(len_ref, lane):
    begin = jnp.zeros_like(lane)
    end = jnp.zeros_like(lane)
    at = jnp.int32(0)
    for j in range(4):
        begin = jnp.where(lane == 3 + j, at, begin)
        at = at + len_ref[j]
        end = jnp.where(lane == 3 + j, at, end)
    return begin, end


def inside(ids, len_ref, shape):
    lane = lanes(shape)
    begin, end = segment_bounds(len_ref, lane)
    return (ids >= begin) & (ids < end), lane


def key_columns(k0, len_ref, rows):
    ids = k0 + lax.broadcasted_iota(jnp.int32, (rows, 128), 0)
    within, lane = inside(ids, len_ref, (rows, 128))
    return jnp.where(lane < 3, 1.0, jnp.where(within, 1.0, 0.0)).astype(bf16)


def query_columns(r0, len_ref, rows):
    ids = r0 + lax.broadcasted_iota(jnp.int32, (rows, 128), 0)
    within, lane = inside(ids, len_ref, (rows, 128))
    return jnp.where((lane < 3) | (lane > 6) | within, 0.0, -FAR)


smem = pl.BlockSpec(memory_space=pltpu.SMEM)
vmem = pl.BlockSpec(memory_space=pltpu.VMEM)


MESH = pl.DeviceIdType.MESH
eps = 1e-05


def rcopy(src, dst, send, recv, device):
    return pltpu.make_async_remote_copy(
        src_ref=src, dst_ref=dst, send_sem=send, recv_sem=recv, device_id=device, device_id_type=MESH
    )


def meet(devices):
    barrier = pltpu.get_barrier_semaphore()
    for device in devices:
        pl.semaphore_signal(barrier, inc=1, device_id=device, device_id_type=MESH)
    pl.semaphore_wait(barrier, len(devices))


class Place:
    def __init__(self):
        self.sp = lax.axis_index("sp")
        self.wt = lax.axis_index("wt")
        self.x, self.y = lax.div(self.sp, 4), lax.rem(self.sp, 4)
        self.z, self.c = lax.div(self.wt, 2), lax.rem(self.wt, 2)
        self.mirror = (15 - self.sp, self.wt)
        self.sibling = (self.sp, self.z * 2 + 1 - self.c)

    def along_x(self, d):
        return (lax.rem(self.x + d, 4) * 4 + self.y, self.wt)

    def along_y(self, d):
        return (self.x * 4 + lax.rem(self.y + d, 4), self.wt)

    def along_z(self, d):
        return (self.sp, lax.rem(self.z + d, 4) * 2 + self.c)

    def along_z_other(self, d):
        return (self.sp, lax.rem(self.z + d, 4) * 2 + 1 - self.c)

    def first(self, h, d):
        return self.along_x(d) if h == 0 else self.along_y(d)

    def second(self, h, d):
        return self.along_y(d) if h == 0 else self.along_x(d)

    def fsp(self, h):
        return self.x if h == 0 else self.y

    def ssp(self, h):
        return self.y if h == 0 else self.x


def spot(h, first, second):
    return (first, second) if h == 0 else (second, first)


ORDER = (2, 1, 3)


def to_blocks(value, rows, put):
    for x in range(4):
        for y in range(4):
            for h in range(2):
                block = value(x)[:, h * 512 + y * 128:h * 512 + y * 128 + 128]
                put(h, *spot(h, x, y), block)


class SpScatter:
    def __init__(self, p, srcs, refs):
        self.p, self.srcs = p, srcs
        self.r1, self.send, self.r2, self.fs, self.fr, self.ss, self.sr = refs
        self.one, self.two = {}, {}

    @staticmethod
    def scratch(n, rows):
        return [
            pltpu.VMEM((n, 2, 3, 4, rows, 128), bf16), pltpu.VMEM((n, 2, 3, rows, 128), bf16),
            pltpu.VMEM((n, 2, 3, rows, 128), bf16),
            DMA((n, 2, 3)), DMA((n, 2, 3)), DMA((n, 2, 3)), DMA((n, 2, 3)),
        ]

    def first(self, i):
        p = self.p
        for d in ORDER:
            for h in range(2):
                self.one[i, h, d] = rcopy(
                    self.srcs[i].at[h, lax.rem(p.fsp(h) + d, 4)], self.r1.at[i, h, d - 1],
                    self.fs.at[i, h, d - 1], self.fr.at[i, h, d - 1], p.first(h, d),
                )
                self.one[i, h, d].start()

    def part(self, i, h, b):
        value = self.srcs[i][h, self.p.fsp(h), b].astype(f32)
        for d in range(3):
            value = value + self.r1[i, h, d, b].astype(f32)
        return value

    def second(self, i):
        p = self.p
        for h in range(2):
            for d in ORDER:
                self.one[i, h, d].wait_recv()
            for e in ORDER:
                self.send[i, h, e - 1] = self.part(i, h, lax.rem(p.ssp(h) + e, 4)).astype(bf16)
                self.two[i, h, e] = rcopy(
                    self.send.at[i, h, e - 1], self.r2.at[i, h, e - 1],
                    self.ss.at[i, h, e - 1], self.sr.at[i, h, e - 1], p.second(h, e),
                )
                self.two[i, h, e].start()

    def own(self, i, h):
        value = self.part(i, h, self.p.ssp(h))
        for e in ORDER:
            self.two[i, h, e].wait_recv()
            value = value + self.r2[i, h, e - 1].astype(f32)
        return value

    def finish(self):
        for copy in list(self.one.values()) + list(self.two.values()):
            copy.wait_send()


class SpGather:
    def __init__(self, p, out, sems):
        self.p, self.out = p, out
        self.fs, self.fr, self.ss, self.sr = sems
        self.one, self.two = {}, {}

    @staticmethod
    def sems(n):
        return [DMA((n, 2, 3)) for _ in range(4)]

    def put(self, i, h, value):
        self.out[i, h, self.p.fsp(h), self.p.ssp(h)] = value

    def first(self, i, h):
        block = self.out.at[i, h, self.p.fsp(h), self.p.ssp(h)]
        for e in ORDER:
            self.one[i, h, e] = rcopy(
                block, block, self.fs.at[i, h, e - 1], self.fr.at[i, h, e - 1], self.p.second(h, e)
            )
            self.one[i, h, e].start()

    def second(self, i, h):
        for e in ORDER:
            self.one[i, h, e].wait_recv()
        block = self.out.at[i, h, self.p.fsp(h)]
        for d in ORDER:
            self.two[i, h, d] = rcopy(
                block, block, self.ss.at[i, h, d - 1], self.sr.at[i, h, d - 1], self.p.first(h, d)
            )
            self.two[i, h, d].start()

    def finish(self):
        for copy in self.one.values():
            copy.wait_send()
        for copy in self.two.values():
            copy.wait()


SPLIT = 2


def sub(s):
    return pl.ds(s * (64 // SPLIT), 64 // SPLIT)


class WtSum:
    def __init__(self, p, part, sib, send, rz, sems):
        self.p, self.part, self.sib, self.send, self.rz = p, part, sib, send, rz
        self.cs, self.cr, self.zs, self.zr = sems
        self.second = {}

    def core(self, zz, s):
        return rcopy(
            self.part.at[zz * 2 + 1 - self.p.c, sub(s)], self.sib.at[zz, sub(s)],
            self.cs.at[zz, s], self.cr.at[zz, s], self.p.sibling,
        )

    def start_core(self, zz):
        for s in range(SPLIT):
            self.core(zz, s).start()

    def pair(self, zz, s):
        return self.part[zz * 2 + self.p.c, sub(s)].astype(f32) + self.sib[zz, sub(s)].astype(f32)

    def send_z(self):
        for s in range(SPLIT):
            for d in ORDER:
                zz = lax.rem(self.p.z + d, 4)
                self.core(zz, s).wait_recv()
                self.send[d - 1, sub(s)] = self.pair(zz, s).astype(bf16)
                copy = rcopy(
                    self.send.at[d - 1, sub(s)], self.rz.at[d - 1, sub(s)],
                    self.zs.at[d - 1, s], self.zr.at[d - 1, s], self.p.along_z(d),
                )
                copy.start()
                self.second[d, s] = copy

    def own(self, s):
        self.core(self.p.z, s).wait_recv()
        value = self.pair(self.p.z, s)
        for d in (1, 3, 2):
            self.second[d, s].wait_recv()
            value = value + self.rz[d - 1, sub(s)].astype(f32)
        return value

    def finish(self):
        for zz in range(4):
            for s in range(SPLIT):
                self.core(zz, s).wait_send()
        for copy in self.second.values():
            copy.wait_send()


class WtGather:
    def __init__(self, p, out, sems):
        self.p, self.out = p, out
        self.zs, self.zr, self.gs, self.gr = sems
        self.far, self.near = {}, {}

    def start(self, s):
        p = self.p
        block = self.out.at[p.wt, sub(s)]
        for d in ORDER:
            self.far[d, s] = rcopy(block, block, self.zs.at[d - 1, s], self.zr.at[d - 1, s], p.along_z(d))
            self.far[d, s].start()
        self.pass_on(0, s)

    def pass_on(self, slot, s):
        p = self.p
        block = self.out.at[lax.rem(p.z + 4 - slot, 4) * 2 + p.c, sub(s)]
        self.near[slot, s] = rcopy(block, block, self.gs.at[slot, s], self.gr.at[slot, s], p.sibling)
        self.near[slot, s].start()

    def forward(self):
        for s in range(SPLIT):
            for d in (1, 3, 2):
                self.far[d, s].wait_recv()
                self.pass_on(d, s)

    def arrived(self):
        for copy in self.near.values():
            copy.wait_recv()

    def finish(self):
        for copy in list(self.far.values()) + list(self.near.values()):
            copy.wait_send()


def rms_of(value):
    return lax.rsqrt(jnp.mean(value * value, axis=-1, keepdims=True) + eps)


def norm_back(values, scale, gain, grad):
    scaled = grad * gain
    inner = jnp.mean(scaled * values, axis=-1, keepdims=True)
    return scale * scaled - values * scale * scale * scale * inner


def wt_peers(p):
    return [p.sibling] + [p.along_z(d) for d in ORDER]


class Flow:
    def __init__(self):
        self.copies = []

    def send(self, *args):
        copy = rcopy(*args)
        copy.start()
        self.copies.append(copy)
        return copy

    def finish(self):
        for copy in self.copies:
            copy.wait_send()


def forward_kernel(
    parts,
    len_ref, q_ref, kv_ref, tok_ref, cot_ref, w_ref, pack_ref,
    all_ref, ext_ref, qa_ref, mixf_ref, mix_ref, nm_ref, mid_ref, cotz_ref,
    qz, base, acc, part, sib, send, rz, ms, mr, cs, cr, zs, zr, az, bz, ag, bg, fs, fr, ss, sr,
):
    p = Place()
    me = p.sp
    meet(wt_peers(p) + [p.along_x(d) for d in ORDER] + [p.along_y(d) for d in ORDER] + [p.mirror])
    flow = Flow()
    first = {}
    for d in ORDER:
        for h in range(2):
            first[h, d] = flow.send(
                kv_ref.at[h], all_ref.at[p.x, p.y, h], fs.at[h, d - 1], fr.at[h, d - 1], p.first(h, d)
            )
    q_mirror = flow.send(q_ref.at[1], qz.at[1], ms.at[0], mr.at[0], p.mirror)

    def pass_on(h, slot):
        a = lax.rem(p.fsp(h) + 4 - slot, 4)
        at = spot(h, a, p.ssp(h))
        for e in ORDER:
            src = kv_ref.at[h] if slot == 0 else all_ref.at[at[0], at[1], h]
            flow.send(src, all_ref.at[at[0], at[1], h], ss.at[h, slot, e - 1], sr.at[h, slot, e - 1], p.second(h, e))

    for h in range(2):
        pass_on(h, 0)
    token_mirror = rcopy(tok_ref.at[p.wt], base, ms.at[1], mr.at[1], p.mirror)

    @pl.when(p.wt >= 4)
    def _():
        token_mirror.start()

    @pl.when(p.wt < 4)
    def _():
        base[...] = tok_ref[p.wt]

    all_ref[p.x, p.y] = kv_ref[...]
    qz[0] = q_ref[0]
    cotz_ref[0:4] = cot_ref[0:4]

    @pl.loop(0, 8)
    def _(b):
        rows = pl.ds(pl.multiple_of(b * 1024, 1024), 1024)
        ext_ref[rows, :] = key_columns(b * 1024, len_ref, 1024)

    lane = lanes((HALF, 128))
    lane2 = lanes((2 * HALF, 128))
    lanek = lanes((CH, 128))
    acc[...] = jnp.zeros_like(acc)
    blocks = (me, parts - 1 - me)
    begins = (me * 512, (parts - 1 - me) * 512 + HALF)

    def prepare(t):
        q = qz[t].astype(f32)
        qa_ref[t, 0:HALF, 0:128] = jnp.where(lane < 64, q, 0.0).astype(bf16)
        qa_ref[t, HALF:, 0:128] = jnp.where(lane < 64, pltpu.roll(q, 64, 1), 0.0).astype(bf16)
        columns = query_columns(begins[t], len_ref, HALF).astype(bf16)
        qa_ref[t, 0:HALF, 128:256] = columns
        qa_ref[t, HALF:, 128:256] = columns

    def step(t, x, y, masked):
        k0 = pl.multiple_of((x * 4 + y) * CH, CH)
        kv = all_ref[x, y].reshape(CH, 128)
        kva = jnp.concatenate([kv, ext_ref[pl.ds(k0, CH), :]], axis=1)
        pr = jnp.exp2(nt(qa_ref[t], kva) * C2)
        if masked:
            rows = begins[t] + lax.rem(lax.broadcasted_iota(jnp.int32, (2 * HALF, 1), 0), HALF)
            keys = k0 + lax.broadcasted_iota(jnp.int32, (2 * HALF, CH), 1)
            pr = jnp.where(keys <= rows, pr, 0.0)
        ones = jnp.where(lanek < 64, jnp.ones_like(kv), kv)
        acc[t] += jnp.dot(pr.astype(bf16), ones, preferred_element_type=f32)

    def both(x, y):
        block = x * 4 + y

        @pl.when(block < blocks[0])
        def _():
            step(0, x, y, False)

        @pl.when(block < blocks[1])
        def _():
            step(1, x, y, False)

        @pl.when(block == blocks[1])
        def _():
            step(1, x, y, True)

    prepare(0)
    step(0, p.x, p.y, True)
    for d in (1, 3, 2):
        for h in range(2):
            first[h, d].wait_recv()
            pass_on(h, d)
    q_mirror.wait_recv()
    prepare(1)

    @pl.when(me < blocks[1])
    def _():
        step(1, p.x, p.y, False)

    def wait_for(x, y, h, slot, e):
        block = all_ref.at[x, y, h]
        rcopy(block, block, ss.at[h, slot, e - 1], sr.at[h, slot, e - 1], p.second(h, 1)).wait_recv()

    @pl.loop(1, 4)
    def _(d):
        x = lax.rem(p.x + 4 - d, 4)
        wait_for(x, p.y, 1, 0, d)
        both(x, p.y)

    @pl.loop(1, 4)
    def _(d):
        y = lax.rem(p.y + 4 - d, 4)
        wait_for(p.x, y, 0, 0, d)
        both(p.x, y)

    @pl.loop(0, 9)
    def _(k):
        dx, dy = 1 + lax.div(k, 3), 1 + lax.rem(k, 3)
        x, y = lax.rem(p.x + 4 - dx, 4), lax.rem(p.y + 4 - dy, 4)
        wait_for(x, y, 0, dx, dy)
        wait_for(x, y, 1, dy, dx)
        both(x, y)

    total = WtSum(p, part, sib, send, rz, (cs, cr, zs, zr))
    cot_mirror = flow.send(cot_ref.at[pl.ds(4, 4)], cotz_ref.at[pl.ds(4, 4)], ms.at[2], mr.at[2], p.mirror)
    for t in range(2):
        value = acc[t]
        swapped = pltpu.roll(value, 64, 1)
        o = swapped / value
        mix = jnp.where(lane < 64, o[:HALF], pltpu.roll(o[HALF:], 64, 1))
        mixf_ref[t] = mix
        mix = mix.astype(bf16)
        mix_ref[t] = mix
        part[t * 4:t * 4 + 4] = jnp.dot(mix, w_ref[...], preferred_element_type=f32).astype(bf16).reshape(4, 64, 1024)
        for zz in (t * 2, t * 2 + 1):
            total.start_core(zz)
    total.send_z()
    for t in range(2):
        value = acc[t]
        weights = jnp.where(lane2 < 64, value, pltpu.roll(value, 64, 1))
        columns = qa_ref[t, :, 128:256].astype(f32)
        qa_ref[t, :, 128:256] = (split3(jnp.log(weights) * (-1.0 / SCALE), lane2) + columns).astype(bf16)

    @pl.when(p.wt >= 4)
    def _():
        token_mirror.wait()

    spread = WtGather(p, nm_ref, (az, bz, ag, bg))
    for s in range(SPLIT):
        middle = base[sub(s)].astype(f32) + total.own(s)
        mid_ref[sub(s)] = middle
        nm_ref[p.wt, sub(s)] = (middle * rms_of(middle) * pack_ref[1:2]).astype(bf16)
        spread.start(s)
    spread.forward()
    cot_mirror.wait_recv()
    spread.arrived()
    for part in (spread, total, flow):
        part.finish()


WT_SEMS = [DMA((n, SPLIT)) for n in (4, 4, 3, 3, 3, 3, 4, 4)]


def comm_call(kernel, number, out_shape, args, scratch, name, limit=10, first=None):
    return pl.pallas_call(
        kernel,
        out_shape=out_shape,
        in_specs=[first or vmem] + [vmem] * (len(args) - 1),
        out_specs=tuple(vmem for _ in out_shape),
        scratch_shapes=scratch,
        compiler_params=pltpu.CompilerParams(
            collective_id=number, has_side_effects=True, vmem_limit_bytes=limit << 20
        ),
        cost_estimate=pl.CostEstimate(flops=8 << 30, bytes_accessed=32 << 20, transcendentals=0),
        name=name,
    )(*args)


def forward(parts, lengths, q, kv, tokens, cotangent, w_out, pack):
    rows = pltpu.VMEM
    half = sds((2, 256, 128), bf16)
    full = sds((8, 64, 1024), bf16)
    return comm_call(
        functools.partial(forward_kernel, parts), 1,
        (sds((4, 4, 2, 256, 128), bf16), sds((8192, 128), bf16), sds((2, 512, 256), bf16), sds((2, 256, 128), f32),
         half, full, sds((64, 1024), f32), full),
        (lengths, q.reshape(2, 256, 128), kv.reshape(2, 256, 128), tokens.reshape(8, 64, 1024),
         cotangent.reshape(8, 64, 1024), w_out, pack),
        [rows((2, 256, 128), bf16), rows((64, 1024), bf16), rows((2, 512, 128), f32), rows((8, 64, 1024), bf16),
         rows((4, 64, 1024), bf16), rows((3, 64, 1024), bf16), rows((3, 64, 1024), bf16), DMA((3,)), DMA((3,))]
        + WT_SEMS + [DMA((2, 3)), DMA((2, 3)), DMA((2, 4, 3)), DMA((2, 4, 3))],
        "forward", 16, smem,
    )


def turned(value, lane):
    return jnp.where(lax.rem(lane, 64) < 32, pltpu.roll(value, 96, 1), pltpu.roll(value, 32, 1))


def head_sums(value, lane):
    s0 = jnp.sum(jnp.where(lane < 64, value, 0.0), axis=1, keepdims=True)
    s1 = jnp.sum(jnp.where(lane < 64, 0.0, value), axis=1, keepdims=True)
    return jnp.where(lane < 64, s0, s1)


def nt(a, b):
    return lax.dot_general(a, b, (((1,), (1,)), ((), ())), preferred_element_type=f32)


def tn(a, b):
    return lax.dot_general(a, b, (((0,), (0,)), ((), ())), preferred_element_type=f32)


FREQS = [float(np.float32(1000000.0 ** (-2.0 * i / 64))) for i in range(32)]


def proj_kernel(len_ref, tok_ref, pack_ref, wq_ref, wkv_ref, n_ref, qp_ref, kvp_ref, q_ref, kv_ref, cos_ref, sin_ref):
    lane = lanes((512, 128))
    ids = lax.axis_index("sp") * 512 + lax.broadcasted_iota(jnp.int32, (1, 512), 1)
    positions = (ids - starts_of(ids, len_ref)).astype(f32)
    row = lax.broadcasted_iota(jnp.int32, (32, 512), 0)
    freqs = jnp.zeros((32, 512), f32)
    for i, freq in enumerate(FREQS):
        freqs = jnp.where(row == i, freq, freqs)
    angles = positions * freqs
    cosine, sine = jnp.cos(angles), jnp.sin(angles)
    cosine = jnp.concatenate([cosine] * 4, axis=0).T
    sine = jnp.concatenate([-sine, sine, -sine, sine], axis=0).T
    cos_ref[...] = cosine
    sin_ref[...] = sine
    base = tok_ref[...].astype(f32)
    normed = (base * rms_of(base) * pack_ref[0:1]).astype(bf16)
    n_ref[...] = normed
    q = jnp.dot(normed, wq_ref[...], preferred_element_type=f32)
    qp_ref[...] = q
    q = q * lax.rsqrt(head_sums(q * q, lane) * (1.0 / 64) + eps) * pack_ref[2:3, 0:128]
    q_ref[...] = (q * cosine + turned(q, lane) * sine).astype(bf16)
    kv = nt(normed, wkv_ref[...])
    kvp_ref[...] = kv
    k = kv * lax.rsqrt(head_sums(kv * kv, lane) * (1.0 / 64) + eps) * pack_ref[2:3, 128:256]
    k = k * cosine + turned(k, lane) * sine
    kv_ref[...] = jnp.where(lane < 64, k, kv).astype(bf16)


def project(*args):
    wide = sds((512, 128), f32)
    out_shape = (sds((512, 1024), bf16), wide, wide, sds((512, 128), bf16), sds((512, 128), bf16), wide, wide)
    return pl.pallas_call(
        proj_kernel,
        out_shape=out_shape,
        in_specs=[smem] + [vmem] * 4,
        out_specs=tuple(vmem for _ in out_shape),
        compiler_params=pltpu.CompilerParams(vmem_limit_bytes=12 << 20),
        name="project",
    )(*args)


def backward_kernel(
    parts,
    dm_ref, mlp_ref, mid_ref, cot_ref, pack_ref, w_ref, g0_ref, g1_ref, g2_ref,
    qa_ref, mixf_ref, kv_ref, ext_ref, mixed_ref,
    qp_ref, kvp_ref, n_ref, wq_ref, wkv_ref, cos_ref, sin_ref, tok_ref,
    out_ref, gt_ref, sums_ref, ff_ref, vec_ref,
    *scratch,
):
    scratch = list(scratch)

    def take(n):
        got = scratch[:n]
        del scratch[:n]
        return got

    p = Place()
    me = p.sp
    meet(
        wt_peers(p) + [p.along_z_other(d) for d in ORDER] + [p.mirror]
        + [p.along_x(d) for d in ORDER] + [p.along_y(d) for d in ORDER]
    )
    flow = Flow()

    def wt_sum(ref):
        sib, send, rz = take(3)
        return WtSum(p, ref, sib, send, rz, take(4))

    da, dz, dmid, dmid_o, out_own = take(5)
    mirror_sems = take(6)
    d_mid_sum = wt_sum(dm_ref)
    da_gather = WtGather(p, da, take(4))
    mlp_sum = wt_sum(mlp_ref)
    out_gather = WtGather(p, out_ref, take(4))
    (ffb,) = take(1)
    ff = SpScatter(p, [ffb.at[i] for i in range(3)], take(7))
    ff_back = SpGather(p, ff_ref, take(4))
    dab, acc, dqt, dqz, dq, dkv, dkv_own = take(7)
    r1, send1, r2, fs, fr, ss, sr = take(7)
    dn, gqkv, gout = take(3)
    dn_sum = wt_sum(dn)
    gt_gather = WtGather(p, gt_ref, take(4))
    sums = SpScatter(p, (gout, gqkv.at[0], gqkv.at[1]), take(7))
    sums_back = SpGather(p, sums_ref, take(4))
    vw, vx, vy, vs1, vr1, vs2, vr2, vs3, vr3 = take(9)
    assert not scratch

    for zz in range(4):
        d_mid_sum.start_core(zz)
    for i, ref in enumerate((g0_ref, g1_ref, g2_ref)):
        def put(h, u, v, block, i=i):
            ffb[i, h, u, v] = block

        to_blocks(lambda x, ref=ref: ref[x], 144, put)
        ff.first(i)
        if i == 0:
            d_mid_sum.send_z()
    vw[0] = jnp.zeros((8, 1024), f32)
    acc[...] = jnp.zeros_like(acc)
    dqt[...] = jnp.zeros_like(dqt)
    for s in range(SPLIT):
        middle = mid_ref[sub(s)]
        scale = rms_of(middle)
        d_mid = d_mid_sum.own(s)
        d_middle = cot_ref[p.wt, sub(s)].astype(f32) + norm_back(middle, scale, pack_ref[1:2], d_mid)
        da[p.wt, sub(s)] = d_middle.astype(bf16)
        da_gather.start(s)
        dmid[sub(s)] = d_middle
        vw[0, 1:2] += jnp.sum(d_mid * middle * scale, axis=0, keepdims=True)
    dmid_mirror = rcopy(dmid, dmid_o, mirror_sems[2], mirror_sems[3], p.mirror)

    @pl.when(p.wt >= 4)
    def _():
        dmid_mirror.start()

    da_gather.forward()
    da_gather.arrived()
    for zz in range(4):
        mlp_sum.start_core(zz)
    dz[...] = nt(da[...].reshape(512, 1024), w_ref[...]).astype(bf16).reshape(2, 256, 128)
    mlp_sum.send_z()

    lane = lanes((HALF, 128))
    for t in range(2):
        do = dz[t].astype(f32)
        prod = do * mixf_ref[t]
        d0 = -jnp.sum(jnp.where(lane < 64, prod, 0.0), axis=1, keepdims=True)
        d1 = -jnp.sum(jnp.where(lane < 64, 0.0, prod), axis=1, keepdims=True)
        dab[t, 0:HALF, 0:128] = jnp.where(lane < 64, 0.0, pltpu.roll(do, 64, 1)).astype(bf16)
        dab[t, HALF:, 0:128] = jnp.where(lane < 64, 0.0, do).astype(bf16)
        dab[t, 0:HALF, 128:256] = split3(jnp.broadcast_to(d0, (HALF, 128)), lane).astype(bf16)
        dab[t, HALF:, 128:256] = split3(jnp.broadcast_to(d1, (HALF, 128)), lane).astype(bf16)
    upper_long = (me < parts // 2).astype(jnp.int32)
    blocks = [me + t * (parts - 1 - 2 * me) for t in (upper_long, 1 - upper_long)]

    def step(k, masked):
        short = (k > blocks[0]).astype(jnp.int32)
        t = upper_long + short * (1 - 2 * upper_long)
        c = k - short * (blocks[0] + 1)
        k0 = pl.multiple_of(c * CH, CH)
        kv = kv_ref[pl.ds(k0, CH), :]
        kva = jnp.concatenate([kv, ext_ref[pl.ds(k0, CH), :]], axis=1)
        qa = qa_ref[t]
        d_out = dab[t]
        pr = jnp.exp2(nt(kva, qa) * C2)
        if masked:
            r0 = c * 512 + t * HALF
            rows = r0 + lax.rem(lax.broadcasted_iota(jnp.int32, (1, 2 * HALF), 1), HALF)
            keys = k0 + lax.broadcasted_iota(jnp.int32, (CH, 2 * HALF), 0)
            pr = jnp.where(keys <= rows, pr, 0.0)
        ds = (pr * nt(kva, d_out)).astype(bf16)
        acc[pl.ds(k0, CH), :] += jnp.dot(
            pr.astype(bf16), d_out[:, 0:128], preferred_element_type=f32
        ) + jnp.dot(ds, qa[:, 0:128], preferred_element_type=f32)
        kt = kv.T[0:64, :]
        dqt[t] += jnp.dot(kt, ds, preferred_element_type=f32)

    def plain(k):
        step(k, False)

    def either(k):
        pl.when(k == blocks[0])(lambda: step(k, True))
        pl.when(k != blocks[0])(lambda: step(k, False))

    ff.second(0)
    ff.second(1)
    pl.loop(0, 3)(plain)
    ff.second(2)
    pl.loop(3, 6)(plain)
    for i in range(3):
        for h in range(2):
            ff_back.put(i, h, ff.own(i, h).astype(bf16))
            ff_back.first(i, h)
    pl.loop(6, 8)(plain)
    for s in range(SPLIT):
        out_own[sub(s)] = (mid_ref[sub(s)] + mlp_sum.own(s)).astype(bf16)
    out_mirror = rcopy(out_own, out_ref.at[p.wt], mirror_sems[4], mirror_sems[5], p.mirror)

    @pl.when(p.wt >= 4)
    def _():
        out_mirror.start()

    @pl.when(p.wt < 4)
    def _():
        out_ref[p.wt] = out_own[...]


    def put_out(h, u, v, block):
        gout[h, u, v] = block

    g_out = tn(mixed_ref[...].reshape(512, 128), da[...].reshape(512, 1024)).astype(bf16)
    to_blocks(lambda x: g_out[x * 32:x * 32 + 32], 32, put_out)
    sums.first(0)
    pl.loop(8, 12)(either)
    for h in range(2):
        ff_back.second(0, h)
    sums.second(0)

    @pl.when(p.wt >= 4)
    def _():
        out_mirror.wait()

    for s in range(SPLIT):
        out_gather.start(s)
    pl.loop(12, 16)(either)
    step(16, True)
    for t in range(2):
        both = jnp.concatenate([dqt[t, :, :HALF], dqt[t, :, HALF:]], axis=0)
        dqz[t] = (both.T * SCALE).astype(bf16)
    weight = jnp.where(lanes((512, 128)) < 64, SCALE, 1.0)

    @pl.loop(0, parts)
    def _(b):
        rows = pl.ds(pl.multiple_of(b * 512, 512), 512)
        dkv[lax.div(b, 4), lax.rem(b, 4)] = (acc[rows, :] * weight).astype(bf16).reshape(2, 256, 128)

    mirror = flow.send(dqz.at[1], dq.at[1], mirror_sems[0], mirror_sems[1], p.mirror)
    dq[0] = dqz[0]
    first, second = {}, {}
    for e in (2, 1, 3, 0):
        for d in ORDER:
            for h in range(2):
                at = spot(h, lax.rem(p.fsp(h) + d, 4), lax.rem(p.ssp(h) + e, 4))
                first[h, d, e] = flow.send(
                    dkv.at[at[0], at[1], h], r1.at[h, d - 1, e], fs.at[h, d - 1, e], fr.at[h, d - 1, e], p.first(h, d)
                )

    def total(h, e):
        at = spot(h, p.fsp(h), lax.rem(p.ssp(h) + e, 4))
        value = dkv[at[0], at[1], h].astype(f32)
        for d in ORDER:
            first[h, d, e].wait_recv()
            value = value + r1[h, d - 1, e].astype(f32)
        return value

    out_gather.forward()
    for e in ORDER:
        for h in range(2):
            send1[h, e - 1] = total(h, e).astype(bf16)
            second[h, e] = flow.send(
                send1.at[h, e - 1], r2.at[h, e - 1], ss.at[h, e - 1], sr.at[h, e - 1], p.second(h, e)
            )
    own = [total(h, 0) for h in range(2)]
    for h in range(2):
        ff_back.second(1, h)
        sums_back.put(0, h, sums.own(0, h).astype(bf16))
        sums_back.first(0, h)
    for h in range(2):
        value = own[h]
        for e in ORDER:
            second[h, e].wait_recv()
            value = value + r2[h, e - 1].astype(f32)
        dkv_own[h] = value.astype(bf16)
    mirror.wait_recv()

    wide = lanes((512, 128))
    cosine, sine = cos_ref[...], sin_ref[...]

    def back(grad, proj, gain):
        grad = grad * cosine - turned(grad, wide) * sine
        scale = lax.rsqrt(head_sums(proj * proj, wide) * (1.0 / 64) + eps)
        scaled = grad * gain
        inner = head_sums(scaled * proj, wide) * (1.0 / 64)
        gains = jnp.sum(grad * proj * scale, axis=0, keepdims=True)
        return scale * scaled - proj * scale * scale * scale * inner, gains

    d_q, gq = back(dq[...].reshape(512, 128).astype(f32), qp_ref[...], pack_ref[2:3, 0:128])
    dkv_in = dkv_own[...].reshape(512, 128).astype(f32)
    d_k, gk = back(dkv_in, kvp_ref[...], pack_ref[2:3, 128:256])
    d_q = d_q.astype(bf16)
    d_kv = jnp.where(wide < 64, d_k, dkv_in).astype(bf16)
    dn[...] = (nt(d_q, wq_ref[...]) + jnp.dot(d_kv, wkv_ref[...], preferred_element_type=f32)).astype(bf16).reshape(8, 64, 1024)
    for zz in range(4):
        dn_sum.start_core(zz)
    normed = n_ref[...]
    for i, grad in enumerate((d_q, d_kv)):
        def put_in(h, u, v, block, i=i):
            gqkv[i, h, u, v] = block

        g_in = tn(grad, normed).astype(bf16)
        to_blocks(lambda x, g_in=g_in: g_in[x * 32:x * 32 + 32], 32, put_in)
    for i in (1, 2):
        sums.first(i)
    dn_sum.send_z()

    gains = jnp.zeros((1, 1024), f32)
    for w in range(8):
        base = tok_ref[w].astype(f32)
        gains = gains + jnp.sum(dn[w].astype(f32) * base * rms_of(base), axis=0, keepdims=True)
    vw[0, 0:1] = gains
    vw[0, 2:3] = jnp.concatenate([gq, gk, jnp.zeros((1, 768), f32)], axis=1)

    def vec_round(buf, devices, sends, recvs):
        return [
            flow.send(buf.at[0], buf.at[i + 1], sends.at[i], recvs.at[i], device) for i, device in enumerate(devices)
        ]

    def vec_total(buf, copies):
        value = buf[0]
        for i, copy in enumerate(copies):
            copy.wait_recv()
            value = value + buf[i + 1]
        return value

    round1 = vec_round(vw, [p.along_z(d) for d in ORDER] + [p.along_z_other(d) for d in ORDER] + [p.sibling], vs1, vr1)
    for i in (1, 2):
        sums.second(i)
    for h in range(2):
        sums_back.second(0, h)
        ff_back.second(2, h)

    @pl.when(p.wt >= 4)
    def _():
        dmid_mirror.wait()

    @pl.when(p.wt < 4)
    def _():
        dmid_o[...] = dmid[...]

    for s in range(SPLIT):
        base = tok_ref[p.wt, sub(s)].astype(f32)
        d_normed = dn_sum.own(s)
        gt_ref[p.wt, sub(s)] = (
            dmid_o[sub(s)] + norm_back(base, rms_of(base), pack_ref[0:1], d_normed)
        ).astype(bf16)
        gt_gather.start(s)
    for i in (1, 2):
        for h in range(2):
            sums_back.put(i, h, sums.own(i, h).astype(bf16))
            sums_back.first(i, h)
    vx[0] = vec_total(vw, round1)
    round2 = vec_round(vx, [p.along_x(d) for d in ORDER], vs2, vr2)
    for i in (1, 2):
        for h in range(2):
            sums_back.second(i, h)
    vy[0] = vec_total(vx, round2)
    round3 = vec_round(vy, [p.along_y(d) for d in ORDER], vs3, vr3)
    gt_gather.forward()
    vec_ref[...] = vec_total(vy, round3)
    out_gather.arrived()
    gt_gather.arrived()
    for part in (d_mid_sum, da_gather, mlp_sum, out_gather, ff, ff_back, dn_sum, gt_gather, sums, sums_back, flow):
        part.finish()


def backward(parts, *args):
    rows = pltpu.VMEM
    wt_rows = [rows((4, 64, 1024), bf16), rows((3, 64, 1024), bf16), rows((3, 64, 1024), bf16)]
    wt_sum = wt_rows + WT_SEMS[:4]
    wt_gather = WT_SEMS[4:]
    half = rows((2, 256, 128), bf16)
    return comm_call(
        functools.partial(backward_kernel, parts), 4,
        (sds((8, 64, 1024), bf16), sds((8, 64, 1024), bf16), sds((3, 2, 4, 4, 32, 128), bf16), sds((3, 2, 4, 4, 144, 128), bf16),
         sds((8, 1024), f32)),
        args,
        [rows((8, 64, 1024), bf16), half, rows((64, 1024), f32), rows((64, 1024), f32), rows((64, 1024), bf16)] + [DMA] * 6
        + wt_sum + wt_gather + wt_sum + wt_gather
        + [rows((3, 2, 4, 4, 144, 128), bf16)] + SpScatter.scratch(3, 144) + SpGather.sems(3)
        + [rows((2, 512, 256), bf16), rows((8192, 128), f32), rows((2, 64, 512), f32), half, half,
           rows((4, 4, 2, 256, 128), bf16), half]
        + [rows((2, 3, 4, 256, 128), bf16), rows((2, 3, 256, 128), bf16), rows((2, 3, 256, 128), bf16)]
        + [DMA((2, 3, 4)), DMA((2, 3, 4)), DMA((2, 3)), DMA((2, 3))]
        + [rows((8, 64, 1024), bf16), rows((2, 2, 4, 4, 32, 128), bf16), rows((2, 4, 4, 32, 128), bf16)]
        + wt_sum + wt_gather
        + SpScatter.scratch(3, 32) + SpGather.sems(3)
        + [rows((8, 8, 1024), f32), rows((4, 8, 1024), f32), rows((4, 8, 1024), f32),
           DMA((7,)), DMA((7,)), DMA((3,)), DMA((3,)), DMA((3,)), DMA((3,))],
        "backward", 30,
    )


def finish_kernel(sums_ref, ff_ref, out_in, gt_in, vec_ref, out_ref, gt_ref, gq_ref, gk_ref, gv_ref, go_ref, gg_ref, gu_ref, gd_ref,
                  ni_ref, nm_ref, qg_ref, kg_ref, wide, tall, big, ff, sems, load_sems):
    copies = []

    def write(src, dst):
        copies.append(pltpu.make_async_copy(src, dst, sems.at[len(copies)]))
        copies[-1].start()

    write(out_in, out_ref)
    write(gt_in, gt_ref)
    loads = [pltpu.make_async_copy(ff_ref.at[i], ff.at[i], load_sems.at[i]) for i in range(3)]
    for load in loads:
        load.start()

    def assemble(out, blocks, x, rows):
        for h in range(2):
            for y in range(4):
                columns = slice(h * 512 + y * 128, h * 512 + y * 128 + 128)
                out[x * rows:(x + 1) * rows, columns] = blocks[(h,) + spot(h, x, y)].astype(f32)

    for i, ref in enumerate((gg_ref, gu_ref, gd_ref)):
        loads[i].wait()
        for x in range(4):
            assemble(big.at[i], ff.at[i], x, 144)
            rows = pl.ds(x * 144, 144)
            write(big.at[i, rows], ref.at[rows])
    for i in range(3):
        for x in range(4):
            assemble(wide.at[i], sums_ref.at[i], x, 32)
    write(wide.at[2, 0:64], gk_ref)
    write(wide.at[2, 64:128], gv_ref)
    write(wide.at[0], go_ref)
    tall[...] = wide[1].T
    write(tall, gq_ref)
    ni_ref[...] = vec_ref[0:1, :]
    nm_ref[...] = vec_ref[1:2, :]
    qg_ref[...] = vec_ref[2:3, 0:64] + vec_ref[2:3, 64:128]
    kg_ref[...] = vec_ref[2:3, 128:192]
    for copy in copies:
        copy.wait()


def finish(sums, ff, output, grad_tokens, vec):
    hbm = pl.BlockSpec(memory_space=pl.ANY)
    rows = sds((576, 1024), f32)
    return pl.pallas_call(
        finish_kernel,
        out_shape=(sds((512, 1024), bf16), sds((512, 1024), bf16), sds((1024, 128), f32), sds((64, 1024), f32), sds((64, 1024), f32),
                   sds((128, 1024), f32), rows, rows, rows,
                   sds((1, 1024), f32), sds((1, 1024), f32), sds((1, 64), f32), sds((1, 64), f32)),
        in_specs=[vmem, hbm, vmem, vmem, vmem],
        out_specs=tuple([hbm] * 9 + [vmem] * 4),
        scratch_shapes=[pltpu.VMEM((3, 128, 1024), f32), pltpu.VMEM((1024, 128), f32), pltpu.VMEM((3, 576, 1024), f32), pltpu.VMEM((3, 2, 4, 4, 144, 128), bf16), DMA((18,)), DMA((3,))],
        compiler_params=pltpu.CompilerParams(vmem_limit_bytes=18 << 20),
        name="finish",
    )(sums, ff, output, grad_tokens, vec)


def body(tokens, norm_in, w_query, w_key, w_value, query_gain, key_gain, w_out, norm_mid, w_gate, w_up, w_down, cotangent, lengths):
    parts = lax.axis_size("sp")
    gains = jnp.concatenate([query_gain, query_gain, key_gain, key_gain, jnp.zeros((768,), f32)])
    pack = jnp.concatenate([norm_in[None], norm_mid[None], gains[None], jnp.zeros((5, 1024), f32)], axis=0)
    wkv = jnp.concatenate([w_key.T, w_value.T], axis=0)

    normed, q_proj, kv_proj, q, kv, cosine, sine = project(lengths, tokens, pack, w_query, wkv)
    kv_all, ext, qa, mix_f, mixed, normed_mid, mid_own, cot = forward(
        parts, lengths, q, kv, tokens, cotangent, w_out, pack
    )
    kv_all = kv_all.reshape(8192, 128)
    normed_mid = normed_mid.reshape(512, 1024)
    cotangent = cot.reshape(512, 1024)

    gate = jnp.dot(normed_mid, w_gate, preferred_element_type=f32)
    up_proj = jnp.dot(normed_mid, w_up, preferred_element_type=f32)
    sigmoid_gate = jax.nn.sigmoid(gate)
    act = (gate * sigmoid_gate * up_proj).astype(bf16)
    mlp_part = jnp.dot(act, w_down, preferred_element_type=f32).astype(bf16)
    d_act = jnp.einsum("td,fd->tf", cotangent, w_down, preferred_element_type=f32)
    d_gate = (d_act * up_proj * sigmoid_gate * (1.0 + gate * (1.0 - sigmoid_gate))).astype(bf16)
    d_up = (d_act * gate * sigmoid_gate).astype(bf16)
    d_mid_part = (
        jnp.einsum("tf,df->td", d_gate, w_gate, preferred_element_type=f32)
        + jnp.einsum("tf,df->td", d_up, w_up, preferred_element_type=f32)
    ).astype(bf16)
    grads = (
        jnp.einsum("tf,td->fd", d_gate, normed_mid, preferred_element_type=f32).astype(bf16),
        jnp.einsum("tf,td->fd", d_up, normed_mid, preferred_element_type=f32).astype(bf16),
        jnp.einsum("tf,td->fd", act, cotangent, preferred_element_type=f32).astype(bf16),
    )
    output, grad_tokens, sums, g_ff, vec = backward(
        parts,
        d_mid_part.reshape(8, 64, 1024), mlp_part.reshape(8, 64, 1024), mid_own, cot,
        pack, w_out, *(g.reshape(4, 144, 1024) for g in grads),
        qa, mix_f, kv_all, ext, mixed,
        q_proj, kv_proj, normed, w_query, wkv, cosine, sine, tokens.reshape(8, 64, 1024),
    )
    (output, grad_tokens, g_query, g_key, g_value, g_out, g_gate, g_up, g_down, g_norm_in, g_norm_mid, g_qg, g_kg) = finish(
        sums, g_ff, output.reshape(512, 1024), grad_tokens.reshape(512, 1024), vec
    )
    return (
        output, grad_tokens, g_norm_in.reshape(1024), g_query, g_key.T, g_value.T, g_qg.reshape(64), g_kg.reshape(64),
        g_out, g_norm_mid.reshape(1024), g_gate.T, g_up.T, g_down,
    )


def solution(mesh):
    placed = (
        P("sp", None), P(), P(None, "wt"), P(None, "wt"), P(None, "wt"), P(), P(), P("wt", None), P(),
        P(None, "wt"), P(None, "wt"), P("wt", None), P("sp", None), P(),
    )
    return jax.shard_map(
        body,
        mesh=mesh,
        in_specs=placed,
        out_specs=(
            P("sp", None), P("sp", None), P(), P(None, "wt"), P(None, "wt"), P(None, "wt"), P(), P(),
            P("wt", None), P(), P(None, "wt"), P(None, "wt"), P("wt", None),
        ),
        check_vma=False,
    )
```

```python
import functools, math
import jax
import jax.numpy as jnp
import numpy as np
from jax import lax
from jax.experimental import pallas as pl
from jax.experimental.pallas import tpu as pltpu
from jax.sharding import PartitionSpec as P

f32 = jnp.float32
bf16 = jnp.bfloat16
sds = jax.ShapeDtypeStruct
DMA = pltpu.SemaphoreType.DMA
CH = 512
HALF = 256
SCALE = 0.125
C2 = SCALE * math.log2(math.e)


def starts_of(ids, len_ref):
    end = jnp.int32(0)
    start = jnp.zeros_like(ids)
    for j in range(4):
        end = end + len_ref[j]
        start = start + jnp.where(ids >= end, len_ref[j], 0)
    return start


def scalar_start(row, len_ref):
    end = jnp.int32(0)
    start = jnp.int32(0)
    for j in range(4):
        end = end + len_ref[j]
        start = start + jnp.where(row >= end, len_ref[j], 0)
    return start


def lanes(shape):
    return lax.broadcasted_iota(jnp.int32, shape, len(shape) - 1)


def split3(value, lane):
    hi = value.astype(bf16).astype(f32)
    rest = value - hi
    mid = rest.astype(bf16).astype(f32)
    low = rest - mid
    return jnp.where(lane == 0, hi, jnp.where(lane == 1, mid, jnp.where(lane == 2, low, 0.0)))


def tile_row(me, t, parts):
    return me * 512 if t == 0 else (parts - 1 - me) * 512 + HALF


FAR = 8192.0


def segment_bounds(len_ref, lane):
    begin = jnp.zeros_like(lane)
    end = jnp.zeros_like(lane)
    at = jnp.int32(0)
    for j in range(4):
        begin = jnp.where(lane == 3 + j, at, begin)
        at = at + len_ref[j]
        end = jnp.where(lane == 3 + j, at, end)
    return begin, end


def inside(ids, len_ref, shape):
    lane = lanes(shape)
    begin, end = segment_bounds(len_ref, lane)
    return (ids >= begin) & (ids < end), lane


def key_columns(k0, len_ref, rows):
    ids = k0 + lax.broadcasted_iota(jnp.int32, (rows, 128), 0)
    within, lane = inside(ids, len_ref, (rows, 128))
    return jnp.where(lane < 3, 1.0, jnp.where(within, 1.0, 0.0)).astype(bf16)


def query_columns(r0, len_ref, rows):
    ids = r0 + lax.broadcasted_iota(jnp.int32, (rows, 128), 0)
    within, lane = inside(ids, len_ref, (rows, 128))
    return jnp.where((lane < 3) | (lane > 6) | within, 0.0, -FAR)


smem = pl.BlockSpec(memory_space=pltpu.SMEM)
vmem = pl.BlockSpec(memory_space=pltpu.VMEM)


MESH = pl.DeviceIdType.MESH
eps = 1e-05


def rcopy(src, dst, send, recv, device):
    return pltpu.make_async_remote_copy(
        src_ref=src, dst_ref=dst, send_sem=send, recv_sem=recv, device_id=device, device_id_type=MESH
    )


def meet(devices):
    barrier = pltpu.get_barrier_semaphore()
    for device in devices:
        pl.semaphore_signal(barrier, inc=1, device_id=device, device_id_type=MESH)
    pl.semaphore_wait(barrier, len(devices))


class Place:
    def __init__(self):
        self.sp = lax.axis_index("sp")
        self.wt = lax.axis_index("wt")
        self.x, self.y = lax.div(self.sp, 4), lax.rem(self.sp, 4)
        self.z, self.c = lax.div(self.wt, 2), lax.rem(self.wt, 2)
        self.mirror = (15 - self.sp, self.wt)
        self.sibling = (self.sp, self.z * 2 + 1 - self.c)

    def along_x(self, d):
        return (lax.rem(self.x + d, 4) * 4 + self.y, self.wt)

    def along_y(self, d):
        return (self.x * 4 + lax.rem(self.y + d, 4), self.wt)

    def along_z(self, d):
        return (self.sp, lax.rem(self.z + d, 4) * 2 + self.c)

    def along_z_other(self, d):
        return (self.sp, lax.rem(self.z + d, 4) * 2 + 1 - self.c)

    def first(self, h, d):
        return self.along_x(d) if h == 0 else self.along_y(d)

    def second(self, h, d):
        return self.along_y(d) if h == 0 else self.along_x(d)

    def fsp(self, h):
        return self.x if h == 0 else self.y

    def ssp(self, h):
        return self.y if h == 0 else self.x


def spot(h, first, second):
    return (first, second) if h == 0 else (second, first)


ORDER = (2, 1, 3)


def to_blocks(value, rows, put):
    for x in range(4):
        for y in range(4):
            for h in range(2):
                block = value(x)[:, h * 512 + y * 128:h * 512 + y * 128 + 128]
                put(h, *spot(h, x, y), block)


class SpScatter:
    def __init__(self, p, srcs, refs):
        self.p, self.srcs = p, srcs
        self.r1, self.send, self.r2, self.fs, self.fr, self.ss, self.sr = refs
        self.one, self.two = {}, {}

    @staticmethod
    def scratch(n, rows):
        return [
            pltpu.VMEM((n, 2, 3, 4, rows, 128), bf16), pltpu.VMEM((n, 2, 3, rows, 128), bf16),
            pltpu.VMEM((n, 2, 3, rows, 128), bf16),
            DMA((n, 2, 3)), DMA((n, 2, 3)), DMA((n, 2, 3)), DMA((n, 2, 3)),
        ]

    def first(self, i):
        p = self.p
        for d in ORDER:
            for h in range(2):
                self.one[i, h, d] = rcopy(
                    self.srcs[i].at[h, lax.rem(p.fsp(h) + d, 4)], self.r1.at[i, h, d - 1],
                    self.fs.at[i, h, d - 1], self.fr.at[i, h, d - 1], p.first(h, d),
                )
                self.one[i, h, d].start()

    def part(self, i, h, b):
        value = self.srcs[i][h, self.p.fsp(h), b].astype(f32)
        for d in range(3):
            value = value + self.r1[i, h, d, b].astype(f32)
        return value

    def second(self, i):
        p = self.p
        for h in range(2):
            for d in ORDER:
                self.one[i, h, d].wait_recv()
            for e in ORDER:
                self.send[i, h, e - 1] = self.part(i, h, lax.rem(p.ssp(h) + e, 4)).astype(bf16)
                self.two[i, h, e] = rcopy(
                    self.send.at[i, h, e - 1], self.r2.at[i, h, e - 1],
                    self.ss.at[i, h, e - 1], self.sr.at[i, h, e - 1], p.second(h, e),
                )
                self.two[i, h, e].start()

    def own(self, i, h):
        value = self.part(i, h, self.p.ssp(h))
        for e in ORDER:
            self.two[i, h, e].wait_recv()
            value = value + self.r2[i, h, e - 1].astype(f32)
        return value

    def finish(self):
        for copy in list(self.one.values()) + list(self.two.values()):
            copy.wait_send()


class SpGather:
    def __init__(self, p, out, sems):
        self.p, self.out = p, out
        self.fs, self.fr, self.ss, self.sr = sems
        self.one, self.two, self.further = {}, {}, {}

    @staticmethod
    def sems(n):
        return [DMA((n, 2, k)) for k in (3, 3, 4, 4)]

    def put(self, i, h, value):
        self.out[i, h, self.p.fsp(h), self.p.ssp(h)] = value

    def first(self, i, h):
        block = self.out.at[i, h, self.p.fsp(h), self.p.ssp(h)]
        for e in ORDER:
            self.one[i, h, e] = rcopy(
                block, block, self.fs.at[i, h, e - 1], self.fr.at[i, h, e - 1], self.p.second(h, e)
            )
            self.one[i, h, e].start()

    def second(self, i, h):
        for e in ORDER:
            self.one[i, h, e].wait_recv()
        block = self.out.at[i, h, self.p.fsp(h)]
        for d in ORDER:
            self.two[i, h, d] = rcopy(
                block, block, self.ss.at[i, h, d - 1], self.sr.at[i, h, d - 1], self.p.first(h, d)
            )
            self.two[i, h, d].start()

    def relayed(self, i, h):
        for e in ORDER:
            self.one[i, h, e].wait_recv()
        block = self.out.at[i, h, self.p.fsp(h)]
        for slot, d in enumerate((1, 3)):
            self.two[i, h, slot] = rcopy(
                block, block, self.ss.at[i, h, slot], self.sr.at[i, h, slot], self.p.first(h, d)
            )
            self.two[i, h, slot].start()

    def relay(self, i, h):
        for slot, d in enumerate((1, 3)):
            self.two[i, h, slot].wait_recv()
            block = self.out.at[i, h, lax.rem(self.p.fsp(h) + 4 - d, 4), pl.ds(2 * slot, 2)]
            self.further[i, h, slot] = rcopy(
                block, block, self.ss.at[i, h, 2 + slot], self.sr.at[i, h, 2 + slot], self.p.first(h, d)
            )
            self.further[i, h, slot].start()

    def finish(self):
        for copy in self.one.values():
            copy.wait_send()
        for copy in self.two.values():
            copy.wait_send() if self.further else copy.wait()
        for copy in self.further.values():
            copy.wait()


SPLIT = 2


def sub(s):
    return pl.ds(s * (64 // SPLIT), 64 // SPLIT)


class WtSum:
    def __init__(self, p, part, sib, send, rz, sems):
        self.p, self.part, self.sib, self.send, self.rz = p, part, sib, send, rz
        self.cs, self.cr, self.zs, self.zr = sems
        self.second = {}

    def core(self, zz, s):
        return rcopy(
            self.part.at[zz * 2 + 1 - self.p.c, sub(s)], self.sib.at[zz, sub(s)],
            self.cs.at[zz, s], self.cr.at[zz, s], self.p.sibling,
        )

    def start_core(self, zz):
        for s in range(SPLIT):
            self.core(zz, s).start()

    def pair(self, zz, s):
        return self.part[zz * 2 + self.p.c, sub(s)].astype(f32) + self.sib[zz, sub(s)].astype(f32)

    def send_z(self):
        for s in range(SPLIT):
            for d in ORDER:
                zz = lax.rem(self.p.z + d, 4)
                self.core(zz, s).wait_recv()
                self.send[d - 1, sub(s)] = self.pair(zz, s).astype(bf16)
                copy = rcopy(
                    self.send.at[d - 1, sub(s)], self.rz.at[d - 1, sub(s)],
                    self.zs.at[d - 1, s], self.zr.at[d - 1, s], self.p.along_z(d),
                )
                copy.start()
                self.second[d, s] = copy

    def own(self, s):
        self.core(self.p.z, s).wait_recv()
        value = self.pair(self.p.z, s)
        for d in (1, 3, 2):
            self.second[d, s].wait_recv()
            value = value + self.rz[d - 1, sub(s)].astype(f32)
        return value

    def finish(self):
        for zz in range(4):
            for s in range(SPLIT):
                self.core(zz, s).wait_send()
        for copy in self.second.values():
            copy.wait_send()


class WtGather:
    def __init__(self, p, out, sems):
        self.p, self.out = p, out
        self.zs, self.zr, self.gs, self.gr = sems
        self.far, self.near = {}, {}

    def start(self, s):
        p = self.p
        block = self.out.at[p.wt, sub(s)]
        for d in ORDER:
            self.far[d, s] = rcopy(block, block, self.zs.at[d - 1, s], self.zr.at[d - 1, s], p.along_z(d))
            self.far[d, s].start()
        self.pass_on(0, s)

    def pass_on(self, slot, s):
        p = self.p
        block = self.out.at[lax.rem(p.z + 4 - slot, 4) * 2 + p.c, sub(s)]
        self.near[slot, s] = rcopy(block, block, self.gs.at[slot, s], self.gr.at[slot, s], p.sibling)
        self.near[slot, s].start()

    def forward(self):
        for s in range(SPLIT):
            for d in (1, 3, 2):
                self.far[d, s].wait_recv()
                self.pass_on(d, s)

    def arrived(self):
        for copy in self.near.values():
            copy.wait_recv()

    def finish(self):
        for copy in list(self.far.values()) + list(self.near.values()):
            copy.wait_send()


def rms_of(value):
    return lax.rsqrt(jnp.mean(value * value, axis=-1, keepdims=True) + eps)


def norm_back(values, scale, gain, grad):
    scaled = grad * gain
    inner = jnp.mean(scaled * values, axis=-1, keepdims=True)
    return scale * scaled - values * scale * scale * scale * inner


def wt_peers(p):
    return [p.sibling] + [p.along_z(d) for d in ORDER]


class Flow:
    def __init__(self):
        self.copies = []

    def send(self, *args):
        copy = rcopy(*args)
        copy.start()
        self.copies.append(copy)
        return copy

    def finish(self):
        for copy in self.copies:
            copy.wait_send()


def forward_kernel(
    parts,
    len_ref, q_ref, kv_ref, tok_ref, cot_ref, w_ref, pack_ref,
    all_ref, ext_ref, qa_ref, mixf_ref, mix_ref, nm_ref, mid_ref, cotz_ref,
    qz, base, acc, part, sib, send, rz, ms, mr, cs, cr, zs, zr, az, bz, ag, bg, fs, fr, ss, sr,
):
    p = Place()
    me = p.sp
    meet(wt_peers(p) + [p.along_x(d) for d in ORDER] + [p.along_y(d) for d in ORDER] + [p.mirror])
    flow = Flow()
    first = {}
    for d in ORDER:
        for h in range(2):
            first[h, d] = flow.send(
                kv_ref.at[h], all_ref.at[p.x, p.y, h], fs.at[h, d - 1], fr.at[h, d - 1], p.first(h, d)
            )
    q_mirror = flow.send(q_ref.at[1], qz.at[1], ms.at[0], mr.at[0], p.mirror)

    def pass_on(h, slot):
        a = lax.rem(p.fsp(h) + 4 - slot, 4)
        at = spot(h, a, p.ssp(h))
        for e in ORDER:
            src = kv_ref.at[h] if slot == 0 else all_ref.at[at[0], at[1], h]
            flow.send(src, all_ref.at[at[0], at[1], h], ss.at[h, slot, e - 1], sr.at[h, slot, e - 1], p.second(h, e))

    for h in range(2):
        pass_on(h, 0)
    token_mirror = rcopy(tok_ref.at[p.wt], base, ms.at[1], mr.at[1], p.mirror)

    @pl.when(p.wt >= 4)
    def _():
        token_mirror.start()

    @pl.when(p.wt < 4)
    def _():
        base[...] = tok_ref[p.wt]

    all_ref[p.x, p.y] = kv_ref[...]
    qz[0] = q_ref[0]
    cotz_ref[0:4] = cot_ref[0:4]

    @pl.loop(0, 8)
    def _(b):
        rows = pl.ds(pl.multiple_of(b * 1024, 1024), 1024)
        ext_ref[rows, :] = key_columns(b * 1024, len_ref, 1024)

    lane = lanes((HALF, 128))
    lane2 = lanes((2 * HALF, 128))
    lanek = lanes((CH, 128))
    acc[...] = jnp.zeros_like(acc)
    blocks = (me, parts - 1 - me)
    begins = (me * 512, (parts - 1 - me) * 512 + HALF)

    def prepare(t):
        q = qz[t].astype(f32)
        qa_ref[t, 0:HALF, 0:128] = jnp.where(lane < 64, q, 0.0).astype(bf16)
        qa_ref[t, HALF:, 0:128] = jnp.where(lane < 64, pltpu.roll(q, 64, 1), 0.0).astype(bf16)
        columns = query_columns(begins[t], len_ref, HALF).astype(bf16)
        qa_ref[t, 0:HALF, 128:256] = columns
        qa_ref[t, HALF:, 128:256] = columns

    def step(t, x, y, masked):
        k0 = pl.multiple_of((x * 4 + y) * CH, CH)
        kv = all_ref[x, y].reshape(CH, 128)
        kva = jnp.concatenate([kv, ext_ref[pl.ds(k0, CH), :]], axis=1)
        pr = jnp.exp2(nt(qa_ref[t], kva) * C2)
        if masked:
            rows = begins[t] + lax.rem(lax.broadcasted_iota(jnp.int32, (2 * HALF, 1), 0), HALF)
            keys = k0 + lax.broadcasted_iota(jnp.int32, (2 * HALF, CH), 1)
            pr = jnp.where(keys <= rows, pr, 0.0)
        ones = jnp.where(lanek < 64, jnp.ones_like(kv), kv)
        acc[t] += jnp.dot(pr.astype(bf16), ones, preferred_element_type=f32)

    def both(x, y):
        block = x * 4 + y

        @pl.when(block < blocks[0])
        def _():
            step(0, x, y, False)

        @pl.when(block < blocks[1])
        def _():
            step(1, x, y, False)

        @pl.when(block == blocks[1])
        def _():
            step(1, x, y, True)

    prepare(0)
    step(0, p.x, p.y, True)
    for d in (1, 3, 2):
        for h in range(2):
            first[h, d].wait_recv()
            pass_on(h, d)
    q_mirror.wait_recv()
    prepare(1)

    @pl.when(me < blocks[1])
    def _():
        step(1, p.x, p.y, False)

    def wait_for(x, y, h, slot, e):
        block = all_ref.at[x, y, h]
        rcopy(block, block, ss.at[h, slot, e - 1], sr.at[h, slot, e - 1], p.second(h, 1)).wait_recv()

    @pl.loop(1, 4)
    def _(d):
        x = lax.rem(p.x + 4 - d, 4)
        wait_for(x, p.y, 1, 0, d)
        both(x, p.y)

    @pl.loop(1, 4)
    def _(d):
        y = lax.rem(p.y + 4 - d, 4)
        wait_for(p.x, y, 0, 0, d)
        both(p.x, y)

    @pl.loop(0, 9)
    def _(k):
        dx, dy = 1 + lax.div(k, 3), 1 + lax.rem(k, 3)
        x, y = lax.rem(p.x + 4 - dx, 4), lax.rem(p.y + 4 - dy, 4)
        wait_for(x, y, 0, dx, dy)
        wait_for(x, y, 1, dy, dx)
        both(x, y)

    total = WtSum(p, part, sib, send, rz, (cs, cr, zs, zr))
    cot_mirror = flow.send(cot_ref.at[pl.ds(4, 4)], cotz_ref.at[pl.ds(4, 4)], ms.at[2], mr.at[2], p.mirror)
    for t in range(2):
        value = acc[t]
        swapped = pltpu.roll(value, 64, 1)
        o = swapped / value
        mix = jnp.where(lane < 64, o[:HALF], pltpu.roll(o[HALF:], 64, 1))
        mixf_ref[t] = mix
        mix = mix.astype(bf16)
        mix_ref[t] = mix
        part[t * 4:t * 4 + 4] = jnp.dot(mix, w_ref[...], preferred_element_type=f32).astype(bf16).reshape(4, 64, 1024)
        for zz in (t * 2, t * 2 + 1):
            total.start_core(zz)
    total.send_z()
    for t in range(2):
        value = acc[t]
        weights = jnp.where(lane2 < 64, value, pltpu.roll(value, 64, 1))
        columns = qa_ref[t, :, 128:256].astype(f32)
        qa_ref[t, :, 128:256] = (split3(jnp.log(weights) * (-1.0 / SCALE), lane2) + columns).astype(bf16)

    @pl.when(p.wt >= 4)
    def _():
        token_mirror.wait()

    spread = WtGather(p, nm_ref, (az, bz, ag, bg))
    for s in range(SPLIT):
        middle = base[sub(s)].astype(f32) + total.own(s)
        mid_ref[sub(s)] = middle
        nm_ref[p.wt, sub(s)] = (middle * rms_of(middle) * pack_ref[1:2]).astype(bf16)
        spread.start(s)
    spread.forward()
    cot_mirror.wait_recv()
    spread.arrived()
    for part in (spread, total, flow):
        part.finish()


WT_SEMS = [DMA((n, SPLIT)) for n in (4, 4, 3, 3, 3, 3, 4, 4)]


def comm_call(kernel, number, out_shape, args, scratch, name, limit=10, first=None):
    return pl.pallas_call(
        kernel,
        out_shape=out_shape,
        in_specs=[first or vmem] + [vmem] * (len(args) - 1),
        out_specs=tuple(vmem for _ in out_shape),
        scratch_shapes=scratch,
        compiler_params=pltpu.CompilerParams(
            collective_id=number, has_side_effects=True, vmem_limit_bytes=limit << 20
        ),
        cost_estimate=pl.CostEstimate(flops=8 << 30, bytes_accessed=32 << 20, transcendentals=0),
        name=name,
    )(*args)


def forward(parts, lengths, q, kv, tokens, cotangent, w_out, pack):
    rows = pltpu.VMEM
    half = sds((2, 256, 128), bf16)
    full = sds((8, 64, 1024), bf16)
    return comm_call(
        functools.partial(forward_kernel, parts), 1,
        (sds((4, 4, 2, 256, 128), bf16), sds((8192, 128), bf16), sds((2, 512, 256), bf16), sds((2, 256, 128), f32),
         half, full, sds((64, 1024), f32), full),
        (lengths, q.reshape(2, 256, 128), kv.reshape(2, 256, 128), tokens.reshape(8, 64, 1024),
         cotangent.reshape(8, 64, 1024), w_out, pack),
        [rows((2, 256, 128), bf16), rows((64, 1024), bf16), rows((2, 512, 128), f32), rows((8, 64, 1024), bf16),
         rows((4, 64, 1024), bf16), rows((3, 64, 1024), bf16), rows((3, 64, 1024), bf16), DMA((3,)), DMA((3,))]
        + WT_SEMS + [DMA((2, 3)), DMA((2, 3)), DMA((2, 4, 3)), DMA((2, 4, 3))],
        "forward", 16, smem,
    )


def turned(value, lane):
    return jnp.where(lax.rem(lane, 64) < 32, pltpu.roll(value, 96, 1), pltpu.roll(value, 32, 1))


def head_sums(value, lane):
    s0 = jnp.sum(jnp.where(lane < 64, value, 0.0), axis=1, keepdims=True)
    s1 = jnp.sum(jnp.where(lane < 64, 0.0, value), axis=1, keepdims=True)
    return jnp.where(lane < 64, s0, s1)


def nt(a, b):
    return lax.dot_general(a, b, (((1,), (1,)), ((), ())), preferred_element_type=f32)


def tn(a, b):
    return lax.dot_general(a, b, (((0,), (0,)), ((), ())), preferred_element_type=f32)


FREQS = [float(np.float32(1000000.0 ** (-2.0 * i / 64))) for i in range(32)]


def proj_kernel(len_ref, tok_ref, pack_ref, wq_ref, wkv_ref, n_ref, qp_ref, kvp_ref, q_ref, kv_ref, cos_ref, sin_ref):
    lane = lanes((512, 128))
    ids = lax.axis_index("sp") * 512 + lax.broadcasted_iota(jnp.int32, (1, 512), 1)
    positions = (ids - starts_of(ids, len_ref)).astype(f32)
    row = lax.broadcasted_iota(jnp.int32, (32, 512), 0)
    freqs = jnp.zeros((32, 512), f32)
    for i, freq in enumerate(FREQS):
        freqs = jnp.where(row == i, freq, freqs)
    angles = positions * freqs
    cosine, sine = jnp.cos(angles), jnp.sin(angles)
    cosine = jnp.concatenate([cosine] * 4, axis=0).T
    sine = jnp.concatenate([-sine, sine, -sine, sine], axis=0).T
    cos_ref[...] = cosine
    sin_ref[...] = sine
    base = tok_ref[...].astype(f32)
    normed = (base * rms_of(base) * pack_ref[0:1]).astype(bf16)
    n_ref[...] = normed
    q = jnp.dot(normed, wq_ref[...], preferred_element_type=f32)
    qp_ref[...] = q
    q = q * lax.rsqrt(head_sums(q * q, lane) * (1.0 / 64) + eps) * pack_ref[2:3, 0:128]
    q_ref[...] = (q * cosine + turned(q, lane) * sine).astype(bf16)
    kv = nt(normed, wkv_ref[...])
    kvp_ref[...] = kv
    k = kv * lax.rsqrt(head_sums(kv * kv, lane) * (1.0 / 64) + eps) * pack_ref[2:3, 128:256]
    k = k * cosine + turned(k, lane) * sine
    kv_ref[...] = jnp.where(lane < 64, k, kv).astype(bf16)


def project(*args):
    wide = sds((512, 128), f32)
    out_shape = (sds((512, 1024), bf16), wide, wide, sds((512, 128), bf16), sds((512, 128), bf16), wide, wide)
    return pl.pallas_call(
        proj_kernel,
        out_shape=out_shape,
        in_specs=[smem] + [vmem] * 4,
        out_specs=tuple(vmem for _ in out_shape),
        compiler_params=pltpu.CompilerParams(vmem_limit_bytes=12 << 20),
        name="project",
    )(*args)


def backward_kernel(
    parts,
    dm_ref, mlp_ref, mid_ref, cot_ref, pack_ref, w_ref, g0_ref, g1_ref, g2_ref,
    qa_ref, mixf_ref, kv_ref, ext_ref, mixed_ref,
    qp_ref, kvp_ref, n_ref, wq_ref, wkv_ref, cos_ref, sin_ref, tok_ref,
    out_ref, gt_ref, sums_ref, ff_ref, vec_ref,
    *scratch,
):
    scratch = list(scratch)

    def take(n):
        got = scratch[:n]
        del scratch[:n]
        return got

    p = Place()
    me = p.sp
    meet(
        wt_peers(p) + [p.along_z_other(d) for d in ORDER] + [p.mirror]
        + [p.along_x(d) for d in ORDER] + [p.along_y(d) for d in ORDER]
    )
    flow = Flow()

    def wt_sum(ref):
        sib, send, rz = take(3)
        return WtSum(p, ref, sib, send, rz, take(4))

    da, dz, dmid, dmid_o, out_own = take(5)
    mirror_sems = take(6)
    d_mid_sum = wt_sum(dm_ref)
    da_gather = WtGather(p, da, take(4))
    mlp_sum = wt_sum(mlp_ref)
    out_gather = WtGather(p, out_ref, take(4))
    (ffb,) = take(1)
    ff = SpScatter(p, [ffb.at[i] for i in range(3)], take(7))
    ff_back = SpGather(p, ff_ref, take(4))
    dab, acc, dqt, dqz, dq, dkv, dkv_own = take(7)
    r1, send1, r2, fs, fr, ss, sr = take(7)
    dn, gqkv, gout = take(3)
    dn_sum = wt_sum(dn)
    gt_gather = WtGather(p, gt_ref, take(4))
    sums = SpScatter(p, (gout, gqkv.at[0], gqkv.at[1]), take(7))
    sums_back = SpGather(p, sums_ref, take(4))
    vw, vx, vy, vs1, vr1, vs2, vr2, vs3, vr3 = take(9)
    assert not scratch

    for zz in range(4):
        d_mid_sum.start_core(zz)
    for i, ref in enumerate((g0_ref, g1_ref, g2_ref)):
        def put(h, u, v, block, i=i):
            ffb[i, h, u, v] = block

        to_blocks(lambda x, ref=ref: ref[x], 144, put)
        ff.first(i)
        if i == 0:
            d_mid_sum.send_z()
    vw[0] = jnp.zeros((8, 1024), f32)
    acc[...] = jnp.zeros_like(acc)
    dqt[...] = jnp.zeros_like(dqt)
    for s in range(SPLIT):
        middle = mid_ref[sub(s)]
        scale = rms_of(middle)
        d_mid = d_mid_sum.own(s)
        d_middle = cot_ref[p.wt, sub(s)].astype(f32) + norm_back(middle, scale, pack_ref[1:2], d_mid)
        da[p.wt, sub(s)] = d_middle.astype(bf16)
        da_gather.start(s)
        dmid[sub(s)] = d_middle
        vw[0, 1:2] += jnp.sum(d_mid * middle * scale, axis=0, keepdims=True)
    dmid_mirror = rcopy(dmid, dmid_o, mirror_sems[2], mirror_sems[3], p.mirror)

    @pl.when(p.wt >= 4)
    def _():
        dmid_mirror.start()

    da_gather.forward()
    da_gather.arrived()
    for zz in range(4):
        mlp_sum.start_core(zz)
    dz[...] = nt(da[...].reshape(512, 1024), w_ref[...]).astype(bf16).reshape(2, 256, 128)
    mlp_sum.send_z()

    lane = lanes((HALF, 128))
    for t in range(2):
        do = dz[t].astype(f32)
        prod = do * mixf_ref[t]
        d0 = -jnp.sum(jnp.where(lane < 64, prod, 0.0), axis=1, keepdims=True)
        d1 = -jnp.sum(jnp.where(lane < 64, 0.0, prod), axis=1, keepdims=True)
        dab[t, 0:HALF, 0:128] = jnp.where(lane < 64, 0.0, pltpu.roll(do, 64, 1)).astype(bf16)
        dab[t, HALF:, 0:128] = jnp.where(lane < 64, 0.0, do).astype(bf16)
        dab[t, 0:HALF, 128:256] = split3(jnp.broadcast_to(d0, (HALF, 128)), lane).astype(bf16)
        dab[t, HALF:, 128:256] = split3(jnp.broadcast_to(d1, (HALF, 128)), lane).astype(bf16)
    upper_long = (me < parts // 2).astype(jnp.int32)
    blocks = [me + t * (parts - 1 - 2 * me) for t in (upper_long, 1 - upper_long)]

    def step(k, masked):
        short = (k > blocks[0]).astype(jnp.int32)
        t = upper_long + short * (1 - 2 * upper_long)
        c = k - short * (blocks[0] + 1)
        k0 = pl.multiple_of(c * CH, CH)
        kv = kv_ref[pl.ds(k0, CH), :]
        kva = jnp.concatenate([kv, ext_ref[pl.ds(k0, CH), :]], axis=1)
        qa = qa_ref[t]
        d_out = dab[t]
        pr = jnp.exp2(nt(kva, qa) * C2)
        if masked:
            r0 = c * 512 + t * HALF
            rows = r0 + lax.rem(lax.broadcasted_iota(jnp.int32, (1, 2 * HALF), 1), HALF)
            keys = k0 + lax.broadcasted_iota(jnp.int32, (CH, 2 * HALF), 0)
            pr = jnp.where(keys <= rows, pr, 0.0)
        ds = (pr * nt(kva, d_out)).astype(bf16)
        acc[pl.ds(k0, CH), :] += jnp.dot(
            pr.astype(bf16), d_out[:, 0:128], preferred_element_type=f32
        ) + jnp.dot(ds, qa[:, 0:128], preferred_element_type=f32)
        kt = kv.T[0:64, :]
        dqt[t] += jnp.dot(kt, ds, preferred_element_type=f32)

    def plain(k):
        step(k, False)

    def either(k):
        pl.when(k == blocks[0])(lambda: step(k, True))
        pl.when(k != blocks[0])(lambda: step(k, False))

    ff.second(0)
    ff.second(1)
    pl.loop(0, 3)(plain)
    ff.second(2)
    pl.loop(3, 5)(plain)
    for i in range(3):
        for h in range(2):
            ff_back.put(i, h, ff.own(i, h).astype(bf16))
            ff_back.first(i, h)
    pl.loop(5, 8)(plain)
    for h in range(2):
        ff_back.relayed(0, h)
    for s in range(SPLIT):
        out_own[sub(s)] = (mid_ref[sub(s)] + mlp_sum.own(s)).astype(bf16)
    out_mirror = rcopy(out_own, out_ref.at[p.wt], mirror_sems[4], mirror_sems[5], p.mirror)

    @pl.when(p.wt >= 4)
    def _():
        out_mirror.start()

    @pl.when(p.wt < 4)
    def _():
        out_ref[p.wt] = out_own[...]

    def put_out(h, u, v, block):
        gout[h, u, v] = block

    g_out = tn(mixed_ref[...].reshape(512, 128), da[...].reshape(512, 1024)).astype(bf16)
    to_blocks(lambda x: g_out[x * 32:x * 32 + 32], 32, put_out)
    sums.first(0)
    pl.loop(8, 12)(either)
    for h in range(2):
        ff_back.relayed(1, h)
    for h in range(2):
        ff_back.relay(0, h)
    sums.second(0)

    @pl.when(p.wt >= 4)
    def _():
        out_mirror.wait()

    for s in range(SPLIT):
        out_gather.start(s)
    pl.loop(12, 16)(either)
    step(16, True)
    for t in range(2):
        both = jnp.concatenate([dqt[t, :, :HALF], dqt[t, :, HALF:]], axis=0)
        dqz[t] = (both.T * SCALE).astype(bf16)
    weight = jnp.where(lanes((512, 128)) < 64, SCALE, 1.0)

    @pl.loop(0, parts)
    def _(b):
        rows = pl.ds(pl.multiple_of(b * 512, 512), 512)
        dkv[lax.div(b, 4), lax.rem(b, 4)] = (acc[rows, :] * weight).astype(bf16).reshape(2, 256, 128)

    mirror = flow.send(dqz.at[1], dq.at[1], mirror_sems[0], mirror_sems[1], p.mirror)
    dq[0] = dqz[0]
    first, second = {}, {}
    for e in (2, 1, 3, 0):
        for d in ORDER:
            for h in range(2):
                at = spot(h, lax.rem(p.fsp(h) + d, 4), lax.rem(p.ssp(h) + e, 4))
                first[h, d, e] = flow.send(
                    dkv.at[at[0], at[1], h], r1.at[h, d - 1, e], fs.at[h, d - 1, e], fr.at[h, d - 1, e], p.first(h, d)
                )

    def total(h, e):
        at = spot(h, p.fsp(h), lax.rem(p.ssp(h) + e, 4))
        value = dkv[at[0], at[1], h].astype(f32)
        for d in ORDER:
            first[h, d, e].wait_recv()
            value = value + r1[h, d - 1, e].astype(f32)
        return value

    out_gather.forward()
    for e in ORDER:
        for h in range(2):
            send1[h, e - 1] = total(h, e).astype(bf16)
            second[h, e] = flow.send(
                send1.at[h, e - 1], r2.at[h, e - 1], ss.at[h, e - 1], sr.at[h, e - 1], p.second(h, e)
            )
    own = [total(h, 0) for h in range(2)]
    for h in range(2):
        ff_back.relayed(2, h)
        ff_back.relay(1, h)
        sums_back.put(0, h, sums.own(0, h).astype(bf16))
        sums_back.first(0, h)
    for h in range(2):
        value = own[h]
        for e in ORDER:
            second[h, e].wait_recv()
            value = value + r2[h, e - 1].astype(f32)
        dkv_own[h] = value.astype(bf16)
    mirror.wait_recv()

    wide = lanes((512, 128))
    cosine, sine = cos_ref[...], sin_ref[...]

    def back(grad, proj, gain):
        grad = grad * cosine - turned(grad, wide) * sine
        scale = lax.rsqrt(head_sums(proj * proj, wide) * (1.0 / 64) + eps)
        scaled = grad * gain
        inner = head_sums(scaled * proj, wide) * (1.0 / 64)
        gains = jnp.sum(grad * proj * scale, axis=0, keepdims=True)
        return scale * scaled - proj * scale * scale * scale * inner, gains

    d_q, gq = back(dq[...].reshape(512, 128).astype(f32), qp_ref[...], pack_ref[2:3, 0:128])
    dkv_in = dkv_own[...].reshape(512, 128).astype(f32)
    d_k, gk = back(dkv_in, kvp_ref[...], pack_ref[2:3, 128:256])
    d_q = d_q.astype(bf16)
    d_kv = jnp.where(wide < 64, d_k, dkv_in).astype(bf16)
    dn[...] = (nt(d_q, wq_ref[...]) + jnp.dot(d_kv, wkv_ref[...], preferred_element_type=f32)).astype(bf16).reshape(8, 64, 1024)
    for zz in range(4):
        dn_sum.start_core(zz)
    normed = n_ref[...]
    for i, grad in enumerate((d_q, d_kv)):
        def put_in(h, u, v, block, i=i):
            gqkv[i, h, u, v] = block

        g_in = tn(grad, normed).astype(bf16)
        to_blocks(lambda x, g_in=g_in: g_in[x * 32:x * 32 + 32], 32, put_in)
    for i in (1, 2):
        sums.first(i)
    dn_sum.send_z()

    gains = jnp.zeros((1, 1024), f32)
    for w in range(8):
        base = tok_ref[w].astype(f32)
        gains = gains + jnp.sum(dn[w].astype(f32) * base * rms_of(base), axis=0, keepdims=True)
    vw[0, 0:1] = gains
    vw[0, 2:3] = jnp.concatenate([gq, gk, jnp.zeros((1, 768), f32)], axis=1)

    def vec_round(buf, devices, sends, recvs):
        return [
            flow.send(buf.at[0], buf.at[i + 1], sends.at[i], recvs.at[i], device) for i, device in enumerate(devices)
        ]

    def vec_total(buf, copies):
        value = buf[0]
        for i, copy in enumerate(copies):
            copy.wait_recv()
            value = value + buf[i + 1]
        return value

    round1 = vec_round(vw, [p.along_z(d) for d in ORDER] + [p.along_z_other(d) for d in ORDER] + [p.sibling], vs1, vr1)
    for i in (1, 2):
        sums.second(i)
    for h in range(2):
        ff_back.relay(2, h)
        sums_back.second(0, h)

    @pl.when(p.wt >= 4)
    def _():
        dmid_mirror.wait()

    @pl.when(p.wt < 4)
    def _():
        dmid_o[...] = dmid[...]

    for s in range(SPLIT):
        base = tok_ref[p.wt, sub(s)].astype(f32)
        d_normed = dn_sum.own(s)
        gt_ref[p.wt, sub(s)] = (
            dmid_o[sub(s)] + norm_back(base, rms_of(base), pack_ref[0:1], d_normed)
        ).astype(bf16)
        gt_gather.start(s)
    for i in (1, 2):
        for h in range(2):
            sums_back.put(i, h, sums.own(i, h).astype(bf16))
            sums_back.first(i, h)
    vx[0] = vec_total(vw, round1)
    round2 = vec_round(vx, [p.along_x(d) for d in ORDER], vs2, vr2)
    for i in (1, 2):
        for h in range(2):
            sums_back.second(i, h)
    vy[0] = vec_total(vx, round2)
    round3 = vec_round(vy, [p.along_y(d) for d in ORDER], vs3, vr3)
    gt_gather.forward()
    vec_ref[...] = vec_total(vy, round3)
    out_gather.arrived()
    gt_gather.arrived()
    for part in (d_mid_sum, da_gather, mlp_sum, out_gather, ff, ff_back, dn_sum, gt_gather, sums, sums_back, flow):
        part.finish()


def backward(parts, *args):
    rows = pltpu.VMEM
    wt_rows = [rows((4, 64, 1024), bf16), rows((3, 64, 1024), bf16), rows((3, 64, 1024), bf16)]
    wt_sum = wt_rows + WT_SEMS[:4]
    wt_gather = WT_SEMS[4:]
    half = rows((2, 256, 128), bf16)
    return comm_call(
        functools.partial(backward_kernel, parts), 4,
        (sds((8, 64, 1024), bf16), sds((8, 64, 1024), bf16), sds((3, 2, 4, 4, 32, 128), bf16), sds((3, 2, 4, 4, 144, 128), bf16),
         sds((8, 1024), f32)),
        args,
        [rows((8, 64, 1024), bf16), half, rows((64, 1024), f32), rows((64, 1024), f32), rows((64, 1024), bf16)] + [DMA] * 6
        + wt_sum + wt_gather + wt_sum + wt_gather
        + [rows((3, 2, 4, 4, 144, 128), bf16)] + SpScatter.scratch(3, 144) + SpGather.sems(3)
        + [rows((2, 512, 256), bf16), rows((8192, 128), f32), rows((2, 64, 512), f32), half, half,
           rows((4, 4, 2, 256, 128), bf16), half]
        + [rows((2, 3, 4, 256, 128), bf16), rows((2, 3, 256, 128), bf16), rows((2, 3, 256, 128), bf16)]
        + [DMA((2, 3, 4)), DMA((2, 3, 4)), DMA((2, 3)), DMA((2, 3))]
        + [rows((8, 64, 1024), bf16), rows((2, 2, 4, 4, 32, 128), bf16), rows((2, 4, 4, 32, 128), bf16)]
        + wt_sum + wt_gather
        + SpScatter.scratch(3, 32) + SpGather.sems(3)
        + [rows((8, 8, 1024), f32), rows((4, 8, 1024), f32), rows((4, 8, 1024), f32),
           DMA((7,)), DMA((7,)), DMA((3,)), DMA((3,)), DMA((3,)), DMA((3,))],
        "backward", 30,
    )


def finish_kernel(sums_ref, ff_ref, out_in, gt_in, vec_ref, out_ref, gt_ref, gq_ref, gk_ref, gv_ref, go_ref, gg_ref, gu_ref, gd_ref,
                  ni_ref, nm_ref, qg_ref, kg_ref, wide, tall, big, ff, sems, load_sems):
    copies = []

    def write(src, dst):
        copies.append(pltpu.make_async_copy(src, dst, sems.at[len(copies)]))
        copies[-1].start()

    write(out_in, out_ref)
    write(gt_in, gt_ref)
    loads = [pltpu.make_async_copy(ff_ref.at[i], ff.at[i], load_sems.at[i]) for i in range(3)]
    for load in loads:
        load.start()

    def assemble(out, blocks, x, rows):
        for h in range(2):
            for y in range(4):
                columns = slice(h * 512 + y * 128, h * 512 + y * 128 + 128)
                out[x * rows:(x + 1) * rows, columns] = blocks[(h,) + spot(h, x, y)].astype(f32)

    for i, ref in enumerate((gg_ref, gu_ref, gd_ref)):
        loads[i].wait()
        for x in range(4):
            assemble(big.at[i], ff.at[i], x, 144)
            rows = pl.ds(x * 144, 144)
            write(big.at[i, rows], ref.at[rows])
    for i in range(3):
        for x in range(4):
            assemble(wide.at[i], sums_ref.at[i], x, 32)
    write(wide.at[2, 0:64], gk_ref)
    write(wide.at[2, 64:128], gv_ref)
    write(wide.at[0], go_ref)
    tall[...] = wide[1].T
    write(tall, gq_ref)
    ni_ref[...] = vec_ref[0:1, :]
    nm_ref[...] = vec_ref[1:2, :]
    qg_ref[...] = vec_ref[2:3, 0:64] + vec_ref[2:3, 64:128]
    kg_ref[...] = vec_ref[2:3, 128:192]
    for copy in copies:
        copy.wait()


def finish(sums, ff, output, grad_tokens, vec):
    hbm = pl.BlockSpec(memory_space=pl.ANY)
    rows = sds((576, 1024), f32)
    return pl.pallas_call(
        finish_kernel,
        out_shape=(sds((512, 1024), bf16), sds((512, 1024), bf16), sds((1024, 128), f32), sds((64, 1024), f32), sds((64, 1024), f32),
                   sds((128, 1024), f32), rows, rows, rows,
                   sds((1, 1024), f32), sds((1, 1024), f32), sds((1, 64), f32), sds((1, 64), f32)),
        in_specs=[vmem, hbm, vmem, vmem, vmem],
        out_specs=tuple([hbm] * 9 + [vmem] * 4),
        scratch_shapes=[pltpu.VMEM((3, 128, 1024), f32), pltpu.VMEM((1024, 128), f32), pltpu.VMEM((3, 576, 1024), f32), pltpu.VMEM((3, 2, 4, 4, 144, 128), bf16), DMA((18,)), DMA((3,))],
        compiler_params=pltpu.CompilerParams(vmem_limit_bytes=18 << 20),
        name="finish",
    )(sums, ff, output, grad_tokens, vec)


def body(tokens, norm_in, w_query, w_key, w_value, query_gain, key_gain, w_out, norm_mid, w_gate, w_up, w_down, cotangent, lengths):
    parts = lax.axis_size("sp")
    gains = jnp.concatenate([query_gain, query_gain, key_gain, key_gain, jnp.zeros((768,), f32)])
    pack = jnp.concatenate([norm_in[None], norm_mid[None], gains[None], jnp.zeros((5, 1024), f32)], axis=0)
    wkv = jnp.concatenate([w_key.T, w_value.T], axis=0)

    normed, q_proj, kv_proj, q, kv, cosine, sine = project(lengths, tokens, pack, w_query, wkv)
    kv_all, ext, qa, mix_f, mixed, normed_mid, mid_own, cot = forward(
        parts, lengths, q, kv, tokens, cotangent, w_out, pack
    )
    kv_all = kv_all.reshape(8192, 128)
    normed_mid = normed_mid.reshape(512, 1024)
    cotangent = cot.reshape(512, 1024)

    gate = jnp.dot(normed_mid, w_gate, preferred_element_type=f32)
    up_proj = jnp.dot(normed_mid, w_up, preferred_element_type=f32)
    sigmoid_gate = jax.nn.sigmoid(gate)
    act = (gate * sigmoid_gate * up_proj).astype(bf16)
    mlp_part = jnp.dot(act, w_down, preferred_element_type=f32).astype(bf16)
    d_act = jnp.einsum("td,fd->tf", cotangent, w_down, preferred_element_type=f32)
    d_gate = (d_act * up_proj * sigmoid_gate * (1.0 + gate * (1.0 - sigmoid_gate))).astype(bf16)
    d_up = (d_act * gate * sigmoid_gate).astype(bf16)
    d_mid_part = (
        jnp.einsum("tf,df->td", d_gate, w_gate, preferred_element_type=f32)
        + jnp.einsum("tf,df->td", d_up, w_up, preferred_element_type=f32)
    ).astype(bf16)
    grads = (
        jnp.einsum("tf,td->fd", d_gate, normed_mid, preferred_element_type=f32).astype(bf16),
        jnp.einsum("tf,td->fd", d_up, normed_mid, preferred_element_type=f32).astype(bf16),
        jnp.einsum("tf,td->fd", act, cotangent, preferred_element_type=f32).astype(bf16),
    )
    output, grad_tokens, sums, g_ff, vec = backward(
        parts,
        d_mid_part.reshape(8, 64, 1024), mlp_part.reshape(8, 64, 1024), mid_own, cot,
        pack, w_out, *(g.reshape(4, 144, 1024) for g in grads),
        qa, mix_f, kv_all, ext, mixed,
        q_proj, kv_proj, normed, w_query, wkv, cosine, sine, tokens.reshape(8, 64, 1024),
    )
    (output, grad_tokens, g_query, g_key, g_value, g_out, g_gate, g_up, g_down, g_norm_in, g_norm_mid, g_qg, g_kg) = finish(
        sums, g_ff, output.reshape(512, 1024), grad_tokens.reshape(512, 1024), vec
    )
    return (
        output, grad_tokens, g_norm_in.reshape(1024), g_query, g_key.T, g_value.T, g_qg.reshape(64), g_kg.reshape(64),
        g_out, g_norm_mid.reshape(1024), g_gate.T, g_up.T, g_down,
    )


def solution(mesh):
    placed = (
        P("sp", None), P(), P(None, "wt"), P(None, "wt"), P(None, "wt"), P(), P(), P("wt", None), P(),
        P(None, "wt"), P(None, "wt"), P("wt", None), P("sp", None), P(),
    )
    return jax.shard_map(
        body,
        mesh=mesh,
        in_specs=placed,
        out_specs=(
            P("sp", None), P("sp", None), P(), P(None, "wt"), P(None, "wt"), P(None, "wt"), P(), P(),
            P("wt", None), P(), P(None, "wt"), P(None, "wt"), P("wt", None),
        ),
        check_vma=False,
    )
```

```python
import functools, math
import jax
import jax.numpy as jnp
import numpy as np
from jax import lax
from jax.experimental import pallas as pl
from jax.experimental.pallas import tpu as pltpu
from jax.sharding import PartitionSpec as P

f32 = jnp.float32
bf16 = jnp.bfloat16
sds = jax.ShapeDtypeStruct
DMA = pltpu.SemaphoreType.DMA
CH = 512
HALF = 256
SCALE = 0.125
C2 = SCALE * math.log2(math.e)


def starts_of(ids, len_ref):
    end = jnp.int32(0)
    start = jnp.zeros_like(ids)
    for j in range(4):
        end = end + len_ref[j]
        start = start + jnp.where(ids >= end, len_ref[j], 0)
    return start


def scalar_start(row, len_ref):
    end = jnp.int32(0)
    start = jnp.int32(0)
    for j in range(4):
        end = end + len_ref[j]
        start = start + jnp.where(row >= end, len_ref[j], 0)
    return start


def lanes(shape):
    return lax.broadcasted_iota(jnp.int32, shape, len(shape) - 1)


def split3(value, lane):
    hi = value.astype(bf16).astype(f32)
    rest = value - hi
    mid = rest.astype(bf16).astype(f32)
    low = rest - mid
    return jnp.where(lane == 0, hi, jnp.where(lane == 1, mid, jnp.where(lane == 2, low, 0.0)))


def tile_row(me, t, parts):
    return me * 512 if t == 0 else (parts - 1 - me) * 512 + HALF


FAR = 8192.0


def segment_bounds(len_ref, lane):
    begin = jnp.zeros_like(lane)
    end = jnp.zeros_like(lane)
    at = jnp.int32(0)
    for j in range(4):
        begin = jnp.where(lane == 3 + j, at, begin)
        at = at + len_ref[j]
        end = jnp.where(lane == 3 + j, at, end)
    return begin, end


def inside(ids, len_ref, shape):
    lane = lanes(shape)
    begin, end = segment_bounds(len_ref, lane)
    return (ids >= begin) & (ids < end), lane


def key_columns(k0, len_ref, rows):
    ids = k0 + lax.broadcasted_iota(jnp.int32, (rows, 128), 0)
    within, lane = inside(ids, len_ref, (rows, 128))
    return jnp.where(lane < 3, 1.0, jnp.where(within, 1.0, 0.0)).astype(bf16)


def query_columns(r0, len_ref, rows):
    ids = r0 + lax.broadcasted_iota(jnp.int32, (rows, 128), 0)
    within, lane = inside(ids, len_ref, (rows, 128))
    return jnp.where((lane < 3) | (lane > 6) | within, 0.0, -FAR)


smem = pl.BlockSpec(memory_space=pltpu.SMEM)
vmem = pl.BlockSpec(memory_space=pltpu.VMEM)


MESH = pl.DeviceIdType.MESH
eps = 1e-05


def rcopy(src, dst, send, recv, device):
    return pltpu.make_async_remote_copy(
        src_ref=src, dst_ref=dst, send_sem=send, recv_sem=recv, device_id=device, device_id_type=MESH
    )


def meet(devices):
    barrier = pltpu.get_barrier_semaphore()
    for device in devices:
        pl.semaphore_signal(barrier, inc=1, device_id=device, device_id_type=MESH)
    pl.semaphore_wait(barrier, len(devices))


class Place:
    def __init__(self):
        self.sp = lax.axis_index("sp")
        self.wt = lax.axis_index("wt")
        self.x, self.y = lax.div(self.sp, 4), lax.rem(self.sp, 4)
        self.z, self.c = lax.div(self.wt, 2), lax.rem(self.wt, 2)
        self.mirror = (15 - self.sp, self.wt)
        self.sibling = (self.sp, self.z * 2 + 1 - self.c)

    def along_x(self, d):
        return (lax.rem(self.x + d, 4) * 4 + self.y, self.wt)

    def along_y(self, d):
        return (self.x * 4 + lax.rem(self.y + d, 4), self.wt)

    def along_z(self, d):
        return (self.sp, lax.rem(self.z + d, 4) * 2 + self.c)

    def along_z_other(self, d):
        return (self.sp, lax.rem(self.z + d, 4) * 2 + 1 - self.c)

    def first(self, h, d):
        return self.along_x(d) if h == 0 else self.along_y(d)

    def second(self, h, d):
        return self.along_y(d) if h == 0 else self.along_x(d)

    def fsp(self, h):
        return self.x if h == 0 else self.y

    def ssp(self, h):
        return self.y if h == 0 else self.x


def spot(h, first, second):
    return (first, second) if h == 0 else (second, first)


ORDER = (2, 1, 3)


def to_blocks(value, rows, put):
    for x in range(4):
        for y in range(4):
            for h in range(2):
                block = value(x)[:, h * 512 + y * 128:h * 512 + y * 128 + 128]
                put(h, *spot(h, x, y), block)


class SpScatter:
    def __init__(self, p, srcs, refs):
        self.p, self.srcs = p, srcs
        self.r1, self.send, self.r2, self.fs, self.fr, self.ss, self.sr = refs
        self.one, self.two = {}, {}

    @staticmethod
    def scratch(n, rows):
        return [
            pltpu.VMEM((n, 2, 3, 4, rows, 128), bf16), pltpu.VMEM((n, 2, 3, rows, 128), bf16),
            pltpu.VMEM((n, 2, 3, rows, 128), bf16),
            DMA((n, 2, 3)), DMA((n, 2, 3)), DMA((n, 2, 3)), DMA((n, 2, 3)),
        ]

    def first(self, i):
        p = self.p
        for d in ORDER:
            for h in range(2):
                self.one[i, h, d] = rcopy(
                    self.srcs[i].at[h, lax.rem(p.fsp(h) + d, 4)], self.r1.at[i, h, d - 1],
                    self.fs.at[i, h, d - 1], self.fr.at[i, h, d - 1], p.first(h, d),
                )
                self.one[i, h, d].start()

    def part(self, i, h, b):
        value = self.srcs[i][h, self.p.fsp(h), b].astype(f32)
        for d in range(3):
            value = value + self.r1[i, h, d, b].astype(f32)
        return value

    def second(self, i):
        p = self.p
        for h in range(2):
            for d in ORDER:
                self.one[i, h, d].wait_recv()
            for e in ORDER:
                self.send[i, h, e - 1] = self.part(i, h, lax.rem(p.ssp(h) + e, 4)).astype(bf16)
                self.two[i, h, e] = rcopy(
                    self.send.at[i, h, e - 1], self.r2.at[i, h, e - 1],
                    self.ss.at[i, h, e - 1], self.sr.at[i, h, e - 1], p.second(h, e),
                )
                self.two[i, h, e].start()

    def own(self, i, h):
        value = self.part(i, h, self.p.ssp(h))
        for e in ORDER:
            self.two[i, h, e].wait_recv()
            value = value + self.r2[i, h, e - 1].astype(f32)
        return value

    def finish(self):
        for copy in list(self.one.values()) + list(self.two.values()):
            copy.wait_send()


class SpGather:
    def __init__(self, p, out, sems):
        self.p, self.out = p, out
        self.fs, self.fr, self.ss, self.sr = sems
        self.one, self.two, self.further = {}, {}, {}

    @staticmethod
    def sems(n):
        return [DMA((n, 2, k)) for k in (3, 3, 4, 4)]

    def put(self, i, h, value):
        self.out[i, h, self.p.fsp(h), self.p.ssp(h)] = value

    def first(self, i, h):
        block = self.out.at[i, h, self.p.fsp(h), self.p.ssp(h)]
        for e in ORDER:
            self.one[i, h, e] = rcopy(
                block, block, self.fs.at[i, h, e - 1], self.fr.at[i, h, e - 1], self.p.second(h, e)
            )
            self.one[i, h, e].start()

    def second(self, i, h):
        for e in ORDER:
            self.one[i, h, e].wait_recv()
        block = self.out.at[i, h, self.p.fsp(h)]
        for d in ORDER:
            self.two[i, h, d] = rcopy(
                block, block, self.ss.at[i, h, d - 1], self.sr.at[i, h, d - 1], self.p.first(h, d)
            )
            self.two[i, h, d].start()

    def relayed(self, i, h):
        for e in ORDER:
            self.one[i, h, e].wait_recv()
        block = self.out.at[i, h, self.p.fsp(h)]
        for slot, d in enumerate((1, 3)):
            self.two[i, h, slot] = rcopy(
                block, block, self.ss.at[i, h, slot], self.sr.at[i, h, slot], self.p.first(h, d)
            )
            self.two[i, h, slot].start()

    def relay(self, i, h):
        for slot, d in enumerate((1, 3)):
            self.two[i, h, slot].wait_recv()
            block = self.out.at[i, h, lax.rem(self.p.fsp(h) + 4 - d, 4), pl.ds(2 * slot, 2)]
            self.further[i, h, slot] = rcopy(
                block, block, self.ss.at[i, h, 2 + slot], self.sr.at[i, h, 2 + slot], self.p.first(h, d)
            )
            self.further[i, h, slot].start()

    def finish(self):
        for copy in self.one.values():
            copy.wait_send()
        for copy in self.two.values():
            copy.wait_send() if self.further else copy.wait()
        for copy in self.further.values():
            copy.wait()


SPLIT = 2


def sub(s):
    return pl.ds(s * (64 // SPLIT), 64 // SPLIT)


class WtSum:
    def __init__(self, p, part, sib, send, rz, sems):
        self.p, self.part, self.sib, self.send, self.rz = p, part, sib, send, rz
        self.cs, self.cr, self.zs, self.zr = sems
        self.second = {}

    def core(self, zz, s):
        return rcopy(
            self.part.at[zz * 2 + 1 - self.p.c, sub(s)], self.sib.at[zz, sub(s)],
            self.cs.at[zz, s], self.cr.at[zz, s], self.p.sibling,
        )

    def start_core(self, zz):
        for s in range(SPLIT):
            self.core(zz, s).start()

    def pair(self, zz, s):
        return self.part[zz * 2 + self.p.c, sub(s)].astype(f32) + self.sib[zz, sub(s)].astype(f32)

    def send_z(self):
        for s in range(SPLIT):
            for d in ORDER:
                zz = lax.rem(self.p.z + d, 4)
                self.core(zz, s).wait_recv()
                self.send[d - 1, sub(s)] = self.pair(zz, s).astype(bf16)
                copy = rcopy(
                    self.send.at[d - 1, sub(s)], self.rz.at[d - 1, sub(s)],
                    self.zs.at[d - 1, s], self.zr.at[d - 1, s], self.p.along_z(d),
                )
                copy.start()
                self.second[d, s] = copy

    def own(self, s):
        self.core(self.p.z, s).wait_recv()
        value = self.pair(self.p.z, s)
        for d in (1, 3, 2):
            self.second[d, s].wait_recv()
            value = value + self.rz[d - 1, sub(s)].astype(f32)
        return value

    def finish(self):
        for zz in range(4):
            for s in range(SPLIT):
                self.core(zz, s).wait_send()
        for copy in self.second.values():
            copy.wait_send()


class WtGather:
    def __init__(self, p, out, sems):
        self.p, self.out = p, out
        self.zs, self.zr, self.gs, self.gr = sems
        self.far, self.near = {}, {}

    def start(self, s):
        p = self.p
        block = self.out.at[p.wt, sub(s)]
        for d in ORDER:
            self.far[d, s] = rcopy(block, block, self.zs.at[d - 1, s], self.zr.at[d - 1, s], p.along_z(d))
            self.far[d, s].start()
        self.pass_on(0, s)

    def pass_on(self, slot, s):
        p = self.p
        block = self.out.at[lax.rem(p.z + 4 - slot, 4) * 2 + p.c, sub(s)]
        self.near[slot, s] = rcopy(block, block, self.gs.at[slot, s], self.gr.at[slot, s], p.sibling)
        self.near[slot, s].start()

    def forward(self):
        for s in range(SPLIT):
            for d in (1, 3, 2):
                self.far[d, s].wait_recv()
                self.pass_on(d, s)

    def arrived(self):
        for copy in self.near.values():
            copy.wait_recv()

    def finish(self):
        for copy in list(self.far.values()) + list(self.near.values()):
            copy.wait_send()


def rms_of(value):
    return lax.rsqrt(jnp.mean(value * value, axis=-1, keepdims=True) + eps)


def norm_back(values, scale, gain, grad):
    scaled = grad * gain
    inner = jnp.mean(scaled * values, axis=-1, keepdims=True)
    return scale * scaled - values * scale * scale * scale * inner


def wt_peers(p):
    return [p.sibling] + [p.along_z(d) for d in ORDER]


class Flow:
    def __init__(self):
        self.copies = []

    def send(self, *args):
        copy = rcopy(*args)
        copy.start()
        self.copies.append(copy)
        return copy

    def finish(self):
        for copy in self.copies:
            copy.wait_send()


def forward_kernel(
    parts,
    len_ref, q_ref, kv_ref, tok_ref, cot_ref, w_ref, pack_ref,
    all_ref, ext_ref, qa_ref, mixf_ref, mix_ref, nm_ref, mid_ref, cotz_ref,
    qz, base, acc, part, sib, send, rz, ms, mr, cs, cr, zs, zr, az, bz, ag, bg, fs, fr, ss, sr,
):
    p = Place()
    me = p.sp
    meet(wt_peers(p) + [p.along_x(d) for d in ORDER] + [p.along_y(d) for d in ORDER] + [p.mirror])
    flow = Flow()
    first = {}
    for d in ORDER:
        for h in range(2):
            first[h, d] = flow.send(
                kv_ref.at[h], all_ref.at[p.x, p.y, h], fs.at[h, d - 1], fr.at[h, d - 1], p.first(h, d)
            )
    q_mirror = flow.send(q_ref.at[1], qz.at[1], ms.at[0], mr.at[0], p.mirror)

    def pass_on(h, slot):
        a = lax.rem(p.fsp(h) + 4 - slot, 4)
        at = spot(h, a, p.ssp(h))
        for e in ORDER:
            src = kv_ref.at[h] if slot == 0 else all_ref.at[at[0], at[1], h]
            flow.send(src, all_ref.at[at[0], at[1], h], ss.at[h, slot, e - 1], sr.at[h, slot, e - 1], p.second(h, e))

    for h in range(2):
        pass_on(h, 0)
    token_mirror = rcopy(tok_ref.at[p.wt], base, ms.at[1], mr.at[1], p.mirror)

    @pl.when(p.wt >= 4)
    def _():
        token_mirror.start()

    @pl.when(p.wt < 4)
    def _():
        base[...] = tok_ref[p.wt]

    all_ref[p.x, p.y] = kv_ref[...]
    qz[0] = q_ref[0]
    cotz_ref[0:4] = cot_ref[0:4]

    @pl.loop(0, 8)
    def _(b):
        rows = pl.ds(pl.multiple_of(b * 1024, 1024), 1024)
        ext_ref[rows, :] = key_columns(b * 1024, len_ref, 1024)

    lane = lanes((HALF, 128))
    lane2 = lanes((2 * HALF, 128))
    lanek = lanes((CH, 128))
    acc[...] = jnp.zeros_like(acc)
    blocks = (me, parts - 1 - me)
    begins = (me * 512, (parts - 1 - me) * 512 + HALF)

    def prepare(t):
        q = qz[t].astype(f32)
        qa_ref[t, 0:HALF, 0:128] = jnp.where(lane < 64, q, 0.0).astype(bf16)
        qa_ref[t, HALF:, 0:128] = jnp.where(lane < 64, pltpu.roll(q, 64, 1), 0.0).astype(bf16)
        columns = query_columns(begins[t], len_ref, HALF).astype(bf16)
        qa_ref[t, 0:HALF, 128:256] = columns
        qa_ref[t, HALF:, 128:256] = columns

    def step(t, x, y, masked):
        k0 = pl.multiple_of((x * 4 + y) * CH, CH)
        kv = all_ref[x, y].reshape(CH, 128)
        kva = jnp.concatenate([kv, ext_ref[pl.ds(k0, CH), :]], axis=1)
        pr = jnp.exp2(nt(qa_ref[t], kva) * C2)
        if masked:
            rows = begins[t] + lax.rem(lax.broadcasted_iota(jnp.int32, (2 * HALF, 1), 0), HALF)
            keys = k0 + lax.broadcasted_iota(jnp.int32, (2 * HALF, CH), 1)
            pr = jnp.where(keys <= rows, pr, 0.0)
        ones = jnp.where(lanek < 64, jnp.ones_like(kv), kv)
        acc[t] += jnp.dot(pr.astype(bf16), ones, preferred_element_type=f32)

    def both(x, y):
        block = x * 4 + y

        @pl.when(block < blocks[0])
        def _():
            step(0, x, y, False)

        @pl.when(block < blocks[1])
        def _():
            step(1, x, y, False)

        @pl.when(block == blocks[1])
        def _():
            step(1, x, y, True)

    prepare(0)
    step(0, p.x, p.y, True)
    for d in (1, 3, 2):
        for h in range(2):
            first[h, d].wait_recv()
            pass_on(h, d)
    q_mirror.wait_recv()
    prepare(1)

    @pl.when(me < blocks[1])
    def _():
        step(1, p.x, p.y, False)

    def wait_for(x, y, h, slot, e):
        block = all_ref.at[x, y, h]
        rcopy(block, block, ss.at[h, slot, e - 1], sr.at[h, slot, e - 1], p.second(h, 1)).wait_recv()

    @pl.loop(1, 4)
    def _(d):
        x = lax.rem(p.x + 4 - d, 4)
        wait_for(x, p.y, 1, 0, d)
        both(x, p.y)

    @pl.loop(1, 4)
    def _(d):
        y = lax.rem(p.y + 4 - d, 4)
        wait_for(p.x, y, 0, 0, d)
        both(p.x, y)

    @pl.loop(0, 9)
    def _(k):
        dx, dy = 1 + lax.div(k, 3), 1 + lax.rem(k, 3)
        x, y = lax.rem(p.x + 4 - dx, 4), lax.rem(p.y + 4 - dy, 4)
        wait_for(x, y, 0, dx, dy)
        wait_for(x, y, 1, dy, dx)
        both(x, y)

    total = WtSum(p, part, sib, send, rz, (cs, cr, zs, zr))
    cot_mirror = flow.send(cot_ref.at[pl.ds(4, 4)], cotz_ref.at[pl.ds(4, 4)], ms.at[2], mr.at[2], p.mirror)
    for t in range(2):
        value = acc[t]
        swapped = pltpu.roll(value, 64, 1)
        o = swapped / value
        mix = jnp.where(lane < 64, o[:HALF], pltpu.roll(o[HALF:], 64, 1))
        mixf_ref[t] = mix
        mix = mix.astype(bf16)
        mix_ref[t] = mix
        part[t * 4:t * 4 + 4] = jnp.dot(mix, w_ref[...], preferred_element_type=f32).astype(bf16).reshape(4, 64, 1024)
        for zz in (t * 2, t * 2 + 1):
            total.start_core(zz)
    total.send_z()
    for t in range(2):
        value = acc[t]
        weights = jnp.where(lane2 < 64, value, pltpu.roll(value, 64, 1))
        columns = qa_ref[t, :, 128:256].astype(f32)
        qa_ref[t, :, 128:256] = (split3(jnp.log(weights) * (-1.0 / SCALE), lane2) + columns).astype(bf16)

    @pl.when(p.wt >= 4)
    def _():
        token_mirror.wait()

    spread = WtGather(p, nm_ref, (az, bz, ag, bg))
    for s in range(SPLIT):
        middle = base[sub(s)].astype(f32) + total.own(s)
        mid_ref[sub(s)] = middle
        nm_ref[p.wt, sub(s)] = (middle * rms_of(middle) * pack_ref[1:2]).astype(bf16)
        spread.start(s)
    spread.forward()
    cot_mirror.wait_recv()
    spread.arrived()
    for part in (spread, total, flow):
        part.finish()


WT_SEMS = [DMA((n, SPLIT)) for n in (4, 4, 3, 3, 3, 3, 4, 4)]


def comm_call(kernel, number, out_shape, args, scratch, name, limit=10, first=None):
    return pl.pallas_call(
        kernel,
        out_shape=out_shape,
        in_specs=[first or vmem] + [vmem] * (len(args) - 1),
        out_specs=tuple(vmem for _ in out_shape),
        scratch_shapes=scratch,
        compiler_params=pltpu.CompilerParams(
            collective_id=number, has_side_effects=True, vmem_limit_bytes=limit << 20
        ),
        cost_estimate=pl.CostEstimate(flops=8 << 30, bytes_accessed=32 << 20, transcendentals=0),
        name=name,
    )(*args)


def forward(parts, lengths, q, kv, tokens, cotangent, w_out, pack):
    rows = pltpu.VMEM
    half = sds((2, 256, 128), bf16)
    full = sds((8, 64, 1024), bf16)
    return comm_call(
        functools.partial(forward_kernel, parts), 1,
        (sds((4, 4, 2, 256, 128), bf16), sds((8192, 128), bf16), sds((2, 512, 256), bf16), sds((2, 256, 128), f32),
         half, full, sds((64, 1024), f32), full),
        (lengths, q.reshape(2, 256, 128), kv.reshape(2, 256, 128), tokens.reshape(8, 64, 1024),
         cotangent.reshape(8, 64, 1024), w_out, pack),
        [rows((2, 256, 128), bf16), rows((64, 1024), bf16), rows((2, 512, 128), f32), rows((8, 64, 1024), bf16),
         rows((4, 64, 1024), bf16), rows((3, 64, 1024), bf16), rows((3, 64, 1024), bf16), DMA((3,)), DMA((3,))]
        + WT_SEMS + [DMA((2, 3)), DMA((2, 3)), DMA((2, 4, 3)), DMA((2, 4, 3))],
        "forward", 16, smem,
    )


def turned(value, lane):
    return jnp.where(lax.rem(lane, 64) < 32, pltpu.roll(value, 96, 1), pltpu.roll(value, 32, 1))


def head_sums(value, lane):
    s0 = jnp.sum(jnp.where(lane < 64, value, 0.0), axis=1, keepdims=True)
    s1 = jnp.sum(jnp.where(lane < 64, 0.0, value), axis=1, keepdims=True)
    return jnp.where(lane < 64, s0, s1)


def nt(a, b):
    return lax.dot_general(a, b, (((1,), (1,)), ((), ())), preferred_element_type=f32)


def tn(a, b):
    return lax.dot_general(a, b, (((0,), (0,)), ((), ())), preferred_element_type=f32)


FREQS = [float(np.float32(1000000.0 ** (-2.0 * i / 64))) for i in range(32)]


def proj_kernel(len_ref, tok_ref, pack_ref, wq_ref, wkv_ref, n_ref, qp_ref, kvp_ref, q_ref, kv_ref, cos_ref, sin_ref):
    lane = lanes((512, 128))
    ids = lax.axis_index("sp") * 512 + lax.broadcasted_iota(jnp.int32, (1, 512), 1)
    positions = (ids - starts_of(ids, len_ref)).astype(f32)
    row = lax.broadcasted_iota(jnp.int32, (32, 512), 0)
    freqs = jnp.zeros((32, 512), f32)
    for i, freq in enumerate(FREQS):
        freqs = jnp.where(row == i, freq, freqs)
    angles = positions * freqs
    cosine, sine = jnp.cos(angles), jnp.sin(angles)
    cosine = jnp.concatenate([cosine] * 4, axis=0).T
    sine = jnp.concatenate([-sine, sine, -sine, sine], axis=0).T
    cos_ref[...] = cosine
    sin_ref[...] = sine
    base = tok_ref[...].astype(f32)
    normed = (base * rms_of(base) * pack_ref[0:1]).astype(bf16)
    n_ref[...] = normed
    q = jnp.dot(normed, wq_ref[...], preferred_element_type=f32)
    qp_ref[...] = q
    q = q * lax.rsqrt(head_sums(q * q, lane) * (1.0 / 64) + eps) * pack_ref[2:3, 0:128]
    q_ref[...] = (q * cosine + turned(q, lane) * sine).astype(bf16)
    kv = nt(normed, wkv_ref[...])
    kvp_ref[...] = kv
    k = kv * lax.rsqrt(head_sums(kv * kv, lane) * (1.0 / 64) + eps) * pack_ref[2:3, 128:256]
    k = k * cosine + turned(k, lane) * sine
    kv_ref[...] = jnp.where(lane < 64, k, kv).astype(bf16)


def project(*args):
    wide = sds((512, 128), f32)
    out_shape = (sds((512, 1024), bf16), wide, wide, sds((512, 128), bf16), sds((512, 128), bf16), wide, wide)
    return pl.pallas_call(
        proj_kernel,
        out_shape=out_shape,
        in_specs=[smem] + [vmem] * 4,
        out_specs=tuple(vmem for _ in out_shape),
        compiler_params=pltpu.CompilerParams(vmem_limit_bytes=12 << 20),
        name="project",
    )(*args)


def backward_kernel(
    parts,
    dm_ref, mlp_ref, mid_ref, cot_ref, pack_ref, w_ref, g0_ref, g1_ref, g2_ref,
    qa_ref, mixf_ref, kv_ref, ext_ref, mixed_ref,
    qp_ref, kvp_ref, n_ref, wq_ref, wkv_ref, cos_ref, sin_ref, tok_ref,
    out_ref, gt_ref, sums_ref, ff_ref, vec_ref,
    *scratch,
):
    scratch = list(scratch)

    def take(n):
        got = scratch[:n]
        del scratch[:n]
        return got

    p = Place()
    me = p.sp
    meet(
        wt_peers(p) + [p.along_z_other(d) for d in ORDER] + [p.mirror]
        + [p.along_x(d) for d in ORDER] + [p.along_y(d) for d in ORDER]
    )
    flow = Flow()

    def wt_sum(ref):
        sib, send, rz = take(3)
        return WtSum(p, ref, sib, send, rz, take(4))

    da, dz, dmid, dmid_o, out_own = take(5)
    mirror_sems = take(6)
    d_mid_sum = wt_sum(dm_ref)
    da_gather = WtGather(p, da, take(4))
    mlp_sum = wt_sum(mlp_ref)
    out_gather = WtGather(p, out_ref, take(4))
    (ffb,) = take(1)
    ff = SpScatter(p, [ffb.at[i] for i in range(3)], take(7))
    ff_back = SpGather(p, ff_ref, take(4))
    dab, acc, dqt, dqz, dq, dkv, dkv_own = take(7)
    r1, send1, r2, fs, fr, ss, sr = take(7)
    dn, gqkv, gout = take(3)
    dn_sum = wt_sum(dn)
    gt_gather = WtGather(p, gt_ref, take(4))
    sums = SpScatter(p, (gout, gqkv.at[0], gqkv.at[1]), take(7))
    sums_back = SpGather(p, sums_ref, take(4))
    vw, vx, vy, vs1, vr1, vs2, vr2, vs3, vr3 = take(9)
    assert not scratch

    for zz in range(4):
        d_mid_sum.start_core(zz)
    for i, ref in enumerate((g0_ref, g1_ref, g2_ref)):
        def put(h, u, v, block, i=i):
            ffb[i, h, u, v] = block

        to_blocks(lambda x, ref=ref: ref[x], 144, put)
        ff.first(i)
        if i == 0:
            d_mid_sum.send_z()
    vw[0] = jnp.zeros((8, 1024), f32)
    acc[...] = jnp.zeros_like(acc)
    dqt[...] = jnp.zeros_like(dqt)
    for s in range(SPLIT):
        middle = mid_ref[sub(s)]
        scale = rms_of(middle)
        d_mid = d_mid_sum.own(s)
        d_middle = cot_ref[p.wt, sub(s)].astype(f32) + norm_back(middle, scale, pack_ref[1:2], d_mid)
        da[p.wt, sub(s)] = d_middle.astype(bf16)
        da_gather.start(s)
        dmid[sub(s)] = d_middle
        vw[0, 1:2] += jnp.sum(d_mid * middle * scale, axis=0, keepdims=True)
    dmid_mirror = rcopy(dmid, dmid_o, mirror_sems[2], mirror_sems[3], p.mirror)

    @pl.when(p.wt >= 4)
    def _():
        dmid_mirror.start()

    da_gather.forward()
    da_gather.arrived()
    for zz in range(4):
        mlp_sum.start_core(zz)
    dz[...] = nt(da[...].reshape(512, 1024), w_ref[...]).astype(bf16).reshape(2, 256, 128)
    mlp_sum.send_z()

    lane = lanes((HALF, 128))
    for t in range(2):
        do = dz[t].astype(f32)
        prod = do * mixf_ref[t]
        d0 = -jnp.sum(jnp.where(lane < 64, prod, 0.0), axis=1, keepdims=True)
        d1 = -jnp.sum(jnp.where(lane < 64, 0.0, prod), axis=1, keepdims=True)
        dab[t, 0:HALF, 0:128] = jnp.where(lane < 64, 0.0, pltpu.roll(do, 64, 1)).astype(bf16)
        dab[t, HALF:, 0:128] = jnp.where(lane < 64, 0.0, do).astype(bf16)
        dab[t, 0:HALF, 128:256] = split3(jnp.broadcast_to(d0, (HALF, 128)), lane).astype(bf16)
        dab[t, HALF:, 128:256] = split3(jnp.broadcast_to(d1, (HALF, 128)), lane).astype(bf16)
    upper_long = (me < parts // 2).astype(jnp.int32)
    blocks = [me + t * (parts - 1 - 2 * me) for t in (upper_long, 1 - upper_long)]

    def step(k, masked):
        short = (k > blocks[0]).astype(jnp.int32)
        t = upper_long + short * (1 - 2 * upper_long)
        c = k - short * (blocks[0] + 1)
        k0 = pl.multiple_of(c * CH, CH)
        kv = kv_ref[pl.ds(k0, CH), :]
        kva = jnp.concatenate([kv, ext_ref[pl.ds(k0, CH), :]], axis=1)
        qa = qa_ref[t]
        d_out = dab[t]
        pr = jnp.exp2(nt(kva, qa) * C2)
        if masked:
            r0 = c * 512 + t * HALF
            rows = r0 + lax.rem(lax.broadcasted_iota(jnp.int32, (1, 2 * HALF), 1), HALF)
            keys = k0 + lax.broadcasted_iota(jnp.int32, (CH, 2 * HALF), 0)
            pr = jnp.where(keys <= rows, pr, 0.0)
        ds = (pr * nt(kva, d_out)).astype(bf16)
        acc[pl.ds(k0, CH), :] += jnp.dot(
            pr.astype(bf16), d_out[:, 0:128], preferred_element_type=f32
        ) + jnp.dot(ds, qa[:, 0:128], preferred_element_type=f32)
        kt = kv.T[0:64, :]
        dqt[t] += jnp.dot(kt, ds, preferred_element_type=f32)

    def plain(k):
        step(k, False)

    def either(k):
        pl.when(k == blocks[0])(lambda: step(k, True))
        pl.when(k != blocks[0])(lambda: step(k, False))

    ff.second(0)
    ff.second(1)
    pl.loop(0, 3)(plain)
    ff.second(2)
    pl.loop(3, 5)(plain)
    for i in range(2):
        for h in range(2):
            ff_back.put(i, h, ff.own(i, h).astype(bf16))
            ff_back.first(i, h)
    pl.loop(5, 8)(plain)
    for h in range(2):
        ff_back.relayed(0, h)
    for h in range(2):
        ff_back.put(2, h, ff.own(2, h).astype(bf16))
        ff_back.first(2, h)
    for s in range(SPLIT):
        out_own[sub(s)] = (mid_ref[sub(s)] + mlp_sum.own(s)).astype(bf16)
    out_mirror = rcopy(out_own, out_ref.at[p.wt], mirror_sems[4], mirror_sems[5], p.mirror)

    @pl.when(p.wt >= 4)
    def _():
        out_mirror.start()

    @pl.when(p.wt < 4)
    def _():
        out_ref[p.wt] = out_own[...]

    def put_out(h, u, v, block):
        gout[h, u, v] = block

    g_out = tn(mixed_ref[...].reshape(512, 128), da[...].reshape(512, 1024)).astype(bf16)
    to_blocks(lambda x: g_out[x * 32:x * 32 + 32], 32, put_out)
    sums.first(0)
    pl.loop(8, 12)(either)
    for h in range(2):
        ff_back.relayed(1, h)
    sums.second(0)

    @pl.when(p.wt >= 4)
    def _():
        out_mirror.wait()

    for s in range(SPLIT):
        out_gather.start(s)
    pl.loop(12, 16)(either)
    step(16, True)
    for t in range(2):
        both = jnp.concatenate([dqt[t, :, :HALF], dqt[t, :, HALF:]], axis=0)
        dqz[t] = (both.T * SCALE).astype(bf16)
    weight = jnp.where(lanes((512, 128)) < 64, SCALE, 1.0)

    @pl.loop(0, parts)
    def _(b):
        rows = pl.ds(pl.multiple_of(b * 512, 512), 512)
        dkv[lax.div(b, 4), lax.rem(b, 4)] = (acc[rows, :] * weight).astype(bf16).reshape(2, 256, 128)

    mirror = flow.send(dqz.at[1], dq.at[1], mirror_sems[0], mirror_sems[1], p.mirror)
    dq[0] = dqz[0]
    first, second = {}, {}
    for e in (2, 1, 3, 0):
        for d in ORDER:
            for h in range(2):
                at = spot(h, lax.rem(p.fsp(h) + d, 4), lax.rem(p.ssp(h) + e, 4))
                first[h, d, e] = flow.send(
                    dkv.at[at[0], at[1], h], r1.at[h, d - 1, e], fs.at[h, d - 1, e], fr.at[h, d - 1, e], p.first(h, d)
                )

    def total(h, e):
        at = spot(h, p.fsp(h), lax.rem(p.ssp(h) + e, 4))
        value = dkv[at[0], at[1], h].astype(f32)
        for d in ORDER:
            first[h, d, e].wait_recv()
            value = value + r1[h, d - 1, e].astype(f32)
        return value

    out_gather.forward()
    for h in range(2):
        ff_back.relay(0, h)
    for e in ORDER:
        for h in range(2):
            send1[h, e - 1] = total(h, e).astype(bf16)
            second[h, e] = flow.send(
                send1.at[h, e - 1], r2.at[h, e - 1], ss.at[h, e - 1], sr.at[h, e - 1], p.second(h, e)
            )
    own = [total(h, 0) for h in range(2)]
    for h in range(2):
        ff_back.relayed(2, h)
        ff_back.relay(1, h)
        sums_back.put(0, h, sums.own(0, h).astype(bf16))
        sums_back.first(0, h)
    for h in range(2):
        value = own[h]
        for e in ORDER:
            second[h, e].wait_recv()
            value = value + r2[h, e - 1].astype(f32)
        dkv_own[h] = value.astype(bf16)
    mirror.wait_recv()

    wide = lanes((512, 128))
    cosine, sine = cos_ref[...], sin_ref[...]

    def back(grad, proj, gain):
        grad = grad * cosine - turned(grad, wide) * sine
        scale = lax.rsqrt(head_sums(proj * proj, wide) * (1.0 / 64) + eps)
        scaled = grad * gain
        inner = head_sums(scaled * proj, wide) * (1.0 / 64)
        gains = jnp.sum(grad * proj * scale, axis=0, keepdims=True)
        return scale * scaled - proj * scale * scale * scale * inner, gains

    d_q, gq = back(dq[...].reshape(512, 128).astype(f32), qp_ref[...], pack_ref[2:3, 0:128])
    dkv_in = dkv_own[...].reshape(512, 128).astype(f32)
    d_k, gk = back(dkv_in, kvp_ref[...], pack_ref[2:3, 128:256])
    d_q = d_q.astype(bf16)
    d_kv = jnp.where(wide < 64, d_k, dkv_in).astype(bf16)
    dn[...] = (nt(d_q, wq_ref[...]) + jnp.dot(d_kv, wkv_ref[...], preferred_element_type=f32)).astype(bf16).reshape(8, 64, 1024)
    for zz in range(4):
        dn_sum.start_core(zz)
    normed = n_ref[...]
    for i, grad in enumerate((d_q, d_kv)):
        def put_in(h, u, v, block, i=i):
            gqkv[i, h, u, v] = block

        g_in = tn(grad, normed).astype(bf16)
        to_blocks(lambda x, g_in=g_in: g_in[x * 32:x * 32 + 32], 32, put_in)
    for i in (1, 2):
        sums.first(i)
    dn_sum.send_z()

    gains = jnp.zeros((1, 1024), f32)
    for w in range(8):
        base = tok_ref[w].astype(f32)
        gains = gains + jnp.sum(dn[w].astype(f32) * base * rms_of(base), axis=0, keepdims=True)
    vw[0, 0:1] = gains
    vw[0, 2:3] = jnp.concatenate([gq, gk, jnp.zeros((1, 768), f32)], axis=1)

    def vec_round(buf, devices, sends, recvs):
        return [
            flow.send(buf.at[0], buf.at[i + 1], sends.at[i], recvs.at[i], device) for i, device in enumerate(devices)
        ]

    def vec_total(buf, copies):
        value = buf[0]
        for i, copy in enumerate(copies):
            copy.wait_recv()
            value = value + buf[i + 1]
        return value

    round1 = vec_round(vw, [p.along_z(d) for d in ORDER] + [p.along_z_other(d) for d in ORDER] + [p.sibling], vs1, vr1)
    for i in (1, 2):
        sums.second(i)
    for h in range(2):
        sums_back.second(0, h)

    @pl.when(p.wt >= 4)
    def _():
        dmid_mirror.wait()

    @pl.when(p.wt < 4)
    def _():
        dmid_o[...] = dmid[...]

    for s in range(SPLIT):
        base = tok_ref[p.wt, sub(s)].astype(f32)
        d_normed = dn_sum.own(s)
        gt_ref[p.wt, sub(s)] = (
            dmid_o[sub(s)] + norm_back(base, rms_of(base), pack_ref[0:1], d_normed)
        ).astype(bf16)
        gt_gather.start(s)
    for h in range(2):
        ff_back.relay(2, h)
    for i in (1, 2):
        for h in range(2):
            sums_back.put(i, h, sums.own(i, h).astype(bf16))
            sums_back.first(i, h)
    vx[0] = vec_total(vw, round1)
    round2 = vec_round(vx, [p.along_x(d) for d in ORDER], vs2, vr2)
    for i in (1, 2):
        for h in range(2):
            sums_back.second(i, h)
    vy[0] = vec_total(vx, round2)
    round3 = vec_round(vy, [p.along_y(d) for d in ORDER], vs3, vr3)
    gt_gather.forward()
    vec_ref[...] = vec_total(vy, round3)
    out_gather.arrived()
    gt_gather.arrived()
    for part in (d_mid_sum, da_gather, mlp_sum, out_gather, ff, ff_back, dn_sum, gt_gather, sums, sums_back, flow):
        part.finish()


def backward(parts, *args):
    rows = pltpu.VMEM
    wt_rows = [rows((4, 64, 1024), bf16), rows((3, 64, 1024), bf16), rows((3, 64, 1024), bf16)]
    wt_sum = wt_rows + WT_SEMS[:4]
    wt_gather = WT_SEMS[4:]
    half = rows((2, 256, 128), bf16)
    return comm_call(
        functools.partial(backward_kernel, parts), 4,
        (sds((8, 64, 1024), bf16), sds((8, 64, 1024), bf16), sds((3, 2, 4, 4, 32, 128), bf16), sds((3, 2, 4, 4, 144, 128), bf16),
         sds((8, 1024), f32)),
        args,
        [rows((8, 64, 1024), bf16), half, rows((64, 1024), f32), rows((64, 1024), f32), rows((64, 1024), bf16)] + [DMA] * 6
        + wt_sum + wt_gather + wt_sum + wt_gather
        + [rows((3, 2, 4, 4, 144, 128), bf16)] + SpScatter.scratch(3, 144) + SpGather.sems(3)
        + [rows((2, 512, 256), bf16), rows((8192, 128), f32), rows((2, 64, 512), f32), half, half,
           rows((4, 4, 2, 256, 128), bf16), half]
        + [rows((2, 3, 4, 256, 128), bf16), rows((2, 3, 256, 128), bf16), rows((2, 3, 256, 128), bf16)]
        + [DMA((2, 3, 4)), DMA((2, 3, 4)), DMA((2, 3)), DMA((2, 3))]
        + [rows((8, 64, 1024), bf16), rows((2, 2, 4, 4, 32, 128), bf16), rows((2, 4, 4, 32, 128), bf16)]
        + wt_sum + wt_gather
        + SpScatter.scratch(3, 32) + SpGather.sems(3)
        + [rows((8, 8, 1024), f32), rows((4, 8, 1024), f32), rows((4, 8, 1024), f32),
           DMA((7,)), DMA((7,)), DMA((3,)), DMA((3,)), DMA((3,)), DMA((3,))],
        "backward", 30,
    )


def finish_kernel(sums_ref, ff_ref, out_in, gt_in, vec_ref, out_ref, gt_ref, gq_ref, gk_ref, gv_ref, go_ref, gg_ref, gu_ref, gd_ref,
                  ni_ref, nm_ref, qg_ref, kg_ref, wide, tall, big, ff, sems, load_sems):
    copies = []

    def write(src, dst):
        copies.append(pltpu.make_async_copy(src, dst, sems.at[len(copies)]))
        copies[-1].start()

    write(out_in, out_ref)
    write(gt_in, gt_ref)
    loads = [pltpu.make_async_copy(ff_ref.at[i], ff.at[i], load_sems.at[i]) for i in range(3)]
    for load in loads:
        load.start()

    def assemble(out, blocks, x, rows):
        for h in range(2):
            for y in range(4):
                columns = slice(h * 512 + y * 128, h * 512 + y * 128 + 128)
                out[x * rows:(x + 1) * rows, columns] = blocks[(h,) + spot(h, x, y)].astype(f32)

    for i, ref in enumerate((gg_ref, gu_ref, gd_ref)):
        loads[i].wait()
        for x in range(4):
            assemble(big.at[i], ff.at[i], x, 144)
            rows = pl.ds(x * 144, 144)
            write(big.at[i, rows], ref.at[rows])
    for i in range(3):
        for x in range(4):
            assemble(wide.at[i], sums_ref.at[i], x, 32)
    write(wide.at[2, 0:64], gk_ref)
    write(wide.at[2, 64:128], gv_ref)
    write(wide.at[0], go_ref)
    tall[...] = wide[1].T
    write(tall, gq_ref)
    ni_ref[...] = vec_ref[0:1, :]
    nm_ref[...] = vec_ref[1:2, :]
    qg_ref[...] = vec_ref[2:3, 0:64] + vec_ref[2:3, 64:128]
    kg_ref[...] = vec_ref[2:3, 128:192]
    for copy in copies:
        copy.wait()


def finish(sums, ff, output, grad_tokens, vec):
    hbm = pl.BlockSpec(memory_space=pl.ANY)
    rows = sds((576, 1024), f32)
    return pl.pallas_call(
        finish_kernel,
        out_shape=(sds((512, 1024), bf16), sds((512, 1024), bf16), sds((1024, 128), f32), sds((64, 1024), f32), sds((64, 1024), f32),
                   sds((128, 1024), f32), rows, rows, rows,
                   sds((1, 1024), f32), sds((1, 1024), f32), sds((1, 64), f32), sds((1, 64), f32)),
        in_specs=[vmem, hbm, vmem, vmem, vmem],
        out_specs=tuple([hbm] * 9 + [vmem] * 4),
        scratch_shapes=[pltpu.VMEM((3, 128, 1024), f32), pltpu.VMEM((1024, 128), f32), pltpu.VMEM((3, 576, 1024), f32), pltpu.VMEM((3, 2, 4, 4, 144, 128), bf16), DMA((18,)), DMA((3,))],
        compiler_params=pltpu.CompilerParams(vmem_limit_bytes=18 << 20),
        name="finish",
    )(sums, ff, output, grad_tokens, vec)


def body(tokens, norm_in, w_query, w_key, w_value, query_gain, key_gain, w_out, norm_mid, w_gate, w_up, w_down, cotangent, lengths):
    parts = lax.axis_size("sp")
    gains = jnp.concatenate([query_gain, query_gain, key_gain, key_gain, jnp.zeros((768,), f32)])
    pack = jnp.concatenate([norm_in[None], norm_mid[None], gains[None], jnp.zeros((5, 1024), f32)], axis=0)
    wkv = jnp.concatenate([w_key.T, w_value.T], axis=0)

    normed, q_proj, kv_proj, q, kv, cosine, sine = project(lengths, tokens, pack, w_query, wkv)
    kv_all, ext, qa, mix_f, mixed, normed_mid, mid_own, cot = forward(
        parts, lengths, q, kv, tokens, cotangent, w_out, pack
    )
    kv_all = kv_all.reshape(8192, 128)
    normed_mid = normed_mid.reshape(512, 1024)
    cotangent = cot.reshape(512, 1024)

    gate = jnp.dot(normed_mid, w_gate, preferred_element_type=f32)
    up_proj = jnp.dot(normed_mid, w_up, preferred_element_type=f32)
    sigmoid_gate = jax.nn.sigmoid(gate)
    act = (gate * sigmoid_gate * up_proj).astype(bf16)
    mlp_part = jnp.dot(act, w_down, preferred_element_type=f32).astype(bf16)
    d_act = jnp.einsum("td,fd->tf", cotangent, w_down, preferred_element_type=f32)
    d_gate = (d_act * up_proj * sigmoid_gate * (1.0 + gate * (1.0 - sigmoid_gate))).astype(bf16)
    d_up = (d_act * gate * sigmoid_gate).astype(bf16)
    d_mid_part = (
        jnp.einsum("tf,df->td", d_gate, w_gate, preferred_element_type=f32)
        + jnp.einsum("tf,df->td", d_up, w_up, preferred_element_type=f32)
    ).astype(bf16)
    grads = (
        jnp.einsum("tf,td->fd", d_gate, normed_mid, preferred_element_type=f32).astype(bf16),
        jnp.einsum("tf,td->fd", d_up, normed_mid, preferred_element_type=f32).astype(bf16),
        jnp.einsum("tf,td->fd", act, cotangent, preferred_element_type=f32).astype(bf16),
    )
    output, grad_tokens, sums, g_ff, vec = backward(
        parts,
        d_mid_part.reshape(8, 64, 1024), mlp_part.reshape(8, 64, 1024), mid_own, cot,
        pack, w_out, *(g.reshape(4, 144, 1024) for g in grads),
        qa, mix_f, kv_all, ext, mixed,
        q_proj, kv_proj, normed, w_query, wkv, cosine, sine, tokens.reshape(8, 64, 1024),
    )
    (output, grad_tokens, g_query, g_key, g_value, g_out, g_gate, g_up, g_down, g_norm_in, g_norm_mid, g_qg, g_kg) = finish(
        sums, g_ff, output.reshape(512, 1024), grad_tokens.reshape(512, 1024), vec
    )
    return (
        output, grad_tokens, g_norm_in.reshape(1024), g_query, g_key.T, g_value.T, g_qg.reshape(64), g_kg.reshape(64),
        g_out, g_norm_mid.reshape(1024), g_gate.T, g_up.T, g_down,
    )


def solution(mesh):
    placed = (
        P("sp", None), P(), P(None, "wt"), P(None, "wt"), P(None, "wt"), P(), P(), P("wt", None), P(),
        P(None, "wt"), P(None, "wt"), P("wt", None), P("sp", None), P(),
    )
    return jax.shard_map(
        body,
        mesh=mesh,
        in_specs=placed,
        out_specs=(
            P("sp", None), P("sp", None), P(), P(None, "wt"), P(None, "wt"), P(None, "wt"), P(), P(),
            P("wt", None), P(), P(None, "wt"), P(None, "wt"), P("wt", None),
        ),
        check_vma=False,
    )
```
